32 devices in a mesh: ctx: 16 (over z, y, x), head: 2 (over core).
Axes of the slice: x: 2, y: 2, z: 4, core: 2. Of those that a mesh axis runs over, the one named last changes fastest.
Arguments:
- inputs: bfloat16 [8192, 4096], P('ctx', 'head'), may hold values from -6 to 6
- w_in: bfloat16 [4096, 4096], P('ctx', 'head'), may hold values from -0.09375 to 0.09375
- b_rows: bfloat16 [8192, 128], P('ctx'), may hold values from -0.5 to 0.5
- c_rows: bfloat16 [8192, 128], P('ctx'), may hold values from -0.5 to 0.5
- log_decay: float32 [64, 8192], P('head', 'ctx'), may hold values from -2.09375 to 0, as said below
- skip_gain: float32 [64], P('head'), may hold values from 0.5 to 2
- grad_out: bfloat16 [8192, 4096], P('ctx', 'head'), may hold values from -6 to 6
Outputs:
- grad_inputs: bfloat16 [8192, 4096], P('ctx', 'head')
- grad_b: float32 [8192, 128], P('ctx')
- grad_c: float32 [8192, 128], P('ctx')
- grad_log_decay: float32 [64, 8192], P('head', 'ctx')
The draws below stay inside these ranges and needn't reach their ends.
Inputs may be any that keep to these rules, and one draw needn't show every extreme that they name: log_decay is negative.
All inputs are finite; a program needn't handle non-finite values.
Results may differ from the reference program's by a relative error of at most 0.017.
Values may be sent and summed in bfloat16 or wider, within the bound.
No kernel may reach another device: no remote copies, remote signals or barrier semaphores. Data moves between devices by JAX's collectives and lax.ppermute only.
A program may use at most 128 MiB of HBM per device.

```python
import math
import jax
import jax.numpy as jnp
from jax import lax

D = 4096
SSD_HEAD_COUNT = 64
P_SIZE = 64
N = 128
SPAN = 256
TOKEN_COUNT = 8192
N_HEAD = 2


def draw_log_decay(key, part):
    key = jax.random.fold_in(key, 17)
    random_subkeys = jax.random.split(key, 8)
    slow_cut = 0.4
    middle_cut = 0.75
    blocks = TOKEN_COUNT // SPAN
    class_draw = jax.random.uniform(random_subkeys[0], (SSD_HEAD_COUNT, 1))
    is_slow = class_draw < slow_cut
    is_middle = jnp.logical_and(class_draw >= slow_cut, class_draw < middle_cut)
    slow_rate = jnp.exp(jax.random.uniform(random_subkeys[1], (SSD_HEAD_COUNT, 1), minval=jnp.log(0.1), maxval=jnp.log(0.4))) / TOKEN_COUNT
    fast_rate = 1.0 / (SPAN * jnp.exp(jax.random.uniform(random_subkeys[2], (SSD_HEAD_COUNT, 1), minval=jnp.log(0.125), maxval=jnp.log(0.2))))
    middle_rate = 1.0 / (SPAN * jnp.exp(jax.random.uniform(random_subkeys[7], (SSD_HEAD_COUNT, 1), minval=jnp.log(0.4), maxval=jnp.log(0.65))))
    base_rate = jnp.where(is_slow, slow_rate, jnp.where(is_middle, middle_rate, fast_rate))
    factor_low = jnp.where(is_middle, jnp.log(0.75), jnp.log(0.5))
    factor_high = jnp.where(is_middle, jnp.log(1.5), jnp.log(2.0))
    factor_draw = jax.random.uniform(random_subkeys[3], (SSD_HEAD_COUNT, blocks, 1))
    block_factor = jnp.exp(factor_low[:, :, None] + factor_draw * (factor_high - factor_low)[:, :, None])
    token_factor = jax.random.uniform(random_subkeys[4], (SSD_HEAD_COUNT, blocks, SPAN), minval=0.5, maxval=1.5)
    decay_speeds = (base_rate[:, :, None] * block_factor * token_factor).reshape(SSD_HEAD_COUNT, TOKEN_COUNT)
    surge_location = jax.random.randint(random_subkeys[5], (SSD_HEAD_COUNT, 2, 1), 0, TOKEN_COUNT)
    token_offsets = lax.broadcasted_iota(jnp.int32, (SSD_HEAD_COUNT, 2, TOKEN_COUNT), 2)
    surge_length = jnp.log(jax.random.uniform(random_subkeys[6], (SSD_HEAD_COUNT, 2, 1), minval=0.5, maxval=0.8))
    surge_events = jnp.sum(jnp.where(token_offsets == surge_location, surge_length, 0.0), axis=1)
    return (surge_events - decay_speeds).astype(jnp.float32)


def steps_of(own_key, shape, cuts, low, high):
    level, own = 1.0, jax.random.fold_in(own_key, 6)
    for axis_at, shards_of in cuts:
        steps = jnp.exp(jax.random.uniform(jax.random.fold_in(own, axis_at), (shards_of,), jnp.float32, low / len(cuts), high / len(cuts)))
        level = level * jnp.repeat(steps, shape[axis_at] // shards_of).reshape([-1 if axis == axis_at else 1 for axis in range(len(shape))])
    return level


def centred(own_key, dims, scale, bound, cuts=(), dtype=jnp.bfloat16):
    result = scale * jax.random.normal(own_key, dims, jnp.float32)
    if cuts:
        result = result * steps_of(own_key, dims, cuts, -0.22, 0.18)
    return jnp.clip(result, -bound, bound).astype(dtype)


def setup_inputs(seed: int = 0) -> dict:
    arg_keys = jax.random.split(jax.random.key(seed), 8)
    inputs = centred(arg_keys[0], (TOKEN_COUNT, D), 1.0, 6.0, ((0, 16), (1, 2)))
    w_in = centred(arg_keys[1], (D, SSD_HEAD_COUNT * P_SIZE), D ** -0.5, 0.09375, ((0, 16), (1, 2)))
    b_rows = centred(arg_keys[2], (TOKEN_COUNT, N), 0.08, 0.5, ((0, 16),))
    c_rows = centred(arg_keys[3], (TOKEN_COUNT, N), 0.08, 0.5, ((0, 16),))
    log_decay = draw_log_decay(jax.random.fold_in(arg_keys[7], 71), 0)
    skip_gain = jnp.clip(jnp.exp(math.log(2.0) - 1.3862944 * jax.random.uniform(arg_keys[5], (SSD_HEAD_COUNT,), jnp.float32) ** steps_of(arg_keys[5], (SSD_HEAD_COUNT,), ((0, 2),), -0.2, 0.2)), 0.5, 2.0)
    grad_out = centred(arg_keys[6], (TOKEN_COUNT, SSD_HEAD_COUNT * P_SIZE), 1.0, 6.0, ((0, 16), (1, 2)))
    return dict(inputs=inputs, w_in=w_in, b_rows=b_rows, c_rows=c_rows, log_decay=log_decay, skip_gain=skip_gain, grad_out=grad_out)


exact_precision = lax.Precision.HIGHEST

def span_state(x_rows, b_rows, log_decay):
    length = x_rows.shape[0]
    heads = log_decay.shape[0]
    x_heads = x_rows.reshape(length, heads, -1)
    running = jnp.cumsum(log_decay, axis=1)
    to_end = jnp.exp(running[:, -1:] - running)
    own_state = jnp.einsum('shp,sn->hpn', x_heads * to_end.T[:, :, None], b_rows, precision=exact_precision)
    return (jnp.exp(running[:, -1]), own_state)

def span_forward(x_rows, b_rows, c_rows, log_decay, state_in, skip_gain):
    length = x_rows.shape[0]
    heads = log_decay.shape[0]
    x_heads = x_rows.reshape(length, heads, -1)
    running = jnp.cumsum(log_decay, axis=1)
    later = lax.broadcasted_iota(jnp.int32, (length, length), 0)
    earlier = lax.broadcasted_iota(jnp.int32, (length, length), 1)
    causal = (later >= earlier)[None]
    spread = running[:, :, None] - running[:, None, :]
    kernel = jnp.where(causal, jnp.exp(jnp.where(causal, spread, 0.0)), 0.0)
    scores = jnp.dot(c_rows, b_rows.T, precision=exact_precision)
    inner = jnp.einsum('hts,shp->thp', kernel * scores[None], x_heads, precision=exact_precision)
    from_state = jnp.einsum('tn,hpn->thp', c_rows, state_in, precision=exact_precision)
    from_state = from_state * jnp.exp(running).T[:, :, None]
    outputs = inner + from_state + skip_gain[None, :, None] * x_heads
    retained, own_state = span_state(x_rows, b_rows, log_decay)
    state_out = retained[:, None, None] * state_in + own_state
    return (outputs.reshape(length, -1), state_out)

def boundary_grad(c_rows, log_decay, g_rows):
    length = g_rows.shape[0]
    heads = log_decay.shape[0]
    g_heads = g_rows.reshape(length, heads, -1)
    running = jnp.cumsum(log_decay, axis=1)
    return jnp.einsum('thp,tn->hpn', g_heads * jnp.exp(running).T[:, :, None], c_rows, precision=exact_precision)

def reference(inputs, w_in, b_rows, c_rows, log_decay, skip_gain, grad_out):
    x_rows = jnp.dot(inputs, w_in, preferred_element_type=jnp.float32).astype(jnp.bfloat16)
    x_float = lax.optimization_barrier(x_rows).astype(jnp.float32)
    blocks = TOKEN_COUNT // SPAN
    x_blocks = x_float.reshape(blocks, SPAN, SSD_HEAD_COUNT * P_SIZE)
    b_blocks = b_rows.astype(jnp.float32).reshape(blocks, SPAN, N)
    c_blocks = c_rows.astype(jnp.float32).reshape(blocks, SPAN, N)
    g_blocks = grad_out.astype(jnp.float32).reshape(blocks, SPAN, SSD_HEAD_COUNT * P_SIZE)
    d_blocks = log_decay.reshape(SSD_HEAD_COUNT, blocks, SPAN).transpose(1, 0, 2)

    def state_of(element):
        return span_state(element[0], element[1], element[2])
    retained, own_states = lax.map(state_of, (x_blocks, b_blocks, d_blocks))
    empty = jnp.zeros((SSD_HEAD_COUNT, P_SIZE, N), jnp.float32)

    def advance(state, element):
        return (element[0][:, None, None] * state + element[1], state)
    _, states_in = lax.scan(advance, empty, (retained, own_states))

    def grad_of(element):
        return boundary_grad(element[0], element[1], element[2])
    state_grads = lax.map(grad_of, (c_blocks, d_blocks, g_blocks))

    def retreat(state, element):
        return (element[1] + element[0][:, None, None] * state, state)
    _, states_out_grad = lax.scan(retreat, empty, (retained, state_grads), reverse=True)

    def block_grads(element):
        x_block, b_block, c_block, d_block, state_in, g_block, state_grad_out = element

        def local_forward(x_value, b_value, c_value, d_value):
            return span_forward(x_value, b_value, c_value, d_value, state_in, skip_gain)
        _, pullback = jax.vjp(local_forward, x_block, b_block, c_block, d_block)
        return pullback((g_block, state_grad_out))
    grad_x, grad_b, grad_c, grad_d = lax.map(block_grads, (x_blocks, b_blocks, c_blocks, d_blocks, states_in, g_blocks, states_out_grad))
    grad_x_rows = grad_x.reshape(TOKEN_COUNT, SSD_HEAD_COUNT * P_SIZE).astype(jnp.bfloat16)
    columns = SSD_HEAD_COUNT * P_SIZE // N_HEAD
    summed = jnp.zeros((TOKEN_COUNT, D), jnp.float32)
    for head_group in range(N_HEAD):
        grad_part = grad_x_rows[:, head_group * columns:(head_group + 1) * columns]
        weight_part = w_in[:, head_group * columns:(head_group + 1) * columns]
        product = lax.dot_general(grad_part, weight_part, (((1,), (1,)), ((), ())), preferred_element_type=jnp.float32)
        summed = summed + product.astype(jnp.bfloat16).astype(jnp.float32)
    grad_inputs = summed.astype(jnp.bfloat16)
    grad_log_decay = grad_d.transpose(1, 0, 2).reshape(SSD_HEAD_COUNT, TOKEN_COUNT)
    return (grad_inputs, grad_b.reshape(TOKEN_COUNT, N), grad_c.reshape(TOKEN_COUNT, N), grad_log_decay)
```

```python
import functools

import jax
import jax.numpy as jnp
from jax import lax
from jax.experimental import pallas as pl
from jax.experimental.pallas import tpu as pltpu
from jax.sharding import PartitionSpec as P

SPAN = 256
HALF = SPAN // 2
P_SIZE = 64
GROUP = 8
WIDE = GROUP * P_SIZE
LOG2E = 1.4426950408889634
NEVER = -1e30

F32 = jnp.float32
BF16 = jnp.bfloat16
EXACT = lax.Precision.HIGHEST


def dot(a, b, dims, precision=None):
    return lax.dot_general(a, b, (dims, ((), ())), precision=precision, preferred_element_type=F32)


def mm(a, b, precision=None):
    return dot(a, b, ((1,), (0,)), precision)


def iota(shape, dim):
    return lax.broadcasted_iota(jnp.int32, shape, dim)


def one_hot(dtype):
    return (iota((GROUP, WIDE), 0) == iota((GROUP, WIDE), 1) // P_SIZE).astype(dtype)


def not_before():
    return (iota((SPAN, SPAN), 0) >= iota((SPAN, SPAN), 1)).astype(F32)


def before():
    return (iota((SPAN, SPAN), 0) < iota((SPAN, SPAN), 1)).astype(F32)


def same():
    return (iota((SPAN, SPAN), 0) == iota((SPAN, SPAN), 1)).astype(F32)


def first_head():
    return iota((SPAN, 2 * P_SIZE), 1) < P_SIZE


def pair_columns(columns, pair):
    shape = (columns.shape[0], 2 * P_SIZE)
    left = jnp.broadcast_to(columns[:, 2 * pair : 2 * pair + 1], shape)
    right = jnp.broadcast_to(columns[:, 2 * pair + 1 : 2 * pair + 2], shape)
    return jnp.where(iota(shape, 1) < P_SIZE, left, right)


def spread_columns(columns):
    return jnp.concatenate([pair_columns(columns, pair) for pair in range(GROUP // 2)], axis=1)


def thirds(value):
    high = value.astype(BF16).astype(F32)
    middle = (value - high).astype(BF16).astype(F32)
    return high, middle, value - high - middle


def sum_over(value, mask):
    rows = value.shape[0]
    parts = mm(jnp.concatenate(thirds(value), axis=0).astype(BF16), mask.astype(BF16))
    return parts[:rows] + parts[rows : 2 * rows] + parts[2 * rows :]


def decay_kernel(d_ref, g_ref, c_ref, r_ref, rt_ref, a_ref, gt_ref):
    row_sums = sum_over(d_ref[...] * LOG2E, 1.0 - not_before() + same())
    r_ref[...] = row_sums
    padded = jnp.concatenate([row_sums, jnp.zeros((2 * P_SIZE - GROUP, SPAN), F32)], axis=0)
    running = padded.T[:, :GROUP]
    rt_ref[0] = running
    growth = jnp.exp2(spread_columns(running))
    a_ref[0] = jnp.broadcast_to(growth[SPAN - 1 : SPAN], (8, WIDE))
    scaled = (g_ref[...].astype(F32) * growth).astype(BF16)
    gt_ref[0] = dot(c_ref[...], scaled, ((0,), (0,)))


def grad_x_kernel(r_ref, rt_ref, g_ref, b_ref, c_ref, q_ref, skip_ref, out_ref):
    b = b_ref[...]
    scores = dot(b, c_ref[...], ((1,), (1,)))
    running = r_ref[...]
    columns = rt_ref[0]
    top_keep = iota((HALF, SPAN), 1) >= iota((HALF, SPAN), 0)
    low_keep = iota((HALF, HALF), 1) >= iota((HALF, HALF), 0)
    to_end = jnp.exp2(spread_columns(columns[SPAN - 1 : SPAN] - columns))
    from_state = mm(b, q_ref[0]) * to_end
    for pair in range(GROUP // 2):
        lanes = slice(pair * 2 * P_SIZE, (pair + 1) * 2 * P_SIZE)
        g = g_ref[:, lanes]
        parts = []
        for head in (2 * pair, 2 * pair + 1):
            row = running[head : head + 1]
            top = jnp.where(top_keep, row - columns[:HALF, head : head + 1], NEVER)
            low = jnp.where(low_keep, row[:, HALF:] - columns[HALF:, head : head + 1], NEVER)
            top = (jnp.exp2(top) * scores[:HALF]).astype(BF16)
            low = (jnp.exp2(low) * scores[HALF:, HALF:]).astype(BF16)
            parts.append(jnp.concatenate([mm(top, g), mm(low, g[HALF:])], axis=0))
        inner = jnp.where(first_head(), parts[0], parts[1])
        total = inner + skip_ref[:, lanes] * g.astype(F32) + from_state[:, lanes]
        out_ref[:, lanes] = total.astype(BF16)


def arrange_kernel(unit, order_ref, f_ref, out_ref):
    for index in range(f_ref.shape[1] // unit):
        source = pl.ds(pl.multiple_of(order_ref[index] * unit, 128), unit)
        out_ref[:, index * unit : (index + 1) * unit] = f_ref[:, source]


def fetch(arrays, places, buffer, sems):
    copies = []
    at = 0
    for index, (ref, column) in enumerate(zip(arrays, places)):
        rows = ref.shape[0]
        source = ref.at[:, pl.ds(column, buffer.shape[1])]
        copy = pltpu.make_async_copy(source, buffer.at[pl.ds(at, rows)], sems.at[index])
        copy.start()
        copies.append(copy)
        at += rows
    return copies


def bundles(count):
    return [range(at, min(at + PLANE, count)) for at in range(0, count, PLANE)]


def forward_kernel(places, f_ref, rt_ref, b_ref, *refs):
    count = len(places)
    arrays, (x_ref, e_ref, buffer, sems) = refs[:count], refs[count:]
    copies = fetch(arrays, places, buffer, sems)
    rows = arrays[0].shape[0]
    total = None
    for bundle in bundles(count):
        for index in bundle:
            copies[index].wait()
        deep = slice(bundle[0] * rows, (bundle[-1] + 1) * rows)
        term = mm(f_ref[:, deep], buffer[deep])
        total = term if total is None else total + term
    x = total.astype(BF16)
    x_ref[...] = x
    for k in range(e_ref.shape[0]):
        rows = slice(k * SPAN, (k + 1) * SPAN)
        for group in range(rt_ref.shape[0]):
            lanes = slice(group * WIDE, (group + 1) * WIDE)
            columns = rt_ref[group, rows]
            to_end = jnp.exp2(spread_columns(columns[SPAN - 1 : SPAN] - columns))
            scaled = (x[rows, lanes].astype(F32) * to_end).astype(BF16)
            e_ref[k, :, lanes] = dot(b_ref[rows], scaled, ((0,), (0,)))


def product_kernel(places, has_before, order_ref, g_ref, *refs):
    count = len(places)
    arrays, refs = refs[:count], refs[count:]
    if has_before:
        before_ref, refs = refs[0], refs[1:]
    out_ref, buffer, slots, sems, out_sems = refs[:5]
    copies = fetch(arrays, places, buffer, sems)
    rows = arrays[0].shape[0]
    where = [pl.ds(pl.multiple_of(order_ref[index] * rows, 128), rows) for index in range(count)]
    if has_before:
        before_slots, before_sems = refs[5:]
        before = []
        for index in range(count):
            source = before_ref.at[:, where[index]]
            copy = pltpu.make_async_copy(source, before_slots.at[index], before_sems.at[index])
            copy.start()
            before.append(copy)
    g = g_ref[...]
    stores = []
    for bundle in bundles(count):
        for index in bundle:
            copies[index].wait()
        product = dot(g, buffer[bundle[0] * rows : (bundle[-1] + 1) * rows], ((1,), (1,)))
        for index in bundle:
            part = product[:, (index - bundle[0]) * rows : (index - bundle[0] + 1) * rows]
            if has_before:
                before[index].wait()
                part = part + before_slots[index].astype(F32)
            slots[index] = part.astype(BF16)
            store = pltpu.make_async_copy(
                slots.at[index], out_ref.at[:, where[index]], out_sems.at[index]
            )
            store.start()
            stores.append(store)
    for store in stores:
        store.wait()


def after_kernel(*refs):
    pass


def inner_kernel(
    r_ref, rt_ref, g_ref, x_ref, b_ref, c_ref, q_ref, *refs
):
    d_ref, grad_b_ref, grad_c_ref, sum_ref = refs[-4:]
    so_far = refs[:-4]
    step = pl.program_id(1)
    b = b_ref[...]
    c = c_ref[...]
    scores = dot(b, c, ((1,), (1,)))
    running = r_ref[...]
    columns = rt_ref[0]
    top_keep = iota((HALF, SPAN), 1) >= iota((HALF, SPAN), 0)
    low_keep = iota((HALF, HALF), 1) >= iota((HALF, HALF), 0)

    @pl.when(step == 0)
    def _():
        sum_ref[...] = jnp.zeros_like(sum_ref)
        grad_b_ref[...] = so_far[0][...] if so_far else jnp.zeros_like(grad_b_ref)

    rows = []
    across = jnp.zeros((SPAN, 2 * P_SIZE), F32)
    lane = iota((SPAN, 2 * P_SIZE), 1)
    top_sum = sum_ref[:HALF]
    low_sum = sum_ref[HALF:, HALF:]
    for pair in range(GROUP // 2):
        lanes = slice(pair * 2 * P_SIZE, (pair + 1) * 2 * P_SIZE)
        g = g_ref[:, lanes]
        x = x_ref[:, lanes]
        for head in (2 * pair, 2 * pair + 1):
            mine = (lane < P_SIZE) if head == 2 * pair else (lane >= P_SIZE)
            x_head = jnp.where(mine, x, jnp.zeros_like(x))
            row = running[head : head + 1]
            top = jnp.where(top_keep, row - columns[:HALF, head : head + 1], NEVER)
            low = jnp.where(low_keep, row[:, HALF:] - columns[HALF:, head : head + 1], NEVER)
            top = jnp.exp2(top) * dot(x_head[:HALF], g, ((1,), (1,)))
            low = jnp.exp2(low) * dot(x_head[HALF:], g[HALF:], ((1,), (1,)))
            top_sum = top_sum + top
            low_sum = low_sum + low
            top = top * scores[:HALF]
            low = low * scores[HALF:, HALF:]
            top_row = jnp.sum(top, axis=0, keepdims=True)
            low_row = jnp.sum(low, axis=0, keepdims=True)
            rows.append(jnp.concatenate([top_row[:, :HALF], top_row[:, HALF:] + low_row], axis=1))
            column = jnp.concatenate(
                [jnp.sum(top, axis=1, keepdims=True), jnp.sum(low, axis=1, keepdims=True)], axis=0
            )
            across = jnp.where(lane == head, column, across)
    sum_ref[:HALF] = top_sum
    sum_ref[HALF:, HALF:] = low_sum
    difference = jnp.concatenate(rows, axis=0) - across.T[:GROUP]
    to_end = jnp.exp2(spread_columns(columns[SPAN - 1 : SPAN] - columns))
    scaled = x_ref[...].astype(F32) * to_end
    ends = dot(one_hot(BF16), (scaled * mm(b, q_ref[0])).astype(BF16), ((1,), (1,)))
    d_ref[...] = sum_over(difference, not_before()) + sum_over(ends, before())
    grad_b_ref[...] += dot(scaled.astype(BF16), q_ref[0], ((1,), (1,)))

    @pl.when(step == pl.num_programs(1) - 1)
    def _():
        total = sum_ref[...].astype(BF16)
        grad_b_ref[...] += mm(total, c)
        part = dot(total, b, ((0,), (0,)))
        grad_c_ref[...] = part + so_far[1][...] if so_far else part


def state_kernel(
    rt_ref, g_ref, c_ref, s_ref, e_ref, q_ref, a_ref, d_part_ref, c_part_ref, d_ref, grad_c_ref, held
):
    span, group = pl.program_id(0), pl.program_id(1)

    @pl.when(group == 0)
    def _():
        grad_c_ref[...] = c_part_ref[...]

    @pl.when(span == 0)
    def _():
        held[group] = s_ref[...]

    state = held[group]
    low = state.astype(BF16)
    scaled = g_ref[...].astype(F32) * jnp.exp2(spread_columns(rt_ref[0]))
    ends = dot(one_hot(BF16), (scaled * mm(c_ref[...], low)).astype(BF16), ((1,), (1,)))
    grad_c_ref[...] += dot(scaled.astype(BF16), low, ((1,), (1,)))
    product = jnp.sum(q_ref[0].astype(F32) * state, axis=0, keepdims=True) * a_ref[0, :1]
    high, middle, last = thirds(product)
    row = iota((8, WIDE), 0)
    stacked = jnp.where(row == 0, high, jnp.where(row == 1, middle, jnp.where(row == 2, last, 0.0)))
    kept = dot(one_hot(BF16), stacked.astype(BF16), ((1,), (1,)))
    kept = jnp.sum(kept, axis=1, keepdims=True)
    d_ref[...] = d_part_ref[...] + sum_over(ends, not_before()) + kept
    held[group] = e_ref[0] + a_ref[0, :1] * state


def call(kernel, grid, in_specs, out_specs, out_shape, flops, size, scratch=()):
    return pl.pallas_call(
        kernel,
        grid=grid,
        in_specs=in_specs,
        out_specs=out_specs,
        out_shape=out_shape,
        scratch_shapes=list(scratch),
        cost_estimate=pl.CostEstimate(flops=flops, bytes_accessed=size, transcendentals=0),
        compiler_params=pltpu.CompilerParams(
            dimension_semantics=("arbitrary",) * len(grid), vmem_limit_bytes=56 * 2**20
        ),
    )


def run_spec(at=0):
    return pl.BlockSpec((GROUP, SPAN), lambda k, h: (h + at, k))


def run_t_spec(at=0):
    return pl.BlockSpec((1, SPAN, GROUP), lambda k, h: (h + at, k, 0))


def rows_spec(at=0):
    return pl.BlockSpec((SPAN, WIDE), lambda k, h: (k, h + at))


def state_spec(at=0):
    return pl.BlockSpec((1, 2 * P_SIZE, WIDE), lambda k, h: (k, 0, h + at))


def kept_spec(at=0):
    return pl.BlockSpec((1, 8, WIDE), lambda k, h: (k, 0, h + at))


SHARED = pl.BlockSpec((SPAN, 2 * P_SIZE), lambda k, h: (k, 0))
GAIN = pl.BlockSpec((1, WIDE), lambda k, h: (0, h))
ANYWHERE = pl.BlockSpec(memory_space=pl.ANY)
SCALARS = pl.BlockSpec(memory_space=pltpu.SMEM)


def shape(*dims, dtype=F32):
    return jax.ShapeDtypeStruct(dims, dtype)


def swap(value, axis, bit):
    count = lax.axis_size(axis)
    return lax.ppermute(value, axis, [(i, i ^ bit) for i in range(count)])


def block_products(kept):
    count = lax.axis_size("ctx")
    place = lax.axis_index("ctx")
    steps = []
    before_me = jnp.ones_like(kept)
    after_me = jnp.ones_like(kept)
    bit = 1
    while bit < count:
        other = swap(kept, "ctx", bit)
        upper = (place & bit) != 0
        steps.append((bit, upper, kept, other, before_me, after_me))
        before_me = jnp.where(upper, before_me * other, before_me)
        after_me = jnp.where(upper, after_me, after_me * other)
        kept = kept * other
        bit *= 2
    return steps


def scan_states(total, steps, reverse):
    entering = jnp.zeros_like(total)
    for bit, upper, kept, other, before_me, after_me in steps:
        got = swap(total.astype(BF16), "ctx", bit).astype(F32)
        if reverse:
            entering = entering + jnp.where(upper, 0.0, after_me) * got
            total = jnp.where(upper, got + other * total, total + kept * got)
        else:
            entering = entering + jnp.where(upper, before_me, 0.0) * got
            total = jnp.where(upper, kept * got + total, other * total + got)
    return entering


def head_sum(value):
    bit = 1
    while bit < lax.axis_size("head"):
        value = value.astype(BF16)
        value = value.astype(F32) + swap(value, "head", bit).astype(F32)
        bit *= 2
    return value


def head_scatter(product):
    count = lax.axis_size("head")
    if count != 2:
        return lax.psum_scatter(product, "head", scatter_dimension=1, tiled=True)
    half = product.shape[1] // 2
    got = swap(product[:, :half], "head", 1)
    return (product[:, half:].astype(F32) + got.astype(F32)).astype(BF16)


PLANE = 4


def after(value, *tokens):
    return pl.pallas_call(
        after_kernel,
        in_specs=[ANYWHERE] * (1 + len(tokens)),
        out_specs=ANYWHERE,
        out_shape=shape(*value.shape, dtype=value.dtype),
        input_output_aliases={0: 0},
        cost_estimate=pl.CostEstimate(flops=0, bytes_accessed=0, transcendentals=0),
    )(value, *tokens)


def shift(value, by):
    count = lax.axis_size("ctx")
    return lax.ppermute(value, "ctx", [(i, (i + PLANE * by) % count) for i in range(count)])


def gather_layered(w, sizes):
    place = lax.axis_index("ctx")
    layers = lax.axis_size("ctx") // PLANE
    layer, spot = place // PLANE, place % PLANE
    turns = (1, 3, 2)
    own_x = swap(w, "ctx", 1)
    own_y = swap(w, "ctx", 2)
    own_across = swap(own_y, "ctx", 1)
    chunks = []
    tokens = ()
    at = 0
    for size in sizes:
        part = w[:, at * P_SIZE : (at + size) * P_SIZE]
        if tokens:
            part = after(part, tokens[0])
        arrays = [w, own_x, own_y, own_across]
        places = [at * P_SIZE] * PLANE + [0] * (PLANE * len(turns))
        moved = [shift(part, by) for by in turns]
        if tokens:
            moved = [after(value, *tokens) for value in moved]
        for index, value in enumerate(moved):
            value_x = swap(value, "ctx", 1)
            value_y = swap(value, "ctx", 2)
            if index == 1:
                across = swap(value_y, "ctx", 1)
            else:
                across = swap(value_x, "ctx", 2)
            arrays += [value, value_x, value_y, across]
        tokens = (arrays[PLANE], arrays[-3], arrays[-2])
        chunks.append((arrays, places))
        at += size
    order = jnp.stack(
        [
            (layer + layers - k) % layers * PLANE + (spot ^ flip)
            for k in (0,) + turns
            for flip in range(PLANE)
        ]
    )
    return chunks, order.astype(jnp.int32)


def gather_plain(w, sizes):
    chunks = []
    at = 0
    for size in sizes:
        part = w[:, at * P_SIZE : (at + size) * P_SIZE]
        chunks.append(([lax.all_gather(part, "ctx", axis=0, tiled=True)], [0]))
        at += size
    return chunks, jnp.zeros((1,), jnp.int32)


def gather_weight(w, sizes):
    if lax.axis_size("ctx") == 4 * PLANE and w.shape[0] % 256 == 0:
        return gather_layered(w, sizes)
    return gather_plain(w, sizes)


def local(inputs, w_in, b_rows, c_rows, log_decay, skip_gain, grad_out):
    length, columns = grad_out.shape
    heads = log_decay.shape[0]
    spans = length // SPAN
    groups = heads // GROUP
    n = b_rows.shape[1]
    grid = (spans, groups)

    sizes = (heads // 2, heads // 2) if heads % (2 * GROUP) == 0 else (heads,)
    chunks, order = gather_weight(w_in, sizes)
    features = lax.all_gather(inputs, "head", axis=1, tiled=True)
    width = features.shape[1]
    unit = width // order.shape[0]
    features = call(
        functools.partial(arrange_kernel, unit),
        (1,),
        [SCALARS, pl.BlockSpec((length, width), lambda h: (0, 0))],
        pl.BlockSpec((length, width), lambda h: (0, 0)),
        shape(length, width, dtype=BF16),
        0,
        4 * length * width,
    )(order, features)

    running, running_t, kept, own_grads = call(
        decay_kernel,
        grid,
        [run_spec(), rows_spec(), SHARED],
        [run_spec(), run_t_spec(), kept_spec(), state_spec()],
        [
            shape(heads, length),
            shape(groups, length, GROUP),
            shape(spans, 8, columns),
            shape(spans, n, columns),
        ],
        2 * length * columns * n,
        6 * length * columns,
    )(log_decay, grad_out, c_rows)

    kept_total = kept[0, :1]
    for k in range(1, spans):
        kept_total = kept_total * kept[k, :1]
    steps = block_products(kept_total)

    total = own_grads[spans - 1]
    for k in range(spans - 2, -1, -1):
        total = own_grads[k] + kept[k, :1] * total
    leaving = [scan_states(total, steps, True)]
    for k in range(spans - 1, 0, -1):
        leaving.insert(0, own_grads[k] + kept[k, :1] * leaving[0])
    leaving = jnp.stack([value.astype(BF16) for value in leaving])

    skip = jnp.repeat(skip_gain, P_SIZE)[None]
    grad_x = call(
        grad_x_kernel,
        grid,
        [run_spec(), run_t_spec(), rows_spec(), SHARED, SHARED, state_spec(), GAIN],
        rows_spec(),
        shape(length, columns, dtype=BF16),
        8 * length * columns * SPAN,
        6 * length * columns,
    )(running, running_t, grad_out, b_rows, c_rows, leaving, skip)

    two = lax.axis_size("head") == 2
    product_order = order
    if two:
        blocks = order.shape[0]
        product_order = (order + (1 - lax.axis_index("head")) * (blocks // 2)) % blocks

    grad_b = grad_c = product = None
    decay_parts = []
    at = 0
    for index, size in enumerate(sizes):
        wide = size * P_SIZE
        here = at // GROUP
        count = size // GROUP
        arrays, places = chunks[index]
        pieces = len(arrays)
        x, own_states = call(
            functools.partial(forward_kernel, places),
            (1,),
            [
                pl.BlockSpec((length, width), lambda h: (0, 0)),
                pl.BlockSpec((count, length, GROUP), lambda h, here=here // count: (here, 0, 0)),
                pl.BlockSpec((length, n), lambda h: (0, 0)),
            ]
            + [ANYWHERE] * pieces,
            [
                pl.BlockSpec((length, wide), lambda h: (0, 0)),
                pl.BlockSpec((spans, n, wide), lambda h: (0, 0, 0)),
            ],
            [shape(length, wide, dtype=BF16), shape(spans, n, wide)],
            2 * length * wide * width,
            2 * wide * width,
            [pltpu.VMEM((width, wide), BF16), pltpu.SemaphoreType.DMA((pieces,))],
        )(features, running_t, b_rows, *arrays)

        chunk = slice(at * P_SIZE, at * P_SIZE + wide)
        total = own_states[0]
        for k in range(1, spans):
            total = kept[k, :1, chunk] * total + own_states[k]
        cut = [step[:2] + tuple(value[:, chunk] for value in step[2:]) for step in steps]
        entering = scan_states(total, cut, False)

        so_far = () if grad_b is None else (grad_b, grad_c)
        decay_part, grad_b, grad_c = call(
            inner_kernel,
            (spans, count),
            [
                run_spec(here),
                run_t_spec(here),
                rows_spec(here),
                rows_spec(),
                SHARED,
                SHARED,
                state_spec(here),
            ]
            + [SHARED] * len(so_far),
            [run_spec(), SHARED, SHARED],
            [shape(size, length), shape(length, n), shape(length, n)],
            12 * length * wide * SPAN,
            6 * length * wide,
            [pltpu.VMEM((SPAN, SPAN), F32)],
        )(running, running_t, grad_out, x, b_rows, c_rows, leaving, *so_far)
        decay_part, grad_c = call(
            state_kernel,
            (spans, count),
            [
                run_t_spec(here),
                rows_spec(here),
                SHARED,
                pl.BlockSpec((n, WIDE), lambda k, h: (0, h)),
                state_spec(),
                state_spec(here),
                kept_spec(here),
                run_spec(),
                SHARED,
            ],
            [run_spec(), SHARED],
            [shape(size, length), shape(length, n)],
            4 * length * wide * n,
            6 * length * wide,
            [pltpu.VMEM((count, n, WIDE), F32)],
        )(running_t, grad_out, c_rows, entering, own_states, leaving, kept, decay_part, grad_c)
        decay_parts.append(decay_part)

        scratch = [
            pltpu.VMEM((width, wide), BF16),
            pltpu.VMEM((pieces, length, unit), BF16),
            pltpu.SemaphoreType.DMA((pieces,)),
            pltpu.SemaphoreType.DMA((pieces,)),
        ]
        earlier = ()
        if product is not None:
            earlier = (product,)
            scratch += [
                pltpu.VMEM((pieces, length, unit), BF16),
                pltpu.SemaphoreType.DMA((pieces,)),
            ]
        product = call(
            functools.partial(product_kernel, places, product is not None),
            (1,),
            [SCALARS, pl.BlockSpec((length, wide), lambda h, index=at // size: (0, index))]
            + [ANYWHERE] * (pieces + len(earlier)),
            ANYWHERE,
            shape(length, width, dtype=BF16),
            2 * length * wide * width,
            2 * wide * width,
            scratch,
        )(product_order, grad_x, *arrays, *earlier)
        at += size

    if two and order.shape[0] == 1:
        product = jnp.roll(product, (1 - lax.axis_index("head")) * (width // 2), axis=1)
    grad_inputs = head_scatter(product)
    return (grad_inputs, head_sum(grad_b), head_sum(grad_c), jnp.concatenate(decay_parts, axis=0))


def solution(mesh):
    in_specs = (
        P("ctx", "head"),
        P("ctx", "head"),
        P("ctx", None),
        P("ctx", None),
        P("head", "ctx"),
        P("head"),
        P("ctx", "head"),
    )
    out_specs = (P("ctx", "head"), P("ctx", None), P("ctx", None), P("head", "ctx"))
    return jax.shard_map(local, mesh=mesh, in_specs=in_specs, out_specs=out_specs, check_vma=False)
```

```python
import functools

import jax
import jax.numpy as jnp
from jax import lax
from jax.experimental import pallas as pl
from jax.experimental.pallas import tpu as pltpu
from jax.sharding import PartitionSpec as P

SPAN = 256
HALF = SPAN // 2
P_SIZE = 64
GROUP = 8
WIDE = GROUP * P_SIZE
LOG2E = 1.4426950408889634
NEVER = -1e30

F32 = jnp.float32
BF16 = jnp.bfloat16
EXACT = lax.Precision.HIGHEST


def dot(a, b, dims, precision=None):
    return lax.dot_general(a, b, (dims, ((), ())), precision=precision, preferred_element_type=F32)


def mm(a, b, precision=None):
    return dot(a, b, ((1,), (0,)), precision)


def iota(shape, dim):
    return lax.broadcasted_iota(jnp.int32, shape, dim)


def one_hot(dtype):
    return (iota((GROUP, WIDE), 0) == iota((GROUP, WIDE), 1) // P_SIZE).astype(dtype)


def not_before():
    return (iota((SPAN, SPAN), 0) >= iota((SPAN, SPAN), 1)).astype(F32)


def before():
    return (iota((SPAN, SPAN), 0) < iota((SPAN, SPAN), 1)).astype(F32)


def same():
    return (iota((SPAN, SPAN), 0) == iota((SPAN, SPAN), 1)).astype(F32)


def first_head():
    return iota((SPAN, 2 * P_SIZE), 1) < P_SIZE


def pair_columns(columns, pair):
    shape = (columns.shape[0], 2 * P_SIZE)
    left = jnp.broadcast_to(columns[:, 2 * pair : 2 * pair + 1], shape)
    right = jnp.broadcast_to(columns[:, 2 * pair + 1 : 2 * pair + 2], shape)
    return jnp.where(iota(shape, 1) < P_SIZE, left, right)


def spread_columns(columns):
    return jnp.concatenate([pair_columns(columns, pair) for pair in range(GROUP // 2)], axis=1)


def thirds(value):
    high = value.astype(BF16).astype(F32)
    middle = (value - high).astype(BF16).astype(F32)
    return high, middle, value - high - middle


def sum_over(value, mask):
    rows = value.shape[0]
    parts = mm(jnp.concatenate(thirds(value), axis=0).astype(BF16), mask.astype(BF16))
    return parts[:rows] + parts[rows : 2 * rows] + parts[2 * rows :]


def decay_kernel(d_ref, g_ref, c_ref, r_ref, rt_ref, a_ref, gt_ref):
    row_sums = sum_over(d_ref[...] * LOG2E, 1.0 - not_before() + same())
    r_ref[...] = row_sums
    padded = jnp.concatenate([row_sums, jnp.zeros((2 * P_SIZE - GROUP, SPAN), F32)], axis=0)
    running = padded.T[:, :GROUP]
    rt_ref[0] = running
    growth = jnp.exp2(spread_columns(running))
    a_ref[0] = jnp.broadcast_to(growth[SPAN - 1 : SPAN], (8, WIDE))
    scaled = (g_ref[...].astype(F32) * growth).astype(BF16)
    gt_ref[0] = dot(c_ref[...], scaled, ((0,), (0,)))


def grad_x_kernel(r_ref, rt_ref, g_ref, b_ref, c_ref, q_ref, skip_ref, out_ref):
    b = b_ref[...]
    scores = dot(b, c_ref[...], ((1,), (1,)))
    running = r_ref[...]
    columns = rt_ref[0]
    top_keep = iota((HALF, SPAN), 1) >= iota((HALF, SPAN), 0)
    low_keep = iota((HALF, HALF), 1) >= iota((HALF, HALF), 0)
    to_end = jnp.exp2(spread_columns(columns[SPAN - 1 : SPAN] - columns))
    from_state = mm(b, q_ref[0]) * to_end
    for pair in range(GROUP // 2):
        lanes = slice(pair * 2 * P_SIZE, (pair + 1) * 2 * P_SIZE)
        g = g_ref[:, lanes]
        parts = []
        for head in (2 * pair, 2 * pair + 1):
            row = running[head : head + 1]
            top = jnp.where(top_keep, row - columns[:HALF, head : head + 1], NEVER)
            low = jnp.where(low_keep, row[:, HALF:] - columns[HALF:, head : head + 1], NEVER)
            top = (jnp.exp2(top) * scores[:HALF]).astype(BF16)
            low = (jnp.exp2(low) * scores[HALF:, HALF:]).astype(BF16)
            parts.append(jnp.concatenate([mm(top, g), mm(low, g[HALF:])], axis=0))
        inner = jnp.where(first_head(), parts[0], parts[1])
        total = inner + skip_ref[:, lanes] * g.astype(F32) + from_state[:, lanes]
        out_ref[:, lanes] = total.astype(BF16)


def forward_kernel(half_ref, own_ref, other_ref, w_ref, rt_ref, b_ref, x_ref, e_ref, total_ref):
    step = pl.program_id(1)

    @pl.when(step == 0)
    def _():
        total_ref[...] = jnp.zeros_like(total_ref)

    half = pl.num_programs(1) // 2

    @pl.when(step < half)
    def _():
        total_ref[...] += mm(own_ref[...], w_ref[...])

    @pl.when(step >= half)
    def _():
        total_ref[...] += mm(other_ref[...], w_ref[...])

    @pl.when(step == pl.num_programs(1) - 1)
    def _():
        x = total_ref[...].astype(BF16)
        x_ref[...] = x
        for k in range(e_ref.shape[0]):
            rows = slice(k * SPAN, (k + 1) * SPAN)
            columns = rt_ref[0, rows]
            to_end = jnp.exp2(spread_columns(columns[SPAN - 1 : SPAN] - columns))
            scaled = (x[rows].astype(F32) * to_end).astype(BF16)
            e_ref[k] = dot(b_ref[rows], scaled, ((0,), (0,)))


def product_kernel(has_before, has_other, half_ref, g_ref, w_ref, *refs):
    refs = list(refs)
    total = dot(g_ref[...], w_ref[...], ((1,), (1,)))
    if has_before:
        total = total + refs.pop(0)[...].astype(F32)
    if has_other:
        total = total.astype(BF16).astype(F32) + refs.pop(0)[...].astype(F32)
    refs[0][...] = total.astype(BF16)


def arrange_kernel(order_ref, own_ref, other_ref, out_ref, both_ref):
    half = own_ref.shape[1]
    both_ref[:, :half] = own_ref[...]
    both_ref[:, half:] = other_ref[...]
    unit = out_ref.shape[1] // order_ref.shape[0]
    for index in range(order_ref.shape[0]):
        source = pl.ds(pl.multiple_of(order_ref[index] * unit, 128), unit)
        out_ref[:, index * unit : (index + 1) * unit] = both_ref[:, source]


def fetch(arrays, columns, buffer, sems):
    copies = []
    for index, (ref, column) in enumerate(zip(arrays, columns)):
        rows = ref.shape[0]
        source = ref.at[:, pl.ds(column, buffer.shape[1])]
        target = buffer.at[pl.ds(index * rows, rows)]
        copy = pltpu.make_async_copy(source, target, sems.at[index])
        copy.start()
        copies.append(copy)
    return copies


def bundles(count):
    return [range(at, at + PLANE) for at in range(0, count, PLANE)]


def pieces_forward_kernel(columns_at, here, f_ref, rt_ref, b_ref, *refs):
    count = len(columns_at)
    arrays, (x_ref, e_ref, buffer, total_ref, features, sems, f_sems) = refs[:count], refs[count:]
    rows = arrays[0].shape[0]
    f_copies = []
    for index, bundle in enumerate(bundles(count)):
        deep = pl.ds(bundle[0] * rows, PLANE * rows)
        copy = pltpu.make_async_copy(f_ref.at[:, deep], features.at[:, deep], f_sems.at[index])
        copy.start()
        f_copies.append(copy)
    copies = fetch(arrays, columns_at, buffer, sems)
    groups = x_ref.shape[1] // WIDE
    for number, bundle in enumerate(bundles(count)):
        f_copies[number].wait()
        for index in bundle:
            copies[index].wait()
        deep = slice(bundle[0] * rows, (bundle[-1] + 1) * rows)
        for group in range(groups):
            lanes = slice(group * WIDE, (group + 1) * WIDE)
            term = mm(features[:, deep], buffer[deep, lanes])
            if number == 0:
                total_ref[:, lanes] = term
            else:
                total_ref[:, lanes] += term
    for group in range(groups):
        lanes = slice(group * WIDE, (group + 1) * WIDE)
        x = total_ref[:, lanes].astype(BF16)
        x_ref[:, lanes] = x
        for k in range(e_ref.shape[0]):
            part = slice(k * SPAN, (k + 1) * SPAN)
            columns = rt_ref[here + group, part]
            to_end = jnp.exp2(spread_columns(columns[SPAN - 1 : SPAN] - columns))
            scaled = (x[part].astype(F32) * to_end).astype(BF16)
            e_ref[k, :, lanes] = dot(b_ref[part], scaled, ((0,), (0,)))


def pieces_product_kernel(columns_at, last, order_ref, g_ref, *refs):
    count = len(columns_at)
    arrays, refs = refs[:count], refs[count:]
    if last:
        before_ref, away_ref, own_ref = refs[:3]
        buffer, slots, sems, out_sems, before_slots, before_sems = refs[3:]
    else:
        away_ref, buffer, slots, sems, out_sems = refs
    copies = fetch(arrays, columns_at, buffer, sems)
    rows = arrays[0].shape[0]
    half = count // 2
    before = []
    if last:
        for index in range(count):
            source = before_ref.at[:, pl.ds(pl.multiple_of(order_ref[index] * rows, 128), rows)]
            copy = pltpu.make_async_copy(source, before_slots.at[index], before_sems.at[index])
            copy.start()
            before.append(copy)
    g = g_ref[...]
    for bundle in bundles(count):
        for index in bundle:
            copies[index].wait()
        product = dot(g, buffer[bundle[0] * rows : (bundle[-1] + 1) * rows], ((1,), (1,)))
        for index in bundle:
            at = (index - bundle[0]) * rows
            part = product[:, at : at + rows]
            place = order_ref[index]
            if last:
                before[index].wait()
                part = part + before_slots[index].astype(F32)
            slots[index] = part.astype(BF16)
            if last:
                lanes = pl.ds(pl.multiple_of(place % half * rows, 128), rows)

                @pl.when(place < half)
                def _():
                    target = away_ref.at[:, lanes]
                    pltpu.make_async_copy(slots.at[index], target, out_sems.at[index]).start()

                @pl.when(place >= half)
                def _():
                    target = own_ref.at[:, lanes]
                    pltpu.make_async_copy(slots.at[index], target, out_sems.at[index]).start()
            else:
                target = away_ref.at[:, pl.ds(pl.multiple_of(place * rows, 128), rows)]
                pltpu.make_async_copy(slots.at[index], target, out_sems.at[index]).start()
    for index in range(count):
        target = away_ref.at[:, pl.ds(0, rows)]
        pltpu.make_async_copy(slots.at[index], target, out_sems.at[index]).wait()


def after_kernel(*refs):
    pass


def inner_kernel(
    r_ref, rt_ref, g_ref, x_ref, b_ref, c_ref, q_ref, *refs
):
    d_ref, grad_b_ref, grad_c_ref, sum_ref = refs[-4:]
    so_far = refs[:-4]
    step = pl.program_id(1)
    b = b_ref[...]
    c = c_ref[...]
    scores = dot(b, c, ((1,), (1,)))
    running = r_ref[...]
    columns = rt_ref[0]
    top_keep = iota((HALF, SPAN), 1) >= iota((HALF, SPAN), 0)
    low_keep = iota((HALF, HALF), 1) >= iota((HALF, HALF), 0)

    @pl.when(step == 0)
    def _():
        sum_ref[...] = jnp.zeros_like(sum_ref)
        grad_b_ref[...] = so_far[0][...] if so_far else jnp.zeros_like(grad_b_ref)

    rows = []
    across = jnp.zeros((SPAN, 2 * P_SIZE), F32)
    lane = iota((SPAN, 2 * P_SIZE), 1)
    top_sum = sum_ref[:HALF]
    low_sum = sum_ref[HALF:, HALF:]
    for pair in range(GROUP // 2):
        lanes = slice(pair * 2 * P_SIZE, (pair + 1) * 2 * P_SIZE)
        g = g_ref[:, lanes]
        x = x_ref[:, lanes]
        for head in (2 * pair, 2 * pair + 1):
            mine = (lane < P_SIZE) if head == 2 * pair else (lane >= P_SIZE)
            x_head = jnp.where(mine, x, jnp.zeros_like(x))
            row = running[head : head + 1]
            top = jnp.where(top_keep, row - columns[:HALF, head : head + 1], NEVER)
            low = jnp.where(low_keep, row[:, HALF:] - columns[HALF:, head : head + 1], NEVER)
            top = jnp.exp2(top) * dot(x_head[:HALF], g, ((1,), (1,)))
            low = jnp.exp2(low) * dot(x_head[HALF:], g[HALF:], ((1,), (1,)))
            top_sum = top_sum + top
            low_sum = low_sum + low
            top = top * scores[:HALF]
            low = low * scores[HALF:, HALF:]
            top_row = jnp.sum(top, axis=0, keepdims=True)
            low_row = jnp.sum(low, axis=0, keepdims=True)
            rows.append(jnp.concatenate([top_row[:, :HALF], top_row[:, HALF:] + low_row], axis=1))
            column = jnp.concatenate(
                [jnp.sum(top, axis=1, keepdims=True), jnp.sum(low, axis=1, keepdims=True)], axis=0
            )
            across = jnp.where(lane == head, column, across)
    sum_ref[:HALF] = top_sum
    sum_ref[HALF:, HALF:] = low_sum
    difference = jnp.concatenate(rows, axis=0) - across.T[:GROUP]
    to_end = jnp.exp2(spread_columns(columns[SPAN - 1 : SPAN] - columns))
    scaled = x_ref[...].astype(F32) * to_end
    ends = dot(one_hot(BF16), (scaled * mm(b, q_ref[0])).astype(BF16), ((1,), (1,)))
    d_ref[...] = sum_over(difference, not_before()) + sum_over(ends, before())
    grad_b_ref[...] += dot(scaled.astype(BF16), q_ref[0], ((1,), (1,)))

    @pl.when(step == pl.num_programs(1) - 1)
    def _():
        total = sum_ref[...].astype(BF16)
        grad_b_ref[...] += mm(total, c)
        part = dot(total, b, ((0,), (0,)))
        grad_c_ref[...] = part + so_far[1][...] if so_far else part


def state_kernel(
    rt_ref, g_ref, c_ref, s_ref, e_ref, q_ref, a_ref, d_part_ref, c_part_ref, d_ref, grad_c_ref, held
):
    span, group = pl.program_id(0), pl.program_id(1)

    @pl.when(group == 0)
    def _():
        grad_c_ref[...] = c_part_ref[...]

    @pl.when(span == 0)
    def _():
        held[group] = s_ref[...]

    state = held[group]
    low = state.astype(BF16)
    scaled = g_ref[...].astype(F32) * jnp.exp2(spread_columns(rt_ref[0]))
    ends = dot(one_hot(BF16), (scaled * mm(c_ref[...], low)).astype(BF16), ((1,), (1,)))
    grad_c_ref[...] += dot(scaled.astype(BF16), low, ((1,), (1,)))
    product = jnp.sum(q_ref[0].astype(F32) * state, axis=0, keepdims=True) * a_ref[0, :1]
    high, middle, last = thirds(product)
    row = iota((8, WIDE), 0)
    stacked = jnp.where(row == 0, high, jnp.where(row == 1, middle, jnp.where(row == 2, last, 0.0)))
    kept = dot(one_hot(BF16), stacked.astype(BF16), ((1,), (1,)))
    kept = jnp.sum(kept, axis=1, keepdims=True)
    d_ref[...] = d_part_ref[...] + sum_over(ends, not_before()) + kept
    held[group] = e_ref[0] + a_ref[0, :1] * state


def call(kernel, grid, in_specs, out_specs, out_shape, flops, size, scratch=()):
    return pl.pallas_call(
        kernel,
        grid=grid,
        in_specs=in_specs,
        out_specs=out_specs,
        out_shape=out_shape,
        scratch_shapes=list(scratch),
        cost_estimate=pl.CostEstimate(flops=flops, bytes_accessed=size, transcendentals=0),
        compiler_params=pltpu.CompilerParams(
            dimension_semantics=("arbitrary",) * len(grid), vmem_limit_bytes=48 * 2**20
        ),
    )


def run_spec(at=0):
    return pl.BlockSpec((GROUP, SPAN), lambda k, h: (h + at, k))


def run_t_spec(at=0):
    return pl.BlockSpec((1, SPAN, GROUP), lambda k, h: (h + at, k, 0))


def rows_spec(at=0):
    return pl.BlockSpec((SPAN, WIDE), lambda k, h: (k, h + at))


def state_spec(at=0):
    return pl.BlockSpec((1, 2 * P_SIZE, WIDE), lambda k, h: (k, 0, h + at))


def kept_spec(at=0):
    return pl.BlockSpec((1, 8, WIDE), lambda k, h: (k, 0, h + at))


SHARED = pl.BlockSpec((SPAN, 2 * P_SIZE), lambda k, h: (k, 0))
GAIN = pl.BlockSpec((1, WIDE), lambda k, h: (0, h))
ANYWHERE = pl.BlockSpec(memory_space=pl.ANY)
SCALARS = pl.BlockSpec(memory_space=pltpu.SMEM)


def shape(*dims, dtype=F32):
    return jax.ShapeDtypeStruct(dims, dtype)


def swap(value, axis, bit):
    count = lax.axis_size(axis)
    return lax.ppermute(value, axis, [(i, i ^ bit) for i in range(count)])


def block_products(kept):
    count = lax.axis_size("ctx")
    place = lax.axis_index("ctx")
    steps = []
    before_me = jnp.ones_like(kept)
    after_me = jnp.ones_like(kept)
    bit = 1
    while bit < count:
        other = swap(kept, "ctx", bit)
        upper = (place & bit) != 0
        steps.append((bit, upper, kept, other, before_me, after_me))
        before_me = jnp.where(upper, before_me * other, before_me)
        after_me = jnp.where(upper, after_me, after_me * other)
        kept = kept * other
        bit *= 2
    return steps


def gathered_products(running, spans):
    count = lax.axis_size("ctx")
    place = lax.axis_index("ctx")
    heads = running.shape[0]
    last = jnp.sum(running.reshape(heads, spans, SPAN)[:, :, SPAN - 1], axis=1)
    every = lax.all_gather(last, "ctx")
    index = jnp.arange(count)
    masks = []
    bits = []
    bit = 1
    while bit < count:
        start = place // bit * bit
        upper = (place & bit) != 0
        beside = jnp.where(upper, start - bit, start + bit)
        for low, high in (
            (start, start + bit),
            (beside, beside + bit),
            (start, place),
            (place + 1, start + bit),
        ):
            masks.append((index >= low) & (index < high))
        bits.append((bit, upper))
        bit *= 2
    products = jnp.exp2(mm(jnp.stack(masks).astype(F32), every, EXACT))
    products = jnp.repeat(products, P_SIZE, axis=1)
    steps = []
    for number, (bit, upper) in enumerate(bits):
        rows = [products[at : at + 1] for at in range(4 * number, 4 * number + 4)]
        steps.append((bit, upper, *rows))
    return steps


def scan_states(total, steps, reverse):
    entering = jnp.zeros_like(total)
    for bit, upper, kept, other, before_me, after_me in steps:
        got = swap(total.astype(BF16), "ctx", bit).astype(F32)
        if reverse:
            entering = entering + jnp.where(upper, 0.0, after_me) * got
            total = jnp.where(upper, got + other * total, total + kept * got)
        else:
            entering = entering + jnp.where(upper, before_me, 0.0) * got
            total = jnp.where(upper, kept * got + total, other * total + got)
    return entering


def head_sum(value):
    bit = 1
    while bit < lax.axis_size("head"):
        value = value.astype(BF16)
        value = value.astype(F32) + swap(value, "head", bit).astype(F32)
        bit *= 2
    return value


PLANE = 4


def after(values, *tokens):
    out = pl.pallas_call(
        after_kernel,
        in_specs=[ANYWHERE] * (len(values) + len(tokens)),
        out_specs=[ANYWHERE] * len(values),
        out_shape=[shape(*value.shape, dtype=value.dtype) for value in values],
        input_output_aliases={index: index for index in range(len(values))},
        cost_estimate=pl.CostEstimate(flops=0, bytes_accessed=0, transcendentals=0),
    )(*values, *tokens)
    return list(out)


def shift(value, by):
    count = lax.axis_size("ctx")
    return lax.ppermute(value, "ctx", [(i, (i + PLANE * by) % count) for i in range(count)])


def swap_x(value):
    return swap(value, "ctx", 1)


def swap_y(value):
    return swap(value, "ctx", 2)


def block_order():
    place = lax.axis_index("ctx")
    layers = lax.axis_size("ctx") // PLANE
    layer, spot = place // PLANE, place % PLANE
    order = [
        (layer + layers - k) % layers * PLANE + (spot ^ flip)
        for k in (0, 1, 3, 2)
        for flip in range(PLANE)
    ]
    return jnp.stack(order).astype(jnp.int32)


def gather_weight(w, sizes):
    ends = [sum(sizes[: j + 1]) * P_SIZE for j in range(len(sizes))]
    parts = [w[:, end - size * P_SIZE : end] for end, size in zip(ends, sizes)]
    return [lax.all_gather(part, "ctx", axis=0, tiled=True) for part in parts]


def forward(features, first, weight, running_t, b_rows, here):
    own, other = features
    length = own.shape[0]
    n = b_rows.shape[1]
    width, wide = weight.shape
    deep = width // 4
    spans = length // SPAN

    def depth(k, first_ref):
        return (k // 2 ^ first_ref[0]) * 2 + k % 2

    return pl.pallas_call(
        forward_kernel,
        grid_spec=pltpu.PrefetchScalarGridSpec(
            num_scalar_prefetch=1,
            grid=(wide // WIDE, 4),
            in_specs=[
                pl.BlockSpec((length, deep), lambda h, k, first_ref: (0, jnp.minimum(k, 1))),
                pl.BlockSpec((length, deep), lambda h, k, first_ref: (0, jnp.maximum(k - 2, 0))),
                pl.BlockSpec((deep, WIDE), lambda h, k, first_ref: (depth(k, first_ref), h)),
                pl.BlockSpec((1, length, GROUP), lambda h, k, first_ref: (h + here, 0, 0)),
                pl.BlockSpec((length, n), lambda h, k, first_ref: (0, 0)),
            ],
            out_specs=[
                pl.BlockSpec((length, WIDE), lambda h, k, first_ref: (0, h)),
                pl.BlockSpec((spans, n, WIDE), lambda h, k, first_ref: (0, 0, h)),
            ],
            scratch_shapes=[pltpu.VMEM((length, WIDE), F32)],
        ),
        out_shape=[shape(length, wide, dtype=BF16), shape(spans, n, wide)],
        cost_estimate=pl.CostEstimate(
            flops=2 * length * wide * width, bytes_accessed=2 * wide * width, transcendentals=0
        ),
        compiler_params=pltpu.CompilerParams(
            dimension_semantics=("arbitrary", "arbitrary"), vmem_limit_bytes=48 * 2**20
        ),
    )(first, own, other, weight, running_t, b_rows)


def multiply(grad_x, weight, at, half, halves, before=None, other=None):
    length = grad_x.shape[0]
    width, wide = weight.shape
    tiles = width // halves // WIDE
    tile = pl.BlockSpec((length, WIDE), lambda j, half_ref: (0, half_ref[0] * tiles + j))
    plain = pl.BlockSpec((length, WIDE), lambda j, half_ref: (0, j))
    in_specs = [
        pl.BlockSpec((length, wide), lambda j, half_ref: (0, at)),
        pl.BlockSpec((WIDE, wide), lambda j, half_ref: (half_ref[0] * tiles + j, 0)),
    ]
    operands = [grad_x, weight]
    if before is not None:
        in_specs.append(tile)
        operands.append(before)
    if other is not None:
        in_specs.append(plain)
        operands.append(other)
    return pl.pallas_call(
        functools.partial(product_kernel, before is not None, other is not None),
        grid_spec=pltpu.PrefetchScalarGridSpec(
            num_scalar_prefetch=1,
            grid=(tiles,),
            in_specs=in_specs,
            out_specs=plain,
        ),
        out_shape=shape(length, width // halves, dtype=BF16),
        cost_estimate=pl.CostEstimate(
            flops=2 * length * wide * width // halves,
            bytes_accessed=2 * wide * width // halves,
            transcendentals=0,
        ),
        compiler_params=pltpu.CompilerParams(
            dimension_semantics=("arbitrary",), vmem_limit_bytes=48 * 2**20
        ),
    )(half, *operands)


def pieces_forward(features, arrays, columns_at, wide, running_t, b_rows, here):
    length, width = features.shape
    n = b_rows.shape[1]
    spans = length // SPAN
    count = len(arrays)
    return call(
        functools.partial(pieces_forward_kernel, columns_at, here),
        (1,),
        [
            ANYWHERE,
            pl.BlockSpec(running_t.shape, lambda h: (0, 0, 0)),
            pl.BlockSpec((length, n), lambda h: (0, 0)),
        ]
        + [ANYWHERE] * count,
        [
            pl.BlockSpec((length, wide), lambda h: (0, 0)),
            pl.BlockSpec((spans, n, wide), lambda h: (0, 0, 0)),
        ],
        [shape(length, wide, dtype=BF16), shape(spans, n, wide)],
        2 * length * wide * width,
        2 * wide * width,
        [
            pltpu.VMEM((width, wide), BF16),
            pltpu.VMEM((length, wide), F32),
            pltpu.VMEM((length, width), BF16),
            pltpu.SemaphoreType.DMA((count,)),
            pltpu.SemaphoreType.DMA((count // PLANE,)),
        ],
    )(features, running_t, b_rows, *arrays)


def pieces_product(order, grad_x, arrays, columns_at, wide, at, before=None):
    length = grad_x.shape[0]
    count = len(arrays)
    rows = arrays[0].shape[0]
    width = rows * count
    last = before is not None
    scratch = [
        pltpu.VMEM((width, wide), BF16),
        pltpu.VMEM((count, length, rows), BF16),
        pltpu.SemaphoreType.DMA((count,)),
        pltpu.SemaphoreType.DMA((count,)),
    ]
    if last:
        scratch += [pltpu.VMEM((count, length, rows), BF16), pltpu.SemaphoreType.DMA((count,))]
    half = shape(length, width // 2, dtype=BF16)
    return call(
        functools.partial(pieces_product_kernel, columns_at, last),
        (1,),
        [SCALARS, pl.BlockSpec((length, wide), lambda h: (0, at))] + [ANYWHERE] * (count + last),
        [ANYWHERE, ANYWHERE] if last else ANYWHERE,
        [half, half] if last else shape(length, width, dtype=BF16),
        2 * length * wide * width,
        2 * wide * width,
        scratch,
    )(order, grad_x, *arrays, *([before] if last else []))


def local(inputs, w_in, b_rows, c_rows, log_decay, skip_gain, grad_out):
    groups = log_decay.shape[0] // GROUP
    layered = lax.axis_size("ctx") == 4 * PLANE and lax.axis_size("head") == 2
    if layered and groups >= 2 and w_in.shape[0] == 256:
        return local_layered(inputs, w_in, b_rows, c_rows, log_decay, skip_gain, grad_out)
    return local_plain(inputs, w_in, b_rows, c_rows, log_decay, skip_gain, grad_out)


def prepare(log_decay, grad_out, c_rows):
    length, columns = grad_out.shape
    heads = log_decay.shape[0]
    spans = length // SPAN
    groups = heads // GROUP
    n = c_rows.shape[1]
    return call(
        decay_kernel,
        (spans, groups),
        [run_spec(), rows_spec(), SHARED],
        [run_spec(), run_t_spec(), kept_spec(), state_spec()],
        [
            shape(heads, length),
            shape(groups, length, GROUP),
            shape(spans, 8, columns),
            shape(spans, n, columns),
        ],
        2 * length * columns * n,
        6 * length * columns,
    )(log_decay, grad_out, c_rows)


def scan_step(total, entering, step, reverse):
    bit, upper, kept, other, before_me, after_me = step
    got = swap(total.astype(BF16), "ctx", bit).astype(F32)
    if reverse:
        entering = entering + jnp.where(upper, 0.0, after_me) * got
        total = jnp.where(upper, got + other * total, total + kept * got)
    else:
        entering = entering + jnp.where(upper, before_me, 0.0) * got
        total = jnp.where(upper, kept * got + total, other * total + got)
    return total, entering


def inner(grid, here, wide, operands, so_far):
    length = operands[2].shape[0]
    n = operands[4].shape[1]
    specs = [
        run_spec(here),
        run_t_spec(here),
        rows_spec(here),
        rows_spec(),
        SHARED,
        SHARED,
        state_spec(here),
    ]
    return call(
        inner_kernel,
        grid,
        specs + [SHARED] * len(so_far),
        [run_spec(), SHARED, SHARED],
        [shape(wide // P_SIZE, length), shape(length, n), shape(length, n)],
        12 * length * wide * SPAN,
        6 * length * wide,
        [pltpu.VMEM((SPAN, SPAN), F32)],
    )(*operands, *so_far)


def state_terms(grid, here, wide, operands):
    length = operands[1].shape[0]
    n = operands[2].shape[1]
    return call(
        state_kernel,
        grid,
        [
            run_t_spec(here),
            rows_spec(here),
            SHARED,
            pl.BlockSpec((n, WIDE), lambda k, h: (0, h)),
            state_spec(),
            state_spec(here),
            kept_spec(here),
            run_spec(),
            SHARED,
        ],
        [run_spec(), SHARED],
        [shape(wide // P_SIZE, length), shape(length, n)],
        4 * length * wide * n,
        6 * length * wide,
        [pltpu.VMEM((grid[1], n, WIDE), F32)],
    )(*operands)


def local_layered(inputs, w_in, b_rows, c_rows, log_decay, skip_gain, grad_out):
    length, columns = grad_out.shape
    heads = log_decay.shape[0]
    spans = length // SPAN
    groups = heads // GROUP
    place = lax.axis_index("head").astype(jnp.int32)
    cut = columns - WIDE
    w_a, w_b = w_in[:, :cut], w_in[:, cut:]
    order = block_order()
    blocks = order.shape[0]
    width = blocks * w_in.shape[0]

    z1a, z3a = shift(w_a, 1), shift(w_a, 3)
    own_x, own_y = swap_x(w_in), swap_y(w_in)
    other = swap(inputs, "head", 1)
    running, running_t, kept, own_grads = prepare(log_decay, grad_out, c_rows)
    steps = gathered_products(running, spans)
    back = own_grads[spans - 1]
    for k in range(spans - 2, -1, -1):
        back = own_grads[k] + kept[k, :1] * back
    leaving = jnp.zeros_like(back)
    back = after([back], z1a, z3a)[0]

    w_a, z1a, z3a = after([w_a, z1a, z3a], own_x, own_y, back)
    z2a = shift(w_a, 2)
    x1a, y1a, x3a, y3a = swap_x(z1a), swap_y(z1a), swap_x(z3a), swap_y(z3a)
    back, leaving = scan_step(back, leaving, steps[0], True)

    z2a, x1a, y3a = after([z2a, x1a, y3a], y1a, x3a, back, other)
    x2a, y2a = swap_x(z2a), swap_y(z2a)
    d1a, d3a = swap_y(x1a), swap_x(y3a)
    back, leaving = scan_step(back, leaving, steps[1], True)

    own_y, x2a, w_b = after([own_y, x2a, w_b], y2a, d1a, d3a, back)
    own_d, d2a = swap_x(own_y), swap_y(x2a)
    z1b, z3b, z2b = shift(w_b, 1), shift(w_b, 3), shift(w_b, 2)
    back, leaving = scan_step(back, leaving, steps[2], True)

    order_own = (order + place * (blocks // 2)) % blocks
    features = call(
        arrange_kernel,
        (1,),
        [SCALARS] + [pl.BlockSpec((length, width // 2), lambda h: (0, 0))] * 2,
        pl.BlockSpec((length, width), lambda h: (0, 0)),
        shape(length, width, dtype=BF16),
        0,
        4 * length * width,
        [pltpu.VMEM((length, width), BF16)],
    )(order_own, inputs, other)

    z1b, z3b, z2b, d2a = after([z1b, z3b, z2b, d2a], own_d, back, features)
    x1b, x3b, x2b = swap_x(z1b), swap_x(z3b), swap_x(z2b)
    y1b, y3b, y2b = swap_y(z1b), swap_y(z3b), swap_y(z2b)
    back, leaving = scan_step(back, leaving, steps[3], True)
    arrays_a = [w_in, own_x, own_y, own_d, z1a, x1a, y1a, d1a, z3a, x3a, y3a, d3a]
    arrays_a += [z2a, x2a, y2a, d2a]
    at_a = [0] * len(arrays_a)
    x_a, states_a = pieces_forward(features, arrays_a, at_a, cut, running_t, b_rows, 0)

    leaving_all = [leaving]
    for k in range(spans - 1, 0, -1):
        leaving_all.insert(0, own_grads[k] + kept[k, :1] * leaving_all[0])
    leaving_all = jnp.stack([value.astype(BF16) for value in leaving_all])
    skip = jnp.repeat(skip_gain, P_SIZE)[None]
    grad_x = grad_rows(running, running_t, grad_out, b_rows, c_rows, leaving_all, skip)

    def forward_total(states, lanes):
        total = states[0]
        for k in range(1, spans):
            total = kept[k, :1, lanes] * total + states[k]
        return total

    def narrow(step, lanes):
        return step[:2] + tuple(value[:, lanes] for value in step[2:])

    lanes_a, lanes_b = slice(0, cut), slice(cut, columns)
    steps_a = [narrow(step, lanes_a) for step in steps]
    steps_b = [narrow(step, lanes_b) for step in steps]
    total_a = forward_total(states_a, lanes_a)
    entering_a = jnp.zeros_like(total_a)
    total_a, entering_a = scan_step(total_a, entering_a, steps_a[0], False)

    x1b, y3b, x2b, x_a, grad_x = after([x1b, y3b, x2b, x_a, grad_x], x3b, y1b, y2b, total_a)
    d1b, d3b, d2b = swap_y(x1b), swap_x(y3b), swap_y(x2b)
    total_a, entering_a = scan_step(total_a, entering_a, steps_a[1], False)

    shared = (running, running_t, grad_out)
    order_away = (order + (1 - place) * (blocks // 2)) % blocks
    grid_a, grid_b = (spans, groups - 1), (spans, 1)
    inner_a = shared + (x_a, b_rows, c_rows, leaving_all)
    decay_a, grad_b, grad_c = inner(grid_a, 0, cut, inner_a, ())
    product = pieces_product(order_away, grad_x, arrays_a, at_a, cut, 0)

    d1b, d3b, d2b = after([d1b, d3b, d2b], product, grad_b, total_a)
    arrays_b = [w_in, own_x, own_y, own_d, z1b, x1b, y1b, d1b, z3b, x3b, y3b, d3b]
    arrays_b += [z2b, x2b, y2b, d2b]
    at_b = [cut] * PLANE + [0] * (len(arrays_b) - PLANE)
    here = groups - 1
    x_b, states_b = pieces_forward(features, arrays_b, at_b, WIDE, running_t, b_rows, here)
    total_b = forward_total(states_b, lanes_b)
    entering_b = jnp.zeros_like(total_b)
    for step_a, step_b in zip(steps_a[2:] + [None] * 2, steps_b):
        if step_a is not None:
            total_a, entering_a = scan_step(total_a, entering_a, step_a, False)
        total_b, entering_b = scan_step(total_b, entering_b, step_b, False)
    inner_b = shared + (x_b, b_rows, c_rows, leaving_all)
    decay_b, grad_b, grad_c = inner(grid_b, here, WIDE, inner_b, (grad_b, grad_c))
    away, own = pieces_product(order_away, grad_x, arrays_b, at_b, WIDE, here, product)
    got = swap(away, "head", 1)
    grad_b = head_sum(grad_b)

    common = (running_t, grad_out, c_rows)
    state_a = common + (entering_a, states_a, leaving_all, kept, decay_a, grad_c)
    decay_a, grad_c = state_terms(grid_a, 0, cut, state_a)
    state_b = common + (entering_b, states_b, leaving_all, kept, decay_b, grad_c)
    decay_b, grad_c = state_terms(grid_b, here, WIDE, state_b)
    grad_inputs = (own.astype(F32) + got.astype(F32)).astype(BF16)
    grad_log_decay = jnp.concatenate([decay_a, decay_b], axis=0)
    return (grad_inputs, grad_b, head_sum(grad_c), grad_log_decay)


def grad_rows(running, running_t, grad_out, b_rows, c_rows, leaving, skip):
    length, columns = grad_out.shape
    return call(
        grad_x_kernel,
        (length // SPAN, running_t.shape[0]),
        [run_spec(), run_t_spec(), rows_spec(), SHARED, SHARED, state_spec(), GAIN],
        rows_spec(),
        shape(length, columns, dtype=BF16),
        8 * length * columns * SPAN,
        6 * length * columns,
    )(running, running_t, grad_out, b_rows, c_rows, leaving, skip)


def local_plain(inputs, w_in, b_rows, c_rows, log_decay, skip_gain, grad_out):
    length, columns = grad_out.shape
    heads = log_decay.shape[0]
    spans = length // SPAN
    groups = heads // GROUP
    n = b_rows.shape[1]
    grid = (spans, groups)

    sizes = (heads // 2, heads // 4, heads // 4) if heads % (4 * GROUP) == 0 else (heads,)
    weights = gather_weight(w_in, sizes)
    two = lax.axis_size("head") == 2
    place = lax.axis_index("head").astype(jnp.int32)[None]
    width = weights[0].shape[0]
    if two:
        features = (inputs, swap(inputs, "head", 1))
        first = place
    else:
        features = lax.all_gather(inputs, "head", axis=1, tiled=True)
        features = (features[:, : width // 2], features[:, width // 2 :])
        first = jnp.zeros((1,), jnp.int32)

    running, running_t, kept, own_grads = call(
        decay_kernel,
        grid,
        [run_spec(), rows_spec(), SHARED],
        [run_spec(), run_t_spec(), kept_spec(), state_spec()],
        [
            shape(heads, length),
            shape(groups, length, GROUP),
            shape(spans, 8, columns),
            shape(spans, n, columns),
        ],
        2 * length * columns * n,
        6 * length * columns,
    )(log_decay, grad_out, c_rows)

    kept_total = kept[0, :1]
    for k in range(1, spans):
        kept_total = kept_total * kept[k, :1]
    steps = block_products(kept_total)

    total = own_grads[spans - 1]
    for k in range(spans - 2, -1, -1):
        total = own_grads[k] + kept[k, :1] * total
    leaving = [scan_states(total, steps, True)]
    for k in range(spans - 1, 0, -1):
        leaving.insert(0, own_grads[k] + kept[k, :1] * leaving[0])
    leaving = jnp.stack([value.astype(BF16) for value in leaving])

    skip = jnp.repeat(skip_gain, P_SIZE)[None]
    grad_x = call(
        grad_x_kernel,
        grid,
        [run_spec(), run_t_spec(), rows_spec(), SHARED, SHARED, state_spec(), GAIN],
        rows_spec(),
        shape(length, columns, dtype=BF16),
        8 * length * columns * SPAN,
        6 * length * columns,
    )(running, running_t, grad_out, b_rows, c_rows, leaving, skip)

    grad_b = grad_c = product = None
    tokens = ()
    decay_parts = []
    at = 0
    for index, size in enumerate(sizes):
        wide = size * P_SIZE
        here = at // GROUP
        count = size // GROUP
        weight = weights[index]
        if tokens:
            weight = after([weight], *tokens)[0]
        x, own_states = forward(features, first, weight, running_t, b_rows, here)

        chunk = slice(at * P_SIZE, at * P_SIZE + wide)
        total = own_states[0]
        for k in range(1, spans):
            total = kept[k, :1, chunk] * total + own_states[k]
        cut = [step[:2] + tuple(value[:, chunk] for value in step[2:]) for step in steps]
        entering = scan_states(total, cut, False)

        so_far = () if grad_b is None else (grad_b, grad_c)
        decay_part, grad_b, grad_c = call(
            inner_kernel,
            (spans, count),
            [
                run_spec(here),
                run_t_spec(here),
                rows_spec(here),
                rows_spec(),
                SHARED,
                SHARED,
                state_spec(here),
            ]
            + [SHARED] * len(so_far),
            [run_spec(), SHARED, SHARED],
            [shape(size, length), shape(length, n), shape(length, n)],
            12 * length * wide * SPAN,
            6 * length * wide,
            [pltpu.VMEM((SPAN, SPAN), F32)],
        )(running, running_t, grad_out, x, b_rows, c_rows, leaving, *so_far)
        decay_part, grad_c = call(
            state_kernel,
            (spans, count),
            [
                run_t_spec(here),
                rows_spec(here),
                SHARED,
                pl.BlockSpec((n, WIDE), lambda k, h: (0, h)),
                state_spec(),
                state_spec(here),
                kept_spec(here),
                run_spec(),
                SHARED,
            ],
            [run_spec(), SHARED],
            [shape(size, length), shape(length, n)],
            4 * length * wide * n,
            6 * length * wide,
            [pltpu.VMEM((count, n, WIDE), F32)],
        )(running_t, grad_out, c_rows, entering, own_states, leaving, kept, decay_part, grad_c)
        decay_parts.append(decay_part)

        if index < len(sizes) - 1:
            zero = jnp.zeros((1,), jnp.int32)
            product = multiply(grad_x, weight, at // size, zero, 1, product)
            tokens = (product, grad_b, entering)
        elif two:
            sent = multiply(grad_x, weight, at // size, 1 - place, 2, product)
            got = swap(sent, "head", 1)
            grad_inputs = multiply(grad_x, weight, at // size, place, 2, product, got)
        else:
            zero = jnp.zeros((1,), jnp.int32)
            product = multiply(grad_x, weight, at // size, zero, 1, product)
            grad_inputs = lax.psum_scatter(product, "head", scatter_dimension=1, tiled=True)
        at += size

    return (grad_inputs, head_sum(grad_b), head_sum(grad_c), jnp.concatenate(decay_parts, axis=0))


def solution(mesh):
    in_specs = (
        P("ctx", "head"),
        P("ctx", "head"),
        P("ctx", None),
        P("ctx", None),
        P("head", "ctx"),
        P("head"),
        P("ctx", "head"),
    )
    out_specs = (P("ctx", "head"), P("ctx", None), P("ctx", None), P("head", "ctx"))
    return jax.shard_map(local, mesh=mesh, in_specs=in_specs, out_specs=out_specs, check_vma=False)
```

```python
import functools

import jax
import jax.numpy as jnp
from jax import lax
from jax.experimental import pallas as pl
from jax.experimental.pallas import tpu as pltpu
from jax.sharding import PartitionSpec as P

SPAN = 256
HALF = SPAN // 2
P_SIZE = 64
GROUP = 8
WIDE = GROUP * P_SIZE
LOG2E = 1.4426950408889634
NEVER = -1e30
GRANT = 58 * 2**20

F32 = jnp.float32
BF16 = jnp.bfloat16
EXACT = lax.Precision.HIGHEST


def dot(a, b, dims, precision=None):
    return lax.dot_general(a, b, (dims, ((), ())), precision=precision, preferred_element_type=F32)


def mm(a, b, precision=None):
    return dot(a, b, ((1,), (0,)), precision)


def iota(shape, dim):
    return lax.broadcasted_iota(jnp.int32, shape, dim)


def one_hot(dtype):
    return (iota((GROUP, WIDE), 0) == iota((GROUP, WIDE), 1) // P_SIZE).astype(dtype)


def not_before():
    return (iota((SPAN, SPAN), 0) >= iota((SPAN, SPAN), 1)).astype(F32)


def before():
    return (iota((SPAN, SPAN), 0) < iota((SPAN, SPAN), 1)).astype(F32)


def same():
    return (iota((SPAN, SPAN), 0) == iota((SPAN, SPAN), 1)).astype(F32)


def first_head():
    return iota((SPAN, 2 * P_SIZE), 1) < P_SIZE


def pair_columns(columns, pair):
    shape = (columns.shape[0], 2 * P_SIZE)
    left = jnp.broadcast_to(columns[:, 2 * pair : 2 * pair + 1], shape)
    right = jnp.broadcast_to(columns[:, 2 * pair + 1 : 2 * pair + 2], shape)
    return jnp.where(iota(shape, 1) < P_SIZE, left, right)


def spread_columns(columns):
    return jnp.concatenate([pair_columns(columns, pair) for pair in range(GROUP // 2)], axis=1)


def thirds(value):
    high = value.astype(BF16).astype(F32)
    middle = (value - high).astype(BF16).astype(F32)
    return high, middle, value - high - middle


def sum_over(value, mask):
    rows = value.shape[0]
    parts = mm(jnp.concatenate(thirds(value), axis=0).astype(BF16), mask.astype(BF16))
    return parts[:rows] + parts[rows : 2 * rows] + parts[2 * rows :]


def decay_kernel(d_ref, g_ref, c_ref, r_ref, rt_ref, a_ref, gt_ref):
    row_sums = sum_over(d_ref[...] * LOG2E, 1.0 - not_before() + same())
    r_ref[...] = row_sums
    padded = jnp.concatenate([row_sums, jnp.zeros((2 * P_SIZE - GROUP, SPAN), F32)], axis=0)
    running = padded.T[:, :GROUP]
    rt_ref[0] = running
    growth = jnp.exp2(spread_columns(running))
    last = spread_columns(running[SPAN - 1 : SPAN])
    a_ref[0] = jnp.where(iota((8, WIDE), 0) < 4, jnp.exp2(last), last)
    scaled = (g_ref[...].astype(F32) * growth).astype(BF16)
    gt_ref[0] = dot(c_ref[...], scaled, ((0,), (0,)))


def grad_x_kernel(r_ref, rt_ref, g_ref, b_ref, c_ref, q_ref, skip_ref, out_ref):
    b = b_ref[...]
    scores = dot(b, c_ref[...], ((1,), (1,)))
    running = r_ref[...]
    columns = rt_ref[0]
    top_keep = iota((HALF, SPAN), 1) >= iota((HALF, SPAN), 0)
    low_keep = iota((HALF, HALF), 1) >= iota((HALF, HALF), 0)
    to_end = jnp.exp2(spread_columns(columns[SPAN - 1 : SPAN] - columns))
    from_state = mm(b, q_ref[0]) * to_end
    for pair in range(GROUP // 2):
        lanes = slice(pair * 2 * P_SIZE, (pair + 1) * 2 * P_SIZE)
        g = g_ref[:, lanes]
        parts = []
        for head in (2 * pair, 2 * pair + 1):
            row = running[head : head + 1]
            top = jnp.where(top_keep, row - columns[:HALF, head : head + 1], NEVER)
            low = jnp.where(low_keep, row[:, HALF:] - columns[HALF:, head : head + 1], NEVER)
            top = (jnp.exp2(top) * scores[:HALF]).astype(BF16)
            low = (jnp.exp2(low) * scores[HALF:, HALF:]).astype(BF16)
            parts.append(jnp.concatenate([mm(top, g), mm(low, g[HALF:])], axis=0))
        inner = jnp.where(first_head(), parts[0], parts[1])
        total = inner + skip_ref[:, lanes] * g.astype(F32) + from_state[:, lanes]
        out_ref[:, lanes] = total.astype(BF16)


def forward_kernel(half_ref, own_ref, other_ref, w_ref, rt_ref, b_ref, x_ref, e_ref, total_ref):
    step = pl.program_id(1)

    @pl.when(step == 0)
    def _():
        total_ref[...] = jnp.zeros_like(total_ref)

    half = pl.num_programs(1) // 2

    @pl.when(step < half)
    def _():
        total_ref[...] += mm(own_ref[...], w_ref[...])

    @pl.when(step >= half)
    def _():
        total_ref[...] += mm(other_ref[...], w_ref[...])

    @pl.when(step == pl.num_programs(1) - 1)
    def _():
        x = total_ref[...].astype(BF16)
        x_ref[...] = x
        for k in range(e_ref.shape[0]):
            rows = slice(k * SPAN, (k + 1) * SPAN)
            columns = rt_ref[0, rows]
            to_end = jnp.exp2(spread_columns(columns[SPAN - 1 : SPAN] - columns))
            scaled = (x[rows].astype(F32) * to_end).astype(BF16)
            e_ref[k] = dot(b_ref[rows], scaled, ((0,), (0,)))


def product_kernel(has_before, has_other, half_ref, g_ref, w_ref, *refs):
    refs = list(refs)
    total = dot(g_ref[...], w_ref[...], ((1,), (1,)))
    if has_before:
        total = total + refs.pop(0)[...].astype(F32)
    if has_other:
        total = total.astype(BF16).astype(F32) + refs.pop(0)[...].astype(F32)
    refs[0][...] = total.astype(BF16)


def arrange_kernel(order_ref, own_ref, other_ref, out_ref, both_ref):
    half = own_ref.shape[1]
    both_ref[:, :half] = own_ref[...]
    both_ref[:, half:] = other_ref[...]
    unit = out_ref.shape[1] // order_ref.shape[0]
    for index in range(order_ref.shape[0]):
        source = pl.ds(pl.multiple_of(order_ref[index] * unit, 128), unit)
        out_ref[:, index * unit : (index + 1) * unit] = both_ref[:, source]


def coefficients_kernel(place_ref, every_ref, out_ref):
    place = place_ref[0]
    count = every_ref.shape[0]
    parts = jnp.concatenate(thirds(every_ref[...]), axis=0).astype(BF16)
    row = iota((8, count), 0)
    column = iota((8, count), 1)
    line = iota((8, every_ref.shape[1]), 0)
    half = out_ref.shape[0] // 2
    for step in range(half):
        bit = 2**step
        start = place // bit * bit
        upper = place // bit % 2
        beside = start + bit - 2 * bit * upper
        low = jnp.where(row == 1, beside, jnp.where(row == 3, place + 1, start))
        high = jnp.where(row == 1, beside + bit, jnp.where(row == 2, place, start + bit))
        mask = ((column >= low) & (column < high)).astype(F32)
        mask = jnp.concatenate([mask, mask, mask], axis=1).astype(BF16)
        factors = jnp.exp2(mm(mask, parts))
        kept, other, before_me, after_me = [factors[k : k + 1] for k in range(4)]
        up = (upper + 0 * line) == 1
        for way in range(2):
            later = up if way == 0 else jnp.logical_not(up)
            passed = before_me if way == 0 else after_me
            first = jnp.where(later, 1.0, other)
            second = jnp.where(later, kept, 1.0)
            third = jnp.where(later, passed, 0.0)
            out_ref[way * half + step] = jnp.where(
                line == 0, first, jnp.where(line == 1, second, third)
            )


def scan_kernel(factor_ref, total_ref, got_ref, *refs):
    entering_ref = refs[0] if len(refs) == 4 else None
    total_out, entering_out, sent_out = refs[-3:]
    factors = factor_ref[0]
    got = got_ref[...].astype(F32)
    total = factors[0:1] * total_ref[...] + factors[1:2] * got
    total_out[...] = total
    sent_out[...] = total.astype(BF16)
    passed = factors[2:3] * got
    entering_out[...] = passed if entering_ref is None else entering_ref[...] + passed


def early_forward_kernel(count, f_ref, *refs):
    pieces, (out_ref, buffer) = refs[:count], refs[count:]
    rows = pieces[0].shape[0]
    for index, piece in enumerate(pieces):
        buffer[index * rows : (index + 1) * rows] = piece[...]
    out_ref[...] = mm(f_ref[...], buffer[...])


def late_forward_kernel(count, f_ref, part_ref, rt_ref, b_ref, kept_ref, *refs):
    pieces, (x_ref, e_ref, total_ref, sent_ref, buffer) = refs[:count], refs[count:]
    rows = pieces[0].shape[0]
    for index, piece in enumerate(pieces):
        buffer[index * rows : (index + 1) * rows] = piece[...]
    x = (part_ref[...] + mm(f_ref[...], buffer[...])).astype(BF16)
    x_ref[...] = x
    total = None
    for k in range(e_ref.shape[0]):
        part = slice(k * SPAN, (k + 1) * SPAN)
        columns = rt_ref[0, part]
        to_end = jnp.exp2(spread_columns(columns[SPAN - 1 : SPAN] - columns))
        scaled = (x[part].astype(F32) * to_end).astype(BF16)
        state = dot(b_ref[part], scaled, ((0,), (0,)))
        e_ref[k] = state
        total = state if total is None else kept_ref[k, :1] * total + state
    total_ref[...] = total
    sent_ref[...] = total.astype(BF16)


def blocks_kernel(halves, has_before, order_ref, g_ref, *refs):
    count = len(halves)
    number = sum(halves)
    arrays, refs = refs[:number], refs[number:]
    if has_before:
        refs = refs[2:]
    away_ref, own_ref, buffer, slots, sems, out_sems = refs
    rows = arrays[0].shape[0]
    wide = g_ref.shape[1]
    copies = []
    at = 0
    for index, parts in enumerate(halves):
        mine = []
        for part in range(parts):
            lanes = pl.ds(part * (wide // parts), wide // parts)
            target = buffer.at[pl.ds(index * rows, rows), lanes]
            copy = pltpu.make_async_copy(arrays[at], target, sems.at[at])
            copy.start()
            mine.append(copy)
            at += 1
        copies.append(mine)
    g = g_ref[...]
    half = away_ref.shape[1] // rows
    for index in range(count):
        for copy in copies[index]:
            copy.wait()
        product = dot(g, buffer[index * rows : (index + 1) * rows], ((1,), (1,)))
        slots[index] = product.astype(BF16)
        place = order_ref[index]
        lanes = pl.ds(pl.multiple_of(place % half * rows, 128), rows)

        @pl.when(place < half)
        def _():
            target = away_ref.at[:, lanes]
            pltpu.make_async_copy(slots.at[index], target, out_sems.at[index]).start()

        @pl.when(place >= half)
        def _():
            target = own_ref.at[:, lanes]
            pltpu.make_async_copy(slots.at[index], target, out_sems.at[index]).start()

    for index in range(count):
        target = away_ref.at[:, pl.ds(0, rows)]
        pltpu.make_async_copy(slots.at[index], target, out_sems.at[index]).wait()


def after_kernel(*refs):
    pass


def inner_kernel(
    r_ref, rt_ref, g_ref, x_ref, b_ref, c_ref, q_ref, *refs
):
    d_ref, grad_b_ref, grad_c_ref, sum_ref = refs[-4:]
    so_far = refs[:-4]
    step = pl.program_id(1)
    b = b_ref[...]
    c = c_ref[...]
    scores = dot(b, c, ((1,), (1,)))
    running = r_ref[...]
    columns = rt_ref[0]
    top_keep = iota((HALF, SPAN), 1) >= iota((HALF, SPAN), 0)
    low_keep = iota((HALF, HALF), 1) >= iota((HALF, HALF), 0)

    @pl.when(step == 0)
    def _():
        sum_ref[...] = jnp.zeros_like(sum_ref)
        grad_b_ref[...] = so_far[0][...] if so_far else jnp.zeros_like(grad_b_ref)

    rows = []
    across = jnp.zeros((SPAN, 2 * P_SIZE), F32)
    lane = iota((SPAN, 2 * P_SIZE), 1)
    top_sum = sum_ref[:HALF]
    low_sum = sum_ref[HALF:, HALF:]
    for pair in range(GROUP // 2):
        lanes = slice(pair * 2 * P_SIZE, (pair + 1) * 2 * P_SIZE)
        g = g_ref[:, lanes]
        x = x_ref[:, lanes]
        for head in (2 * pair, 2 * pair + 1):
            mine = (lane < P_SIZE) if head == 2 * pair else (lane >= P_SIZE)
            x_head = jnp.where(mine, x, jnp.zeros_like(x))
            row = running[head : head + 1]
            top = jnp.where(top_keep, row - columns[:HALF, head : head + 1], NEVER)
            low = jnp.where(low_keep, row[:, HALF:] - columns[HALF:, head : head + 1], NEVER)
            top = jnp.exp2(top) * dot(x_head[:HALF], g, ((1,), (1,)))
            low = jnp.exp2(low) * dot(x_head[HALF:], g[HALF:], ((1,), (1,)))
            top_sum = top_sum + top
            low_sum = low_sum + low
            top = top * scores[:HALF]
            low = low * scores[HALF:, HALF:]
            top_row = jnp.sum(top, axis=0, keepdims=True)
            low_row = jnp.sum(low, axis=0, keepdims=True)
            rows.append(jnp.concatenate([top_row[:, :HALF], top_row[:, HALF:] + low_row], axis=1))
            column = jnp.concatenate(
                [jnp.sum(top, axis=1, keepdims=True), jnp.sum(low, axis=1, keepdims=True)], axis=0
            )
            across = jnp.where(lane == head, column, across)
    sum_ref[:HALF] = top_sum
    sum_ref[HALF:, HALF:] = low_sum
    difference = jnp.concatenate(rows, axis=0) - across.T[:GROUP]
    to_end = jnp.exp2(spread_columns(columns[SPAN - 1 : SPAN] - columns))
    scaled = x_ref[...].astype(F32) * to_end
    ends = dot(one_hot(BF16), (scaled * mm(b, q_ref[0])).astype(BF16), ((1,), (1,)))
    d_ref[...] = sum_over(difference, not_before()) + sum_over(ends, before())
    grad_b_ref[...] += dot(scaled.astype(BF16), q_ref[0], ((1,), (1,)))

    @pl.when(step == pl.num_programs(1) - 1)
    def _():
        total = sum_ref[...].astype(BF16)
        grad_b_ref[...] += mm(total, c)
        part = dot(total, b, ((0,), (0,)))
        grad_c_ref[...] = part + so_far[1][...] if so_far else part


def state_kernel(
    rt_ref, g_ref, c_ref, s_ref, e_ref, q_ref, a_ref, d_part_ref, c_part_ref, d_ref, grad_c_ref, held
):
    span, group = pl.program_id(0), pl.program_id(1)

    @pl.when(group == 0)
    def _():
        grad_c_ref[...] = c_part_ref[...]

    @pl.when(span == 0)
    def _():
        held[group] = s_ref[...]

    state = held[group]
    low = state.astype(BF16)
    scaled = g_ref[...].astype(F32) * jnp.exp2(spread_columns(rt_ref[0]))
    ends = dot(one_hot(BF16), (scaled * mm(c_ref[...], low)).astype(BF16), ((1,), (1,)))
    grad_c_ref[...] += dot(scaled.astype(BF16), low, ((1,), (1,)))
    product = jnp.sum(q_ref[0].astype(F32) * state, axis=0, keepdims=True) * a_ref[0, :1]
    high, middle, last = thirds(product)
    row = iota((8, WIDE), 0)
    stacked = jnp.where(row == 0, high, jnp.where(row == 1, middle, jnp.where(row == 2, last, 0.0)))
    kept = dot(one_hot(BF16), stacked.astype(BF16), ((1,), (1,)))
    kept = jnp.sum(kept, axis=1, keepdims=True)
    d_ref[...] = d_part_ref[...] + sum_over(ends, not_before()) + kept
    held[group] = e_ref[0] + a_ref[0, :1] * state


def call(kernel, grid, in_specs, out_specs, out_shape, flops, size, scratch=()):
    return pl.pallas_call(
        kernel,
        grid=grid,
        in_specs=in_specs,
        out_specs=out_specs,
        out_shape=out_shape,
        scratch_shapes=list(scratch),
        cost_estimate=pl.CostEstimate(flops=flops, bytes_accessed=size, transcendentals=0),
        compiler_params=pltpu.CompilerParams(
            dimension_semantics=("arbitrary",) * len(grid), vmem_limit_bytes=GRANT
        ),
    )


def run_spec(at=0):
    return pl.BlockSpec((GROUP, SPAN), lambda k, h: (h + at, k))


def run_t_spec(at=0):
    return pl.BlockSpec((1, SPAN, GROUP), lambda k, h: (h + at, k, 0))


def rows_spec(at=0):
    return pl.BlockSpec((SPAN, WIDE), lambda k, h: (k, h + at))


def state_spec(at=0):
    return pl.BlockSpec((1, 2 * P_SIZE, WIDE), lambda k, h: (k, 0, h + at))


def kept_spec(at=0):
    return pl.BlockSpec((1, 8, WIDE), lambda k, h: (k, 0, h + at))


SHARED = pl.BlockSpec((SPAN, 2 * P_SIZE), lambda k, h: (k, 0))
GAIN = pl.BlockSpec((1, WIDE), lambda k, h: (0, h))
ANYWHERE = pl.BlockSpec(memory_space=pl.ANY)
SCALARS = pl.BlockSpec(memory_space=pltpu.SMEM)


def shape(*dims, dtype=F32):
    return jax.ShapeDtypeStruct(dims, dtype)


def swap(value, axis, bit):
    count = lax.axis_size(axis)
    return lax.ppermute(value, axis, [(i, i ^ bit) for i in range(count)])


def block_products(kept):
    count = lax.axis_size("ctx")
    place = lax.axis_index("ctx")
    steps = []
    before_me = jnp.ones_like(kept)
    after_me = jnp.ones_like(kept)
    bit = 1
    while bit < count:
        other = swap(kept, "ctx", bit)
        upper = (place & bit) != 0
        steps.append((bit, upper, kept, other, before_me, after_me))
        before_me = jnp.where(upper, before_me * other, before_me)
        after_me = jnp.where(upper, after_me, after_me * other)
        kept = kept * other
        bit *= 2
    return steps


def scan_states(total, steps, reverse):
    entering = jnp.zeros_like(total)
    for bit, upper, kept, other, before_me, after_me in steps:
        got = swap(total.astype(BF16), "ctx", bit).astype(F32)
        if reverse:
            entering = entering + jnp.where(upper, 0.0, after_me) * got
            total = jnp.where(upper, got + other * total, total + kept * got)
        else:
            entering = entering + jnp.where(upper, before_me, 0.0) * got
            total = jnp.where(upper, kept * got + total, other * total + got)
    return entering


def head_sum(value):
    bit = 1
    while bit < lax.axis_size("head"):
        value = value.astype(BF16)
        value = value.astype(F32) + swap(value, "head", bit).astype(F32)
        bit *= 2
    return value


PLANE = 4


def after(values, *tokens):
    out = pl.pallas_call(
        after_kernel,
        in_specs=[ANYWHERE] * (len(values) + len(tokens)),
        out_specs=[ANYWHERE] * len(values),
        out_shape=[shape(*value.shape, dtype=value.dtype) for value in values],
        input_output_aliases={index: index for index in range(len(values))},
        cost_estimate=pl.CostEstimate(flops=0, bytes_accessed=0, transcendentals=0),
    )(*values, *tokens)
    return list(out)


def shift(value, by):
    count = lax.axis_size("ctx")
    return lax.ppermute(value, "ctx", [(i, (i + PLANE * by) % count) for i in range(count)])


def swap_x(value):
    return swap(value, "ctx", 1)


def swap_y(value):
    return swap(value, "ctx", 2)


EARLY = [(k, flip) for k in (0, 1, 3) for flip in range(3)]
LATE = [(0, 3), (1, 3), (3, 3), (2, 0), (2, 1), (2, 2), (2, 3)]


def block_order():
    place = lax.axis_index("ctx")
    layers = lax.axis_size("ctx") // PLANE
    layer, spot = place // PLANE, place % PLANE
    order = [(layer + layers - k) % layers * PLANE + (spot ^ flip) for k, flip in EARLY + LATE]
    return jnp.stack(order).astype(jnp.int32)


def gather_weight(w, sizes):
    ends = [sum(sizes[: j + 1]) * P_SIZE for j in range(len(sizes))]
    parts = [w[:, end - size * P_SIZE : end] for end, size in zip(ends, sizes)]
    return [lax.all_gather(part, "ctx", axis=0, tiled=True) for part in parts]


def forward(features, first, weight, running_t, b_rows, here):
    own, other = features
    length = own.shape[0]
    n = b_rows.shape[1]
    width, wide = weight.shape
    deep = width // 4
    spans = length // SPAN

    def depth(k, first_ref):
        return (k // 2 ^ first_ref[0]) * 2 + k % 2

    return pl.pallas_call(
        forward_kernel,
        grid_spec=pltpu.PrefetchScalarGridSpec(
            num_scalar_prefetch=1,
            grid=(wide // WIDE, 4),
            in_specs=[
                pl.BlockSpec((length, deep), lambda h, k, first_ref: (0, jnp.minimum(k, 1))),
                pl.BlockSpec((length, deep), lambda h, k, first_ref: (0, jnp.maximum(k - 2, 0))),
                pl.BlockSpec((deep, WIDE), lambda h, k, first_ref: (depth(k, first_ref), h)),
                pl.BlockSpec((1, length, GROUP), lambda h, k, first_ref: (h + here, 0, 0)),
                pl.BlockSpec((length, n), lambda h, k, first_ref: (0, 0)),
            ],
            out_specs=[
                pl.BlockSpec((length, WIDE), lambda h, k, first_ref: (0, h)),
                pl.BlockSpec((spans, n, WIDE), lambda h, k, first_ref: (0, 0, h)),
            ],
            scratch_shapes=[pltpu.VMEM((length, WIDE), F32)],
        ),
        out_shape=[shape(length, wide, dtype=BF16), shape(spans, n, wide)],
        cost_estimate=pl.CostEstimate(
            flops=2 * length * wide * width, bytes_accessed=2 * wide * width, transcendentals=0
        ),
        compiler_params=pltpu.CompilerParams(
            dimension_semantics=("arbitrary", "arbitrary"), vmem_limit_bytes=GRANT
        ),
    )(first, own, other, weight, running_t, b_rows)


def multiply(grad_x, weight, at, half, halves, before=None, other=None):
    length = grad_x.shape[0]
    width, wide = weight.shape
    tiles = width // halves // WIDE
    tile = pl.BlockSpec((length, WIDE), lambda j, half_ref: (0, half_ref[0] * tiles + j))
    plain = pl.BlockSpec((length, WIDE), lambda j, half_ref: (0, j))
    in_specs = [
        pl.BlockSpec((length, wide), lambda j, half_ref: (0, at)),
        pl.BlockSpec((WIDE, wide), lambda j, half_ref: (half_ref[0] * tiles + j, 0)),
    ]
    operands = [grad_x, weight]
    if before is not None:
        in_specs.append(tile)
        operands.append(before)
    if other is not None:
        in_specs.append(plain)
        operands.append(other)
    return pl.pallas_call(
        functools.partial(product_kernel, before is not None, other is not None),
        grid_spec=pltpu.PrefetchScalarGridSpec(
            num_scalar_prefetch=1,
            grid=(tiles,),
            in_specs=in_specs,
            out_specs=plain,
        ),
        out_shape=shape(length, width // halves, dtype=BF16),
        cost_estimate=pl.CostEstimate(
            flops=2 * length * wide * width // halves,
            bytes_accessed=2 * wide * width // halves,
            transcendentals=0,
        ),
        compiler_params=pltpu.CompilerParams(
            dimension_semantics=("arbitrary",), vmem_limit_bytes=GRANT
        ),
    )(half, *operands)


def early_forward(features, pieces):
    length = features.shape[0]
    rows, columns = pieces[0].shape
    deep = rows * len(pieces)
    return call(
        functools.partial(early_forward_kernel, len(pieces)),
        (columns // WIDE,),
        [pl.BlockSpec((length, deep), lambda h: (0, 0))]
        + [pl.BlockSpec((rows, WIDE), lambda h: (0, h))] * len(pieces),
        pl.BlockSpec((length, WIDE), lambda h: (0, h)),
        shape(length, columns),
        2 * length * columns * deep,
        2 * columns * deep,
        [pltpu.VMEM((deep, WIDE), BF16)],
    )(features, *pieces)


def late_forward(features, part, pieces, running_t, b_rows, kept, here):
    length = features.shape[0]
    rows, columns = pieces[0].shape
    deep = rows * len(pieces)
    n = b_rows.shape[1]
    spans = length // SPAN
    state = pl.BlockSpec((n, WIDE), lambda h: (0, h))
    return call(
        functools.partial(late_forward_kernel, len(pieces)),
        (columns // WIDE,),
        [
            pl.BlockSpec((length, deep), lambda h: (0, 0)),
            pl.BlockSpec((length, WIDE), lambda h: (0, h + here)),
            pl.BlockSpec((1, length, GROUP), lambda h: (h + here, 0, 0)),
            pl.BlockSpec((length, n), lambda h: (0, 0)),
            pl.BlockSpec((spans, 8, WIDE), lambda h: (0, 0, h + here)),
        ]
        + [pl.BlockSpec((rows, WIDE), lambda h: (0, h))] * len(pieces),
        [
            pl.BlockSpec((length, WIDE), lambda h: (0, h)),
            pl.BlockSpec((spans, n, WIDE), lambda h: (0, 0, h)),
            state,
            state,
        ],
        [
            shape(length, columns, dtype=BF16),
            shape(spans, n, columns),
            shape(n, columns),
            shape(n, columns, dtype=BF16),
        ],
        2 * length * columns * deep,
        2 * columns * deep,
        [pltpu.VMEM((deep, WIDE), BF16)],
    )(features, part, running_t, b_rows, kept, *pieces)


def multiply_blocks(order, grad_x, pieces, so_far):
    length, columns = grad_x.shape
    arrays = [array for piece in pieces for array in piece]
    rows = arrays[0].shape[0]
    count = len(pieces)
    half = shape(length, lax.axis_size("ctx") * rows // 2, dtype=BF16)
    first = 2 + len(arrays)
    return pl.pallas_call(
        functools.partial(blocks_kernel, [len(piece) for piece in pieces], bool(so_far)),
        grid=(1,),
        in_specs=[SCALARS, pl.BlockSpec((length, columns), lambda h: (0, 0))]
        + [ANYWHERE] * (len(arrays) + len(so_far)),
        out_specs=[ANYWHERE, ANYWHERE],
        out_shape=[half, half],
        input_output_aliases={first + k: k for k in range(len(so_far))},
        scratch_shapes=[
            pltpu.VMEM((rows * count, columns), BF16),
            pltpu.VMEM((count, length, rows), BF16),
            pltpu.SemaphoreType.DMA((len(arrays),)),
            pltpu.SemaphoreType.DMA((count,)),
        ],
        cost_estimate=pl.CostEstimate(
            flops=2 * length * columns * rows * count,
            bytes_accessed=2 * columns * rows * count,
            transcendentals=0,
        ),
        compiler_params=pltpu.CompilerParams(
            dimension_semantics=("arbitrary",), vmem_limit_bytes=GRANT
        ),
    )(order, grad_x, *arrays, *so_far)


def coefficients(logs):
    count = lax.axis_size("ctx")
    place = lax.axis_index("ctx").astype(jnp.int32)[None]
    columns = logs.shape[1]
    every = lax.all_gather(logs, "ctx").reshape(count, columns)
    steps = count.bit_length() - 1
    return call(
        coefficients_kernel,
        (1,),
        [SCALARS, pl.BlockSpec((count, columns), lambda h: (0, 0))],
        pl.BlockSpec((2 * steps, 8, columns), lambda h: (0, 0, 0)),
        shape(2 * steps, 8, columns),
        0,
        256 * columns,
    )(place, every)


def scan_step(factors, number, here, total, sent, entering, bit):
    got = swap(sent, "ctx", bit)
    n, columns = total.shape
    block = pl.BlockSpec((n, WIDE), lambda h: (0, h))
    return call(
        scan_kernel,
        (columns // WIDE,),
        [pl.BlockSpec((1, 8, WIDE), lambda h: (number, 0, h + here)), block, block]
        + [block] * len(entering),
        [block, block, block],
        [shape(n, columns), shape(n, columns), shape(n, columns, dtype=BF16)],
        0,
        14 * n * columns,
    )(factors, total, got, *entering)


def local(inputs, w_in, b_rows, c_rows, log_decay, skip_gain, grad_out):
    groups = log_decay.shape[0] // GROUP
    layered = lax.axis_size("ctx") == 4 * PLANE and lax.axis_size("head") == 2
    if layered and groups % 2 == 0 and w_in.shape[0] == 256:
        return local_layered(inputs, w_in, b_rows, c_rows, log_decay, skip_gain, grad_out)
    return local_plain(inputs, w_in, b_rows, c_rows, log_decay, skip_gain, grad_out)


def prepare(log_decay, grad_out, c_rows):
    length, columns = grad_out.shape
    heads = log_decay.shape[0]
    spans = length // SPAN
    groups = heads // GROUP
    n = c_rows.shape[1]
    return call(
        decay_kernel,
        (spans, groups),
        [run_spec(), rows_spec(), SHARED],
        [run_spec(), run_t_spec(), kept_spec(), state_spec()],
        [
            shape(heads, length),
            shape(groups, length, GROUP),
            shape(spans, 8, columns),
            shape(spans, n, columns),
        ],
        2 * length * columns * n,
        6 * length * columns,
    )(log_decay, grad_out, c_rows)


def inner(grid, here, wide, operands, so_far):
    length = operands[2].shape[0]
    n = operands[4].shape[1]
    specs = [
        run_spec(here),
        run_t_spec(here),
        rows_spec(here),
        rows_spec(),
        SHARED,
        SHARED,
        state_spec(here),
    ]
    return call(
        inner_kernel,
        grid,
        specs + [SHARED] * len(so_far),
        [run_spec(), SHARED, SHARED],
        [shape(wide // P_SIZE, length), shape(length, n), shape(length, n)],
        12 * length * wide * SPAN,
        6 * length * wide,
        [pltpu.VMEM((SPAN, SPAN), F32)],
    )(*operands, *so_far)


def state_terms(grid, here, wide, operands):
    length = operands[1].shape[0]
    n = operands[2].shape[1]
    return call(
        state_kernel,
        grid,
        [
            run_t_spec(here),
            rows_spec(here),
            SHARED,
            pl.BlockSpec((n, WIDE), lambda k, h: (0, h)),
            state_spec(),
            state_spec(here),
            kept_spec(here),
            run_spec(),
            SHARED,
        ],
        [run_spec(), SHARED],
        [shape(wide // P_SIZE, length), shape(length, n)],
        4 * length * wide * n,
        6 * length * wide,
        [pltpu.VMEM((grid[1], n, WIDE), F32)],
    )(*operands)


def local_layered(inputs, w_in, b_rows, c_rows, log_decay, skip_gain, grad_out):
    length, columns = grad_out.shape
    heads = log_decay.shape[0]
    spans = length // SPAN
    groups = heads // GROUP
    place = lax.axis_index("head").astype(jnp.int32)
    half = columns // 2
    w_a, w_b = w_in[:, :half], w_in[:, half:]
    order = block_order()
    blocks = order.shape[0]
    width = blocks * w_in.shape[0]

    z1, z3 = shift(w_in, 1), shift(w_in, 3)
    own_x, own_y = swap_x(w_in), swap_y(w_in)
    other = swap(inputs, "head", 1)
    running, running_t, kept, own_grads = prepare(log_decay, grad_out, c_rows)
    factors = coefficients(jnp.sum(kept[:, 4:5], axis=0))
    back = own_grads[spans - 1]
    for k in range(spans - 2, -1, -1):
        back = own_grads[k] + kept[k, :1] * back
    sent = back.astype(BF16)
    sent = after([sent], other)[0]
    back, leaving, sent = scan_step(factors, 4, 0, back, sent, (), 1)

    z1, w_a, w_b = after([z1, w_a, w_b], own_x, own_y, z3)
    z2a, z2b = shift(w_a, 2), shift(w_b, 2)
    x1, y1 = swap_x(z1), swap_y(z1)
    z3 = after([z3], sent)[0]
    x3, y3 = swap_x(z3), swap_y(z3)
    back, leaving, sent = scan_step(factors, 5, 0, back, sent, (leaving,), 2)
    order_own = (order + place * (blocks // 2)) % blocks
    features = call(
        arrange_kernel,
        (1,),
        [SCALARS] + [pl.BlockSpec((length, width // 2), lambda h: (0, 0))] * 2,
        pl.BlockSpec((length, width), lambda h: (0, 0)),
        shape(length, width, dtype=BF16),
        0,
        4 * length * width,
        [pltpu.VMEM((length, width), BF16)],
    )(order_own, inputs, other)
    cut = len(EARLY) * w_in.shape[0]
    early_features, late_features = features[:, :cut], features[:, cut:]

    z2a, x1, y3, own_y = after(
        [z2a, x1, y3, own_y], y1, x3, z2b, sent, early_features, late_features
    )
    x1_a, x1_b = x1[:, :half], x1[:, half:]
    y3_a, y3_b = y3[:, :half], y3[:, half:]
    own_y_a, own_y_b = own_y[:, :half], own_y[:, half:]
    x2a, y2a = swap_x(z2a), swap_y(z2a)
    d3a, d1a = swap_x(y3_a), swap_y(x1_a)
    back, leaving, sent = scan_step(factors, 6, 0, back, sent, (leaving,), 4)
    early = [w_in, own_x, own_y, z1, x1, y1, z3, x3, y3]
    part = early_forward(early_features, early)

    own_y_a, x2a, z2b, y3_b, x1_b = after(
        [own_y_a, x2a, z2b, y3_b, x1_b], y2a, d3a, d1a, part, sent
    )
    d0a, d2a = swap_x(own_y_a), swap_y(x2a)
    x2b, y2b = swap_x(z2b), swap_y(z2b)
    d3b, d1b = swap_x(y3_b), swap_y(x1_b)
    back, leaving, sent = scan_step(factors, 7, 0, back, sent, (leaving,), 8)
    leaving_all = [leaving]
    for k in range(spans - 1, 0, -1):
        leaving_all.insert(0, own_grads[k] + kept[k, :1] * leaving_all[0])
    leaving_all = jnp.stack([value.astype(BF16) for value in leaving_all])
    skip = jnp.repeat(skip_gain, P_SIZE)[None]
    grad_x = grad_rows(running, running_t, grad_out, b_rows, c_rows, leaving_all, skip)
    late_a = [d0a, d1a, d3a, z2a, x2a, y2a, d2a]
    x_a, states_a, total_a, sent_a = late_forward(
        late_features, part, late_a, running_t, b_rows, kept, 0
    )

    own_y_b, x2b, sent_a = after([own_y_b, x2b, sent_a], y2b, d3b, d1b, grad_x)
    d0b, d2b = swap_x(own_y_b), swap_y(x2b)
    total_a, entering_a, sent_a = scan_step(factors, 0, 0, total_a, sent_a, (), 1)
    order_away = (order + (1 - place) * (blocks // 2)) % blocks
    early_order, late_order = order_away[: len(EARLY)], order_away[len(EARLY) :]
    product = multiply_blocks(early_order, grad_x, [[piece] for piece in early], ())

    d0b, d2b = after([d0b, d2b], sent_a, product[0])
    late_b = [d0b, d1b, d3b, z2b, x2b, y2b, d2b]
    here = groups // 2
    x_b, states_b, total_b, sent_b = late_forward(
        late_features, part, late_b, running_t, b_rows, kept, here
    )
    pairs = list(zip(late_a, late_b))
    product = after(list(product), sent_b)
    away, own = multiply_blocks(late_order, grad_x, pairs, product)
    got = swap(away, "head", 1)
    entering_b = ()
    for number, bit in enumerate((1, 2, 4, 8)):
        if number > 0:
            total_a, entering_a, sent_a = scan_step(
                factors, number, 0, total_a, sent_a, (entering_a,), bit
            )
        total_b, entering_b, sent_b = scan_step(
            factors, number, here, total_b, sent_b, entering_b, bit
        )
        entering_b = (entering_b,)
    entering_b = entering_b[0]
    shared = (running, running_t, grad_out)
    grid = (spans, here)
    inner_a = shared + (x_a, b_rows, c_rows, leaving_all)
    decay_a, grad_b, grad_c = inner(grid, 0, half, inner_a, ())
    inner_b = shared + (x_b, b_rows, c_rows, leaving_all)
    decay_b, grad_b, grad_c = inner(grid, here, half, inner_b, (grad_b, grad_c))
    grad_b = head_sum(grad_b)

    common = (running_t, grad_out, c_rows)
    state_a = common + (entering_a, states_a, leaving_all, kept, decay_a, grad_c)
    decay_a, grad_c = state_terms(grid, 0, half, state_a)
    state_b = common + (entering_b, states_b, leaving_all, kept, decay_b, grad_c)
    decay_b, grad_c = state_terms(grid, here, half, state_b)
    grad_inputs = (own.astype(F32) + got.astype(F32)).astype(BF16)
    grad_log_decay = jnp.concatenate([decay_a, decay_b], axis=0)
    return (grad_inputs, grad_b, head_sum(grad_c), grad_log_decay)


def grad_rows(running, running_t, grad_out, b_rows, c_rows, leaving, skip):
    length, columns = grad_out.shape
    return call(
        grad_x_kernel,
        (length // SPAN, running_t.shape[0]),
        [run_spec(), run_t_spec(), rows_spec(), SHARED, SHARED, state_spec(), GAIN],
        rows_spec(),
        shape(length, columns, dtype=BF16),
        8 * length * columns * SPAN,
        6 * length * columns,
    )(running, running_t, grad_out, b_rows, c_rows, leaving, skip)


def local_plain(inputs, w_in, b_rows, c_rows, log_decay, skip_gain, grad_out):
    length, columns = grad_out.shape
    heads = log_decay.shape[0]
    spans = length // SPAN
    groups = heads // GROUP
    n = b_rows.shape[1]
    grid = (spans, groups)

    sizes = (heads // 2, heads // 4, heads // 4) if heads % (4 * GROUP) == 0 else (heads,)
    weights = gather_weight(w_in, sizes)
    two = lax.axis_size("head") == 2
    place = lax.axis_index("head").astype(jnp.int32)[None]
    width = weights[0].shape[0]
    if two:
        features = (inputs, swap(inputs, "head", 1))
        first = place
    else:
        features = lax.all_gather(inputs, "head", axis=1, tiled=True)
        features = (features[:, : width // 2], features[:, width // 2 :])
        first = jnp.zeros((1,), jnp.int32)

    running, running_t, kept, own_grads = call(
        decay_kernel,
        grid,
        [run_spec(), rows_spec(), SHARED],
        [run_spec(), run_t_spec(), kept_spec(), state_spec()],
        [
            shape(heads, length),
            shape(groups, length, GROUP),
            shape(spans, 8, columns),
            shape(spans, n, columns),
        ],
        2 * length * columns * n,
        6 * length * columns,
    )(log_decay, grad_out, c_rows)

    kept_total = kept[0, :1]
    for k in range(1, spans):
        kept_total = kept_total * kept[k, :1]
    steps = block_products(kept_total)

    total = own_grads[spans - 1]
    for k in range(spans - 2, -1, -1):
        total = own_grads[k] + kept[k, :1] * total
    leaving = [scan_states(total, steps, True)]
    for k in range(spans - 1, 0, -1):
        leaving.insert(0, own_grads[k] + kept[k, :1] * leaving[0])
    leaving = jnp.stack([value.astype(BF16) for value in leaving])

    skip = jnp.repeat(skip_gain, P_SIZE)[None]
    grad_x = call(
        grad_x_kernel,
        grid,
        [run_spec(), run_t_spec(), rows_spec(), SHARED, SHARED, state_spec(), GAIN],
        rows_spec(),
        shape(length, columns, dtype=BF16),
        8 * length * columns * SPAN,
        6 * length * columns,
    )(running, running_t, grad_out, b_rows, c_rows, leaving, skip)

    grad_b = grad_c = product = None
    tokens = ()
    decay_parts = []
    at = 0
    for index, size in enumerate(sizes):
        wide = size * P_SIZE
        here = at // GROUP
        count = size // GROUP
        weight = weights[index]
        if tokens:
            weight = after([weight], *tokens)[0]
        x, own_states = forward(features, first, weight, running_t, b_rows, here)

        chunk = slice(at * P_SIZE, at * P_SIZE + wide)
        total = own_states[0]
        for k in range(1, spans):
            total = kept[k, :1, chunk] * total + own_states[k]
        cut = [step[:2] + tuple(value[:, chunk] for value in step[2:]) for step in steps]
        entering = scan_states(total, cut, False)

        so_far = () if grad_b is None else (grad_b, grad_c)
        decay_part, grad_b, grad_c = call(
            inner_kernel,
            (spans, count),
            [
                run_spec(here),
                run_t_spec(here),
                rows_spec(here),
                rows_spec(),
                SHARED,
                SHARED,
                state_spec(here),
            ]
            + [SHARED] * len(so_far),
            [run_spec(), SHARED, SHARED],
            [shape(size, length), shape(length, n), shape(length, n)],
            12 * length * wide * SPAN,
            6 * length * wide,
            [pltpu.VMEM((SPAN, SPAN), F32)],
        )(running, running_t, grad_out, x, b_rows, c_rows, leaving, *so_far)
        decay_part, grad_c = call(
            state_kernel,
            (spans, count),
            [
                run_t_spec(here),
                rows_spec(here),
                SHARED,
                pl.BlockSpec((n, WIDE), lambda k, h: (0, h)),
                state_spec(),
                state_spec(here),
                kept_spec(here),
                run_spec(),
                SHARED,
            ],
            [run_spec(), SHARED],
            [shape(size, length), shape(length, n)],
            4 * length * wide * n,
            6 * length * wide,
            [pltpu.VMEM((count, n, WIDE), F32)],
        )(running_t, grad_out, c_rows, entering, own_states, leaving, kept, decay_part, grad_c)
        decay_parts.append(decay_part)

        if index < len(sizes) - 1:
            zero = jnp.zeros((1,), jnp.int32)
            product = multiply(grad_x, weight, at // size, zero, 1, product)
            tokens = (product, grad_b, entering)
        elif two:
            sent = multiply(grad_x, weight, at // size, 1 - place, 2, product)
            got = swap(sent, "head", 1)
            grad_inputs = multiply(grad_x, weight, at // size, place, 2, product, got)
        else:
            zero = jnp.zeros((1,), jnp.int32)
            product = multiply(grad_x, weight, at // size, zero, 1, product)
            grad_inputs = lax.psum_scatter(product, "head", scatter_dimension=1, tiled=True)
        at += size

    return (grad_inputs, head_sum(grad_b), head_sum(grad_c), jnp.concatenate(decay_parts, axis=0))


def solution(mesh):
    in_specs = (
        P("ctx", "head"),
        P("ctx", "head"),
        P("ctx", None),
        P("ctx", None),
        P("head", "ctx"),
        P("head"),
        P("ctx", "head"),
    )
    out_specs = (P("ctx", "head"), P("ctx", None), P("ctx", None), P("head", "ctx"))
    return jax.shard_map(local, mesh=mesh, in_specs=in_specs, out_specs=out_specs, check_vma=False)
```

```python
import functools

import jax
import jax.numpy as jnp
from jax import lax
from jax.experimental import pallas as pl
from jax.experimental.pallas import tpu as pltpu
from jax.sharding import PartitionSpec as P

SPAN = 256
HALF = SPAN // 2
P_SIZE = 64
GROUP = 8
WIDE = GROUP * P_SIZE
LOG2E = 1.4426950408889634
NEVER = -1e30
GRANT = 62 * 2**20

F32 = jnp.float32
BF16 = jnp.bfloat16
EXACT = lax.Precision.HIGHEST


def dot(a, b, dims, precision=None):
    return lax.dot_general(a, b, (dims, ((), ())), precision=precision, preferred_element_type=F32)


def mm(a, b, precision=None):
    return dot(a, b, ((1,), (0,)), precision)


def iota(shape, dim):
    return lax.broadcasted_iota(jnp.int32, shape, dim)


def one_hot(dtype):
    return (iota((GROUP, WIDE), 0) == iota((GROUP, WIDE), 1) // P_SIZE).astype(dtype)


def not_before():
    return (iota((SPAN, SPAN), 0) >= iota((SPAN, SPAN), 1)).astype(F32)


def before():
    return (iota((SPAN, SPAN), 0) < iota((SPAN, SPAN), 1)).astype(F32)


def same():
    return (iota((SPAN, SPAN), 0) == iota((SPAN, SPAN), 1)).astype(F32)


def first_head():
    return iota((SPAN, 2 * P_SIZE), 1) < P_SIZE


def pair_columns(columns, pair):
    shape = (columns.shape[0], 2 * P_SIZE)
    left = jnp.broadcast_to(columns[:, 2 * pair : 2 * pair + 1], shape)
    right = jnp.broadcast_to(columns[:, 2 * pair + 1 : 2 * pair + 2], shape)
    return jnp.where(iota(shape, 1) < P_SIZE, left, right)


def spread_columns(columns):
    return jnp.concatenate([pair_columns(columns, pair) for pair in range(GROUP // 2)], axis=1)


def thirds(value):
    high = value.astype(BF16).astype(F32)
    middle = (value - high).astype(BF16).astype(F32)
    return high, middle, value - high - middle


def sum_over(value, mask):
    rows = value.shape[0]
    parts = mm(jnp.concatenate(thirds(value), axis=0).astype(BF16), mask.astype(BF16))
    return parts[:rows] + parts[rows : 2 * rows] + parts[2 * rows :]


def decay_kernel(d_ref, g_ref, c_ref, r_ref, rt_ref, a_ref, gt_ref):
    row_sums = sum_over(d_ref[...] * LOG2E, 1.0 - not_before() + same())
    r_ref[...] = row_sums
    padded = jnp.concatenate([row_sums, jnp.zeros((2 * P_SIZE - GROUP, SPAN), F32)], axis=0)
    running = padded.T[:, :GROUP]
    rt_ref[0] = running
    growth = jnp.exp2(spread_columns(running))
    last = spread_columns(running[SPAN - 1 : SPAN])
    a_ref[0] = jnp.where(iota((8, WIDE), 0) < 4, jnp.exp2(last), last)
    scaled = (g_ref[...].astype(F32) * growth).astype(BF16)
    gt_ref[0] = dot(c_ref[...], scaled, ((0,), (0,)))


def grad_x_kernel(transposed, r_ref, rt_ref, g_ref, b_ref, c_ref, q_ref, skip_ref, out_ref):
    b = b_ref[...]
    scores = dot(b, c_ref[...], ((1,), (1,)))
    running = r_ref[...]
    columns = rt_ref[0]
    top_keep = iota((HALF, SPAN), 1) >= iota((HALF, SPAN), 0)
    low_keep = iota((HALF, HALF), 1) >= iota((HALF, HALF), 0)
    to_end = jnp.exp2(spread_columns(columns[SPAN - 1 : SPAN] - columns))
    from_state = mm(b, q_ref[0]) * to_end
    for pair in range(GROUP // 2):
        lanes = slice(pair * 2 * P_SIZE, (pair + 1) * 2 * P_SIZE)
        g = g_ref[:, lanes]
        parts = []
        for head in (2 * pair, 2 * pair + 1):
            row = running[head : head + 1]
            top = jnp.where(top_keep, row - columns[:HALF, head : head + 1], NEVER)
            low = jnp.where(low_keep, row[:, HALF:] - columns[HALF:, head : head + 1], NEVER)
            top = (jnp.exp2(top) * scores[:HALF]).astype(BF16)
            low = (jnp.exp2(low) * scores[HALF:, HALF:]).astype(BF16)
            parts.append(jnp.concatenate([mm(top, g), mm(low, g[HALF:])], axis=0))
        inner = jnp.where(first_head(), parts[0], parts[1])
        total = inner + skip_ref[:, lanes] * g.astype(F32) + from_state[:, lanes]
        if transposed:
            out_ref[lanes, :] = total.T.astype(BF16)
        else:
            out_ref[:, lanes] = total.astype(BF16)


def forward_kernel(half_ref, own_ref, other_ref, w_ref, rt_ref, b_ref, x_ref, e_ref, total_ref):
    step = pl.program_id(1)

    @pl.when(step == 0)
    def _():
        total_ref[...] = jnp.zeros_like(total_ref)

    half = pl.num_programs(1) // 2

    @pl.when(step < half)
    def _():
        total_ref[...] += mm(own_ref[...], w_ref[...])

    @pl.when(step >= half)
    def _():
        total_ref[...] += mm(other_ref[...], w_ref[...])

    @pl.when(step == pl.num_programs(1) - 1)
    def _():
        x = total_ref[...].astype(BF16)
        x_ref[...] = x
        for k in range(e_ref.shape[0]):
            rows = slice(k * SPAN, (k + 1) * SPAN)
            columns = rt_ref[0, rows]
            to_end = jnp.exp2(spread_columns(columns[SPAN - 1 : SPAN] - columns))
            scaled = (x[rows].astype(F32) * to_end).astype(BF16)
            e_ref[k] = dot(b_ref[rows], scaled, ((0,), (0,)))


def product_kernel(has_before, has_other, half_ref, g_ref, w_ref, *refs):
    refs = list(refs)
    total = dot(g_ref[...], w_ref[...], ((1,), (1,)))
    if has_before:
        total = total + refs.pop(0)[...].astype(F32)
    if has_other:
        total = total.astype(BF16).astype(F32) + refs.pop(0)[...].astype(F32)
    refs[0][...] = total.astype(BF16)


def arrange_kernel(order_ref, own_ref, other_ref, early_ref, late_ref, both_ref):
    half = own_ref.shape[1]
    both_ref[:, :half] = own_ref[...]
    both_ref[:, half:] = other_ref[...]
    unit = 2 * half // order_ref.shape[0]
    cut = early_ref.shape[1]
    for index in range(order_ref.shape[0]):
        source = pl.ds(pl.multiple_of(order_ref[index] * unit, 128), unit)
        at = index * unit
        if at < cut:
            early_ref[:, at : at + unit] = both_ref[:, source]
        else:
            late_ref[:, at - cut : at - cut + unit] = both_ref[:, source]


TAIL = 16


def message(total, log):
    high, middle, last = thirds(log)
    line = iota((TAIL, total.shape[1]), 0)
    tail = jnp.where(line == 0, high, jnp.where(line == 1, middle, jnp.where(line == 2, last, 0.0)))
    return total.astype(BF16), tail.astype(BF16)


def start_kernel(own_ref, kept_ref, total_ref, log_ref, sent_ref):
    spans = own_ref.shape[0]
    total = own_ref[spans - 1]
    log = kept_ref[spans - 1, 4:5]
    for k in range(spans - 2, -1, -1):
        total = own_ref[k] + kept_ref[k, :1] * total
        log = log + kept_ref[k, 4:5]
    total_ref[...] = total
    line = iota(log_ref.shape, 0)
    log_ref[...] = jnp.where(line == 0, log, 0.0)
    n = total.shape[0]
    sent_ref[:n], sent_ref[n:] = message(total, log)


def back_kernel(bit, place_ref, log_ref, total_ref, got_ref, *refs):
    entering_ref = refs[0] if len(refs) == 6 else None
    total_out, entering_out, sent_out, log_out, factor_out = refs[-5:]
    n = total_ref.shape[0]
    got = got_ref[:n].astype(F32)
    tail = got_ref[n:].astype(F32)
    other_log = tail[0:1] + tail[1:2] + tail[2:3]
    log, before_me, after_me = log_ref[0:1], log_ref[1:2], log_ref[2:3]
    line = iota(log_ref.shape, 0)
    upper = (place_ref[0] // bit % 2 + 0 * line[0:1]) == 1
    kept, other = jnp.exp2(log), jnp.exp2(other_log)
    total = jnp.where(upper, other, 1.0) * total_ref[...] + jnp.where(upper, 1.0, kept) * got
    passed = jnp.where(upper, 0.0, jnp.exp2(after_me)) * got
    total_out[...] = total
    entering_out[...] = passed if entering_ref is None else entering_ref[...] + passed
    first = jnp.where(upper, 1.0, other)
    second = jnp.where(upper, kept, 1.0)
    third = jnp.where(upper, jnp.exp2(before_me), 0.0)
    factor_out[...] = jnp.where(line == 0, first, jnp.where(line == 1, second, third))
    log = log + other_log
    before_me = jnp.where(upper, before_me + other_log, before_me)
    after_me = jnp.where(upper, after_me, after_me + other_log)
    log_out[...] = jnp.where(line == 0, log, jnp.where(line == 1, before_me, after_me))
    sent_out[:n], sent_out[n:] = message(total, log)


def scan_kernel(factor_ref, total_ref, got_ref, *refs):
    entering_ref = refs[0] if len(refs) == 4 else None
    total_out, entering_out, sent_out = refs[-3:]
    factors = factor_ref[...]
    got = got_ref[...].astype(F32)
    total = factors[0:1] * total_ref[...] + factors[1:2] * got
    total_out[...] = total
    sent_out[...] = total.astype(BF16)
    passed = factors[2:3] * got
    entering_out[...] = passed if entering_ref is None else entering_ref[...] + passed


def early_forward_kernel(count, f_ref, *refs):
    pieces, (out_ref, buffer) = refs[:count], refs[count:]
    rows = pieces[0].shape[0]
    for index, piece in enumerate(pieces):
        buffer[index * rows : (index + 1) * rows] = piece[...]
    out_ref[...] = mm(f_ref[...], buffer[...])


def late_forward_kernel(count, f_ref, part_ref, rt_ref, b_ref, kept_ref, *refs):
    pieces, (x_ref, e_ref, total_ref, sent_ref, buffer) = refs[:count], refs[count:]
    rows = pieces[0].shape[0]
    for index, piece in enumerate(pieces):
        buffer[index * rows : (index + 1) * rows] = piece[...]
    x = (part_ref[...] + mm(f_ref[...], buffer[...])).astype(BF16)
    x_ref[...] = x
    total = None
    for k in range(e_ref.shape[0]):
        part = slice(k * SPAN, (k + 1) * SPAN)
        columns = rt_ref[0, part]
        to_end = jnp.exp2(spread_columns(columns[SPAN - 1 : SPAN] - columns))
        scaled = (x[part].astype(F32) * to_end).astype(BF16)
        state = dot(b_ref[part], scaled, ((0,), (0,)))
        e_ref[k] = state
        total = state if total is None else kept_ref[k, :1] * total + state
    total_ref[...] = total
    sent_ref[...] = total.astype(BF16)


def blocks_kernel(halves, has_before, order_ref, g_ref, *refs):
    count = len(halves)
    number = sum(halves)
    arrays, refs = refs[:number], refs[number:]
    if has_before:
        refs = refs[2:]
    away_ref, own_ref, buffer, slots, sems, out_sems = refs
    rows = arrays[0].shape[0]
    wide = g_ref.shape[0]
    copies = []
    at = 0
    for index, parts in enumerate(halves):
        mine = []
        for part in range(parts):
            lanes = pl.ds(part * (wide // parts), wide // parts)
            target = buffer.at[pl.ds(index * rows, rows), lanes]
            copy = pltpu.make_async_copy(arrays[at], target, sems.at[at])
            copy.start()
            mine.append(copy)
            at += 1
        copies.append(mine)
    g = g_ref[...]
    half = away_ref.shape[1] // rows
    bundle = 3 if count % 3 == 0 else count
    for index in range(count):
        for copy in copies[index]:
            copy.wait()
        if (index + 1) % bundle:
            continue
        start = index + 1 - bundle
        product = mm(buffer[start * rows : (index + 1) * rows], g)
        for done in range(start, index + 1):
            part = product[(done - start) * rows : (done - start + 1) * rows]
            slots[done] = part.T.astype(BF16)
            place = order_ref[done]
            lanes = pl.ds(pl.multiple_of(place % half * rows, 128), rows)

            @pl.when(place < half)
            def _():
                target = away_ref.at[:, lanes]
                pltpu.make_async_copy(slots.at[done], target, out_sems.at[done]).start()

            @pl.when(place >= half)
            def _():
                target = own_ref.at[:, lanes]
                pltpu.make_async_copy(slots.at[done], target, out_sems.at[done]).start()

    for index in range(count):
        target = away_ref.at[:, pl.ds(0, rows)]
        pltpu.make_async_copy(slots.at[index], target, out_sems.at[index]).wait()


def after_kernel(*refs):
    pass


def inner_kernel(
    r_ref, rt_ref, g_ref, x_ref, b_ref, c_ref, q_ref, *refs
):
    d_ref, grad_b_ref, grad_c_ref, sum_ref = refs[-4:]
    so_far = refs[:-4]
    step = pl.program_id(1)
    b = b_ref[...]
    c = c_ref[...]
    scores = dot(b, c, ((1,), (1,)))
    running = r_ref[...]
    columns = rt_ref[0]
    top_keep = iota((HALF, SPAN), 1) >= iota((HALF, SPAN), 0)
    low_keep = iota((HALF, HALF), 1) >= iota((HALF, HALF), 0)

    @pl.when(step == 0)
    def _():
        sum_ref[...] = jnp.zeros_like(sum_ref)
        grad_b_ref[...] = so_far[0][...] if so_far else jnp.zeros_like(grad_b_ref)

    rows = []
    lane = iota((SPAN, 2 * P_SIZE), 1)
    later = not_before().astype(BF16)
    top_less = iota((HALF, SPAN), 1) > iota((HALF, SPAN), 0)
    low_less = iota((HALF, HALF), 1) > iota((HALF, HALF), 0)
    top_sum = sum_ref[:HALF]
    low_sum = sum_ref[HALF:, HALF:]
    for pair in range(GROUP // 2):
        lanes = slice(pair * 2 * P_SIZE, (pair + 1) * 2 * P_SIZE)
        g = g_ref[:, lanes].T
        x = x_ref[:, lanes]
        for head in (2 * pair, 2 * pair + 1):
            mine = (lane < P_SIZE) if head == 2 * pair else (lane >= P_SIZE)
            x_head = jnp.where(mine, x, jnp.zeros_like(x))
            row = running[head : head + 1]
            top = jnp.where(top_keep, row - columns[:HALF, head : head + 1], NEVER)
            low = jnp.where(low_keep, row[:, HALF:] - columns[HALF:, head : head + 1], NEVER)
            top = jnp.exp2(top) * mm(x_head[:HALF], g)
            low = jnp.exp2(low) * mm(x_head[HALF:], g[:, HALF:])
            top_sum = top_sum + top
            low_sum = low_sum + low
            top = mm((top * scores[:HALF]).astype(BF16), later)
            low = mm((low * scores[HALF:, HALF:]).astype(BF16), later[HALF:, HALF:])
            top_row = jnp.sum(jnp.where(top_less, top, 0.0), axis=0, keepdims=True)
            low_row = jnp.sum(jnp.where(low_less, low, 0.0), axis=0, keepdims=True)
            rows.append(jnp.concatenate([top_row[:, :HALF], top_row[:, HALF:] + low_row], axis=1))
    sum_ref[:HALF] = top_sum
    sum_ref[HALF:, HALF:] = low_sum
    to_end = jnp.exp2(spread_columns(columns[SPAN - 1 : SPAN] - columns))
    scaled = x_ref[...].astype(F32) * to_end
    ends = dot(one_hot(BF16), (scaled * mm(b, q_ref[0])).astype(BF16), ((1,), (1,)))
    d_ref[...] = jnp.concatenate(rows, axis=0) + sum_over(ends, before())
    grad_b_ref[...] += dot(scaled.astype(BF16), q_ref[0], ((1,), (1,)))

    @pl.when(step == pl.num_programs(1) - 1)
    def _():
        total = sum_ref[...].astype(BF16)
        grad_b_ref[...] += mm(total, c)
        part = dot(total, b, ((0,), (0,)))
        grad_c_ref[...] = part + so_far[1][...] if so_far else part


def state_kernel(
    rt_ref, g_ref, c_ref, s_ref, e_ref, q_ref, a_ref, d_part_ref, c_part_ref, d_ref, grad_c_ref, held
):
    span, group = pl.program_id(0), pl.program_id(1)

    @pl.when(group == 0)
    def _():
        grad_c_ref[...] = c_part_ref[...]

    @pl.when(span == 0)
    def _():
        held[group] = s_ref[...]

    state = held[group]
    low = state.astype(BF16)
    scaled = g_ref[...].astype(F32) * jnp.exp2(spread_columns(rt_ref[0]))
    ends = dot(one_hot(BF16), (scaled * mm(c_ref[...], low)).astype(BF16), ((1,), (1,)))
    grad_c_ref[...] += dot(scaled.astype(BF16), low, ((1,), (1,)))
    product = jnp.sum(q_ref[0].astype(F32) * state, axis=0, keepdims=True) * a_ref[0, :1]
    high, middle, last = thirds(product)
    row = iota((8, WIDE), 0)
    stacked = jnp.where(row == 0, high, jnp.where(row == 1, middle, jnp.where(row == 2, last, 0.0)))
    kept = dot(one_hot(BF16), stacked.astype(BF16), ((1,), (1,)))
    kept = jnp.sum(kept, axis=1, keepdims=True)
    d_ref[...] = d_part_ref[...] + sum_over(ends, not_before()) + kept
    held[group] = e_ref[0] + a_ref[0, :1] * state


def call(kernel, grid, in_specs, out_specs, out_shape, flops, size, scratch=()):
    return pl.pallas_call(
        kernel,
        grid=grid,
        in_specs=in_specs,
        out_specs=out_specs,
        out_shape=out_shape,
        scratch_shapes=list(scratch),
        cost_estimate=pl.CostEstimate(flops=flops, bytes_accessed=size, transcendentals=0),
        compiler_params=pltpu.CompilerParams(
            dimension_semantics=("arbitrary",) * len(grid), vmem_limit_bytes=GRANT
        ),
    )


def run_spec(at=0):
    return pl.BlockSpec((GROUP, SPAN), lambda k, h: (h + at, k))


def run_t_spec(at=0):
    return pl.BlockSpec((1, SPAN, GROUP), lambda k, h: (h + at, k, 0))


def rows_spec(at=0):
    return pl.BlockSpec((SPAN, WIDE), lambda k, h: (k, h + at))


def state_spec(at=0):
    return pl.BlockSpec((1, 2 * P_SIZE, WIDE), lambda k, h: (k, 0, h + at))


def kept_spec(at=0):
    return pl.BlockSpec((1, 8, WIDE), lambda k, h: (k, 0, h + at))


SHARED = pl.BlockSpec((SPAN, 2 * P_SIZE), lambda k, h: (k, 0))
GAIN = pl.BlockSpec((1, WIDE), lambda k, h: (0, h))
ANYWHERE = pl.BlockSpec(memory_space=pl.ANY)
SCALARS = pl.BlockSpec(memory_space=pltpu.SMEM)


def shape(*dims, dtype=F32):
    return jax.ShapeDtypeStruct(dims, dtype)


def swap(value, axis, bit):
    count = lax.axis_size(axis)
    return lax.ppermute(value, axis, [(i, i ^ bit) for i in range(count)])


def block_products(kept):
    count = lax.axis_size("ctx")
    place = lax.axis_index("ctx")
    steps = []
    before_me = jnp.ones_like(kept)
    after_me = jnp.ones_like(kept)
    bit = 1
    while bit < count:
        other = swap(kept, "ctx", bit)
        upper = (place & bit) != 0
        steps.append((bit, upper, kept, other, before_me, after_me))
        before_me = jnp.where(upper, before_me * other, before_me)
        after_me = jnp.where(upper, after_me, after_me * other)
        kept = kept * other
        bit *= 2
    return steps


def scan_states(total, steps, reverse):
    entering = jnp.zeros_like(total)
    for bit, upper, kept, other, before_me, after_me in steps:
        got = swap(total.astype(BF16), "ctx", bit).astype(F32)
        if reverse:
            entering = entering + jnp.where(upper, 0.0, after_me) * got
            total = jnp.where(upper, got + other * total, total + kept * got)
        else:
            entering = entering + jnp.where(upper, before_me, 0.0) * got
            total = jnp.where(upper, kept * got + total, other * total + got)
    return entering


def head_sum(value):
    bit = 1
    while bit < lax.axis_size("head"):
        value = value.astype(BF16)
        value = value.astype(F32) + swap(value, "head", bit).astype(F32)
        bit *= 2
    return value


PLANE = 4


def after(values, *tokens):
    out = pl.pallas_call(
        after_kernel,
        in_specs=[ANYWHERE] * (len(values) + len(tokens)),
        out_specs=[ANYWHERE] * len(values),
        out_shape=[shape(*value.shape, dtype=value.dtype) for value in values],
        input_output_aliases={index: index for index in range(len(values))},
        cost_estimate=pl.CostEstimate(flops=0, bytes_accessed=0, transcendentals=0),
    )(*values, *tokens)
    return list(out)


def shift(value, by):
    count = lax.axis_size("ctx")
    return lax.ppermute(value, "ctx", [(i, (i + PLANE * by) % count) for i in range(count)])


def swap_x(value):
    return swap(value, "ctx", 1)


def swap_y(value):
    return swap(value, "ctx", 2)


EARLY = [(k, flip) for k in (0, 1, 3) for flip in range(3)]
LATE = [(0, 3), (1, 3), (3, 3), (2, 0), (2, 1), (2, 2), (2, 3)]


def block_order():
    place = lax.axis_index("ctx")
    layers = lax.axis_size("ctx") // PLANE
    layer, spot = place // PLANE, place % PLANE
    order = [(layer + layers - k) % layers * PLANE + (spot ^ flip) for k, flip in EARLY + LATE]
    return jnp.stack(order).astype(jnp.int32)


def gather_weight(w, sizes):
    ends = [sum(sizes[: j + 1]) * P_SIZE for j in range(len(sizes))]
    parts = [w[:, end - size * P_SIZE : end] for end, size in zip(ends, sizes)]
    return [lax.all_gather(part, "ctx", axis=0, tiled=True) for part in parts]


def forward(features, first, weight, running_t, b_rows, here):
    own, other = features
    length = own.shape[0]
    n = b_rows.shape[1]
    width, wide = weight.shape
    deep = width // 4
    spans = length // SPAN

    def depth(k, first_ref):
        return (k // 2 ^ first_ref[0]) * 2 + k % 2

    return pl.pallas_call(
        forward_kernel,
        grid_spec=pltpu.PrefetchScalarGridSpec(
            num_scalar_prefetch=1,
            grid=(wide // WIDE, 4),
            in_specs=[
                pl.BlockSpec((length, deep), lambda h, k, first_ref: (0, jnp.minimum(k, 1))),
                pl.BlockSpec((length, deep), lambda h, k, first_ref: (0, jnp.maximum(k - 2, 0))),
                pl.BlockSpec((deep, WIDE), lambda h, k, first_ref: (depth(k, first_ref), h)),
                pl.BlockSpec((1, length, GROUP), lambda h, k, first_ref: (h + here, 0, 0)),
                pl.BlockSpec((length, n), lambda h, k, first_ref: (0, 0)),
            ],
            out_specs=[
                pl.BlockSpec((length, WIDE), lambda h, k, first_ref: (0, h)),
                pl.BlockSpec((spans, n, WIDE), lambda h, k, first_ref: (0, 0, h)),
            ],
            scratch_shapes=[pltpu.VMEM((length, WIDE), F32)],
        ),
        out_shape=[shape(length, wide, dtype=BF16), shape(spans, n, wide)],
        cost_estimate=pl.CostEstimate(
            flops=2 * length * wide * width, bytes_accessed=2 * wide * width, transcendentals=0
        ),
        compiler_params=pltpu.CompilerParams(
            dimension_semantics=("arbitrary", "arbitrary"), vmem_limit_bytes=GRANT
        ),
    )(first, own, other, weight, running_t, b_rows)


def multiply(grad_x, weight, at, half, halves, before=None, other=None):
    length = grad_x.shape[0]
    width, wide = weight.shape
    tiles = width // halves // WIDE
    tile = pl.BlockSpec((length, WIDE), lambda j, half_ref: (0, half_ref[0] * tiles + j))
    plain = pl.BlockSpec((length, WIDE), lambda j, half_ref: (0, j))
    in_specs = [
        pl.BlockSpec((length, wide), lambda j, half_ref: (0, at)),
        pl.BlockSpec((WIDE, wide), lambda j, half_ref: (half_ref[0] * tiles + j, 0)),
    ]
    operands = [grad_x, weight]
    if before is not None:
        in_specs.append(tile)
        operands.append(before)
    if other is not None:
        in_specs.append(plain)
        operands.append(other)
    return pl.pallas_call(
        functools.partial(product_kernel, before is not None, other is not None),
        grid_spec=pltpu.PrefetchScalarGridSpec(
            num_scalar_prefetch=1,
            grid=(tiles,),
            in_specs=in_specs,
            out_specs=plain,
        ),
        out_shape=shape(length, width // halves, dtype=BF16),
        cost_estimate=pl.CostEstimate(
            flops=2 * length * wide * width // halves,
            bytes_accessed=2 * wide * width // halves,
            transcendentals=0,
        ),
        compiler_params=pltpu.CompilerParams(
            dimension_semantics=("arbitrary",), vmem_limit_bytes=GRANT
        ),
    )(half, *operands)


def early_forward(features, pieces):
    length = features.shape[0]
    rows, columns = pieces[0].shape
    deep = rows * len(pieces)
    return call(
        functools.partial(early_forward_kernel, len(pieces)),
        (columns // WIDE,),
        [pl.BlockSpec((length, deep), lambda h: (0, 0))]
        + [pl.BlockSpec((rows, WIDE), lambda h: (0, h))] * len(pieces),
        pl.BlockSpec((length, WIDE), lambda h: (0, h)),
        shape(length, columns),
        2 * length * columns * deep,
        2 * columns * deep,
        [pltpu.VMEM((deep, WIDE), BF16)],
    )(features, *pieces)


def late_forward(features, part, pieces, running_t, b_rows, kept, here):
    length = features.shape[0]
    rows, columns = pieces[0].shape
    deep = rows * len(pieces)
    n = b_rows.shape[1]
    spans = length // SPAN
    state = pl.BlockSpec((n, WIDE), lambda h: (0, h))
    return call(
        functools.partial(late_forward_kernel, len(pieces)),
        (columns // WIDE,),
        [
            pl.BlockSpec((length, deep), lambda h: (0, 0)),
            pl.BlockSpec((length, WIDE), lambda h: (0, h + here)),
            pl.BlockSpec((1, length, GROUP), lambda h: (h + here, 0, 0)),
            pl.BlockSpec((length, n), lambda h: (0, 0)),
            pl.BlockSpec((spans, 8, WIDE), lambda h: (0, 0, h + here)),
        ]
        + [pl.BlockSpec((rows, WIDE), lambda h: (0, h))] * len(pieces),
        [
            pl.BlockSpec((length, WIDE), lambda h: (0, h)),
            pl.BlockSpec((spans, n, WIDE), lambda h: (0, 0, h)),
            state,
            state,
        ],
        [
            shape(length, columns, dtype=BF16),
            shape(spans, n, columns),
            shape(n, columns),
            shape(n, columns, dtype=BF16),
        ],
        2 * length * columns * deep,
        2 * columns * deep,
        [pltpu.VMEM((deep, WIDE), BF16)],
    )(features, part, running_t, b_rows, kept, *pieces)


def multiply_blocks(order, grad_x, pieces, so_far):
    columns, length = grad_x.shape
    arrays = [array for piece in pieces for array in piece]
    rows = arrays[0].shape[0]
    count = len(pieces)
    half = shape(length, lax.axis_size("ctx") * rows // 2, dtype=BF16)
    first = 2 + len(arrays)
    return pl.pallas_call(
        functools.partial(blocks_kernel, [len(piece) for piece in pieces], bool(so_far)),
        grid=(1,),
        in_specs=[SCALARS, pl.BlockSpec((columns, length), lambda h: (0, 0))]
        + [ANYWHERE] * (len(arrays) + len(so_far)),
        out_specs=[ANYWHERE, ANYWHERE],
        out_shape=[half, half],
        input_output_aliases={first + k: k for k in range(len(so_far))},
        scratch_shapes=[
            pltpu.VMEM((rows * count, columns), BF16),
            pltpu.VMEM((count, length, rows), BF16),
            pltpu.SemaphoreType.DMA((len(arrays),)),
            pltpu.SemaphoreType.DMA((count,)),
        ],
        cost_estimate=pl.CostEstimate(
            flops=2 * length * columns * rows * count,
            bytes_accessed=2 * columns * rows * count,
            transcendentals=0,
        ),
        compiler_params=pltpu.CompilerParams(
            dimension_semantics=("arbitrary",), vmem_limit_bytes=GRANT
        ),
    )(order, grad_x, *arrays, *so_far)


def back_start(own_grads, kept):
    spans, n, columns = own_grads.shape
    return call(
        start_kernel,
        (columns // WIDE,),
        [
            pl.BlockSpec((spans, n, WIDE), lambda h: (0, 0, h)),
            pl.BlockSpec((spans, 8, WIDE), lambda h: (0, 0, h)),
        ],
        [pl.BlockSpec((rows, WIDE), lambda h: (0, h)) for rows in (n, 8, n + TAIL)],
        [shape(n, columns), shape(8, columns), shape(n + TAIL, columns, dtype=BF16)],
        0,
        14 * n * columns,
    )(own_grads, kept)


def back_step(place, log, total, sent, entering, bit):
    got = swap(sent, "ctx", bit)
    n, columns = total.shape
    tall = [pl.BlockSpec((rows, WIDE), lambda h: (0, h)) for rows in (8, n, n + TAIL)]
    return call(
        functools.partial(back_kernel, bit),
        (columns // WIDE,),
        [SCALARS] + tall + [tall[1]] * len(entering),
        [tall[1], tall[1], tall[2], tall[0], tall[0]],
        [
            shape(n, columns),
            shape(n, columns),
            shape(n + TAIL, columns, dtype=BF16),
            shape(8, columns),
            shape(8, columns),
        ],
        0,
        18 * n * columns,
    )(place, log, total, got, *entering)


def scan_step(factors, here, total, sent, entering, bit):
    got = swap(sent, "ctx", bit)
    n, columns = total.shape
    block = pl.BlockSpec((n, WIDE), lambda h: (0, h))
    return call(
        scan_kernel,
        (columns // WIDE,),
        [pl.BlockSpec((8, WIDE), lambda h: (0, h + here)), block, block]
        + [block] * len(entering),
        [block, block, block],
        [shape(n, columns), shape(n, columns), shape(n, columns, dtype=BF16)],
        0,
        14 * n * columns,
    )(factors, total, got, *entering)


def local(inputs, w_in, b_rows, c_rows, log_decay, skip_gain, grad_out):
    groups = log_decay.shape[0] // GROUP
    layered = lax.axis_size("ctx") == 4 * PLANE and lax.axis_size("head") == 2
    if layered and groups % 2 == 0 and w_in.shape[0] == 256:
        return local_layered(inputs, w_in, b_rows, c_rows, log_decay, skip_gain, grad_out)
    return local_plain(inputs, w_in, b_rows, c_rows, log_decay, skip_gain, grad_out)


def prepare(log_decay, grad_out, c_rows):
    length, columns = grad_out.shape
    heads = log_decay.shape[0]
    spans = length // SPAN
    groups = heads // GROUP
    n = c_rows.shape[1]
    return call(
        decay_kernel,
        (spans, groups),
        [run_spec(), rows_spec(), SHARED],
        [run_spec(), run_t_spec(), kept_spec(), state_spec()],
        [
            shape(heads, length),
            shape(groups, length, GROUP),
            shape(spans, 8, columns),
            shape(spans, n, columns),
        ],
        2 * length * columns * n,
        6 * length * columns,
    )(log_decay, grad_out, c_rows)


def inner(grid, here, wide, operands, so_far):
    length = operands[2].shape[0]
    n = operands[4].shape[1]
    specs = [
        run_spec(here),
        run_t_spec(here),
        rows_spec(here),
        rows_spec(),
        SHARED,
        SHARED,
        state_spec(here),
    ]
    return call(
        inner_kernel,
        grid,
        specs + [SHARED] * len(so_far),
        [run_spec(), SHARED, SHARED],
        [shape(wide // P_SIZE, length), shape(length, n), shape(length, n)],
        12 * length * wide * SPAN,
        6 * length * wide,
        [pltpu.VMEM((SPAN, SPAN), F32)],
    )(*operands, *so_far)


def state_terms(grid, here, wide, operands):
    length = operands[1].shape[0]
    n = operands[2].shape[1]
    return call(
        state_kernel,
        grid,
        [
            run_t_spec(here),
            rows_spec(here),
            SHARED,
            pl.BlockSpec((n, WIDE), lambda k, h: (0, h)),
            state_spec(),
            state_spec(here),
            kept_spec(here),
            run_spec(),
            SHARED,
        ],
        [run_spec(), SHARED],
        [shape(wide // P_SIZE, length), shape(length, n)],
        4 * length * wide * n,
        6 * length * wide,
        [pltpu.VMEM((grid[1], n, WIDE), F32)],
    )(*operands)


def local_layered(inputs, w_in, b_rows, c_rows, log_decay, skip_gain, grad_out):
    length, columns = grad_out.shape
    heads = log_decay.shape[0]
    spans = length // SPAN
    groups = heads // GROUP
    place = lax.axis_index("head").astype(jnp.int32)
    half = columns // 2
    w_a, w_b = w_in[:, :half], w_in[:, half:]
    order = block_order()
    blocks = order.shape[0]
    width = blocks * w_in.shape[0]

    z1, z3 = shift(w_in, 1), shift(w_in, 3)
    own_x, own_y = swap_x(w_in), swap_y(w_in)
    other = swap(inputs, "head", 1)
    running, running_t, kept, own_grads = prepare(log_decay, grad_out, c_rows)
    spot = lax.axis_index("ctx").astype(jnp.int32)[None]
    back, log, sent = back_start(own_grads, kept)
    sent = after([sent], other)[0]
    back, leaving, sent, log, factors_1 = back_step(spot, log, back, sent, (), 1)

    z1, w_a, w_b = after([z1, w_a, w_b], own_x, own_y, z3)
    z2a, z2b = shift(w_a, 2), shift(w_b, 2)
    x1, y1 = swap_x(z1), swap_y(z1)
    z3 = after([z3], sent)[0]
    x3, y3 = swap_x(z3), swap_y(z3)
    back, leaving, sent, log, factors_2 = back_step(spot, log, back, sent, (leaving,), 2)
    order_own = (order + place * (blocks // 2)) % blocks
    cut = len(EARLY) * w_in.shape[0]
    early_features, late_features = call(
        arrange_kernel,
        (1,),
        [SCALARS] + [pl.BlockSpec((length, width // 2), lambda h: (0, 0))] * 2,
        [pl.BlockSpec((length, wide), lambda h: (0, 0)) for wide in (cut, width - cut)],
        [shape(length, wide, dtype=BF16) for wide in (cut, width - cut)],
        0,
        4 * length * width,
        [pltpu.VMEM((length, width), BF16)],
    )(order_own, inputs, other)

    z2a, x1, y3, own_y = after(
        [z2a, x1, y3, own_y], y1, x3, z2b, sent, early_features, late_features
    )
    x1_a, x1_b = x1[:, :half], x1[:, half:]
    y3_a, y3_b = y3[:, :half], y3[:, half:]
    own_y_a, own_y_b = own_y[:, :half], own_y[:, half:]
    x2a, y2a = swap_x(z2a), swap_y(z2a)
    d3a, d1a = swap_x(y3_a), swap_y(x1_a)
    back, leaving, sent, log, factors_4 = back_step(spot, log, back, sent, (leaving,), 4)
    early = [w_in, own_x, own_y, z1, x1, y1, z3, x3, y3]
    part = early_forward(early_features, early)

    own_y_a, x2a, z2b, y3_b, x1_b = after(
        [own_y_a, x2a, z2b, y3_b, x1_b], y2a, d3a, d1a, part, sent
    )
    d0a, d2a = swap_x(own_y_a), swap_y(x2a)
    x2b, y2b = swap_x(z2b), swap_y(z2b)
    d3b, d1b = swap_x(y3_b), swap_y(x1_b)
    back, leaving, sent, log, factors_8 = back_step(spot, log, back, sent, (leaving,), 8)
    leaving_all = [leaving]
    for k in range(spans - 1, 0, -1):
        leaving_all.insert(0, own_grads[k] + kept[k, :1] * leaving_all[0])
    leaving_all = jnp.stack([value.astype(BF16) for value in leaving_all])
    skip = jnp.repeat(skip_gain, P_SIZE)[None]
    grad_x = grad_rows(running, running_t, grad_out, b_rows, c_rows, leaving_all, skip, True)
    late_a = [d0a, d1a, d3a, z2a, x2a, y2a, d2a]
    x_a, states_a, total_a, sent_a = late_forward(
        late_features, part, late_a, running_t, b_rows, kept, 0
    )

    own_y_b, x2b, sent_a = after([own_y_b, x2b, sent_a], y2b, d3b, d1b, grad_x)
    d0b, d2b = swap_x(own_y_b), swap_y(x2b)
    total_a, entering_a, sent_a = scan_step(factors_1, 0, total_a, sent_a, (), 1)
    order_away = (order + (1 - place) * (blocks // 2)) % blocks
    early_order, late_order = order_away[: len(EARLY)], order_away[len(EARLY) :]
    product = multiply_blocks(early_order, grad_x, [[piece] for piece in early], ())

    d0b, d2b = after([d0b, d2b], sent_a, product[0])
    late_b = [d0b, d1b, d3b, z2b, x2b, y2b, d2b]
    here = groups // 2
    x_b, states_b, total_b, sent_b = late_forward(
        late_features, part, late_b, running_t, b_rows, kept, here
    )
    pairs = list(zip(late_a, late_b))
    shared = (running, running_t, grad_out)
    grid = (spans, here)
    entering_b = ()
    for factors, bit in ((factors_1, 1), (factors_2, 2), (factors_4, 4), (factors_8, 8)):
        if bit > 1:
            total_a, entering_a, sent_a = scan_step(
                factors, 0, total_a, sent_a, (entering_a,), bit
            )
        if bit == 4:
            sent_b = after([sent_b], away)[0]
        if bit == 8:
            sent_b = after([sent_b], grad_b)[0]
        total_b, entering_b, sent_b = scan_step(factors, here, total_b, sent_b, entering_b, bit)
        entering_b = (entering_b,)
        if bit == 1:
            product = after(list(product), sent_b)
            away, own = multiply_blocks(late_order, grad_x, pairs, product)
            got = swap(away, "head", 1)
        if bit == 2:
            x_a = after([x_a], sent_b)[0]
            inner_a = shared + (x_a, b_rows, c_rows, leaving_all)
            decay_a, grad_b, grad_c = inner(grid, 0, half, inner_a, ())
        if bit == 4:
            x_b = after([x_b], sent_b)[0]
            inner_b = shared + (x_b, b_rows, c_rows, leaving_all)
            decay_b, grad_b, grad_c = inner(grid, here, half, inner_b, (grad_b, grad_c))
    entering_b = entering_b[0]
    grad_b = head_sum(grad_b)

    common = (running_t, grad_out, c_rows)
    state_a = common + (entering_a, states_a, leaving_all, kept, decay_a, grad_c)
    decay_a, grad_c = state_terms(grid, 0, half, state_a)
    state_b = common + (entering_b, states_b, leaving_all, kept, decay_b, grad_c)
    decay_b, grad_c = state_terms(grid, here, half, state_b)
    grad_inputs = (own.astype(F32) + got.astype(F32)).astype(BF16)
    grad_log_decay = jnp.concatenate([decay_a, decay_b], axis=0)
    return (grad_inputs, grad_b, head_sum(grad_c), grad_log_decay)


def grad_rows(running, running_t, grad_out, b_rows, c_rows, leaving, skip, transposed):
    length, columns = grad_out.shape
    spec, dims = rows_spec(), (length, columns)
    if transposed:
        spec, dims = pl.BlockSpec((WIDE, SPAN), lambda k, h: (h, k)), (columns, length)
    return call(
        functools.partial(grad_x_kernel, transposed),
        (length // SPAN, running_t.shape[0]),
        [run_spec(), run_t_spec(), rows_spec(), SHARED, SHARED, state_spec(), GAIN],
        spec,
        shape(*dims, dtype=BF16),
        8 * length * columns * SPAN,
        6 * length * columns,
    )(running, running_t, grad_out, b_rows, c_rows, leaving, skip)


def local_plain(inputs, w_in, b_rows, c_rows, log_decay, skip_gain, grad_out):
    length, columns = grad_out.shape
    heads = log_decay.shape[0]
    spans = length // SPAN
    groups = heads // GROUP
    n = b_rows.shape[1]
    grid = (spans, groups)

    sizes = (heads // 2, heads // 4, heads // 4) if heads % (4 * GROUP) == 0 else (heads,)
    weights = gather_weight(w_in, sizes)
    two = lax.axis_size("head") == 2
    place = lax.axis_index("head").astype(jnp.int32)[None]
    width = weights[0].shape[0]
    if two:
        features = (inputs, swap(inputs, "head", 1))
        first = place
    else:
        features = lax.all_gather(inputs, "head", axis=1, tiled=True)
        features = (features[:, : width // 2], features[:, width // 2 :])
        first = jnp.zeros((1,), jnp.int32)

    running, running_t, kept, own_grads = call(
        decay_kernel,
        grid,
        [run_spec(), rows_spec(), SHARED],
        [run_spec(), run_t_spec(), kept_spec(), state_spec()],
        [
            shape(heads, length),
            shape(groups, length, GROUP),
            shape(spans, 8, columns),
            shape(spans, n, columns),
        ],
        2 * length * columns * n,
        6 * length * columns,
    )(log_decay, grad_out, c_rows)

    kept_total = kept[0, :1]
    for k in range(1, spans):
        kept_total = kept_total * kept[k, :1]
    steps = block_products(kept_total)

    total = own_grads[spans - 1]
    for k in range(spans - 2, -1, -1):
        total = own_grads[k] + kept[k, :1] * total
    leaving = [scan_states(total, steps, True)]
    for k in range(spans - 1, 0, -1):
        leaving.insert(0, own_grads[k] + kept[k, :1] * leaving[0])
    leaving = jnp.stack([value.astype(BF16) for value in leaving])

    skip = jnp.repeat(skip_gain, P_SIZE)[None]
    grad_x = grad_rows(running, running_t, grad_out, b_rows, c_rows, leaving, skip, False)

    grad_b = grad_c = product = None
    tokens = ()
    decay_parts = []
    at = 0
    for index, size in enumerate(sizes):
        wide = size * P_SIZE
        here = at // GROUP
        count = size // GROUP
        weight = weights[index]
        if tokens:
            weight = after([weight], *tokens)[0]
        x, own_states = forward(features, first, weight, running_t, b_rows, here)

        chunk = slice(at * P_SIZE, at * P_SIZE + wide)
        total = own_states[0]
        for k in range(1, spans):
            total = kept[k, :1, chunk] * total + own_states[k]
        cut = [step[:2] + tuple(value[:, chunk] for value in step[2:]) for step in steps]
        entering = scan_states(total, cut, False)

        so_far = () if grad_b is None else (grad_b, grad_c)
        decay_part, grad_b, grad_c = call(
            inner_kernel,
            (spans, count),
            [
                run_spec(here),
                run_t_spec(here),
                rows_spec(here),
                rows_spec(),
                SHARED,
                SHARED,
                state_spec(here),
            ]
            + [SHARED] * len(so_far),
            [run_spec(), SHARED, SHARED],
            [shape(size, length), shape(length, n), shape(length, n)],
            12 * length * wide * SPAN,
            6 * length * wide,
            [pltpu.VMEM((SPAN, SPAN), F32)],
        )(running, running_t, grad_out, x, b_rows, c_rows, leaving, *so_far)
        decay_part, grad_c = call(
            state_kernel,
            (spans, count),
            [
                run_t_spec(here),
                rows_spec(here),
                SHARED,
                pl.BlockSpec((n, WIDE), lambda k, h: (0, h)),
                state_spec(),
                state_spec(here),
                kept_spec(here),
                run_spec(),
                SHARED,
            ],
            [run_spec(), SHARED],
            [shape(size, length), shape(length, n)],
            4 * length * wide * n,
            6 * length * wide,
            [pltpu.VMEM((count, n, WIDE), F32)],
        )(running_t, grad_out, c_rows, entering, own_states, leaving, kept, decay_part, grad_c)
        decay_parts.append(decay_part)

        if index < len(sizes) - 1:
            zero = jnp.zeros((1,), jnp.int32)
            product = multiply(grad_x, weight, at // size, zero, 1, product)
            tokens = (product, grad_b, entering)
        elif two:
            sent = multiply(grad_x, weight, at // size, 1 - place, 2, product)
            got = swap(sent, "head", 1)
            grad_inputs = multiply(grad_x, weight, at // size, place, 2, product, got)
        else:
            zero = jnp.zeros((1,), jnp.int32)
            product = multiply(grad_x, weight, at // size, zero, 1, product)
            grad_inputs = lax.psum_scatter(product, "head", scatter_dimension=1, tiled=True)
        at += size

    return (grad_inputs, head_sum(grad_b), head_sum(grad_c), jnp.concatenate(decay_parts, axis=0))


def solution(mesh):
    in_specs = (
        P("ctx", "head"),
        P("ctx", "head"),
        P("ctx", None),
        P("ctx", None),
        P("head", "ctx"),
        P("head"),
        P("ctx", "head"),
    )
    out_specs = (P("ctx", "head"), P("ctx", None), P("ctx", None), P("head", "ctx"))
    return jax.shard_map(local, mesh=mesh, in_specs=in_specs, out_specs=out_specs, check_vma=False)
```

```python
import functools

import jax
import jax.numpy as jnp
from jax import lax
from jax.experimental import pallas as pl
from jax.experimental.pallas import tpu as pltpu
from jax.sharding import PartitionSpec as P

SPAN = 256
HALF = SPAN // 2
P_SIZE = 64
GROUP = 8
WIDE = GROUP * P_SIZE
LOG2E = 1.4426950408889634
NEVER = -1e30
GRANT = 62 * 2**20

F32 = jnp.float32
BF16 = jnp.bfloat16
EXACT = lax.Precision.HIGHEST


def dot(a, b, dims, precision=None):
    return lax.dot_general(a, b, (dims, ((), ())), precision=precision, preferred_element_type=F32)


def mm(a, b, precision=None):
    return dot(a, b, ((1,), (0,)), precision)


def iota(shape, dim):
    return lax.broadcasted_iota(jnp.int32, shape, dim)


def one_hot(dtype):
    return (iota((GROUP, WIDE), 0) == iota((GROUP, WIDE), 1) // P_SIZE).astype(dtype)


def not_before():
    return (iota((SPAN, SPAN), 0) >= iota((SPAN, SPAN), 1)).astype(F32)


def before():
    return (iota((SPAN, SPAN), 0) < iota((SPAN, SPAN), 1)).astype(F32)


def same():
    return (iota((SPAN, SPAN), 0) == iota((SPAN, SPAN), 1)).astype(F32)


def first_head():
    return iota((SPAN, 2 * P_SIZE), 1) < P_SIZE


def pair_columns(columns, pair):
    shape = (columns.shape[0], 2 * P_SIZE)
    left = jnp.broadcast_to(columns[:, 2 * pair : 2 * pair + 1], shape)
    right = jnp.broadcast_to(columns[:, 2 * pair + 1 : 2 * pair + 2], shape)
    return jnp.where(iota(shape, 1) < P_SIZE, left, right)


def spread_columns(columns):
    return jnp.concatenate([pair_columns(columns, pair) for pair in range(GROUP // 2)], axis=1)


def thirds(value):
    high = value.astype(BF16).astype(F32)
    middle = (value - high).astype(BF16).astype(F32)
    return high, middle, value - high - middle


def sum_over(value, mask):
    rows = value.shape[0]
    parts = mm(jnp.concatenate(thirds(value), axis=0).astype(BF16), mask.astype(BF16))
    return parts[:rows] + parts[rows : 2 * rows] + parts[2 * rows :]


def decay_kernel(d_ref, g_ref, c_ref, r_ref, rt_ref, a_ref, gt_ref):
    row_sums = sum_over(d_ref[...] * LOG2E, 1.0 - not_before() + same())
    r_ref[...] = row_sums
    padded = jnp.concatenate([row_sums, jnp.zeros((2 * P_SIZE - GROUP, SPAN), F32)], axis=0)
    running = padded.T[:, :GROUP]
    rt_ref[0] = running
    growth = jnp.exp2(spread_columns(running))
    last = spread_columns(running[SPAN - 1 : SPAN])
    a_ref[0] = jnp.where(iota((8, WIDE), 0) < 4, jnp.exp2(last), last)
    scaled = (g_ref[...].astype(F32) * growth).astype(BF16)
    gt_ref[0] = dot(c_ref[...], scaled, ((0,), (0,)))


def grad_x_kernel(transposed, r_ref, rt_ref, g_ref, b_ref, c_ref, q_ref, skip_ref, out_ref):
    b = b_ref[...]
    scores = dot(b, c_ref[...], ((1,), (1,)))
    running = r_ref[...]
    columns = rt_ref[0]
    top_keep = iota((HALF, SPAN), 1) >= iota((HALF, SPAN), 0)
    low_keep = iota((HALF, HALF), 1) >= iota((HALF, HALF), 0)
    to_end = jnp.exp2(spread_columns(columns[SPAN - 1 : SPAN] - columns))
    from_state = mm(b, q_ref[0]) * to_end
    for pair in range(GROUP // 2):
        lanes = slice(pair * 2 * P_SIZE, (pair + 1) * 2 * P_SIZE)
        g = g_ref[:, lanes]
        parts = []
        for head in (2 * pair, 2 * pair + 1):
            row = running[head : head + 1]
            top = jnp.where(top_keep, row - columns[:HALF, head : head + 1], NEVER)
            low = jnp.where(low_keep, row[:, HALF:] - columns[HALF:, head : head + 1], NEVER)
            parts.append((jnp.exp2(top) * scores[:HALF]).astype(BF16))
            low = (jnp.exp2(low) * scores[HALF:, HALF:]).astype(BF16)
            parts.append(jnp.concatenate([jnp.zeros((HALF, HALF), BF16), low], axis=1))
        product = mm(jnp.concatenate(parts, axis=0), g)
        parts = [product[:SPAN], product[SPAN:]]
        inner = jnp.where(first_head(), parts[0], parts[1])
        total = inner + skip_ref[:, lanes] * g.astype(F32) + from_state[:, lanes]
        if transposed:
            out_ref[lanes, :] = total.T.astype(BF16)
        else:
            out_ref[:, lanes] = total.astype(BF16)


def forward_kernel(half_ref, own_ref, other_ref, w_ref, rt_ref, b_ref, x_ref, e_ref, total_ref):
    step = pl.program_id(1)

    @pl.when(step == 0)
    def _():
        total_ref[...] = jnp.zeros_like(total_ref)

    half = pl.num_programs(1) // 2

    @pl.when(step < half)
    def _():
        total_ref[...] += mm(own_ref[...], w_ref[...])

    @pl.when(step >= half)
    def _():
        total_ref[...] += mm(other_ref[...], w_ref[...])

    @pl.when(step == pl.num_programs(1) - 1)
    def _():
        x = total_ref[...].astype(BF16)
        x_ref[...] = x
        for k in range(e_ref.shape[0]):
            rows = slice(k * SPAN, (k + 1) * SPAN)
            columns = rt_ref[0, rows]
            to_end = jnp.exp2(spread_columns(columns[SPAN - 1 : SPAN] - columns))
            scaled = (x[rows].astype(F32) * to_end).astype(BF16)
            e_ref[k] = dot(b_ref[rows], scaled, ((0,), (0,)))


def product_kernel(has_before, has_other, half_ref, g_ref, w_ref, *refs):
    refs = list(refs)
    total = dot(g_ref[...], w_ref[...], ((1,), (1,)))
    if has_before:
        total = total + refs.pop(0)[...].astype(F32)
    if has_other:
        total = total.astype(BF16).astype(F32) + refs.pop(0)[...].astype(F32)
    refs[0][...] = total.astype(BF16)


def arrange_kernel(order_ref, own_ref, other_ref, early_ref, late_ref, both_ref):
    half = own_ref.shape[1]
    both_ref[:, :half] = own_ref[...]
    both_ref[:, half:] = other_ref[...]
    unit = 2 * half // order_ref.shape[0]
    cut = early_ref.shape[1]
    for index in range(order_ref.shape[0]):
        source = pl.ds(pl.multiple_of(order_ref[index] * unit, 128), unit)
        at = index * unit
        if at < cut:
            early_ref[:, at : at + unit] = both_ref[:, source]
        else:
            late_ref[:, at - cut : at - cut + unit] = both_ref[:, source]


TAIL = 16


def message(total, log):
    high, middle, last = thirds(log)
    line = iota((TAIL, total.shape[1]), 0)
    tail = jnp.where(line == 0, high, jnp.where(line == 1, middle, jnp.where(line == 2, last, 0.0)))
    return total.astype(BF16), tail.astype(BF16)


def start_kernel(own_ref, kept_ref, total_ref, log_ref, sent_ref):
    spans = own_ref.shape[0]
    total = own_ref[spans - 1]
    log = kept_ref[spans - 1, 4:5]
    for k in range(spans - 2, -1, -1):
        total = own_ref[k] + kept_ref[k, :1] * total
        log = log + kept_ref[k, 4:5]
    total_ref[...] = total
    line = iota(log_ref.shape, 0)
    log_ref[...] = jnp.where(line == 0, log, 0.0)
    n = total.shape[0]
    sent_ref[:n], sent_ref[n:] = message(total, log)


def back_kernel(bit, place_ref, log_ref, total_ref, got_ref, *refs):
    entering_ref = refs[0] if len(refs) == 6 else None
    total_out, entering_out, sent_out, log_out, factor_out = refs[-5:]
    n = total_ref.shape[0]
    got = got_ref[:n].astype(F32)
    tail = got_ref[n:].astype(F32)
    other_log = tail[0:1] + tail[1:2] + tail[2:3]
    log, before_me, after_me = log_ref[0:1], log_ref[1:2], log_ref[2:3]
    line = iota(log_ref.shape, 0)
    upper = (place_ref[0] // bit % 2 + 0 * line[0:1]) == 1
    kept, other = jnp.exp2(log), jnp.exp2(other_log)
    total = jnp.where(upper, other, 1.0) * total_ref[...] + jnp.where(upper, 1.0, kept) * got
    passed = jnp.where(upper, 0.0, jnp.exp2(after_me)) * got
    total_out[...] = total
    entering_out[...] = passed if entering_ref is None else entering_ref[...] + passed
    first = jnp.where(upper, 1.0, other)
    second = jnp.where(upper, kept, 1.0)
    third = jnp.where(upper, jnp.exp2(before_me), 0.0)
    factor_out[...] = jnp.where(line == 0, first, jnp.where(line == 1, second, third))
    log = log + other_log
    before_me = jnp.where(upper, before_me + other_log, before_me)
    after_me = jnp.where(upper, after_me, after_me + other_log)
    log_out[...] = jnp.where(line == 0, log, jnp.where(line == 1, before_me, after_me))
    sent_out[:n], sent_out[n:] = message(total, log)


def scan_kernel(factor_ref, total_ref, got_ref, *refs):
    entering_ref = refs[0] if len(refs) == 4 else None
    total_out, entering_out, sent_out = refs[-3:]
    factors = factor_ref[...]
    got = got_ref[...].astype(F32)
    total = factors[0:1] * total_ref[...] + factors[1:2] * got
    total_out[...] = total
    sent_out[...] = total.astype(BF16)
    passed = factors[2:3] * got
    entering_out[...] = passed if entering_ref is None else entering_ref[...] + passed


def early_forward_kernel(count, f_ref, *refs):
    pieces, (out_ref, buffer) = refs[:count], refs[count:]
    rows = pieces[0].shape[0]
    for index, piece in enumerate(pieces):
        buffer[index * rows : (index + 1) * rows] = piece[...]
    out_ref[...] = mm(f_ref[...], buffer[...])


def late_forward_kernel(count, f_ref, part_ref, rt_ref, b_ref, kept_ref, *refs):
    pieces, (x_ref, e_ref, total_ref, sent_ref, buffer) = refs[:count], refs[count:]
    rows = pieces[0].shape[0]
    for index, piece in enumerate(pieces):
        buffer[index * rows : (index + 1) * rows] = piece[...]
    x = (part_ref[...] + mm(f_ref[...], buffer[...])).astype(BF16)
    x_ref[...] = x
    total = None
    for k in range(e_ref.shape[0]):
        part = slice(k * SPAN, (k + 1) * SPAN)
        columns = rt_ref[0, part]
        to_end = jnp.exp2(spread_columns(columns[SPAN - 1 : SPAN] - columns))
        scaled = (x[part].astype(F32) * to_end).astype(BF16)
        state = dot(b_ref[part], scaled, ((0,), (0,)))
        e_ref[k] = state
        total = state if total is None else kept_ref[k, :1] * total + state
    total_ref[...] = total
    sent_ref[...] = total.astype(BF16)


def blocks_kernel(halves, has_before, order_ref, g_ref, *refs):
    count = len(halves)
    number = sum(halves)
    arrays, refs = refs[:number], refs[number:]
    if has_before:
        refs = refs[2:]
    away_ref, own_ref, buffer, slots, sems, out_sems = refs
    rows = arrays[0].shape[0]
    wide = g_ref.shape[0]
    copies = []
    at = 0
    for index, parts in enumerate(halves):
        mine = []
        for part in range(parts):
            lanes = pl.ds(part * (wide // parts), wide // parts)
            target = buffer.at[pl.ds(index * rows, rows), lanes]
            copy = pltpu.make_async_copy(arrays[at], target, sems.at[at])
            copy.start()
            mine.append(copy)
            at += 1
        copies.append(mine)
    g = g_ref[...]
    half = away_ref.shape[1] // rows
    bundle = 3 if count % 3 == 0 else count
    for index in range(count):
        for copy in copies[index]:
            copy.wait()
        if (index + 1) % bundle:
            continue
        start = index + 1 - bundle
        product = mm(buffer[start * rows : (index + 1) * rows], g)
        for done in range(start, index + 1):
            part = product[(done - start) * rows : (done - start + 1) * rows]
            slots[done] = part.T.astype(BF16)
            place = order_ref[done]
            lanes = pl.ds(pl.multiple_of(place % half * rows, 128), rows)

            @pl.when(place < half)
            def _():
                target = away_ref.at[:, lanes]
                pltpu.make_async_copy(slots.at[done], target, out_sems.at[done]).start()

            @pl.when(place >= half)
            def _():
                target = own_ref.at[:, lanes]
                pltpu.make_async_copy(slots.at[done], target, out_sems.at[done]).start()

    for index in range(count):
        target = away_ref.at[:, pl.ds(0, rows)]
        pltpu.make_async_copy(slots.at[index], target, out_sems.at[index]).wait()


def after_kernel(*refs):
    pass


def inner_kernel(
    r_ref, rt_ref, g_ref, x_ref, b_ref, c_ref, q_ref, *refs
):
    d_ref, grad_b_ref, grad_c_ref, sum_ref, top_ref, low_ref = refs[-6:]
    so_far = refs[:-6]
    step = pl.program_id(1)
    b = b_ref[...]
    c = c_ref[...]
    scores = dot(b, c, ((1,), (1,)))
    running = r_ref[...]
    columns = rt_ref[0]
    top_keep = iota((HALF, SPAN), 1) >= iota((HALF, SPAN), 0)
    low_keep = iota((HALF, HALF), 1) >= iota((HALF, HALF), 0)

    @pl.when(step == 0)
    def _():
        sum_ref[...] = jnp.zeros_like(sum_ref)
        grad_b_ref[...] = so_far[0][...] if so_far else jnp.zeros_like(grad_b_ref)

    rows = []
    lane = iota((SPAN, 2 * P_SIZE), 1)
    later = not_before().astype(BF16)
    top_less = iota((HALF, SPAN), 1) > iota((HALF, SPAN), 0)
    low_less = iota((HALF, HALF), 1) > iota((HALF, HALF), 0)
    for pair in range(GROUP // 2):
        lanes = slice(pair * 2 * P_SIZE, (pair + 1) * 2 * P_SIZE)
        x = x_ref[:, lanes]
        none = jnp.zeros_like(x)
        x = [jnp.where(lane < P_SIZE, x, none), jnp.where(lane < P_SIZE, none, x)]
        product = mm(jnp.concatenate(x, axis=0), g_ref[:, lanes].T)
        top_sum = low_sum = None
        for number in range(2):
            head = 2 * pair + number
            row = running[head : head + 1]
            at = number * SPAN
            top = jnp.where(top_keep, row - columns[:HALF, head : head + 1], NEVER)
            low = jnp.where(low_keep, row[:, HALF:] - columns[HALF:, head : head + 1], NEVER)
            top = jnp.exp2(top) * product[at : at + HALF]
            low = jnp.exp2(low) * product[at + HALF : at + SPAN, HALF:]
            top_sum = top if number == 0 else top_sum + top
            low_sum = low if number == 0 else low_sum + low
            part = slice(head * HALF, (head + 1) * HALF)
            top_ref[part] = (top * scores[:HALF]).astype(BF16)
            low_ref[part] = (low * scores[HALF:, HALF:]).astype(BF16)
        sum_ref[:HALF] += top_sum
        sum_ref[HALF:, HALF:] += low_sum
    top = mm(top_ref[...], later)
    low = mm(low_ref[...], later[HALF:, HALF:])
    for head in range(GROUP):
        part = slice(head * HALF, (head + 1) * HALF)
        top_row = jnp.sum(jnp.where(top_less, top[part], 0.0), axis=0, keepdims=True)
        low_row = jnp.sum(jnp.where(low_less, low[part], 0.0), axis=0, keepdims=True)
        rows.append(jnp.concatenate([top_row[:, :HALF], top_row[:, HALF:] + low_row], axis=1))
    to_end = jnp.exp2(spread_columns(columns[SPAN - 1 : SPAN] - columns))
    scaled = x_ref[...].astype(F32) * to_end
    ends = dot(one_hot(BF16), (scaled * mm(b, q_ref[0])).astype(BF16), ((1,), (1,)))
    d_ref[...] = jnp.concatenate(rows, axis=0) + sum_over(ends, before())
    grad_b_ref[...] += dot(scaled.astype(BF16), q_ref[0], ((1,), (1,)))

    @pl.when(step == pl.num_programs(1) - 1)
    def _():
        total = sum_ref[...].astype(BF16)
        grad_b_ref[...] += mm(total, c)
        part = dot(total, b, ((0,), (0,)))
        grad_c_ref[...] = part + so_far[1][...] if so_far else part


def state_kernel(
    rt_ref, g_ref, c_ref, s_ref, e_ref, q_ref, a_ref, d_part_ref, c_part_ref, d_ref, grad_c_ref, held
):
    span, group = pl.program_id(0), pl.program_id(1)

    @pl.when(group == 0)
    def _():
        grad_c_ref[...] = c_part_ref[...]

    @pl.when(span == 0)
    def _():
        held[group] = s_ref[...]

    state = held[group]
    low = state.astype(BF16)
    scaled = g_ref[...].astype(F32) * jnp.exp2(spread_columns(rt_ref[0]))
    ends = dot(one_hot(BF16), (scaled * mm(c_ref[...], low)).astype(BF16), ((1,), (1,)))
    grad_c_ref[...] += dot(scaled.astype(BF16), low, ((1,), (1,)))
    product = jnp.sum(q_ref[0].astype(F32) * state, axis=0, keepdims=True) * a_ref[0, :1]
    high, middle, last = thirds(product)
    row = iota((8, WIDE), 0)
    stacked = jnp.where(row == 0, high, jnp.where(row == 1, middle, jnp.where(row == 2, last, 0.0)))
    kept = dot(one_hot(BF16), stacked.astype(BF16), ((1,), (1,)))
    kept = jnp.sum(kept, axis=1, keepdims=True)
    d_ref[...] = d_part_ref[...] + sum_over(ends, not_before()) + kept
    held[group] = e_ref[0] + a_ref[0, :1] * state


def call(kernel, grid, in_specs, out_specs, out_shape, flops, size, scratch=()):
    return pl.pallas_call(
        kernel,
        grid=grid,
        in_specs=in_specs,
        out_specs=out_specs,
        out_shape=out_shape,
        scratch_shapes=list(scratch),
        cost_estimate=pl.CostEstimate(flops=flops, bytes_accessed=size, transcendentals=0),
        compiler_params=pltpu.CompilerParams(
            dimension_semantics=("arbitrary",) * len(grid), vmem_limit_bytes=GRANT
        ),
    )


def run_spec(at=0):
    return pl.BlockSpec((GROUP, SPAN), lambda k, h: (h + at, k))


def run_t_spec(at=0):
    return pl.BlockSpec((1, SPAN, GROUP), lambda k, h: (h + at, k, 0))


def rows_spec(at=0):
    return pl.BlockSpec((SPAN, WIDE), lambda k, h: (k, h + at))


def state_spec(at=0):
    return pl.BlockSpec((1, 2 * P_SIZE, WIDE), lambda k, h: (k, 0, h + at))


def kept_spec(at=0):
    return pl.BlockSpec((1, 8, WIDE), lambda k, h: (k, 0, h + at))


SHARED = pl.BlockSpec((SPAN, 2 * P_SIZE), lambda k, h: (k, 0))
GAIN = pl.BlockSpec((1, WIDE), lambda k, h: (0, h))
ANYWHERE = pl.BlockSpec(memory_space=pl.ANY)
INNER_SCRATCH = [
    pltpu.VMEM((SPAN, SPAN), F32),
    pltpu.VMEM((GROUP * HALF, SPAN), BF16),
    pltpu.VMEM((GROUP * HALF, HALF), BF16),
]
SCALARS = pl.BlockSpec(memory_space=pltpu.SMEM)


def shape(*dims, dtype=F32):
    return jax.ShapeDtypeStruct(dims, dtype)


def swap(value, axis, bit):
    count = lax.axis_size(axis)
    return lax.ppermute(value, axis, [(i, i ^ bit) for i in range(count)])


def block_products(kept):
    count = lax.axis_size("ctx")
    place = lax.axis_index("ctx")
    steps = []
    before_me = jnp.ones_like(kept)
    after_me = jnp.ones_like(kept)
    bit = 1
    while bit < count:
        other = swap(kept, "ctx", bit)
        upper = (place & bit) != 0
        steps.append((bit, upper, kept, other, before_me, after_me))
        before_me = jnp.where(upper, before_me * other, before_me)
        after_me = jnp.where(upper, after_me, after_me * other)
        kept = kept * other
        bit *= 2
    return steps


def scan_states(total, steps, reverse):
    entering = jnp.zeros_like(total)
    for bit, upper, kept, other, before_me, after_me in steps:
        got = swap(total.astype(BF16), "ctx", bit).astype(F32)
        if reverse:
            entering = entering + jnp.where(upper, 0.0, after_me) * got
            total = jnp.where(upper, got + other * total, total + kept * got)
        else:
            entering = entering + jnp.where(upper, before_me, 0.0) * got
            total = jnp.where(upper, kept * got + total, other * total + got)
    return entering


def head_sum(value):
    bit = 1
    while bit < lax.axis_size("head"):
        value = value.astype(BF16)
        value = value.astype(F32) + swap(value, "head", bit).astype(F32)
        bit *= 2
    return value


PLANE = 4


def after(values, *tokens):
    out = pl.pallas_call(
        after_kernel,
        in_specs=[ANYWHERE] * (len(values) + len(tokens)),
        out_specs=[ANYWHERE] * len(values),
        out_shape=[shape(*value.shape, dtype=value.dtype) for value in values],
        input_output_aliases={index: index for index in range(len(values))},
        cost_estimate=pl.CostEstimate(flops=0, bytes_accessed=0, transcendentals=0),
    )(*values, *tokens)
    return list(out)


def along_z(value, by):
    count = lax.axis_size("ctx")
    pairs = [(i, i + PLANE * by) for i in range(count) if 0 <= i + PLANE * by < count]
    return lax.ppermute(value, "ctx", pairs)


def swap_x(value):
    return swap(value, "ctx", 1)


def swap_y(value):
    return swap(value, "ctx", 2)


LAYERS = ((0, 1, 2, 3), (1, 0, 1, 2), (2, 2, 3, 1), (3, 3, 0, 0))
EARLY = [(k, flip) for k in (0, 1, 2) for flip in range(3)]
LATE = [(0, 3), (1, 3), (2, 3), (3, 0), (3, 1), (3, 2), (3, 3)]


def block_order():
    place = lax.axis_index("ctx")
    layer, spot = place // PLANE, place % PLANE
    layers = jnp.array(LAYERS, jnp.int32)[:, layer]
    order = [layers[k] * PLANE + (spot ^ flip) for k, flip in EARLY + LATE]
    return jnp.stack(order).astype(jnp.int32)


def gather_weight(w, sizes):
    ends = [sum(sizes[: j + 1]) * P_SIZE for j in range(len(sizes))]
    parts = [w[:, end - size * P_SIZE : end] for end, size in zip(ends, sizes)]
    return [lax.all_gather(part, "ctx", axis=0, tiled=True) for part in parts]


def forward(features, first, weight, running_t, b_rows, here):
    own, other = features
    length = own.shape[0]
    n = b_rows.shape[1]
    width, wide = weight.shape
    deep = width // 4
    spans = length // SPAN

    def depth(k, first_ref):
        return (k // 2 ^ first_ref[0]) * 2 + k % 2

    return pl.pallas_call(
        forward_kernel,
        grid_spec=pltpu.PrefetchScalarGridSpec(
            num_scalar_prefetch=1,
            grid=(wide // WIDE, 4),
            in_specs=[
                pl.BlockSpec((length, deep), lambda h, k, first_ref: (0, jnp.minimum(k, 1))),
                pl.BlockSpec((length, deep), lambda h, k, first_ref: (0, jnp.maximum(k - 2, 0))),
                pl.BlockSpec((deep, WIDE), lambda h, k, first_ref: (depth(k, first_ref), h)),
                pl.BlockSpec((1, length, GROUP), lambda h, k, first_ref: (h + here, 0, 0)),
                pl.BlockSpec((length, n), lambda h, k, first_ref: (0, 0)),
            ],
            out_specs=[
                pl.BlockSpec((length, WIDE), lambda h, k, first_ref: (0, h)),
                pl.BlockSpec((spans, n, WIDE), lambda h, k, first_ref: (0, 0, h)),
            ],
            scratch_shapes=[pltpu.VMEM((length, WIDE), F32)],
        ),
        out_shape=[shape(length, wide, dtype=BF16), shape(spans, n, wide)],
        cost_estimate=pl.CostEstimate(
            flops=2 * length * wide * width, bytes_accessed=2 * wide * width, transcendentals=0
        ),
        compiler_params=pltpu.CompilerParams(
            dimension_semantics=("arbitrary", "arbitrary"), vmem_limit_bytes=GRANT
        ),
    )(first, own, other, weight, running_t, b_rows)


def multiply(grad_x, weight, at, half, halves, before=None, other=None):
    length = grad_x.shape[0]
    width, wide = weight.shape
    tiles = width // halves // WIDE
    tile = pl.BlockSpec((length, WIDE), lambda j, half_ref: (0, half_ref[0] * tiles + j))
    plain = pl.BlockSpec((length, WIDE), lambda j, half_ref: (0, j))
    in_specs = [
        pl.BlockSpec((length, wide), lambda j, half_ref: (0, at)),
        pl.BlockSpec((WIDE, wide), lambda j, half_ref: (half_ref[0] * tiles + j, 0)),
    ]
    operands = [grad_x, weight]
    if before is not None:
        in_specs.append(tile)
        operands.append(before)
    if other is not None:
        in_specs.append(plain)
        operands.append(other)
    return pl.pallas_call(
        functools.partial(product_kernel, before is not None, other is not None),
        grid_spec=pltpu.PrefetchScalarGridSpec(
            num_scalar_prefetch=1,
            grid=(tiles,),
            in_specs=in_specs,
            out_specs=plain,
        ),
        out_shape=shape(length, width // halves, dtype=BF16),
        cost_estimate=pl.CostEstimate(
            flops=2 * length * wide * width // halves,
            bytes_accessed=2 * wide * width // halves,
            transcendentals=0,
        ),
        compiler_params=pltpu.CompilerParams(
            dimension_semantics=("arbitrary",), vmem_limit_bytes=GRANT
        ),
    )(half, *operands)


def early_forward(features, pieces):
    length = features.shape[0]
    rows, columns = pieces[0].shape
    deep = rows * len(pieces)
    return call(
        functools.partial(early_forward_kernel, len(pieces)),
        (columns // WIDE,),
        [pl.BlockSpec((length, deep), lambda h: (0, 0))]
        + [pl.BlockSpec((rows, WIDE), lambda h: (0, h))] * len(pieces),
        pl.BlockSpec((length, WIDE), lambda h: (0, h)),
        shape(length, columns),
        2 * length * columns * deep,
        2 * columns * deep,
        [pltpu.VMEM((deep, WIDE), BF16)],
    )(features, *pieces)


def late_forward(features, part, pieces, running_t, b_rows, kept, here):
    length = features.shape[0]
    rows, columns = pieces[0].shape
    deep = rows * len(pieces)
    n = b_rows.shape[1]
    spans = length // SPAN
    state = pl.BlockSpec((n, WIDE), lambda h: (0, h))
    return call(
        functools.partial(late_forward_kernel, len(pieces)),
        (columns // WIDE,),
        [
            pl.BlockSpec((length, deep), lambda h: (0, 0)),
            pl.BlockSpec((length, WIDE), lambda h: (0, h + here)),
            pl.BlockSpec((1, length, GROUP), lambda h: (h + here, 0, 0)),
            pl.BlockSpec((length, n), lambda h: (0, 0)),
            pl.BlockSpec((spans, 8, WIDE), lambda h: (0, 0, h + here)),
        ]
        + [pl.BlockSpec((rows, WIDE), lambda h: (0, h))] * len(pieces),
        [
            pl.BlockSpec((length, WIDE), lambda h: (0, h)),
            pl.BlockSpec((spans, n, WIDE), lambda h: (0, 0, h)),
            state,
            state,
        ],
        [
            shape(length, columns, dtype=BF16),
            shape(spans, n, columns),
            shape(n, columns),
            shape(n, columns, dtype=BF16),
        ],
        2 * length * columns * deep,
        2 * columns * deep,
        [pltpu.VMEM((deep, WIDE), BF16)],
    )(features, part, running_t, b_rows, kept, *pieces)


def multiply_blocks(order, grad_x, pieces, so_far):
    columns, length = grad_x.shape
    arrays = [array for piece in pieces for array in piece]
    rows = arrays[0].shape[0]
    count = len(pieces)
    half = shape(length, lax.axis_size("ctx") * rows // 2, dtype=BF16)
    first = 2 + len(arrays)
    return pl.pallas_call(
        functools.partial(blocks_kernel, [len(piece) for piece in pieces], bool(so_far)),
        grid=(1,),
        in_specs=[SCALARS, pl.BlockSpec((columns, length), lambda h: (0, 0))]
        + [ANYWHERE] * (len(arrays) + len(so_far)),
        out_specs=[ANYWHERE, ANYWHERE],
        out_shape=[half, half],
        input_output_aliases={first + k: k for k in range(len(so_far))},
        scratch_shapes=[
            pltpu.VMEM((rows * count, columns), BF16),
            pltpu.VMEM((count, length, rows), BF16),
            pltpu.SemaphoreType.DMA((len(arrays),)),
            pltpu.SemaphoreType.DMA((count,)),
        ],
        cost_estimate=pl.CostEstimate(
            flops=2 * length * columns * rows * count,
            bytes_accessed=2 * columns * rows * count,
            transcendentals=0,
        ),
        compiler_params=pltpu.CompilerParams(
            dimension_semantics=("arbitrary",), vmem_limit_bytes=GRANT
        ),
    )(order, grad_x, *arrays, *so_far)


def back_start(own_grads, kept):
    spans, n, columns = own_grads.shape
    return call(
        start_kernel,
        (columns // WIDE,),
        [
            pl.BlockSpec((spans, n, WIDE), lambda h: (0, 0, h)),
            pl.BlockSpec((spans, 8, WIDE), lambda h: (0, 0, h)),
        ],
        [pl.BlockSpec((rows, WIDE), lambda h: (0, h)) for rows in (n, 8, n + TAIL)],
        [shape(n, columns), shape(8, columns), shape(n + TAIL, columns, dtype=BF16)],
        0,
        14 * n * columns,
    )(own_grads, kept)


def back_step(place, log, total, sent, entering, bit):
    got = swap(sent, "ctx", bit)
    n, columns = total.shape
    tall = [pl.BlockSpec((rows, WIDE), lambda h: (0, h)) for rows in (8, n, n + TAIL)]
    return call(
        functools.partial(back_kernel, bit),
        (columns // WIDE,),
        [SCALARS] + tall + [tall[1]] * len(entering),
        [tall[1], tall[1], tall[2], tall[0], tall[0]],
        [
            shape(n, columns),
            shape(n, columns),
            shape(n + TAIL, columns, dtype=BF16),
            shape(8, columns),
            shape(8, columns),
        ],
        0,
        18 * n * columns,
    )(place, log, total, got, *entering)


def scan_step(factors, here, total, sent, entering, bit):
    got = swap(sent, "ctx", bit)
    n, columns = total.shape
    block = pl.BlockSpec((n, WIDE), lambda h: (0, h))
    return call(
        scan_kernel,
        (columns // WIDE,),
        [pl.BlockSpec((8, WIDE), lambda h: (0, h + here)), block, block]
        + [block] * len(entering),
        [block, block, block],
        [shape(n, columns), shape(n, columns), shape(n, columns, dtype=BF16)],
        0,
        14 * n * columns,
    )(factors, total, got, *entering)


def local(inputs, w_in, b_rows, c_rows, log_decay, skip_gain, grad_out):
    groups = log_decay.shape[0] // GROUP
    layered = lax.axis_size("ctx") == 4 * PLANE and lax.axis_size("head") == 2
    if layered and groups % 2 == 0 and w_in.shape[0] == 256:
        return local_layered(inputs, w_in, b_rows, c_rows, log_decay, skip_gain, grad_out)
    return local_plain(inputs, w_in, b_rows, c_rows, log_decay, skip_gain, grad_out)


def prepare(log_decay, grad_out, c_rows):
    length, columns = grad_out.shape
    heads = log_decay.shape[0]
    spans = length // SPAN
    groups = heads // GROUP
    n = c_rows.shape[1]
    return call(
        decay_kernel,
        (spans, groups),
        [run_spec(), rows_spec(), SHARED],
        [run_spec(), run_t_spec(), kept_spec(), state_spec()],
        [
            shape(heads, length),
            shape(groups, length, GROUP),
            shape(spans, 8, columns),
            shape(spans, n, columns),
        ],
        2 * length * columns * n,
        6 * length * columns,
    )(log_decay, grad_out, c_rows)


def inner(grid, here, wide, operands, so_far):
    length = operands[2].shape[0]
    n = operands[4].shape[1]
    specs = [
        run_spec(here),
        run_t_spec(here),
        rows_spec(here),
        rows_spec(),
        SHARED,
        SHARED,
        state_spec(here),
    ]
    return call(
        inner_kernel,
        grid,
        specs + [SHARED] * len(so_far),
        [run_spec(), SHARED, SHARED],
        [shape(wide // P_SIZE, length), shape(length, n), shape(length, n)],
        12 * length * wide * SPAN,
        6 * length * wide,
        INNER_SCRATCH,
    )(*operands, *so_far)


def state_terms(grid, here, wide, operands):
    length = operands[1].shape[0]
    n = operands[2].shape[1]
    return call(
        state_kernel,
        grid,
        [
            run_t_spec(here),
            rows_spec(here),
            SHARED,
            pl.BlockSpec((n, WIDE), lambda k, h: (0, h)),
            state_spec(),
            state_spec(here),
            kept_spec(here),
            run_spec(),
            SHARED,
        ],
        [run_spec(), SHARED],
        [shape(wide // P_SIZE, length), shape(length, n)],
        4 * length * wide * n,
        6 * length * wide,
        [pltpu.VMEM((grid[1], n, WIDE), F32)],
    )(*operands)


def local_layered(inputs, w_in, b_rows, c_rows, log_decay, skip_gain, grad_out):
    length, columns = grad_out.shape
    heads = log_decay.shape[0]
    spans = length // SPAN
    groups = heads // GROUP
    place = lax.axis_index("head").astype(jnp.int32)
    half = columns // 2
    order = block_order()
    blocks = order.shape[0]
    width = blocks * w_in.shape[0]

    layer = lax.axis_index("ctx") // PLANE
    up1, down1 = along_z(w_in, 1), along_z(w_in, -1)
    own_x, own_y = swap_x(w_in), swap_y(w_in)
    other = swap(inputs, "head", 1)
    running, running_t, kept, own_grads = prepare(log_decay, grad_out, c_rows)
    spot = lax.axis_index("ctx").astype(jnp.int32)[None]
    back, log, sent = back_start(own_grads, kept)
    sent = after([sent], other)[0]
    back, leaving, sent, log, factors_1 = back_step(spot, log, back, sent, (), 1)

    up1, down1 = after([up1, down1], own_x, own_y)
    up2, down2 = along_z(up1, 1), along_z(down1, -1)
    z1 = jnp.where(layer == 0, down1, up1)
    x1, y1 = swap_x(z1), swap_y(z1)
    z3 = jnp.where(layer == 0, down2, jnp.where(layer == 3, up2, down1))
    up2, down2, z3 = after([up2, down2, z3], sent)
    up3, down3 = along_z(up2, 1), along_z(down2, -1)
    x3, y3 = swap_x(z3), swap_y(z3)
    back, leaving, sent, log, factors_2 = back_step(spot, log, back, sent, (leaving,), 2)
    order_own = (order + place * (blocks // 2)) % blocks
    cut = len(EARLY) * w_in.shape[0]
    early_features, late_features = call(
        arrange_kernel,
        (1,),
        [SCALARS] + [pl.BlockSpec((length, width // 2), lambda h: (0, 0))] * 2,
        [pl.BlockSpec((length, wide), lambda h: (0, 0)) for wide in (cut, width - cut)],
        [shape(length, wide, dtype=BF16) for wide in (cut, width - cut)],
        0,
        4 * length * width,
        [pltpu.VMEM((length, width), BF16)],
    )(order_own, inputs, other)

    z2 = jnp.where(layer == 1, down2, jnp.where(layer == 2, up2, up3 + down3))
    z2a, z2b = z2[:, :half], z2[:, half:]
    z2a, x1, y3, own_y = after(
        [z2a, x1, y3, own_y], y1, x3, z2b, sent, early_features, late_features
    )
    x1_a, x1_b = x1[:, :half], x1[:, half:]
    y3_a, y3_b = y3[:, :half], y3[:, half:]
    own_y_a, own_y_b = own_y[:, :half], own_y[:, half:]
    x2a, y2a = swap_x(z2a), swap_y(z2a)
    d3a, d1a = swap_x(y3_a), swap_y(x1_a)
    back, leaving, sent, log, factors_4 = back_step(spot, log, back, sent, (leaving,), 4)
    early = [w_in, own_x, own_y, z1, x1, y1, z3, x3, y3]
    part = early_forward(early_features, early)

    own_y_a, x2a, z2b, y3_b, x1_b = after(
        [own_y_a, x2a, z2b, y3_b, x1_b], y2a, d3a, d1a, part, sent
    )
    d0a, d2a = swap_x(own_y_a), swap_y(x2a)
    x2b, y2b = swap_x(z2b), swap_y(z2b)
    d3b, d1b = swap_x(y3_b), swap_y(x1_b)
    back, leaving, sent, log, factors_8 = back_step(spot, log, back, sent, (leaving,), 8)
    leaving_all = [leaving]
    for k in range(spans - 1, 0, -1):
        leaving_all.insert(0, own_grads[k] + kept[k, :1] * leaving_all[0])
    leaving_all = jnp.stack([value.astype(BF16) for value in leaving_all])
    skip = jnp.repeat(skip_gain, P_SIZE)[None]
    grad_x = grad_rows(running, running_t, grad_out, b_rows, c_rows, leaving_all, skip, True)
    late_a = [d0a, d1a, d3a, z2a, x2a, y2a, d2a]
    x_a, states_a, total_a, sent_a = late_forward(
        late_features, part, late_a, running_t, b_rows, kept, 0
    )

    own_y_b, x2b, sent_a = after([own_y_b, x2b, sent_a], y2b, d3b, d1b, grad_x)
    d0b, d2b = swap_x(own_y_b), swap_y(x2b)
    total_a, entering_a, sent_a = scan_step(factors_1, 0, total_a, sent_a, (), 1)
    order_away = (order + (1 - place) * (blocks // 2)) % blocks
    early_order, late_order = order_away[: len(EARLY)], order_away[len(EARLY) :]
    product = multiply_blocks(early_order, grad_x, [[piece] for piece in early], ())

    d0b, d2b = after([d0b, d2b], sent_a, product[0])
    late_b = [d0b, d1b, d3b, z2b, x2b, y2b, d2b]
    here = groups // 2
    x_b, states_b, total_b, sent_b = late_forward(
        late_features, part, late_b, running_t, b_rows, kept, here
    )
    pairs = list(zip(late_a, late_b))
    shared = (running, running_t, grad_out)
    grid = (spans, here)
    entering_b = ()
    for factors, bit in ((factors_1, 1), (factors_2, 2), (factors_4, 4), (factors_8, 8)):
        if bit > 1:
            total_a, entering_a, sent_a = scan_step(
                factors, 0, total_a, sent_a, (entering_a,), bit
            )
        if bit == 4:
            sent_b = after([sent_b], away)[0]
        if bit == 8:
            sent_b = after([sent_b], grad_b)[0]
        total_b, entering_b, sent_b = scan_step(factors, here, total_b, sent_b, entering_b, bit)
        entering_b = (entering_b,)
        if bit == 1:
            product = after(list(product), sent_b)
            away, own = multiply_blocks(late_order, grad_x, pairs, product)
            got = swap(away, "head", 1)
        if bit == 2:
            x_a = after([x_a], sent_b)[0]
            inner_a = shared + (x_a, b_rows, c_rows, leaving_all)
            decay_a, grad_b, grad_c = inner(grid, 0, half, inner_a, ())
        if bit == 4:
            x_b = after([x_b], sent_b)[0]
            inner_b = shared + (x_b, b_rows, c_rows, leaving_all)
            decay_b, grad_b, grad_c = inner(grid, here, half, inner_b, (grad_b, grad_c))
    entering_b = entering_b[0]
    grad_b = head_sum(grad_b)

    common = (running_t, grad_out, c_rows)
    state_a = common + (entering_a, states_a, leaving_all, kept, decay_a, grad_c)
    decay_a, grad_c = state_terms(grid, 0, half, state_a)
    state_b = common + (entering_b, states_b, leaving_all, kept, decay_b, grad_c)
    decay_b, grad_c = state_terms(grid, here, half, state_b)
    grad_inputs = (own.astype(F32) + got.astype(F32)).astype(BF16)
    grad_log_decay = jnp.concatenate([decay_a, decay_b], axis=0)
    return (grad_inputs, grad_b, head_sum(grad_c), grad_log_decay)


def grad_rows(running, running_t, grad_out, b_rows, c_rows, leaving, skip, transposed):
    length, columns = grad_out.shape
    spec, dims = rows_spec(), (length, columns)
    if transposed:
        spec, dims = pl.BlockSpec((WIDE, SPAN), lambda k, h: (h, k)), (columns, length)
    return call(
        functools.partial(grad_x_kernel, transposed),
        (length // SPAN, running_t.shape[0]),
        [run_spec(), run_t_spec(), rows_spec(), SHARED, SHARED, state_spec(), GAIN],
        spec,
        shape(*dims, dtype=BF16),
        8 * length * columns * SPAN,
        6 * length * columns,
    )(running, running_t, grad_out, b_rows, c_rows, leaving, skip)


def local_plain(inputs, w_in, b_rows, c_rows, log_decay, skip_gain, grad_out):
    length, columns = grad_out.shape
    heads = log_decay.shape[0]
    spans = length // SPAN
    groups = heads // GROUP
    n = b_rows.shape[1]
    grid = (spans, groups)

    sizes = (heads // 2, heads // 4, heads // 4) if heads % (4 * GROUP) == 0 else (heads,)
    weights = gather_weight(w_in, sizes)
    two = lax.axis_size("head") == 2
    place = lax.axis_index("head").astype(jnp.int32)[None]
    width = weights[0].shape[0]
    if two:
        features = (inputs, swap(inputs, "head", 1))
        first = place
    else:
        features = lax.all_gather(inputs, "head", axis=1, tiled=True)
        features = (features[:, : width // 2], features[:, width // 2 :])
        first = jnp.zeros((1,), jnp.int32)

    running, running_t, kept, own_grads = call(
        decay_kernel,
        grid,
        [run_spec(), rows_spec(), SHARED],
        [run_spec(), run_t_spec(), kept_spec(), state_spec()],
        [
            shape(heads, length),
            shape(groups, length, GROUP),
            shape(spans, 8, columns),
            shape(spans, n, columns),
        ],
        2 * length * columns * n,
        6 * length * columns,
    )(log_decay, grad_out, c_rows)

    kept_total = kept[0, :1]
    for k in range(1, spans):
        kept_total = kept_total * kept[k, :1]
    steps = block_products(kept_total)

    total = own_grads[spans - 1]
    for k in range(spans - 2, -1, -1):
        total = own_grads[k] + kept[k, :1] * total
    leaving = [scan_states(total, steps, True)]
    for k in range(spans - 1, 0, -1):
        leaving.insert(0, own_grads[k] + kept[k, :1] * leaving[0])
    leaving = jnp.stack([value.astype(BF16) for value in leaving])

    skip = jnp.repeat(skip_gain, P_SIZE)[None]
    grad_x = grad_rows(running, running_t, grad_out, b_rows, c_rows, leaving, skip, False)

    grad_b = grad_c = product = None
    tokens = ()
    decay_parts = []
    at = 0
    for index, size in enumerate(sizes):
        wide = size * P_SIZE
        here = at // GROUP
        count = size // GROUP
        weight = weights[index]
        if tokens:
            weight = after([weight], *tokens)[0]
        x, own_states = forward(features, first, weight, running_t, b_rows, here)

        chunk = slice(at * P_SIZE, at * P_SIZE + wide)
        total = own_states[0]
        for k in range(1, spans):
            total = kept[k, :1, chunk] * total + own_states[k]
        cut = [step[:2] + tuple(value[:, chunk] for value in step[2:]) for step in steps]
        entering = scan_states(total, cut, False)

        so_far = () if grad_b is None else (grad_b, grad_c)
        decay_part, grad_b, grad_c = call(
            inner_kernel,
            (spans, count),
            [
                run_spec(here),
                run_t_spec(here),
                rows_spec(here),
                rows_spec(),
                SHARED,
                SHARED,
                state_spec(here),
            ]
            + [SHARED] * len(so_far),
            [run_spec(), SHARED, SHARED],
            [shape(size, length), shape(length, n), shape(length, n)],
            12 * length * wide * SPAN,
            6 * length * wide,
            INNER_SCRATCH,
        )(running, running_t, grad_out, x, b_rows, c_rows, leaving, *so_far)
        decay_part, grad_c = call(
            state_kernel,
            (spans, count),
            [
                run_t_spec(here),
                rows_spec(here),
                SHARED,
                pl.BlockSpec((n, WIDE), lambda k, h: (0, h)),
                state_spec(),
                state_spec(here),
                kept_spec(here),
                run_spec(),
                SHARED,
            ],
            [run_spec(), SHARED],
            [shape(size, length), shape(length, n)],
            4 * length * wide * n,
            6 * length * wide,
            [pltpu.VMEM((count, n, WIDE), F32)],
        )(running_t, grad_out, c_rows, entering, own_states, leaving, kept, decay_part, grad_c)
        decay_parts.append(decay_part)

        if index < len(sizes) - 1:
            zero = jnp.zeros((1,), jnp.int32)
            product = multiply(grad_x, weight, at // size, zero, 1, product)
            tokens = (product, grad_b, entering)
        elif two:
            sent = multiply(grad_x, weight, at // size, 1 - place, 2, product)
            got = swap(sent, "head", 1)
            grad_inputs = multiply(grad_x, weight, at // size, place, 2, product, got)
        else:
            zero = jnp.zeros((1,), jnp.int32)
            product = multiply(grad_x, weight, at // size, zero, 1, product)
            grad_inputs = lax.psum_scatter(product, "head", scatter_dimension=1, tiled=True)
        at += size

    return (grad_inputs, head_sum(grad_b), head_sum(grad_c), jnp.concatenate(decay_parts, axis=0))


def solution(mesh):
    in_specs = (
        P("ctx", "head"),
        P("ctx", "head"),
        P("ctx", None),
        P("ctx", None),
        P("head", "ctx"),
        P("head"),
        P("ctx", "head"),
    )
    out_specs = (P("ctx", "head"), P("ctx", None), P("ctx", None), P("head", "ctx"))
    return jax.shard_map(local, mesh=mesh, in_specs=in_specs, out_specs=out_specs, check_vma=False)
```

```python
import functools

import jax
import jax.numpy as jnp
from jax import lax
from jax.experimental import pallas as pl
from jax.experimental.pallas import tpu as pltpu
from jax.sharding import PartitionSpec as P

SPAN = 256
HALF = SPAN // 2
P_SIZE = 64
GROUP = 8
WIDE = GROUP * P_SIZE
LOG2E = 1.4426950408889634
NEVER = -1e30
GRANT = 62 * 2**20

F32 = jnp.float32
BF16 = jnp.bfloat16
EXACT = lax.Precision.HIGHEST


def dot(a, b, dims, precision=None):
    return lax.dot_general(a, b, (dims, ((), ())), precision=precision, preferred_element_type=F32)


def mm(a, b, precision=None):
    return dot(a, b, ((1,), (0,)), precision)


def iota(shape, dim):
    return lax.broadcasted_iota(jnp.int32, shape, dim)


def one_hot(dtype):
    return (iota((GROUP, WIDE), 0) == iota((GROUP, WIDE), 1) // P_SIZE).astype(dtype)


def not_before():
    return (iota((SPAN, SPAN), 0) >= iota((SPAN, SPAN), 1)).astype(F32)


def before():
    return (iota((SPAN, SPAN), 0) < iota((SPAN, SPAN), 1)).astype(F32)


def same():
    return (iota((SPAN, SPAN), 0) == iota((SPAN, SPAN), 1)).astype(F32)


def first_head():
    return iota((SPAN, 2 * P_SIZE), 1) < P_SIZE


def pair_columns(columns, pair):
    shape = (columns.shape[0], 2 * P_SIZE)
    left = jnp.broadcast_to(columns[:, 2 * pair : 2 * pair + 1], shape)
    right = jnp.broadcast_to(columns[:, 2 * pair + 1 : 2 * pair + 2], shape)
    return jnp.where(iota(shape, 1) < P_SIZE, left, right)


def spread_columns(columns):
    return jnp.concatenate([pair_columns(columns, pair) for pair in range(GROUP // 2)], axis=1)


def thirds(value):
    high = value.astype(BF16).astype(F32)
    middle = (value - high).astype(BF16).astype(F32)
    return high, middle, value - high - middle


def sum_over(value, mask):
    rows = value.shape[0]
    parts = mm(jnp.concatenate(thirds(value), axis=0).astype(BF16), mask.astype(BF16))
    return parts[:rows] + parts[rows : 2 * rows] + parts[2 * rows :]


def decay_kernel(d_ref, g_ref, c_ref, r_ref, rt_ref, a_ref, gt_ref):
    row_sums = sum_over(d_ref[...] * LOG2E, 1.0 - not_before() + same())
    r_ref[...] = row_sums
    padded = jnp.concatenate([row_sums, jnp.zeros((2 * P_SIZE - GROUP, SPAN), F32)], axis=0)
    running = padded.T[:, :GROUP]
    rt_ref[0] = running
    growth = jnp.exp2(spread_columns(running))
    last = spread_columns(running[SPAN - 1 : SPAN])
    a_ref[0] = jnp.where(iota((8, WIDE), 0) < 4, jnp.exp2(last), last)
    scaled = (g_ref[...].astype(F32) * growth).astype(BF16)
    gt_ref[0] = dot(c_ref[...], scaled, ((0,), (0,)))


def grad_x_kernel(transposed, r_ref, rt_ref, g_ref, b_ref, c_ref, q_ref, skip_ref, out_ref):
    b = b_ref[...]
    scores = dot(b, c_ref[...], ((1,), (1,)))
    running = r_ref[...]
    columns = rt_ref[0]
    top_keep = iota((HALF, SPAN), 1) >= iota((HALF, SPAN), 0)
    low_keep = iota((HALF, HALF), 1) >= iota((HALF, HALF), 0)
    to_end = jnp.exp2(spread_columns(columns[SPAN - 1 : SPAN] - columns))
    from_state = mm(b, q_ref[0]) * to_end
    for pair in range(GROUP // 2):
        lanes = slice(pair * 2 * P_SIZE, (pair + 1) * 2 * P_SIZE)
        g = g_ref[:, lanes]
        parts = []
        for head in (2 * pair, 2 * pair + 1):
            row = running[head : head + 1]
            top = jnp.where(top_keep, row - columns[:HALF, head : head + 1], NEVER)
            low = jnp.where(low_keep, row[:, HALF:] - columns[HALF:, head : head + 1], NEVER)
            parts.append((jnp.exp2(top) * scores[:HALF]).astype(BF16))
            low = (jnp.exp2(low) * scores[HALF:, HALF:]).astype(BF16)
            parts.append(jnp.concatenate([jnp.zeros((HALF, HALF), BF16), low], axis=1))
        product = mm(jnp.concatenate(parts, axis=0), g)
        parts = [product[:SPAN], product[SPAN:]]
        inner = jnp.where(first_head(), parts[0], parts[1])
        total = inner + skip_ref[:, lanes] * g.astype(F32) + from_state[:, lanes]
        if transposed:
            out_ref[lanes, :] = total.T.astype(BF16)
        else:
            out_ref[:, lanes] = total.astype(BF16)


def forward_kernel(half_ref, own_ref, other_ref, w_ref, rt_ref, b_ref, x_ref, e_ref, total_ref):
    step = pl.program_id(1)

    @pl.when(step == 0)
    def _():
        total_ref[...] = jnp.zeros_like(total_ref)

    half = pl.num_programs(1) // 2

    @pl.when(step < half)
    def _():
        total_ref[...] += mm(own_ref[...], w_ref[...])

    @pl.when(step >= half)
    def _():
        total_ref[...] += mm(other_ref[...], w_ref[...])

    @pl.when(step == pl.num_programs(1) - 1)
    def _():
        x = total_ref[...].astype(BF16)
        x_ref[...] = x
        for k in range(e_ref.shape[0]):
            rows = slice(k * SPAN, (k + 1) * SPAN)
            columns = rt_ref[0, rows]
            to_end = jnp.exp2(spread_columns(columns[SPAN - 1 : SPAN] - columns))
            scaled = (x[rows].astype(F32) * to_end).astype(BF16)
            e_ref[k] = dot(b_ref[rows], scaled, ((0,), (0,)))


def product_kernel(has_before, has_other, half_ref, g_ref, w_ref, *refs):
    refs = list(refs)
    total = dot(g_ref[...], w_ref[...], ((1,), (1,)))
    if has_before:
        total = total + refs.pop(0)[...].astype(F32)
    if has_other:
        total = total.astype(BF16).astype(F32) + refs.pop(0)[...].astype(F32)
    refs[0][...] = total.astype(BF16)


def arrange_kernel(order_ref, own_ref, other_ref, early_ref, late_ref, both_ref):
    half = own_ref.shape[1]
    both_ref[:, :half] = own_ref[...]
    both_ref[:, half:] = other_ref[...]
    unit = 2 * half // order_ref.shape[0]
    cut = early_ref.shape[1]
    for index in range(order_ref.shape[0]):
        source = pl.ds(pl.multiple_of(order_ref[index] * unit, 128), unit)
        at = index * unit
        if at < cut:
            early_ref[:, at : at + unit] = both_ref[:, source]
        else:
            late_ref[:, at - cut : at - cut + unit] = both_ref[:, source]


TAIL = 16


def message(total, log):
    high, middle, last = thirds(log)
    line = iota((TAIL, total.shape[1]), 0)
    tail = jnp.where(line == 0, high, jnp.where(line == 1, middle, jnp.where(line == 2, last, 0.0)))
    return total.astype(BF16), tail.astype(BF16)


def start_kernel(own_ref, kept_ref, total_ref, log_ref, sent_ref):
    spans = own_ref.shape[0]
    total = own_ref[spans - 1]
    log = kept_ref[spans - 1, 4:5]
    for k in range(spans - 2, -1, -1):
        total = own_ref[k] + kept_ref[k, :1] * total
        log = log + kept_ref[k, 4:5]
    total_ref[...] = total
    line = iota(log_ref.shape, 0)
    log_ref[...] = jnp.where(line == 0, log, 0.0)
    n = total.shape[0]
    sent_ref[:n], sent_ref[n:] = message(total, log)


def back_kernel(bit, place_ref, log_ref, total_ref, got_ref, *refs):
    entering_ref = refs[0] if len(refs) == 6 else None
    total_out, entering_out, sent_out, log_out, factor_out = refs[-5:]
    n = total_ref.shape[0]
    got = got_ref[:n].astype(F32)
    tail = got_ref[n:].astype(F32)
    other_log = tail[0:1] + tail[1:2] + tail[2:3]
    log, before_me, after_me = log_ref[0:1], log_ref[1:2], log_ref[2:3]
    line = iota(log_ref.shape, 0)
    upper = (place_ref[0] // bit % 2 + 0 * line[0:1]) == 1
    kept, other = jnp.exp2(log), jnp.exp2(other_log)
    total = jnp.where(upper, other, 1.0) * total_ref[...] + jnp.where(upper, 1.0, kept) * got
    passed = jnp.where(upper, 0.0, jnp.exp2(after_me)) * got
    total_out[...] = total
    entering_out[...] = passed if entering_ref is None else entering_ref[...] + passed
    first = jnp.where(upper, 1.0, other)
    second = jnp.where(upper, kept, 1.0)
    third = jnp.where(upper, jnp.exp2(before_me), 0.0)
    factor_out[...] = jnp.where(line == 0, first, jnp.where(line == 1, second, third))
    log = log + other_log
    before_me = jnp.where(upper, before_me + other_log, before_me)
    after_me = jnp.where(upper, after_me, after_me + other_log)
    log_out[...] = jnp.where(line == 0, log, jnp.where(line == 1, before_me, after_me))
    sent_out[:n], sent_out[n:] = message(total, log)


def scan_kernel(factor_ref, total_ref, got_ref, *refs):
    refs = list(refs)
    entering_ref = refs.pop(0) if len(refs) % 2 == 0 else None
    factors = factor_ref[...]
    got = got_ref[...].astype(F32)
    entering_out = refs[0]
    if len(refs) == 3:
        total = factors[0:1] * total_ref[...] + factors[1:2] * got
        refs[1][...] = total
        refs[2][...] = total.astype(BF16)
    passed = factors[2:3] * got
    entering_out[...] = passed if entering_ref is None else entering_ref[...] + passed


def early_forward_kernel(count, f_ref, *refs):
    pieces, (out_ref, buffer) = refs[:count], refs[count:]
    rows = pieces[0].shape[0]
    for index, piece in enumerate(pieces):
        buffer[index * rows : (index + 1) * rows] = piece[...]
    out_ref[...] = mm(f_ref[...], buffer[...])


def late_forward_kernel(count, f_ref, part_ref, rt_ref, b_ref, kept_ref, *refs):
    pieces, (x_ref, e_ref, total_ref, sent_ref, buffer) = refs[:count], refs[count:]
    rows = pieces[0].shape[0]
    for index, piece in enumerate(pieces):
        buffer[index * rows : (index + 1) * rows] = piece[...]
    x = (part_ref[...] + mm(f_ref[...], buffer[...])).astype(BF16)
    x_ref[...] = x
    total = None
    for k in range(e_ref.shape[0]):
        part = slice(k * SPAN, (k + 1) * SPAN)
        columns = rt_ref[0, part]
        to_end = jnp.exp2(spread_columns(columns[SPAN - 1 : SPAN] - columns))
        scaled = (x[part].astype(F32) * to_end).astype(BF16)
        state = dot(b_ref[part], scaled, ((0,), (0,)))
        e_ref[k] = state
        total = state if total is None else kept_ref[k, :1] * total + state
    total_ref[...] = total
    sent_ref[...] = total.astype(BF16)


def blocks_kernel(halves, has_before, order_ref, g_ref, *refs):
    count = len(halves)
    number = sum(halves)
    arrays, refs = refs[:number], refs[number:]
    if has_before:
        refs = refs[2:]
    away_ref, own_ref, buffer, slots, sems, out_sems = refs
    rows = arrays[0].shape[0]
    wide = g_ref.shape[0]
    copies = []
    at = 0
    for index, parts in enumerate(halves):
        mine = []
        for part in range(parts):
            lanes = pl.ds(part * (wide // parts), wide // parts)
            target = buffer.at[pl.ds(index * rows, rows), lanes]
            copy = pltpu.make_async_copy(arrays[at], target, sems.at[at])
            copy.start()
            mine.append(copy)
            at += 1
        copies.append(mine)
    g = g_ref[...]
    half = away_ref.shape[1] // rows
    bundle = 3 if count % 3 == 0 else count
    for index in range(count):
        for copy in copies[index]:
            copy.wait()
        if (index + 1) % bundle:
            continue
        start = index + 1 - bundle
        product = mm(buffer[start * rows : (index + 1) * rows], g)
        for done in range(start, index + 1):
            part = product[(done - start) * rows : (done - start + 1) * rows]
            slots[done] = part.T.astype(BF16)
            place = order_ref[done]
            lanes = pl.ds(pl.multiple_of(place % half * rows, 128), rows)

            @pl.when(place < half)
            def _():
                target = away_ref.at[:, lanes]
                pltpu.make_async_copy(slots.at[done], target, out_sems.at[done]).start()

            @pl.when(place >= half)
            def _():
                target = own_ref.at[:, lanes]
                pltpu.make_async_copy(slots.at[done], target, out_sems.at[done]).start()

    for index in range(count):
        target = away_ref.at[:, pl.ds(0, rows)]
        pltpu.make_async_copy(slots.at[index], target, out_sems.at[index]).wait()


def after_kernel(*refs):
    pass


def inner_kernel(
    r_ref, rt_ref, g_ref, x_ref, b_ref, c_ref, q_ref, *refs
):
    d_ref, grad_b_ref, grad_c_ref, sum_ref, top_ref, low_ref = refs[-6:]
    so_far = refs[:-6]
    step = pl.program_id(1)
    b = b_ref[...]
    c = c_ref[...]
    scores = dot(b, c, ((1,), (1,)))
    running = r_ref[...]
    columns = rt_ref[0]
    top_keep = iota((HALF, SPAN), 1) >= iota((HALF, SPAN), 0)
    low_keep = iota((HALF, HALF), 1) >= iota((HALF, HALF), 0)

    @pl.when(step == 0)
    def _():
        sum_ref[...] = jnp.zeros_like(sum_ref)
        grad_b_ref[...] = so_far[0][...] if so_far else jnp.zeros_like(grad_b_ref)

    rows = []
    lane = iota((SPAN, 2 * P_SIZE), 1)
    later = not_before().astype(BF16)
    top_less = iota((HALF, SPAN), 1) > iota((HALF, SPAN), 0)
    low_less = iota((HALF, HALF), 1) > iota((HALF, HALF), 0)
    for pair in range(GROUP // 2):
        lanes = slice(pair * 2 * P_SIZE, (pair + 1) * 2 * P_SIZE)
        x = x_ref[:, lanes]
        none = jnp.zeros_like(x)
        x = [jnp.where(lane < P_SIZE, x, none), jnp.where(lane < P_SIZE, none, x)]
        product = mm(jnp.concatenate(x, axis=0), g_ref[:, lanes].T)
        top_sum = low_sum = None
        for number in range(2):
            head = 2 * pair + number
            row = running[head : head + 1]
            at = number * SPAN
            top = jnp.where(top_keep, row - columns[:HALF, head : head + 1], NEVER)
            low = jnp.where(low_keep, row[:, HALF:] - columns[HALF:, head : head + 1], NEVER)
            top = jnp.exp2(top) * product[at : at + HALF]
            low = jnp.exp2(low) * product[at + HALF : at + SPAN, HALF:]
            top_sum = top if number == 0 else top_sum + top
            low_sum = low if number == 0 else low_sum + low
            part = slice(head * HALF, (head + 1) * HALF)
            top_ref[part] = (top * scores[:HALF]).astype(BF16)
            low_ref[part] = (low * scores[HALF:, HALF:]).astype(BF16)
        sum_ref[:HALF] += top_sum
        sum_ref[HALF:, HALF:] += low_sum
    top = mm(top_ref[...], later)
    low = mm(low_ref[...], later[HALF:, HALF:])
    for head in range(GROUP):
        part = slice(head * HALF, (head + 1) * HALF)
        top_row = jnp.sum(jnp.where(top_less, top[part], 0.0), axis=0, keepdims=True)
        low_row = jnp.sum(jnp.where(low_less, low[part], 0.0), axis=0, keepdims=True)
        rows.append(jnp.concatenate([top_row[:, :HALF], top_row[:, HALF:] + low_row], axis=1))
    to_end = jnp.exp2(spread_columns(columns[SPAN - 1 : SPAN] - columns))
    scaled = x_ref[...].astype(F32) * to_end
    ends = dot(one_hot(BF16), (scaled * mm(b, q_ref[0])).astype(BF16), ((1,), (1,)))
    d_ref[...] = jnp.concatenate(rows, axis=0) + sum_over(ends, before())
    grad_b_ref[...] += dot(scaled.astype(BF16), q_ref[0], ((1,), (1,)))

    @pl.when(step == pl.num_programs(1) - 1)
    def _():
        total = sum_ref[...].astype(BF16)
        grad_b_ref[...] += mm(total, c)
        part = dot(total, b, ((0,), (0,)))
        grad_c_ref[...] = part + so_far[1][...] if so_far else part


def state_kernel(
    rt_ref, g_ref, c_ref, s_ref, e_ref, q_ref, a_ref, d_part_ref, c_part_ref, *refs
):
    d_ref, grad_c_ref, held = refs[-3:]
    span, group = pl.program_id(0), pl.program_id(1)

    @pl.when(group == 0)
    def _():
        grad_c_ref[...] = c_part_ref[...]

    @pl.when(span == 0)
    def _():
        held[group] = s_ref[...]

    state = held[group]
    low = state.astype(BF16)
    scaled = g_ref[...].astype(F32) * jnp.exp2(spread_columns(rt_ref[0]))
    ends = dot(one_hot(BF16), (scaled * mm(c_ref[...], low)).astype(BF16), ((1,), (1,)))
    grad_c_ref[...] += dot(scaled.astype(BF16), low, ((1,), (1,)))
    product = jnp.sum(q_ref[0].astype(F32) * state, axis=0, keepdims=True) * a_ref[0, :1]
    high, middle, last = thirds(product)
    row = iota((8, WIDE), 0)
    stacked = jnp.where(row == 0, high, jnp.where(row == 1, middle, jnp.where(row == 2, last, 0.0)))
    kept = dot(one_hot(BF16), stacked.astype(BF16), ((1,), (1,)))
    kept = jnp.sum(kept, axis=1, keepdims=True)
    d_ref[...] = d_part_ref[...] + sum_over(ends, not_before()) + kept
    held[group] = e_ref[0] + a_ref[0, :1] * state


def call(kernel, grid, in_specs, out_specs, out_shape, flops, size, scratch=()):
    return pl.pallas_call(
        kernel,
        grid=grid,
        in_specs=in_specs,
        out_specs=out_specs,
        out_shape=out_shape,
        scratch_shapes=list(scratch),
        cost_estimate=pl.CostEstimate(flops=flops, bytes_accessed=size, transcendentals=0),
        compiler_params=pltpu.CompilerParams(
            dimension_semantics=("arbitrary",) * len(grid), vmem_limit_bytes=GRANT
        ),
    )


def run_spec(at=0):
    return pl.BlockSpec((GROUP, SPAN), lambda k, h: (h + at, k))


def run_t_spec(at=0):
    return pl.BlockSpec((1, SPAN, GROUP), lambda k, h: (h + at, k, 0))


def rows_spec(at=0):
    return pl.BlockSpec((SPAN, WIDE), lambda k, h: (k, h + at))


def state_spec(at=0):
    return pl.BlockSpec((1, 2 * P_SIZE, WIDE), lambda k, h: (k, 0, h + at))


def kept_spec(at=0):
    return pl.BlockSpec((1, 8, WIDE), lambda k, h: (k, 0, h + at))


SHARED = pl.BlockSpec((SPAN, 2 * P_SIZE), lambda k, h: (k, 0))
GAIN = pl.BlockSpec((1, WIDE), lambda k, h: (0, h))
ANYWHERE = pl.BlockSpec(memory_space=pl.ANY)
INNER_SCRATCH = [
    pltpu.VMEM((SPAN, SPAN), F32),
    pltpu.VMEM((GROUP * HALF, SPAN), BF16),
    pltpu.VMEM((GROUP * HALF, HALF), BF16),
]
SCALARS = pl.BlockSpec(memory_space=pltpu.SMEM)


def shape(*dims, dtype=F32):
    return jax.ShapeDtypeStruct(dims, dtype)


def swap(value, axis, bit):
    count = lax.axis_size(axis)
    return lax.ppermute(value, axis, [(i, i ^ bit) for i in range(count)])


def block_products(kept):
    count = lax.axis_size("ctx")
    place = lax.axis_index("ctx")
    steps = []
    before_me = jnp.ones_like(kept)
    after_me = jnp.ones_like(kept)
    bit = 1
    while bit < count:
        other = swap(kept, "ctx", bit)
        upper = (place & bit) != 0
        steps.append((bit, upper, kept, other, before_me, after_me))
        before_me = jnp.where(upper, before_me * other, before_me)
        after_me = jnp.where(upper, after_me, after_me * other)
        kept = kept * other
        bit *= 2
    return steps


def scan_states(total, steps, reverse):
    entering = jnp.zeros_like(total)
    for bit, upper, kept, other, before_me, after_me in steps:
        got = swap(total.astype(BF16), "ctx", bit).astype(F32)
        if reverse:
            entering = entering + jnp.where(upper, 0.0, after_me) * got
            total = jnp.where(upper, got + other * total, total + kept * got)
        else:
            entering = entering + jnp.where(upper, before_me, 0.0) * got
            total = jnp.where(upper, kept * got + total, other * total + got)
    return entering


def head_sum(value):
    bit = 1
    while bit < lax.axis_size("head"):
        value = value.astype(BF16)
        value = value.astype(F32) + swap(value, "head", bit).astype(F32)
        bit *= 2
    return value


PLANE = 4


def after(values, *tokens):
    out = pl.pallas_call(
        after_kernel,
        in_specs=[ANYWHERE] * (len(values) + len(tokens)),
        out_specs=[ANYWHERE] * len(values),
        out_shape=[shape(*value.shape, dtype=value.dtype) for value in values],
        input_output_aliases={index: index for index in range(len(values))},
        cost_estimate=pl.CostEstimate(flops=0, bytes_accessed=0, transcendentals=0),
    )(*values, *tokens)
    return list(out)


def along_z(value, by):
    count = lax.axis_size("ctx")
    pairs = [(i, i + PLANE * by) for i in range(count) if 0 <= i + PLANE * by < count]
    return lax.ppermute(value, "ctx", pairs)


def swap_x(value):
    return swap(value, "ctx", 1)


def swap_y(value):
    return swap(value, "ctx", 2)


LAYERS = ((0, 1, 2, 3), (1, 0, 1, 2), (2, 2, 3, 1), (3, 3, 0, 0))
EARLY = [(k, flip) for k in (0, 1, 2) for flip in range(3)]
LATE = [(0, 3), (1, 3), (2, 3), (3, 0), (3, 1), (3, 2), (3, 3)]


def block_order():
    place = lax.axis_index("ctx")
    layer, spot = place // PLANE, place % PLANE
    layers = jnp.array(LAYERS, jnp.int32)[:, layer]
    order = [layers[k] * PLANE + (spot ^ flip) for k, flip in EARLY + LATE]
    return jnp.stack(order).astype(jnp.int32)


def gather_weight(w, sizes):
    ends = [sum(sizes[: j + 1]) * P_SIZE for j in range(len(sizes))]
    parts = [w[:, end - size * P_SIZE : end] for end, size in zip(ends, sizes)]
    return [lax.all_gather(part, "ctx", axis=0, tiled=True) for part in parts]


def forward(features, first, weight, running_t, b_rows, here):
    own, other = features
    length = own.shape[0]
    n = b_rows.shape[1]
    width, wide = weight.shape
    deep = width // 4
    spans = length // SPAN

    def depth(k, first_ref):
        return (k // 2 ^ first_ref[0]) * 2 + k % 2

    return pl.pallas_call(
        forward_kernel,
        grid_spec=pltpu.PrefetchScalarGridSpec(
            num_scalar_prefetch=1,
            grid=(wide // WIDE, 4),
            in_specs=[
                pl.BlockSpec((length, deep), lambda h, k, first_ref: (0, jnp.minimum(k, 1))),
                pl.BlockSpec((length, deep), lambda h, k, first_ref: (0, jnp.maximum(k - 2, 0))),
                pl.BlockSpec((deep, WIDE), lambda h, k, first_ref: (depth(k, first_ref), h)),
                pl.BlockSpec((1, length, GROUP), lambda h, k, first_ref: (h + here, 0, 0)),
                pl.BlockSpec((length, n), lambda h, k, first_ref: (0, 0)),
            ],
            out_specs=[
                pl.BlockSpec((length, WIDE), lambda h, k, first_ref: (0, h)),
                pl.BlockSpec((spans, n, WIDE), lambda h, k, first_ref: (0, 0, h)),
            ],
            scratch_shapes=[pltpu.VMEM((length, WIDE), F32)],
        ),
        out_shape=[shape(length, wide, dtype=BF16), shape(spans, n, wide)],
        cost_estimate=pl.CostEstimate(
            flops=2 * length * wide * width, bytes_accessed=2 * wide * width, transcendentals=0
        ),
        compiler_params=pltpu.CompilerParams(
            dimension_semantics=("arbitrary", "arbitrary"), vmem_limit_bytes=GRANT
        ),
    )(first, own, other, weight, running_t, b_rows)


def multiply(grad_x, weight, at, half, halves, before=None, other=None):
    length = grad_x.shape[0]
    width, wide = weight.shape
    tiles = width // halves // WIDE
    tile = pl.BlockSpec((length, WIDE), lambda j, half_ref: (0, half_ref[0] * tiles + j))
    plain = pl.BlockSpec((length, WIDE), lambda j, half_ref: (0, j))
    in_specs = [
        pl.BlockSpec((length, wide), lambda j, half_ref: (0, at)),
        pl.BlockSpec((WIDE, wide), lambda j, half_ref: (half_ref[0] * tiles + j, 0)),
    ]
    operands = [grad_x, weight]
    if before is not None:
        in_specs.append(tile)
        operands.append(before)
    if other is not None:
        in_specs.append(plain)
        operands.append(other)
    return pl.pallas_call(
        functools.partial(product_kernel, before is not None, other is not None),
        grid_spec=pltpu.PrefetchScalarGridSpec(
            num_scalar_prefetch=1,
            grid=(tiles,),
            in_specs=in_specs,
            out_specs=plain,
        ),
        out_shape=shape(length, width // halves, dtype=BF16),
        cost_estimate=pl.CostEstimate(
            flops=2 * length * wide * width // halves,
            bytes_accessed=2 * wide * width // halves,
            transcendentals=0,
        ),
        compiler_params=pltpu.CompilerParams(
            dimension_semantics=("arbitrary",), vmem_limit_bytes=GRANT
        ),
    )(half, *operands)


def early_forward(features, pieces):
    length = features.shape[0]
    rows, columns = pieces[0].shape
    deep = rows * len(pieces)
    return call(
        functools.partial(early_forward_kernel, len(pieces)),
        (columns // WIDE,),
        [pl.BlockSpec((length, deep), lambda h: (0, 0))]
        + [pl.BlockSpec((rows, WIDE), lambda h: (0, h))] * len(pieces),
        pl.BlockSpec((length, WIDE), lambda h: (0, h)),
        shape(length, columns),
        2 * length * columns * deep,
        2 * columns * deep,
        [pltpu.VMEM((deep, WIDE), BF16)],
    )(features, *pieces)


def late_forward(features, part, pieces, running_t, b_rows, kept, here):
    length = features.shape[0]
    rows, columns = pieces[0].shape
    deep = rows * len(pieces)
    n = b_rows.shape[1]
    spans = length // SPAN
    state = pl.BlockSpec((n, WIDE), lambda h: (0, h))
    return call(
        functools.partial(late_forward_kernel, len(pieces)),
        (columns // WIDE,),
        [
            pl.BlockSpec((length, deep), lambda h: (0, 0)),
            pl.BlockSpec((length, WIDE), lambda h: (0, h + here)),
            pl.BlockSpec((1, length, GROUP), lambda h: (h + here, 0, 0)),
            pl.BlockSpec((length, n), lambda h: (0, 0)),
            pl.BlockSpec((spans, 8, WIDE), lambda h: (0, 0, h + here)),
        ]
        + [pl.BlockSpec((rows, WIDE), lambda h: (0, h))] * len(pieces),
        [
            pl.BlockSpec((length, WIDE), lambda h: (0, h)),
            pl.BlockSpec((spans, n, WIDE), lambda h: (0, 0, h)),
            state,
            state,
        ],
        [
            shape(length, columns, dtype=BF16),
            shape(spans, n, columns),
            shape(n, columns),
            shape(n, columns, dtype=BF16),
        ],
        2 * length * columns * deep,
        2 * columns * deep,
        [pltpu.VMEM((deep, WIDE), BF16)],
    )(features, part, running_t, b_rows, kept, *pieces)


def multiply_blocks(order, grad_x, pieces, so_far):
    columns, length = grad_x.shape
    arrays = [array for piece in pieces for array in piece]
    rows = arrays[0].shape[0]
    count = len(pieces)
    half = shape(length, lax.axis_size("ctx") * rows // 2, dtype=BF16)
    first = 2 + len(arrays)
    return pl.pallas_call(
        functools.partial(blocks_kernel, [len(piece) for piece in pieces], bool(so_far)),
        grid=(1,),
        in_specs=[SCALARS, pl.BlockSpec((columns, length), lambda h: (0, 0))]
        + [ANYWHERE] * (len(arrays) + len(so_far)),
        out_specs=[ANYWHERE, ANYWHERE],
        out_shape=[half, half],
        input_output_aliases={first + k: k for k in range(len(so_far))},
        scratch_shapes=[
            pltpu.VMEM((rows * count, columns), BF16),
            pltpu.VMEM((count, length, rows), BF16),
            pltpu.SemaphoreType.DMA((len(arrays),)),
            pltpu.SemaphoreType.DMA((count,)),
        ],
        cost_estimate=pl.CostEstimate(
            flops=2 * length * columns * rows * count,
            bytes_accessed=2 * columns * rows * count,
            transcendentals=0,
        ),
        compiler_params=pltpu.CompilerParams(
            dimension_semantics=("arbitrary",), vmem_limit_bytes=GRANT
        ),
    )(order, grad_x, *arrays, *so_far)


def back_start(own_grads, kept):
    spans, n, columns = own_grads.shape
    return call(
        start_kernel,
        (columns // WIDE,),
        [
            pl.BlockSpec((spans, n, WIDE), lambda h: (0, 0, h)),
            pl.BlockSpec((spans, 8, WIDE), lambda h: (0, 0, h)),
        ],
        [pl.BlockSpec((rows, WIDE), lambda h: (0, h)) for rows in (n, 8, n + TAIL)],
        [shape(n, columns), shape(8, columns), shape(n + TAIL, columns, dtype=BF16)],
        0,
        14 * n * columns,
    )(own_grads, kept)


def back_step(place, log, total, sent, entering, bit):
    got = swap(sent, "ctx", bit)
    n, columns = total.shape
    tall = [pl.BlockSpec((rows, WIDE), lambda h: (0, h)) for rows in (8, n, n + TAIL)]
    return call(
        functools.partial(back_kernel, bit),
        (columns // WIDE,),
        [SCALARS] + tall + [tall[1]] * len(entering),
        [tall[1], tall[1], tall[2], tall[0], tall[0]],
        [
            shape(n, columns),
            shape(n, columns),
            shape(n + TAIL, columns, dtype=BF16),
            shape(8, columns),
            shape(8, columns),
        ],
        0,
        18 * n * columns,
    )(place, log, total, got, *entering)


def scan_step(factors, here, total, sent, entering, bit, last=False):
    got = swap(sent, "ctx", bit)
    n, columns = total.shape
    block = pl.BlockSpec((n, WIDE), lambda h: (0, h))
    outs = [shape(n, columns), shape(n, columns), shape(n, columns, dtype=BF16)]
    outs = outs[:1] if last else outs
    out = call(
        scan_kernel,
        (columns // WIDE,),
        [pl.BlockSpec((8, WIDE), lambda h: (0, h + here)), block, block] + [block] * len(entering),
        [block] * len(outs),
        outs,
        0,
        14 * n * columns,
    )(factors, total, got, *entering)
    return out if last else (out[1], out[0], out[2])


def local(inputs, w_in, b_rows, c_rows, log_decay, skip_gain, grad_out):
    groups = log_decay.shape[0] // GROUP
    layered = lax.axis_size("ctx") == 4 * PLANE and lax.axis_size("head") == 2
    if layered and groups % 2 == 0 and w_in.shape[0] == 256:
        return local_layered(inputs, w_in, b_rows, c_rows, log_decay, skip_gain, grad_out)
    return local_plain(inputs, w_in, b_rows, c_rows, log_decay, skip_gain, grad_out)


def prepare(log_decay, grad_out, c_rows):
    length, columns = grad_out.shape
    heads = log_decay.shape[0]
    spans = length // SPAN
    groups = heads // GROUP
    n = c_rows.shape[1]
    return call(
        decay_kernel,
        (spans, groups),
        [run_spec(), rows_spec(), SHARED],
        [run_spec(), run_t_spec(), kept_spec(), state_spec()],
        [
            shape(heads, length),
            shape(groups, length, GROUP),
            shape(spans, 8, columns),
            shape(spans, n, columns),
        ],
        2 * length * columns * n,
        6 * length * columns,
    )(log_decay, grad_out, c_rows)


def inner(grid, here, wide, operands, so_far):
    length = operands[2].shape[0]
    n = operands[4].shape[1]
    specs = [
        run_spec(here),
        run_t_spec(here),
        rows_spec(here),
        rows_spec(),
        SHARED,
        SHARED,
        state_spec(here),
    ]
    return call(
        inner_kernel,
        grid,
        specs + [SHARED] * len(so_far),
        [run_spec(), SHARED, SHARED],
        [shape(wide // P_SIZE, length), shape(length, n), shape(length, n)],
        12 * length * wide * SPAN,
        6 * length * wide,
        INNER_SCRATCH,
    )(*operands, *so_far)


def state_terms(grid, here, wide, operands, heads=None, so_far=None):
    length = operands[1].shape[0]
    n = operands[2].shape[1]
    heads = heads or wide // P_SIZE
    at = here if heads > wide // P_SIZE else 0
    extra = () if so_far is None else (so_far,)
    return pl.pallas_call(
        state_kernel,
        grid=grid,
        in_specs=[
            run_t_spec(here),
            rows_spec(here),
            SHARED,
            pl.BlockSpec((n, WIDE), lambda k, h: (0, h)),
            state_spec(),
            state_spec(here),
            kept_spec(here),
            run_spec(),
            SHARED,
        ]
        + [ANYWHERE] * len(extra),
        out_specs=[run_spec(at), SHARED],
        out_shape=[shape(heads, length), shape(length, n)],
        scratch_shapes=[pltpu.VMEM((grid[1], n, WIDE), F32)],
        input_output_aliases={len(operands): 0} if extra else {},
        cost_estimate=pl.CostEstimate(
            flops=4 * length * wide * n, bytes_accessed=6 * length * wide, transcendentals=0
        ),
        compiler_params=pltpu.CompilerParams(
            dimension_semantics=("arbitrary", "arbitrary"), vmem_limit_bytes=GRANT
        ),
    )(*operands, *extra)


def local_layered(inputs, w_in, b_rows, c_rows, log_decay, skip_gain, grad_out):
    length, columns = grad_out.shape
    heads = log_decay.shape[0]
    spans = length // SPAN
    groups = heads // GROUP
    place = lax.axis_index("head").astype(jnp.int32)
    half = columns // 2
    order = block_order()
    blocks = order.shape[0]
    width = blocks * w_in.shape[0]

    layer = lax.axis_index("ctx") // PLANE
    up1, down1 = along_z(w_in, 1), along_z(w_in, -1)
    own_x, own_y = swap_x(w_in), swap_y(w_in)
    other = swap(inputs, "head", 1)
    running, running_t, kept, own_grads = prepare(log_decay, grad_out, c_rows)
    spot = lax.axis_index("ctx").astype(jnp.int32)[None]
    back, log, sent = back_start(own_grads, kept)
    sent = after([sent], other)[0]
    back, leaving, sent, log, factors_1 = back_step(spot, log, back, sent, (), 1)

    up1, down1, sent = after([up1, down1, sent], own_x, own_y)
    up2, down2 = along_z(up1, 1), along_z(down1, -1)
    z1 = jnp.where(layer == 0, down1, up1)
    x1, y1 = swap_x(z1), swap_y(z1)
    back, leaving, sent, log, factors_2 = back_step(spot, log, back, sent, (leaving,), 2)
    order_own = (order + place * (blocks // 2)) % blocks
    cut = len(EARLY) * w_in.shape[0]
    early_features, late_features = call(
        arrange_kernel,
        (1,),
        [SCALARS] + [pl.BlockSpec((length, width // 2), lambda h: (0, 0))] * 2,
        [pl.BlockSpec((length, wide), lambda h: (0, 0)) for wide in (cut, width - cut)],
        [shape(length, wide, dtype=BF16) for wide in (cut, width - cut)],
        0,
        4 * length * width,
        [pltpu.VMEM((length, width), BF16)],
    )(order_own, inputs, other)

    up2, down2, down1, sent = after([up2, down2, down1, sent], x1, y1, early_features)
    z3 = jnp.where(layer == 0, down2, jnp.where(layer == 3, up2, down1))
    up3, down3 = along_z(up2, 1), along_z(down2, -1)
    x3, y3 = swap_x(z3), swap_y(z3)
    back, leaving, sent, log, factors_4 = back_step(spot, log, back, sent, (leaving,), 4)
    z2 = jnp.where(layer == 1, down2, jnp.where(layer == 2, up2, up3 + down3))
    z2a, z2b = z2[:, :half], z2[:, half:]

    z2a, x1, y3, own_y, sent = after([z2a, x1, y3, own_y, sent], x3, z2b)
    x1_a, x1_b = x1[:, :half], x1[:, half:]
    y3_a, y3_b = y3[:, :half], y3[:, half:]
    own_y_a, own_y_b = own_y[:, :half], own_y[:, half:]
    x2a, y2a = swap_x(z2a), swap_y(z2a)
    d3a, d1a = swap_x(y3_a), swap_y(x1_a)
    back, leaving, sent, log, factors_8 = back_step(spot, log, back, sent, (leaving,), 8)
    early = [w_in, own_x, own_y, z1, x1, y1, z3, x3, y3]
    part = early_forward(early_features, early)

    own_y_a, x2a, z2b, y3_b, x1_b, leaving = after(
        [own_y_a, x2a, z2b, y3_b, x1_b, leaving], y2a, d3a, d1a, part
    )
    d0a, d2a = swap_x(own_y_a), swap_y(x2a)
    x2b, y2b = swap_x(z2b), swap_y(z2b)
    d3b, d1b = swap_x(y3_b), swap_y(x1_b)
    leaving_all = [leaving]
    for k in range(spans - 1, 0, -1):
        leaving_all.insert(0, own_grads[k] + kept[k, :1] * leaving_all[0])
    leaving_all = jnp.stack([value.astype(BF16) for value in leaving_all])
    skip = jnp.repeat(skip_gain, P_SIZE)[None]
    grad_x = grad_rows(running, running_t, grad_out, b_rows, c_rows, leaving_all, skip, True)
    order_away = (order + (1 - place) * (blocks // 2)) % blocks
    early_order, late_order = order_away[: len(EARLY)], order_away[len(EARLY) :]
    product = multiply_blocks(early_order, grad_x, [[piece] for piece in early], ())
    late_a = [d0a, d1a, d3a, z2a, x2a, y2a, d2a]
    x_a, states_a, total_a, sent_a = late_forward(
        late_features, part, late_a, running_t, b_rows, kept, 0
    )

    own_y_b, x2b, sent_a, x_a = after(
        [own_y_b, x2b, sent_a, x_a], y2b, d3b, d1b, product[0]
    )
    d0b, d2b = swap_x(own_y_b), swap_y(x2b)
    total_a, entering_a, sent_a = scan_step(factors_1, 0, total_a, sent_a, (), 1)
    shared = (running, running_t, grad_out)
    here = groups // 2
    grid = (spans, here)
    inner_a = shared + (x_a, b_rows, c_rows, leaving_all)
    decay_a, grad_b, grad_c = inner(grid, 0, half, inner_a, ())

    d0b, d2b = after([d0b, d2b], sent_a, grad_b)
    late_b = [d0b, d1b, d3b, z2b, x2b, y2b, d2b]
    x_b, states_b, total_b, sent_b = late_forward(
        late_features, part, late_b, running_t, b_rows, kept, here
    )
    pairs = list(zip(late_a, late_b))
    sent_a, sent_b, *product = after([sent_a, sent_b, *product])
    total_b, entering_b, sent_b = scan_step(factors_1, here, total_b, sent_b, (), 1)
    total_a, entering_a, sent_a = scan_step(factors_2, 0, total_a, sent_a, (entering_a,), 2)
    away, own = multiply_blocks(late_order, grad_x, pairs, product)

    sent_a, sent_b, x_b, away = after([sent_a, sent_b, x_b, away])
    total_b, entering_b, sent_b = scan_step(factors_2, here, total_b, sent_b, (entering_b,), 2)
    total_a, entering_a, sent_a = scan_step(factors_4, 0, total_a, sent_a, (entering_a,), 4)
    got = swap(away, "head", 1)
    inner_b = shared + (x_b, b_rows, c_rows, leaving_all)
    decay_b, grad_b, grad_c = inner(grid, here, half, inner_b, (grad_b, grad_c))

    sent_a, sent_b, got, grad_b = after([sent_a, sent_b, got, grad_b])
    total_b, entering_b, sent_b = scan_step(factors_4, here, total_b, sent_b, (entering_b,), 4)
    (entering_a,) = scan_step(factors_8, 0, total_a, sent_a, (entering_a,), 8, True)
    grad_inputs = (own.astype(F32) + got.astype(F32)).astype(BF16)
    grad_b = head_sum(grad_b)

    sent_b, entering_a = after([sent_b, entering_a], grad_inputs, grad_b)
    (entering_b,) = scan_step(factors_8, here, total_b, sent_b, (entering_b,), 8, True)
    common = (running_t, grad_out, c_rows)
    state_a = common + (entering_a, states_a, leaving_all, kept, decay_a, grad_c)
    decays, grad_c = state_terms(grid, 0, half, state_a, heads)
    state_b = common + (entering_b, states_b, leaving_all, kept, decay_b, grad_c)
    decays, grad_c = state_terms(grid, here, half, state_b, heads, decays)
    return (grad_inputs, grad_b, head_sum(grad_c), decays)


def grad_rows(running, running_t, grad_out, b_rows, c_rows, leaving, skip, transposed):
    length, columns = grad_out.shape
    spec, dims = rows_spec(), (length, columns)
    if transposed:
        spec, dims = pl.BlockSpec((WIDE, SPAN), lambda k, h: (h, k)), (columns, length)
    return call(
        functools.partial(grad_x_kernel, transposed),
        (length // SPAN, running_t.shape[0]),
        [run_spec(), run_t_spec(), rows_spec(), SHARED, SHARED, state_spec(), GAIN],
        spec,
        shape(*dims, dtype=BF16),
        8 * length * columns * SPAN,
        6 * length * columns,
    )(running, running_t, grad_out, b_rows, c_rows, leaving, skip)


def local_plain(inputs, w_in, b_rows, c_rows, log_decay, skip_gain, grad_out):
    length, columns = grad_out.shape
    heads = log_decay.shape[0]
    spans = length // SPAN
    groups = heads // GROUP
    n = b_rows.shape[1]
    grid = (spans, groups)

    sizes = (heads // 2, heads // 4, heads // 4) if heads % (4 * GROUP) == 0 else (heads,)
    weights = gather_weight(w_in, sizes)
    two = lax.axis_size("head") == 2
    place = lax.axis_index("head").astype(jnp.int32)[None]
    width = weights[0].shape[0]
    if two:
        features = (inputs, swap(inputs, "head", 1))
        first = place
    else:
        features = lax.all_gather(inputs, "head", axis=1, tiled=True)
        features = (features[:, : width // 2], features[:, width // 2 :])
        first = jnp.zeros((1,), jnp.int32)

    running, running_t, kept, own_grads = call(
        decay_kernel,
        grid,
        [run_spec(), rows_spec(), SHARED],
        [run_spec(), run_t_spec(), kept_spec(), state_spec()],
        [
            shape(heads, length),
            shape(groups, length, GROUP),
            shape(spans, 8, columns),
            shape(spans, n, columns),
        ],
        2 * length * columns * n,
        6 * length * columns,
    )(log_decay, grad_out, c_rows)

    kept_total = kept[0, :1]
    for k in range(1, spans):
        kept_total = kept_total * kept[k, :1]
    steps = block_products(kept_total)

    total = own_grads[spans - 1]
    for k in range(spans - 2, -1, -1):
        total = own_grads[k] + kept[k, :1] * total
    leaving = [scan_states(total, steps, True)]
    for k in range(spans - 1, 0, -1):
        leaving.insert(0, own_grads[k] + kept[k, :1] * leaving[0])
    leaving = jnp.stack([value.astype(BF16) for value in leaving])

    skip = jnp.repeat(skip_gain, P_SIZE)[None]
    grad_x = grad_rows(running, running_t, grad_out, b_rows, c_rows, leaving, skip, False)

    grad_b = grad_c = product = None
    tokens = ()
    decay_parts = []
    at = 0
    for index, size in enumerate(sizes):
        wide = size * P_SIZE
        here = at // GROUP
        count = size // GROUP
        weight = weights[index]
        if tokens:
            weight = after([weight], *tokens)[0]
        x, own_states = forward(features, first, weight, running_t, b_rows, here)

        chunk = slice(at * P_SIZE, at * P_SIZE + wide)
        total = own_states[0]
        for k in range(1, spans):
            total = kept[k, :1, chunk] * total + own_states[k]
        cut = [step[:2] + tuple(value[:, chunk] for value in step[2:]) for step in steps]
        entering = scan_states(total, cut, False)

        so_far = () if grad_b is None else (grad_b, grad_c)
        decay_part, grad_b, grad_c = call(
            inner_kernel,
            (spans, count),
            [
                run_spec(here),
                run_t_spec(here),
                rows_spec(here),
                rows_spec(),
                SHARED,
                SHARED,
                state_spec(here),
            ]
            + [SHARED] * len(so_far),
            [run_spec(), SHARED, SHARED],
            [shape(size, length), shape(length, n), shape(length, n)],
            12 * length * wide * SPAN,
            6 * length * wide,
            INNER_SCRATCH,
        )(running, running_t, grad_out, x, b_rows, c_rows, leaving, *so_far)
        decay_part, grad_c = call(
            state_kernel,
            (spans, count),
            [
                run_t_spec(here),
                rows_spec(here),
                SHARED,
                pl.BlockSpec((n, WIDE), lambda k, h: (0, h)),
                state_spec(),
                state_spec(here),
                kept_spec(here),
                run_spec(),
                SHARED,
            ],
            [run_spec(), SHARED],
            [shape(size, length), shape(length, n)],
            4 * length * wide * n,
            6 * length * wide,
            [pltpu.VMEM((count, n, WIDE), F32)],
        )(running_t, grad_out, c_rows, entering, own_states, leaving, kept, decay_part, grad_c)
        decay_parts.append(decay_part)

        if index < len(sizes) - 1:
            zero = jnp.zeros((1,), jnp.int32)
            product = multiply(grad_x, weight, at // size, zero, 1, product)
            tokens = (product, grad_b, entering)
        elif two:
            sent = multiply(grad_x, weight, at // size, 1 - place, 2, product)
            got = swap(sent, "head", 1)
            grad_inputs = multiply(grad_x, weight, at // size, place, 2, product, got)
        else:
            zero = jnp.zeros((1,), jnp.int32)
            product = multiply(grad_x, weight, at // size, zero, 1, product)
            grad_inputs = lax.psum_scatter(product, "head", scatter_dimension=1, tiled=True)
        at += size

    return (grad_inputs, head_sum(grad_b), head_sum(grad_c), jnp.concatenate(decay_parts, axis=0))


def solution(mesh):
    in_specs = (
        P("ctx", "head"),
        P("ctx", "head"),
        P("ctx", None),
        P("ctx", None),
        P("head", "ctx"),
        P("head"),
        P("ctx", "head"),
    )
    out_specs = (P("ctx", "head"), P("ctx", None), P("ctx", None), P("head", "ctx"))
    return jax.shard_map(local, mesh=mesh, in_specs=in_specs, out_specs=out_specs, check_vma=False)
```

```python
import functools

import jax
import jax.numpy as jnp
from jax import lax
from jax.experimental import pallas as pl
from jax.experimental.pallas import tpu as pltpu
from jax.sharding import PartitionSpec as P

SPAN = 256
HALF = SPAN // 2
P_SIZE = 64
GROUP = 8
WIDE = GROUP * P_SIZE
LOG2E = 1.4426950408889634
NEVER = -1e30
GRANT = 24 * 2**20
LARGE = 30 * 2**20

F32 = jnp.float32
BF16 = jnp.bfloat16
EXACT = lax.Precision.HIGHEST


def dot(a, b, dims, precision=None):
    return lax.dot_general(a, b, (dims, ((), ())), precision=precision, preferred_element_type=F32)


def mm(a, b, precision=None):
    return dot(a, b, ((1,), (0,)), precision)


def iota(shape, dim):
    return lax.broadcasted_iota(jnp.int32, shape, dim)


def one_hot(dtype):
    return (iota((GROUP, WIDE), 0) == iota((GROUP, WIDE), 1) // P_SIZE).astype(dtype)


def not_before():
    return (iota((SPAN, SPAN), 0) >= iota((SPAN, SPAN), 1)).astype(F32)


def before():
    return (iota((SPAN, SPAN), 0) < iota((SPAN, SPAN), 1)).astype(F32)


def same():
    return (iota((SPAN, SPAN), 0) == iota((SPAN, SPAN), 1)).astype(F32)


def first_head():
    return iota((SPAN, 2 * P_SIZE), 1) < P_SIZE


def pair_columns(columns, pair):
    shape = (columns.shape[0], 2 * P_SIZE)
    left = jnp.broadcast_to(columns[:, 2 * pair : 2 * pair + 1], shape)
    right = jnp.broadcast_to(columns[:, 2 * pair + 1 : 2 * pair + 2], shape)
    return jnp.where(iota(shape, 1) < P_SIZE, left, right)


def spread_columns(columns):
    return jnp.concatenate([pair_columns(columns, pair) for pair in range(GROUP // 2)], axis=1)


def thirds(value):
    high = value.astype(BF16).astype(F32)
    middle = (value - high).astype(BF16).astype(F32)
    return high, middle, value - high - middle


def sum_over(value, mask):
    rows = value.shape[0]
    parts = mm(jnp.concatenate(thirds(value), axis=0).astype(BF16), mask.astype(BF16))
    return parts[:rows] + parts[rows : 2 * rows] + parts[2 * rows :]


def decay_kernel(d_ref, g_ref, c_ref, r_ref, rt_ref, a_ref, gt_ref):
    row_sums = sum_over(d_ref[...] * LOG2E, 1.0 - not_before() + same())
    r_ref[...] = row_sums
    padded = jnp.concatenate([row_sums, jnp.zeros((2 * P_SIZE - GROUP, SPAN), F32)], axis=0)
    running = padded.T[:, :GROUP]
    rt_ref[0] = running
    growth = jnp.exp2(spread_columns(running))
    last = spread_columns(running[SPAN - 1 : SPAN])
    a_ref[0] = jnp.where(iota((8, WIDE), 0) < 4, jnp.exp2(last), last)
    scaled = (g_ref[...].astype(F32) * growth).astype(BF16)
    gt_ref[0] = dot(c_ref[...], scaled, ((0,), (0,)))


def grad_x_kernel(transposed, r_ref, rt_ref, g_ref, b_ref, c_ref, q_ref, skip_ref, out_ref):
    b = b_ref[...]
    scores = dot(b, c_ref[...], ((1,), (1,)))
    running = r_ref[...]
    columns = rt_ref[0]
    top_keep = iota((HALF, SPAN), 1) >= iota((HALF, SPAN), 0)
    low_keep = iota((HALF, HALF), 1) >= iota((HALF, HALF), 0)
    to_end = jnp.exp2(spread_columns(columns[SPAN - 1 : SPAN] - columns))
    from_state = mm(b, q_ref[0]) * to_end
    for pair in range(GROUP // 2):
        lanes = slice(pair * 2 * P_SIZE, (pair + 1) * 2 * P_SIZE)
        g = g_ref[:, lanes]
        parts = []
        for head in (2 * pair, 2 * pair + 1):
            row = running[head : head + 1]
            top = jnp.where(top_keep, row - columns[:HALF, head : head + 1], NEVER)
            low = jnp.where(low_keep, row[:, HALF:] - columns[HALF:, head : head + 1], NEVER)
            parts.append((jnp.exp2(top) * scores[:HALF]).astype(BF16))
            low = (jnp.exp2(low) * scores[HALF:, HALF:]).astype(BF16)
            parts.append(jnp.concatenate([jnp.zeros((HALF, HALF), BF16), low], axis=1))
        product = mm(jnp.concatenate(parts, axis=0), g)
        parts = [product[:SPAN], product[SPAN:]]
        inner = jnp.where(first_head(), parts[0], parts[1])
        total = inner + skip_ref[:, lanes] * g.astype(F32) + from_state[:, lanes]
        if transposed:
            out_ref[lanes, :] = total.T.astype(BF16)
        else:
            out_ref[:, lanes] = total.astype(BF16)


def forward_kernel(half_ref, own_ref, other_ref, w_ref, rt_ref, b_ref, x_ref, e_ref, total_ref):
    step = pl.program_id(1)

    @pl.when(step == 0)
    def _():
        total_ref[...] = jnp.zeros_like(total_ref)

    half = pl.num_programs(1) // 2

    @pl.when(step < half)
    def _():
        total_ref[...] += mm(own_ref[...], w_ref[...])

    @pl.when(step >= half)
    def _():
        total_ref[...] += mm(other_ref[...], w_ref[...])

    @pl.when(step == pl.num_programs(1) - 1)
    def _():
        x = total_ref[...].astype(BF16)
        x_ref[...] = x
        for k in range(e_ref.shape[0]):
            rows = slice(k * SPAN, (k + 1) * SPAN)
            columns = rt_ref[0, rows]
            to_end = jnp.exp2(spread_columns(columns[SPAN - 1 : SPAN] - columns))
            scaled = (x[rows].astype(F32) * to_end).astype(BF16)
            e_ref[k] = dot(b_ref[rows], scaled, ((0,), (0,)))


def product_kernel(has_before, has_other, half_ref, g_ref, w_ref, *refs):
    refs = list(refs)
    total = dot(g_ref[...], w_ref[...], ((1,), (1,)))
    if has_before:
        total = total + refs.pop(0)[...].astype(F32)
    if has_other:
        total = total.astype(BF16).astype(F32) + refs.pop(0)[...].astype(F32)
    refs[0][...] = total.astype(BF16)


def arrange_kernel(order_ref, own_ref, other_ref, early_ref, late_ref, both_ref):
    half = own_ref.shape[1]
    both_ref[:, :half] = own_ref[...]
    both_ref[:, half:] = other_ref[...]
    unit = 2 * half // order_ref.shape[0]
    cut = early_ref.shape[1]
    for index in range(order_ref.shape[0]):
        source = pl.ds(pl.multiple_of(order_ref[index] * unit, 128), unit)
        at = index * unit
        if at < cut:
            early_ref[:, at : at + unit] = both_ref[:, source]
        else:
            late_ref[:, at - cut : at - cut + unit] = both_ref[:, source]


TAIL = 16


def message(total, log):
    high, middle, last = thirds(log)
    line = iota((TAIL, total.shape[1]), 0)
    tail = jnp.where(line == 0, high, jnp.where(line == 1, middle, jnp.where(line == 2, last, 0.0)))
    return total.astype(BF16), tail.astype(BF16)


def start_kernel(own_ref, kept_ref, total_ref, log_ref, sent_ref):
    spans = own_ref.shape[0]
    total = own_ref[spans - 1]
    log = kept_ref[spans - 1, 4:5]
    for k in range(spans - 2, -1, -1):
        total = own_ref[k] + kept_ref[k, :1] * total
        log = log + kept_ref[k, 4:5]
    total_ref[...] = total
    line = iota(log_ref.shape, 0)
    log_ref[...] = jnp.where(line == 0, log, 0.0)
    n = total.shape[0]
    sent_ref[:n], sent_ref[n:] = message(total, log)


def back_kernel(bit, place_ref, log_ref, total_ref, got_ref, *refs):
    entering_ref = refs[0] if len(refs) == 6 else None
    total_out, entering_out, sent_out, log_out, factor_out = refs[-5:]
    n = total_ref.shape[0]
    got = got_ref[:n].astype(F32)
    tail = got_ref[n:].astype(F32)
    other_log = tail[0:1] + tail[1:2] + tail[2:3]
    log, before_me, after_me = log_ref[0:1], log_ref[1:2], log_ref[2:3]
    line = iota(log_ref.shape, 0)
    upper = (place_ref[0] // bit % 2 + 0 * line[0:1]) == 1
    kept, other = jnp.exp2(log), jnp.exp2(other_log)
    total = jnp.where(upper, other, 1.0) * total_ref[...] + jnp.where(upper, 1.0, kept) * got
    passed = jnp.where(upper, 0.0, jnp.exp2(after_me)) * got
    total_out[...] = total
    entering_out[...] = passed if entering_ref is None else entering_ref[...] + passed
    first = jnp.where(upper, 1.0, other)
    second = jnp.where(upper, kept, 1.0)
    third = jnp.where(upper, jnp.exp2(before_me), 0.0)
    factor_out[...] = jnp.where(line == 0, first, jnp.where(line == 1, second, third))
    log = log + other_log
    before_me = jnp.where(upper, before_me + other_log, before_me)
    after_me = jnp.where(upper, after_me, after_me + other_log)
    log_out[...] = jnp.where(line == 0, log, jnp.where(line == 1, before_me, after_me))
    sent_out[:n], sent_out[n:] = message(total, log)


def scan_kernel(factor_ref, total_ref, got_ref, *refs):
    refs = list(refs)
    entering_ref = refs.pop(0) if len(refs) % 2 == 0 else None
    factors = factor_ref[...]
    got = got_ref[...].astype(F32)
    entering_out = refs[0]
    if len(refs) == 3:
        total = factors[0:1] * total_ref[...] + factors[1:2] * got
        refs[1][...] = total
        refs[2][...] = total.astype(BF16)
    passed = factors[2:3] * got
    entering_out[...] = passed if entering_ref is None else entering_ref[...] + passed


def early_forward_kernel(count, f_ref, *refs):
    pieces, (out_ref, buffer) = refs[:count], refs[count:]
    rows = pieces[0].shape[0]
    for index, piece in enumerate(pieces):
        buffer[index * rows : (index + 1) * rows] = piece[...]
    out_ref[...] = mm(f_ref[...], buffer[...])


def late_forward_kernel(count, f_ref, part_ref, rt_ref, b_ref, kept_ref, *refs):
    pieces, (x_ref, e_ref, total_ref, sent_ref, buffer) = refs[:count], refs[count:]
    rows = pieces[0].shape[0]
    for index, piece in enumerate(pieces):
        buffer[index * rows : (index + 1) * rows] = piece[...]
    x = (part_ref[...] + mm(f_ref[...], buffer[...])).astype(BF16)
    x_ref[...] = x
    total = None
    for k in range(e_ref.shape[0]):
        part = slice(k * SPAN, (k + 1) * SPAN)
        columns = rt_ref[0, part]
        to_end = jnp.exp2(spread_columns(columns[SPAN - 1 : SPAN] - columns))
        scaled = (x[part].astype(F32) * to_end).astype(BF16)
        state = dot(b_ref[part], scaled, ((0,), (0,)))
        e_ref[k] = state
        total = state if total is None else kept_ref[k, :1] * total + state
    total_ref[...] = total
    sent_ref[...] = total.astype(BF16)


def blocks_kernel(halves, has_before, order_ref, g_ref, *refs):
    count = len(halves)
    number = sum(halves)
    arrays, refs = refs[:number], refs[number:]
    if has_before:
        refs = refs[2:]
    away_ref, own_ref, buffer, slots, sems, out_sems = refs
    rows = arrays[0].shape[0]
    wide = g_ref.shape[0]
    copies = []
    at = 0
    for index, parts in enumerate(halves):
        mine = []
        for part in range(parts):
            lanes = pl.ds(part * (wide // parts), wide // parts)
            target = buffer.at[pl.ds(index * rows, rows), lanes]
            copy = pltpu.make_async_copy(arrays[at], target, sems.at[at])
            copy.start()
            mine.append(copy)
            at += 1
        copies.append(mine)
    g = g_ref[...]
    half = away_ref.shape[1] // rows
    bundle = 3 if count % 3 == 0 else count
    for index in range(count):
        for copy in copies[index]:
            copy.wait()
        if (index + 1) % bundle:
            continue
        start = index + 1 - bundle
        product = mm(buffer[start * rows : (index + 1) * rows], g)
        for done in range(start, index + 1):
            part = product[(done - start) * rows : (done - start + 1) * rows]
            slots[done] = part.T.astype(BF16)
            place = order_ref[done]
            lanes = pl.ds(pl.multiple_of(place % half * rows, 128), rows)

            @pl.when(place < half)
            def _():
                target = away_ref.at[:, lanes]
                pltpu.make_async_copy(slots.at[done], target, out_sems.at[done]).start()

            @pl.when(place >= half)
            def _():
                target = own_ref.at[:, lanes]
                pltpu.make_async_copy(slots.at[done], target, out_sems.at[done]).start()

    for index in range(count):
        target = away_ref.at[:, pl.ds(0, rows)]
        pltpu.make_async_copy(slots.at[index], target, out_sems.at[index]).wait()


def after_kernel(*refs):
    pass


def inner_kernel(
    r_ref, rt_ref, g_ref, x_ref, b_ref, c_ref, q_ref, *refs
):
    d_ref, grad_b_ref, grad_c_ref, sum_ref, top_ref, low_ref = refs[-6:]
    so_far = refs[:-6]
    step = pl.program_id(1)
    b = b_ref[...]
    c = c_ref[...]
    scores = dot(b, c, ((1,), (1,)))
    running = r_ref[...]
    columns = rt_ref[0]
    top_keep = iota((HALF, SPAN), 1) >= iota((HALF, SPAN), 0)
    low_keep = iota((HALF, HALF), 1) >= iota((HALF, HALF), 0)

    @pl.when(step == 0)
    def _():
        sum_ref[...] = jnp.zeros_like(sum_ref)
        grad_b_ref[...] = so_far[0][...] if so_far else jnp.zeros_like(grad_b_ref)

    rows = []
    lane = iota((SPAN, 2 * P_SIZE), 1)
    later = not_before().astype(BF16)
    top_less = iota((HALF, SPAN), 1) > iota((HALF, SPAN), 0)
    low_less = iota((HALF, HALF), 1) > iota((HALF, HALF), 0)
    for pair in range(GROUP // 2):
        lanes = slice(pair * 2 * P_SIZE, (pair + 1) * 2 * P_SIZE)
        x = x_ref[:, lanes]
        none = jnp.zeros_like(x)
        x = [jnp.where(lane < P_SIZE, x, none), jnp.where(lane < P_SIZE, none, x)]
        product = mm(jnp.concatenate(x, axis=0), g_ref[:, lanes].T)
        top_sum = low_sum = None
        for number in range(2):
            head = 2 * pair + number
            row = running[head : head + 1]
            at = number * SPAN
            top = jnp.where(top_keep, row - columns[:HALF, head : head + 1], NEVER)
            low = jnp.where(low_keep, row[:, HALF:] - columns[HALF:, head : head + 1], NEVER)
            top = jnp.exp2(top) * product[at : at + HALF]
            low = jnp.exp2(low) * product[at + HALF : at + SPAN, HALF:]
            top_sum = top if number == 0 else top_sum + top
            low_sum = low if number == 0 else low_sum + low
            part = slice(head * HALF, (head + 1) * HALF)
            top_ref[part] = (top * scores[:HALF]).astype(BF16)
            low_ref[part] = (low * scores[HALF:, HALF:]).astype(BF16)
        sum_ref[:HALF] += top_sum
        sum_ref[HALF:, HALF:] += low_sum
    top = mm(top_ref[...], later)
    low = mm(low_ref[...], later[HALF:, HALF:])
    for head in range(GROUP):
        part = slice(head * HALF, (head + 1) * HALF)
        top_row = jnp.sum(jnp.where(top_less, top[part], 0.0), axis=0, keepdims=True)
        low_row = jnp.sum(jnp.where(low_less, low[part], 0.0), axis=0, keepdims=True)
        rows.append(jnp.concatenate([top_row[:, :HALF], top_row[:, HALF:] + low_row], axis=1))
    to_end = jnp.exp2(spread_columns(columns[SPAN - 1 : SPAN] - columns))
    scaled = x_ref[...].astype(F32) * to_end
    ends = dot(one_hot(BF16), (scaled * mm(b, q_ref[0])).astype(BF16), ((1,), (1,)))
    d_ref[...] = jnp.concatenate(rows, axis=0) + sum_over(ends, before())
    grad_b_ref[...] += dot(scaled.astype(BF16), q_ref[0], ((1,), (1,)))

    @pl.when(step == pl.num_programs(1) - 1)
    def _():
        total = sum_ref[...].astype(BF16)
        grad_b_ref[...] += mm(total, c)
        part = dot(total, b, ((0,), (0,)))
        grad_c_ref[...] = part + so_far[1][...] if so_far else part


def state_kernel(
    rt_ref, g_ref, c_ref, s_ref, e_ref, q_ref, a_ref, d_part_ref, c_part_ref, *refs
):
    d_ref, grad_c_ref, held = refs[-3:]
    span, group = pl.program_id(0), pl.program_id(1)

    @pl.when(group == 0)
    def _():
        grad_c_ref[...] = c_part_ref[...]

    @pl.when(span == 0)
    def _():
        held[group] = s_ref[...]

    state = held[group]
    low = state.astype(BF16)
    scaled = g_ref[...].astype(F32) * jnp.exp2(spread_columns(rt_ref[0]))
    ends = dot(one_hot(BF16), (scaled * mm(c_ref[...], low)).astype(BF16), ((1,), (1,)))
    grad_c_ref[...] += dot(scaled.astype(BF16), low, ((1,), (1,)))
    product = jnp.sum(q_ref[0].astype(F32) * state, axis=0, keepdims=True) * a_ref[0, :1]
    high, middle, last = thirds(product)
    row = iota((8, WIDE), 0)
    stacked = jnp.where(row == 0, high, jnp.where(row == 1, middle, jnp.where(row == 2, last, 0.0)))
    kept = dot(one_hot(BF16), stacked.astype(BF16), ((1,), (1,)))
    kept = jnp.sum(kept, axis=1, keepdims=True)
    d_ref[...] = d_part_ref[...] + sum_over(ends, not_before()) + kept
    held[group] = e_ref[0] + a_ref[0, :1] * state


def call(kernel, grid, in_specs, out_specs, out_shape, flops, size, scratch=()):
    return pl.pallas_call(
        kernel,
        grid=grid,
        in_specs=in_specs,
        out_specs=out_specs,
        out_shape=out_shape,
        scratch_shapes=list(scratch),
        cost_estimate=pl.CostEstimate(flops=flops, bytes_accessed=size, transcendentals=0),
        compiler_params=pltpu.CompilerParams(
            dimension_semantics=("arbitrary",) * len(grid), vmem_limit_bytes=GRANT
        ),
    )


def run_spec(at=0):
    return pl.BlockSpec((GROUP, SPAN), lambda k, h: (h + at, k))


def run_t_spec(at=0):
    return pl.BlockSpec((1, SPAN, GROUP), lambda k, h: (h + at, k, 0))


def rows_spec(at=0):
    return pl.BlockSpec((SPAN, WIDE), lambda k, h: (k, h + at))


def state_spec(at=0):
    return pl.BlockSpec((1, 2 * P_SIZE, WIDE), lambda k, h: (k, 0, h + at))


def kept_spec(at=0):
    return pl.BlockSpec((1, 8, WIDE), lambda k, h: (k, 0, h + at))


SHARED = pl.BlockSpec((SPAN, 2 * P_SIZE), lambda k, h: (k, 0))
GAIN = pl.BlockSpec((1, WIDE), lambda k, h: (0, h))
ANYWHERE = pl.BlockSpec(memory_space=pl.ANY)
INNER_SCRATCH = [
    pltpu.VMEM((SPAN, SPAN), F32),
    pltpu.VMEM((GROUP * HALF, SPAN), BF16),
    pltpu.VMEM((GROUP * HALF, HALF), BF16),
]
SCALARS = pl.BlockSpec(memory_space=pltpu.SMEM)


def shape(*dims, dtype=F32):
    return jax.ShapeDtypeStruct(dims, dtype)


def swap(value, axis, bit):
    count = lax.axis_size(axis)
    return lax.ppermute(value, axis, [(i, i ^ bit) for i in range(count)])


def block_products(kept):
    count = lax.axis_size("ctx")
    place = lax.axis_index("ctx")
    steps = []
    before_me = jnp.ones_like(kept)
    after_me = jnp.ones_like(kept)
    bit = 1
    while bit < count:
        other = swap(kept, "ctx", bit)
        upper = (place & bit) != 0
        steps.append((bit, upper, kept, other, before_me, after_me))
        before_me = jnp.where(upper, before_me * other, before_me)
        after_me = jnp.where(upper, after_me, after_me * other)
        kept = kept * other
        bit *= 2
    return steps


def scan_states(total, steps, reverse):
    entering = jnp.zeros_like(total)
    for bit, upper, kept, other, before_me, after_me in steps:
        got = swap(total.astype(BF16), "ctx", bit).astype(F32)
        if reverse:
            entering = entering + jnp.where(upper, 0.0, after_me) * got
            total = jnp.where(upper, got + other * total, total + kept * got)
        else:
            entering = entering + jnp.where(upper, before_me, 0.0) * got
            total = jnp.where(upper, kept * got + total, other * total + got)
    return entering


def head_sum(value):
    bit = 1
    while bit < lax.axis_size("head"):
        value = value.astype(BF16)
        value = value.astype(F32) + swap(value, "head", bit).astype(F32)
        bit *= 2
    return value


PLANE = 4


def after(values, *tokens):
    out = pl.pallas_call(
        after_kernel,
        in_specs=[ANYWHERE] * (len(values) + len(tokens)),
        out_specs=[ANYWHERE] * len(values),
        out_shape=[shape(*value.shape, dtype=value.dtype) for value in values],
        input_output_aliases={index: index for index in range(len(values))},
        cost_estimate=pl.CostEstimate(flops=0, bytes_accessed=0, transcendentals=0),
    )(*values, *tokens)
    return list(out)


def along_z(value, moves):
    pairs = [(a * PLANE + i, b * PLANE + i) for a, b in moves for i in range(PLANE)]
    return lax.ppermute(value, "ctx", pairs)


MIDDLE = ((1, 2), (2, 1))
OUTWARD = ((1, 0), (2, 3))


def swap_x(value):
    return swap(value, "ctx", 1)


def swap_y(value):
    return swap(value, "ctx", 2)


LAYERS = ((0, 1, 2, 3), (1, 0, 3, 2), (2, 2, 1, 1), (3, 3, 0, 0))
EARLY = [(k, flip) for k in (0, 1, 2) for flip in range(3)]
LATE = [(0, 3), (1, 3), (2, 3), (3, 0), (3, 1), (3, 2), (3, 3)]


def block_order():
    place = lax.axis_index("ctx")
    layer, spot = place // PLANE, place % PLANE
    layers = jnp.array(LAYERS, jnp.int32)[:, layer]
    order = [layers[k] * PLANE + (spot ^ flip) for k, flip in EARLY + LATE]
    return jnp.stack(order).astype(jnp.int32)


def gather_weight(w, sizes):
    ends = [sum(sizes[: j + 1]) * P_SIZE for j in range(len(sizes))]
    parts = [w[:, end - size * P_SIZE : end] for end, size in zip(ends, sizes)]
    return [lax.all_gather(part, "ctx", axis=0, tiled=True) for part in parts]


def forward(features, first, weight, running_t, b_rows, here):
    own, other = features
    length = own.shape[0]
    n = b_rows.shape[1]
    width, wide = weight.shape
    deep = width // 4
    spans = length // SPAN

    def depth(k, first_ref):
        return (k // 2 ^ first_ref[0]) * 2 + k % 2

    return pl.pallas_call(
        forward_kernel,
        grid_spec=pltpu.PrefetchScalarGridSpec(
            num_scalar_prefetch=1,
            grid=(wide // WIDE, 4),
            in_specs=[
                pl.BlockSpec((length, deep), lambda h, k, first_ref: (0, jnp.minimum(k, 1))),
                pl.BlockSpec((length, deep), lambda h, k, first_ref: (0, jnp.maximum(k - 2, 0))),
                pl.BlockSpec((deep, WIDE), lambda h, k, first_ref: (depth(k, first_ref), h)),
                pl.BlockSpec((1, length, GROUP), lambda h, k, first_ref: (h + here, 0, 0)),
                pl.BlockSpec((length, n), lambda h, k, first_ref: (0, 0)),
            ],
            out_specs=[
                pl.BlockSpec((length, WIDE), lambda h, k, first_ref: (0, h)),
                pl.BlockSpec((spans, n, WIDE), lambda h, k, first_ref: (0, 0, h)),
            ],
            scratch_shapes=[pltpu.VMEM((length, WIDE), F32)],
        ),
        out_shape=[shape(length, wide, dtype=BF16), shape(spans, n, wide)],
        cost_estimate=pl.CostEstimate(
            flops=2 * length * wide * width, bytes_accessed=2 * wide * width, transcendentals=0
        ),
        compiler_params=pltpu.CompilerParams(
            dimension_semantics=("arbitrary", "arbitrary"), vmem_limit_bytes=GRANT
        ),
    )(first, own, other, weight, running_t, b_rows)


def multiply(grad_x, weight, at, half, halves, before=None, other=None):
    length = grad_x.shape[0]
    width, wide = weight.shape
    tiles = width // halves // WIDE
    tile = pl.BlockSpec((length, WIDE), lambda j, half_ref: (0, half_ref[0] * tiles + j))
    plain = pl.BlockSpec((length, WIDE), lambda j, half_ref: (0, j))
    in_specs = [
        pl.BlockSpec((length, wide), lambda j, half_ref: (0, at)),
        pl.BlockSpec((WIDE, wide), lambda j, half_ref: (half_ref[0] * tiles + j, 0)),
    ]
    operands = [grad_x, weight]
    if before is not None:
        in_specs.append(tile)
        operands.append(before)
    if other is not None:
        in_specs.append(plain)
        operands.append(other)
    return pl.pallas_call(
        functools.partial(product_kernel, before is not None, other is not None),
        grid_spec=pltpu.PrefetchScalarGridSpec(
            num_scalar_prefetch=1,
            grid=(tiles,),
            in_specs=in_specs,
            out_specs=plain,
        ),
        out_shape=shape(length, width // halves, dtype=BF16),
        cost_estimate=pl.CostEstimate(
            flops=2 * length * wide * width // halves,
            bytes_accessed=2 * wide * width // halves,
            transcendentals=0,
        ),
        compiler_params=pltpu.CompilerParams(
            dimension_semantics=("arbitrary",), vmem_limit_bytes=GRANT
        ),
    )(half, *operands)


def early_forward(features, pieces):
    length = features.shape[0]
    rows, columns = pieces[0].shape
    deep = rows * len(pieces)
    return call(
        functools.partial(early_forward_kernel, len(pieces)),
        (columns // WIDE,),
        [pl.BlockSpec((length, deep), lambda h: (0, 0))]
        + [pl.BlockSpec((rows, WIDE), lambda h: (0, h))] * len(pieces),
        pl.BlockSpec((length, WIDE), lambda h: (0, h)),
        shape(length, columns),
        2 * length * columns * deep,
        2 * columns * deep,
        [pltpu.VMEM((deep, WIDE), BF16)],
    )(features, *pieces)


def late_forward(features, part, pieces, running_t, b_rows, kept, here):
    length = features.shape[0]
    rows, columns = pieces[0].shape
    deep = rows * len(pieces)
    n = b_rows.shape[1]
    spans = length // SPAN
    state = pl.BlockSpec((n, WIDE), lambda h: (0, h))
    return call(
        functools.partial(late_forward_kernel, len(pieces)),
        (columns // WIDE,),
        [
            pl.BlockSpec((length, deep), lambda h: (0, 0)),
            pl.BlockSpec((length, WIDE), lambda h: (0, h + here)),
            pl.BlockSpec((1, length, GROUP), lambda h: (h + here, 0, 0)),
            pl.BlockSpec((length, n), lambda h: (0, 0)),
            pl.BlockSpec((spans, 8, WIDE), lambda h: (0, 0, h + here)),
        ]
        + [pl.BlockSpec((rows, WIDE), lambda h: (0, h))] * len(pieces),
        [
            pl.BlockSpec((length, WIDE), lambda h: (0, h)),
            pl.BlockSpec((spans, n, WIDE), lambda h: (0, 0, h)),
            state,
            state,
        ],
        [
            shape(length, columns, dtype=BF16),
            shape(spans, n, columns),
            shape(n, columns),
            shape(n, columns, dtype=BF16),
        ],
        2 * length * columns * deep,
        2 * columns * deep,
        [pltpu.VMEM((deep, WIDE), BF16)],
    )(features, part, running_t, b_rows, kept, *pieces)


def multiply_blocks(order, grad_x, pieces, so_far):
    columns, length = grad_x.shape
    arrays = [array for piece in pieces for array in piece]
    rows = arrays[0].shape[0]
    count = len(pieces)
    half = shape(length, lax.axis_size("ctx") * rows // 2, dtype=BF16)
    first = 2 + len(arrays)
    return pl.pallas_call(
        functools.partial(blocks_kernel, [len(piece) for piece in pieces], bool(so_far)),
        grid=(1,),
        in_specs=[SCALARS, pl.BlockSpec((columns, length), lambda h: (0, 0))]
        + [ANYWHERE] * (len(arrays) + len(so_far)),
        out_specs=[ANYWHERE, ANYWHERE],
        out_shape=[half, half],
        input_output_aliases={first + k: k for k in range(len(so_far))},
        scratch_shapes=[
            pltpu.VMEM((rows * count, columns), BF16),
            pltpu.VMEM((count, length, rows), BF16),
            pltpu.SemaphoreType.DMA((len(arrays),)),
            pltpu.SemaphoreType.DMA((count,)),
        ],
        cost_estimate=pl.CostEstimate(
            flops=2 * length * columns * rows * count,
            bytes_accessed=2 * columns * rows * count,
            transcendentals=0,
        ),
        compiler_params=pltpu.CompilerParams(
            dimension_semantics=("arbitrary",), vmem_limit_bytes=LARGE
        ),
    )(order, grad_x, *arrays, *so_far)


def back_start(own_grads, kept):
    spans, n, columns = own_grads.shape
    return call(
        start_kernel,
        (columns // WIDE,),
        [
            pl.BlockSpec((spans, n, WIDE), lambda h: (0, 0, h)),
            pl.BlockSpec((spans, 8, WIDE), lambda h: (0, 0, h)),
        ],
        [pl.BlockSpec((rows, WIDE), lambda h: (0, h)) for rows in (n, 8, n + TAIL)],
        [shape(n, columns), shape(8, columns), shape(n + TAIL, columns, dtype=BF16)],
        0,
        14 * n * columns,
    )(own_grads, kept)


def back_step(place, log, total, sent, entering, bit):
    got = swap(sent, "ctx", bit)
    n, columns = total.shape
    tall = [pl.BlockSpec((rows, WIDE), lambda h: (0, h)) for rows in (8, n, n + TAIL)]
    return call(
        functools.partial(back_kernel, bit),
        (columns // WIDE,),
        [SCALARS] + tall + [tall[1]] * len(entering),
        [tall[1], tall[1], tall[2], tall[0], tall[0]],
        [
            shape(n, columns),
            shape(n, columns),
            shape(n + TAIL, columns, dtype=BF16),
            shape(8, columns),
            shape(8, columns),
        ],
        0,
        18 * n * columns,
    )(place, log, total, got, *entering)


def scan_step(factors, here, total, sent, entering, bit, last=False):
    got = swap(sent, "ctx", bit)
    n, columns = total.shape
    block = pl.BlockSpec((n, WIDE), lambda h: (0, h))
    outs = [shape(n, columns), shape(n, columns), shape(n, columns, dtype=BF16)]
    outs = outs[:1] if last else outs
    out = call(
        scan_kernel,
        (columns // WIDE,),
        [pl.BlockSpec((8, WIDE), lambda h: (0, h + here)), block, block] + [block] * len(entering),
        [block] * len(outs),
        outs,
        0,
        14 * n * columns,
    )(factors, total, got, *entering)
    return out if last else (out[1], out[0], out[2])


def local(inputs, w_in, b_rows, c_rows, log_decay, skip_gain, grad_out):
    groups = log_decay.shape[0] // GROUP
    layered = lax.axis_size("ctx") == 4 * PLANE and lax.axis_size("head") == 2
    if layered and groups % 2 == 0 and w_in.shape[0] == 256:
        return local_layered(inputs, w_in, b_rows, c_rows, log_decay, skip_gain, grad_out)
    return local_plain(inputs, w_in, b_rows, c_rows, log_decay, skip_gain, grad_out)


def prepare(log_decay, grad_out, c_rows):
    length, columns = grad_out.shape
    heads = log_decay.shape[0]
    spans = length // SPAN
    groups = heads // GROUP
    n = c_rows.shape[1]
    return call(
        decay_kernel,
        (spans, groups),
        [run_spec(), rows_spec(), SHARED],
        [run_spec(), run_t_spec(), kept_spec(), state_spec()],
        [
            shape(heads, length),
            shape(groups, length, GROUP),
            shape(spans, 8, columns),
            shape(spans, n, columns),
        ],
        2 * length * columns * n,
        6 * length * columns,
    )(log_decay, grad_out, c_rows)


def inner(grid, here, wide, operands, so_far):
    length = operands[2].shape[0]
    n = operands[4].shape[1]
    specs = [
        run_spec(here),
        run_t_spec(here),
        rows_spec(here),
        rows_spec(),
        SHARED,
        SHARED,
        state_spec(here),
    ]
    return call(
        inner_kernel,
        grid,
        specs + [SHARED] * len(so_far),
        [run_spec(), SHARED, SHARED],
        [shape(wide // P_SIZE, length), shape(length, n), shape(length, n)],
        12 * length * wide * SPAN,
        6 * length * wide,
        INNER_SCRATCH,
    )(*operands, *so_far)


def state_terms(grid, here, wide, operands, heads=None, so_far=None):
    length = operands[1].shape[0]
    n = operands[2].shape[1]
    heads = heads or wide // P_SIZE
    at = here if heads > wide // P_SIZE else 0
    extra = () if so_far is None else (so_far,)
    return pl.pallas_call(
        state_kernel,
        grid=grid,
        in_specs=[
            run_t_spec(here),
            rows_spec(here),
            SHARED,
            pl.BlockSpec((n, WIDE), lambda k, h: (0, h)),
            state_spec(),
            state_spec(here),
            kept_spec(here),
            run_spec(),
            SHARED,
        ]
        + [ANYWHERE] * len(extra),
        out_specs=[run_spec(at), SHARED],
        out_shape=[shape(heads, length), shape(length, n)],
        scratch_shapes=[pltpu.VMEM((grid[1], n, WIDE), F32)],
        input_output_aliases={len(operands): 0} if extra else {},
        cost_estimate=pl.CostEstimate(
            flops=4 * length * wide * n, bytes_accessed=6 * length * wide, transcendentals=0
        ),
        compiler_params=pltpu.CompilerParams(
            dimension_semantics=("arbitrary", "arbitrary"), vmem_limit_bytes=GRANT
        ),
    )(*operands, *extra)


def local_layered(inputs, w_in, b_rows, c_rows, log_decay, skip_gain, grad_out):
    length, columns = grad_out.shape
    heads = log_decay.shape[0]
    spans = length // SPAN
    groups = heads // GROUP
    place = lax.axis_index("head").astype(jnp.int32)
    half = columns // 2
    order = block_order()
    blocks = order.shape[0]
    width = blocks * w_in.shape[0]

    z1, inner2 = swap(w_in, "ctx", PLANE), along_z(w_in, MIDDLE)
    own_x, own_y = swap_x(w_in), swap_y(w_in)
    other = swap(inputs, "head", 1)
    running, running_t, kept, own_grads = prepare(log_decay, grad_out, c_rows)
    spot = lax.axis_index("ctx").astype(jnp.int32)[None]
    back, log, sent = back_start(own_grads, kept)
    sent = after([sent], other)[0]
    back, leaving, sent, log, factors_1 = back_step(spot, log, back, sent, (), 1)

    z1, inner2, own_y, sent = after([z1, inner2, own_y, sent], own_x)
    x1, y1 = swap_x(z1), swap_y(z1)
    inner3, outer2 = along_z(z1, MIDDLE), along_z(inner2, OUTWARD)
    own_y_a, own_y_b = own_y[:, :half], own_y[:, half:]
    back, leaving, sent, log, factors_2 = back_step(spot, log, back, sent, (leaving,), 2)
    order_own = (order + place * (blocks // 2)) % blocks
    cut = len(EARLY) * w_in.shape[0]
    early_features, late_features = call(
        arrange_kernel,
        (1,),
        [SCALARS] + [pl.BlockSpec((length, width // 2), lambda h: (0, 0))] * 2,
        [pl.BlockSpec((length, wide), lambda h: (0, 0)) for wide in (cut, width - cut)],
        [shape(length, wide, dtype=BF16) for wide in (cut, width - cut)],
        0,
        4 * length * width,
        [pltpu.VMEM((length, width), BF16)],
    )(order_own, inputs, other)

    inner2, inner3, outer2, x1, sent, own_y_a, own_y_b = after(
        [inner2, inner3, outer2, x1, sent, own_y_a, own_y_b], y1, early_features
    )
    z3 = inner2 + outer2
    x3, y3 = swap_x(z3), swap_y(z3)
    outer3 = along_z(inner3, OUTWARD)
    x1_a, x1_b = x1[:, :half], x1[:, half:]
    back, leaving, sent, log, factors_4 = back_step(spot, log, back, sent, (leaving,), 4)

    inner3, outer3, y3, x1_a, x1_b, sent = after([inner3, outer3, y3, x1_a, x1_b, sent], x3)
    z2a = inner3[:, :half] + outer3[:, :half]
    z2b = inner3[:, half:] + outer3[:, half:]
    y3_a, y3_b = y3[:, :half], y3[:, half:]
    x2a, y2a = swap_x(z2a), swap_y(z2a)
    d3a, d1a = swap_x(y3_a), swap_y(x1_a)
    back, leaving, sent, log, factors_8 = back_step(spot, log, back, sent, (leaving,), 8)
    early = [w_in, own_x, own_y, z1, x1, y1, z3, x3, y3]
    part = early_forward(early_features, early)

    own_y_a, x2a, z2b, y3_b, x1_b, leaving = after(
        [own_y_a, x2a, z2b, y3_b, x1_b, leaving], y2a, d3a, d1a, part
    )
    d0a, d2a = swap_x(own_y_a), swap_y(x2a)
    x2b, y2b = swap_x(z2b), swap_y(z2b)
    d3b, d1b = swap_x(y3_b), swap_y(x1_b)
    leaving_all = [leaving]
    for k in range(spans - 1, 0, -1):
        leaving_all.insert(0, own_grads[k] + kept[k, :1] * leaving_all[0])
    leaving_all = jnp.stack([value.astype(BF16) for value in leaving_all])
    skip = jnp.repeat(skip_gain, P_SIZE)[None]
    grad_x = grad_rows(running, running_t, grad_out, b_rows, c_rows, leaving_all, skip, True)
    order_away = (order + (1 - place) * (blocks // 2)) % blocks
    early_order, late_order = order_away[: len(EARLY)], order_away[len(EARLY) :]
    product = multiply_blocks(early_order, grad_x, [[piece] for piece in early], ())
    late_a = [d0a, d1a, d3a, z2a, x2a, y2a, d2a]
    x_a, states_a, total_a, sent_a = late_forward(
        late_features, part, late_a, running_t, b_rows, kept, 0
    )

    own_y_b, x2b, sent_a, x_a = after(
        [own_y_b, x2b, sent_a, x_a], y2b, d3b, d1b, product[0]
    )
    d0b, d2b = swap_x(own_y_b), swap_y(x2b)
    total_a, entering_a, sent_a = scan_step(factors_1, 0, total_a, sent_a, (), 1)
    shared = (running, running_t, grad_out)
    here = groups // 2
    grid = (spans, here)
    inner_a = shared + (x_a, b_rows, c_rows, leaving_all)
    decay_a, grad_b, grad_c = inner(grid, 0, half, inner_a, ())

    d0b, d2b = after([d0b, d2b], sent_a, grad_b)
    late_b = [d0b, d1b, d3b, z2b, x2b, y2b, d2b]
    x_b, states_b, total_b, sent_b = late_forward(
        late_features, part, late_b, running_t, b_rows, kept, here
    )
    pairs = list(zip(late_a, late_b))
    sent_a, sent_b, *product = after([sent_a, sent_b, *product])
    total_b, entering_b, sent_b = scan_step(factors_1, here, total_b, sent_b, (), 1)
    total_a, entering_a, sent_a = scan_step(factors_2, 0, total_a, sent_a, (entering_a,), 2)
    away, own = multiply_blocks(late_order, grad_x, pairs, product)

    sent_a, sent_b, x_b, away = after([sent_a, sent_b, x_b, away])
    total_b, entering_b, sent_b = scan_step(factors_2, here, total_b, sent_b, (entering_b,), 2)
    total_a, entering_a, sent_a = scan_step(factors_4, 0, total_a, sent_a, (entering_a,), 4)
    got = swap(away, "head", 1)
    inner_b = shared + (x_b, b_rows, c_rows, leaving_all)
    decay_b, grad_b, grad_c = inner(grid, here, half, inner_b, (grad_b, grad_c))

    sent_a, sent_b, got, grad_b = after([sent_a, sent_b, got, grad_b])
    total_b, entering_b, sent_b = scan_step(factors_4, here, total_b, sent_b, (entering_b,), 4)
    (entering_a,) = scan_step(factors_8, 0, total_a, sent_a, (entering_a,), 8, True)
    grad_inputs = (own.astype(F32) + got.astype(F32)).astype(BF16)
    grad_b = head_sum(grad_b)

    sent_b, entering_a = after([sent_b, entering_a], grad_inputs, grad_b)
    (entering_b,) = scan_step(factors_8, here, total_b, sent_b, (entering_b,), 8, True)
    common = (running_t, grad_out, c_rows)
    state_a = common + (entering_a, states_a, leaving_all, kept, decay_a, grad_c)
    decays, grad_c = state_terms(grid, 0, half, state_a, heads)
    state_b = common + (entering_b, states_b, leaving_all, kept, decay_b, grad_c)
    decays, grad_c = state_terms(grid, here, half, state_b, heads, decays)
    return (grad_inputs, grad_b, head_sum(grad_c), decays)


def grad_rows(running, running_t, grad_out, b_rows, c_rows, leaving, skip, transposed):
    length, columns = grad_out.shape
    spec, dims = rows_spec(), (length, columns)
    if transposed:
        spec, dims = pl.BlockSpec((WIDE, SPAN), lambda k, h: (h, k)), (columns, length)
    return call(
        functools.partial(grad_x_kernel, transposed),
        (length // SPAN, running_t.shape[0]),
        [run_spec(), run_t_spec(), rows_spec(), SHARED, SHARED, state_spec(), GAIN],
        spec,
        shape(*dims, dtype=BF16),
        8 * length * columns * SPAN,
        6 * length * columns,
    )(running, running_t, grad_out, b_rows, c_rows, leaving, skip)


def local_plain(inputs, w_in, b_rows, c_rows, log_decay, skip_gain, grad_out):
    length, columns = grad_out.shape
    heads = log_decay.shape[0]
    spans = length // SPAN
    groups = heads // GROUP
    n = b_rows.shape[1]
    grid = (spans, groups)

    sizes = (heads // 2, heads // 4, heads // 4) if heads % (4 * GROUP) == 0 else (heads,)
    weights = gather_weight(w_in, sizes)
    two = lax.axis_size("head") == 2
    place = lax.axis_index("head").astype(jnp.int32)[None]
    width = weights[0].shape[0]
    if two:
        features = (inputs, swap(inputs, "head", 1))
        first = place
    else:
        features = lax.all_gather(inputs, "head", axis=1, tiled=True)
        features = (features[:, : width // 2], features[:, width // 2 :])
        first = jnp.zeros((1,), jnp.int32)

    running, running_t, kept, own_grads = call(
        decay_kernel,
        grid,
        [run_spec(), rows_spec(), SHARED],
        [run_spec(), run_t_spec(), kept_spec(), state_spec()],
        [
            shape(heads, length),
            shape(groups, length, GROUP),
            shape(spans, 8, columns),
            shape(spans, n, columns),
        ],
        2 * length * columns * n,
        6 * length * columns,
    )(log_decay, grad_out, c_rows)

    kept_total = kept[0, :1]
    for k in range(1, spans):
        kept_total = kept_total * kept[k, :1]
    steps = block_products(kept_total)

    total = own_grads[spans - 1]
    for k in range(spans - 2, -1, -1):
        total = own_grads[k] + kept[k, :1] * total
    leaving = [scan_states(total, steps, True)]
    for k in range(spans - 1, 0, -1):
        leaving.insert(0, own_grads[k] + kept[k, :1] * leaving[0])
    leaving = jnp.stack([value.astype(BF16) for value in leaving])

    skip = jnp.repeat(skip_gain, P_SIZE)[None]
    grad_x = grad_rows(running, running_t, grad_out, b_rows, c_rows, leaving, skip, False)

    grad_b = grad_c = product = None
    tokens = ()
    decay_parts = []
    at = 0
    for index, size in enumerate(sizes):
        wide = size * P_SIZE
        here = at // GROUP
        count = size // GROUP
        weight = weights[index]
        if tokens:
            weight = after([weight], *tokens)[0]
        x, own_states = forward(features, first, weight, running_t, b_rows, here)

        chunk = slice(at * P_SIZE, at * P_SIZE + wide)
        total = own_states[0]
        for k in range(1, spans):
            total = kept[k, :1, chunk] * total + own_states[k]
        cut = [step[:2] + tuple(value[:, chunk] for value in step[2:]) for step in steps]
        entering = scan_states(total, cut, False)

        so_far = () if grad_b is None else (grad_b, grad_c)
        decay_part, grad_b, grad_c = call(
            inner_kernel,
            (spans, count),
            [
                run_spec(here),
                run_t_spec(here),
                rows_spec(here),
                rows_spec(),
                SHARED,
                SHARED,
                state_spec(here),
            ]
            + [SHARED] * len(so_far),
            [run_spec(), SHARED, SHARED],
            [shape(size, length), shape(length, n), shape(length, n)],
            12 * length * wide * SPAN,
            6 * length * wide,
            INNER_SCRATCH,
        )(running, running_t, grad_out, x, b_rows, c_rows, leaving, *so_far)
        decay_part, grad_c = call(
            state_kernel,
            (spans, count),
            [
                run_t_spec(here),
                rows_spec(here),
                SHARED,
                pl.BlockSpec((n, WIDE), lambda k, h: (0, h)),
                state_spec(),
                state_spec(here),
                kept_spec(here),
                run_spec(),
                SHARED,
            ],
            [run_spec(), SHARED],
            [shape(size, length), shape(length, n)],
            4 * length * wide * n,
            6 * length * wide,
            [pltpu.VMEM((count, n, WIDE), F32)],
        )(running_t, grad_out, c_rows, entering, own_states, leaving, kept, decay_part, grad_c)
        decay_parts.append(decay_part)

        if index < len(sizes) - 1:
            zero = jnp.zeros((1,), jnp.int32)
            product = multiply(grad_x, weight, at // size, zero, 1, product)
            tokens = (product, grad_b, entering)
        elif two:
            sent = multiply(grad_x, weight, at // size, 1 - place, 2, product)
            got = swap(sent, "head", 1)
            grad_inputs = multiply(grad_x, weight, at // size, place, 2, product, got)
        else:
            zero = jnp.zeros((1,), jnp.int32)
            product = multiply(grad_x, weight, at // size, zero, 1, product)
            grad_inputs = lax.psum_scatter(product, "head", scatter_dimension=1, tiled=True)
        at += size

    return (grad_inputs, head_sum(grad_b), head_sum(grad_c), jnp.concatenate(decay_parts, axis=0))


def solution(mesh):
    in_specs = (
        P("ctx", "head"),
        P("ctx", "head"),
        P("ctx", None),
        P("ctx", None),
        P("head", "ctx"),
        P("head"),
        P("ctx", "head"),
    )
    out_specs = (P("ctx", "head"), P("ctx", None), P("ctx", None), P("head", "ctx"))
    return jax.shard_map(local, mesh=mesh, in_specs=in_specs, out_specs=out_specs, check_vma=False)
```

```python
import functools

import jax
import jax.numpy as jnp
from jax import lax
from jax.experimental import pallas as pl
from jax.experimental.pallas import tpu as pltpu
from jax.sharding import PartitionSpec as P

SPAN = 256
HALF = SPAN // 2
P_SIZE = 64
GROUP = 8
WIDE = GROUP * P_SIZE
LOG2E = 1.4426950408889634
NEVER = -1e30
GRANT = 64 * 2**20

F32 = jnp.float32
BF16 = jnp.bfloat16
EXACT = lax.Precision.HIGHEST


def dot(a, b, dims, precision=None):
    return lax.dot_general(a, b, (dims, ((), ())), precision=precision, preferred_element_type=F32)


def mm(a, b, precision=None):
    return dot(a, b, ((1,), (0,)), precision)


def iota(shape, dim):
    return lax.broadcasted_iota(jnp.int32, shape, dim)


def one_hot(dtype):
    return (iota((GROUP, WIDE), 0) == iota((GROUP, WIDE), 1) // P_SIZE).astype(dtype)


def not_before():
    return (iota((SPAN, SPAN), 0) >= iota((SPAN, SPAN), 1)).astype(F32)


def before():
    return (iota((SPAN, SPAN), 0) < iota((SPAN, SPAN), 1)).astype(F32)


def same():
    return (iota((SPAN, SPAN), 0) == iota((SPAN, SPAN), 1)).astype(F32)


def first_head():
    return iota((SPAN, 2 * P_SIZE), 1) < P_SIZE


def pair_columns(columns, pair):
    shape = (columns.shape[0], 2 * P_SIZE)
    left = jnp.broadcast_to(columns[:, 2 * pair : 2 * pair + 1], shape)
    right = jnp.broadcast_to(columns[:, 2 * pair + 1 : 2 * pair + 2], shape)
    return jnp.where(iota(shape, 1) < P_SIZE, left, right)


def spread_columns(columns):
    return jnp.concatenate([pair_columns(columns, pair) for pair in range(GROUP // 2)], axis=1)


def thirds(value):
    high = value.astype(BF16).astype(F32)
    middle = (value - high).astype(BF16).astype(F32)
    return high, middle, value - high - middle


def sum_over(value, mask):
    rows = value.shape[0]
    parts = mm(jnp.concatenate(thirds(value), axis=0).astype(BF16), mask.astype(BF16))
    return parts[:rows] + parts[rows : 2 * rows] + parts[2 * rows :]


def decay_kernel(d_ref, g_ref, c_ref, r_ref, rt_ref, a_ref, gt_ref):
    row_sums = sum_over(d_ref[...] * LOG2E, 1.0 - not_before() + same())
    r_ref[...] = row_sums
    padded = jnp.concatenate([row_sums, jnp.zeros((2 * P_SIZE - GROUP, SPAN), F32)], axis=0)
    running = padded.T[:, :GROUP]
    rt_ref[0] = running
    growth = jnp.exp2(spread_columns(running))
    last = spread_columns(running[SPAN - 1 : SPAN])
    a_ref[0] = jnp.where(iota((8, WIDE), 0) < 4, jnp.exp2(last), last)
    scaled = (g_ref[...].astype(F32) * growth).astype(BF16)
    gt_ref[0] = dot(c_ref[...], scaled, ((0,), (0,)))


def grad_x_kernel(transposed, r_ref, rt_ref, g_ref, b_ref, c_ref, q_ref, skip_ref, out_ref):
    b = b_ref[...]
    scores = dot(b, c_ref[...], ((1,), (1,)))
    running = r_ref[...]
    columns = rt_ref[0]
    top_keep = iota((HALF, SPAN), 1) >= iota((HALF, SPAN), 0)
    low_keep = iota((HALF, HALF), 1) >= iota((HALF, HALF), 0)
    to_end = jnp.exp2(spread_columns(columns[SPAN - 1 : SPAN] - columns))
    from_state = mm(b, q_ref[0]) * to_end
    for pair in range(GROUP // 2):
        lanes = slice(pair * 2 * P_SIZE, (pair + 1) * 2 * P_SIZE)
        g = g_ref[:, lanes]
        parts = []
        for head in (2 * pair, 2 * pair + 1):
            row = running[head : head + 1]
            top = jnp.where(top_keep, row - columns[:HALF, head : head + 1], NEVER)
            low = jnp.where(low_keep, row[:, HALF:] - columns[HALF:, head : head + 1], NEVER)
            parts.append((jnp.exp2(top) * scores[:HALF]).astype(BF16))
            low = (jnp.exp2(low) * scores[HALF:, HALF:]).astype(BF16)
            parts.append(jnp.concatenate([jnp.zeros((HALF, HALF), BF16), low], axis=1))
        product = mm(jnp.concatenate(parts, axis=0), g)
        parts = [product[:SPAN], product[SPAN:]]
        inner = jnp.where(first_head(), parts[0], parts[1])
        total = inner + skip_ref[:, lanes] * g.astype(F32) + from_state[:, lanes]
        if transposed:
            out_ref[lanes, :] = total.T.astype(BF16)
        else:
            out_ref[:, lanes] = total.astype(BF16)


def forward_kernel(half_ref, own_ref, other_ref, w_ref, rt_ref, b_ref, x_ref, e_ref, total_ref):
    step = pl.program_id(1)

    @pl.when(step == 0)
    def _():
        total_ref[...] = jnp.zeros_like(total_ref)

    half = pl.num_programs(1) // 2

    @pl.when(step < half)
    def _():
        total_ref[...] += mm(own_ref[...], w_ref[...])

    @pl.when(step >= half)
    def _():
        total_ref[...] += mm(other_ref[...], w_ref[...])

    @pl.when(step == pl.num_programs(1) - 1)
    def _():
        x = total_ref[...].astype(BF16)
        x_ref[...] = x
        for k in range(e_ref.shape[0]):
            rows = slice(k * SPAN, (k + 1) * SPAN)
            columns = rt_ref[0, rows]
            to_end = jnp.exp2(spread_columns(columns[SPAN - 1 : SPAN] - columns))
            scaled = (x[rows].astype(F32) * to_end).astype(BF16)
            e_ref[k] = dot(b_ref[rows], scaled, ((0,), (0,)))


def product_kernel(has_before, has_other, half_ref, g_ref, w_ref, *refs):
    refs = list(refs)
    total = dot(g_ref[...], w_ref[...], ((1,), (1,)))
    if has_before:
        total = total + refs.pop(0)[...].astype(F32)
    if has_other:
        total = total.astype(BF16).astype(F32) + refs.pop(0)[...].astype(F32)
    refs[0][...] = total.astype(BF16)


def arrange_kernel(order_ref, own_ref, other_ref, early_ref, late_ref, both_ref):
    half = own_ref.shape[1]
    both_ref[:, :half] = own_ref[...]
    both_ref[:, half:] = other_ref[...]
    unit = 2 * half // order_ref.shape[0]
    cut = early_ref.shape[1]
    for index in range(order_ref.shape[0]):
        source = pl.ds(pl.multiple_of(order_ref[index] * unit, 128), unit)
        at = index * unit
        if at < cut:
            early_ref[:, at : at + unit] = both_ref[:, source]
        else:
            late_ref[:, at - cut : at - cut + unit] = both_ref[:, source]


TAIL = 16


def message(total, log):
    high, middle, last = thirds(log)
    line = iota((TAIL, total.shape[1]), 0)
    tail = jnp.where(line == 0, high, jnp.where(line == 1, middle, jnp.where(line == 2, last, 0.0)))
    return total.astype(BF16), tail.astype(BF16)


def start_kernel(own_ref, kept_ref, total_ref, log_ref, sent_ref):
    spans = own_ref.shape[0]
    total = own_ref[spans - 1]
    log = kept_ref[spans - 1, 4:5]
    for k in range(spans - 2, -1, -1):
        total = own_ref[k] + kept_ref[k, :1] * total
        log = log + kept_ref[k, 4:5]
    total_ref[...] = total
    line = iota(log_ref.shape, 0)
    log_ref[...] = jnp.where(line == 0, log, 0.0)
    n = total.shape[0]
    sent_ref[:n], sent_ref[n:] = message(total, log)


def back_kernel(bit, place_ref, log_ref, total_ref, got_ref, *refs):
    entering_ref = refs[0] if len(refs) == 6 else None
    total_out, entering_out, sent_out, log_out, factor_out = refs[-5:]
    n = total_ref.shape[0]
    got = got_ref[:n].astype(F32)
    tail = got_ref[n:].astype(F32)
    other_log = tail[0:1] + tail[1:2] + tail[2:3]
    log, before_me, after_me = log_ref[0:1], log_ref[1:2], log_ref[2:3]
    line = iota(log_ref.shape, 0)
    upper = (place_ref[0] // bit % 2 + 0 * line[0:1]) == 1
    kept, other = jnp.exp2(log), jnp.exp2(other_log)
    total = jnp.where(upper, other, 1.0) * total_ref[...] + jnp.where(upper, 1.0, kept) * got
    passed = jnp.where(upper, 0.0, jnp.exp2(after_me)) * got
    total_out[...] = total
    entering_out[...] = passed if entering_ref is None else entering_ref[...] + passed
    first = jnp.where(upper, 1.0, other)
    second = jnp.where(upper, kept, 1.0)
    third = jnp.where(upper, jnp.exp2(before_me), 0.0)
    factor_out[...] = jnp.where(line == 0, first, jnp.where(line == 1, second, third))
    log = log + other_log
    before_me = jnp.where(upper, before_me + other_log, before_me)
    after_me = jnp.where(upper, after_me, after_me + other_log)
    log_out[...] = jnp.where(line == 0, log, jnp.where(line == 1, before_me, after_me))
    sent_out[:n], sent_out[n:] = message(total, log)


def scan_kernel(factor_ref, total_ref, got_ref, *refs):
    refs = list(refs)
    entering_ref = refs.pop(0) if len(refs) % 2 == 0 else None
    factors = factor_ref[...]
    got = got_ref[...].astype(F32)
    entering_out = refs[0]
    if len(refs) == 3:
        total = factors[0:1] * total_ref[...] + factors[1:2] * got
        refs[1][...] = total
        refs[2][...] = total.astype(BF16)
    passed = factors[2:3] * got
    entering_out[...] = passed if entering_ref is None else entering_ref[...] + passed


def early_forward_kernel(count, f_ref, *refs):
    pieces, (out_ref, buffer) = refs[:count], refs[count:]
    rows = pieces[0].shape[0]
    for index, piece in enumerate(pieces):
        buffer[index * rows : (index + 1) * rows] = piece[...]
    out_ref[...] = mm(f_ref[...], buffer[...])


def late_forward_kernel(count, f_ref, part_ref, rt_ref, b_ref, kept_ref, *refs):
    pieces, (x_ref, e_ref, total_ref, sent_ref, buffer) = refs[:count], refs[count:]
    rows = pieces[0].shape[0]
    for index, piece in enumerate(pieces):
        buffer[index * rows : (index + 1) * rows] = piece[...]
    x = (part_ref[...] + mm(f_ref[...], buffer[...])).astype(BF16)
    x_ref[...] = x
    total = None
    for k in range(e_ref.shape[0]):
        part = slice(k * SPAN, (k + 1) * SPAN)
        columns = rt_ref[0, part]
        to_end = jnp.exp2(spread_columns(columns[SPAN - 1 : SPAN] - columns))
        scaled = (x[part].astype(F32) * to_end).astype(BF16)
        state = dot(b_ref[part], scaled, ((0,), (0,)))
        e_ref[k] = state
        total = state if total is None else kept_ref[k, :1] * total + state
    total_ref[...] = total
    sent_ref[...] = total.astype(BF16)


def blocks_kernel(halves, has_before, order_ref, g_ref, *refs):
    count = len(halves)
    number = sum(halves)
    arrays, refs = refs[:number], refs[number:]
    if has_before:
        refs = refs[2:]
    away_ref, own_ref, buffer, slots, sems, out_sems = refs
    rows = arrays[0].shape[0]
    wide = g_ref.shape[0]
    copies = []
    at = 0
    for index, parts in enumerate(halves):
        mine = []
        for part in range(parts):
            lanes = pl.ds(part * (wide // parts), wide // parts)
            target = buffer.at[pl.ds(index * rows, rows), lanes]
            copy = pltpu.make_async_copy(arrays[at], target, sems.at[at])
            copy.start()
            mine.append(copy)
            at += 1
        copies.append(mine)
    g = g_ref[...]
    half = away_ref.shape[1] // rows
    bundle = 3 if count % 3 == 0 else count
    for index in range(count):
        for copy in copies[index]:
            copy.wait()
        if (index + 1) % bundle:
            continue
        start = index + 1 - bundle
        product = mm(buffer[start * rows : (index + 1) * rows], g)
        for done in range(start, index + 1):
            part = product[(done - start) * rows : (done - start + 1) * rows]
            slots[done] = part.T.astype(BF16)
            place = order_ref[done]
            lanes = pl.ds(pl.multiple_of(place % half * rows, 128), rows)

            @pl.when(place < half)
            def _():
                target = away_ref.at[:, lanes]
                pltpu.make_async_copy(slots.at[done], target, out_sems.at[done]).start()

            @pl.when(place >= half)
            def _():
                target = own_ref.at[:, lanes]
                pltpu.make_async_copy(slots.at[done], target, out_sems.at[done]).start()

    for index in range(count):
        target = away_ref.at[:, pl.ds(0, rows)]
        pltpu.make_async_copy(slots.at[index], target, out_sems.at[index]).wait()


def after_kernel(*refs):
    pass


def inner_kernel(
    r_ref, rt_ref, g_ref, x_ref, b_ref, c_ref, q_ref, *refs
):
    d_ref, grad_b_ref, grad_c_ref, sum_ref, top_ref, low_ref = refs[-6:]
    so_far = refs[:-6]
    step = pl.program_id(1)
    b = b_ref[...]
    c = c_ref[...]
    scores = dot(b, c, ((1,), (1,)))
    running = r_ref[...]
    columns = rt_ref[0]
    top_keep = iota((HALF, SPAN), 1) >= iota((HALF, SPAN), 0)
    low_keep = iota((HALF, HALF), 1) >= iota((HALF, HALF), 0)

    @pl.when(step == 0)
    def _():
        sum_ref[...] = jnp.zeros_like(sum_ref)
        grad_b_ref[...] = so_far[0][...] if so_far else jnp.zeros_like(grad_b_ref)

    rows = []
    lane = iota((SPAN, 2 * P_SIZE), 1)
    later = not_before().astype(BF16)
    top_less = iota((HALF, SPAN), 1) > iota((HALF, SPAN), 0)
    low_less = iota((HALF, HALF), 1) > iota((HALF, HALF), 0)
    for pair in range(GROUP // 2):
        lanes = slice(pair * 2 * P_SIZE, (pair + 1) * 2 * P_SIZE)
        x = x_ref[:, lanes]
        none = jnp.zeros_like(x)
        x = [jnp.where(lane < P_SIZE, x, none), jnp.where(lane < P_SIZE, none, x)]
        product = mm(jnp.concatenate(x, axis=0), g_ref[:, lanes].T)
        top_sum = low_sum = None
        for number in range(2):
            head = 2 * pair + number
            row = running[head : head + 1]
            at = number * SPAN
            top = jnp.where(top_keep, row - columns[:HALF, head : head + 1], NEVER)
            low = jnp.where(low_keep, row[:, HALF:] - columns[HALF:, head : head + 1], NEVER)
            top = jnp.exp2(top) * product[at : at + HALF]
            low = jnp.exp2(low) * product[at + HALF : at + SPAN, HALF:]
            top_sum = top if number == 0 else top_sum + top
            low_sum = low if number == 0 else low_sum + low
            part = slice(head * HALF, (head + 1) * HALF)
            top_ref[part] = (top * scores[:HALF]).astype(BF16)
            low_ref[part] = (low * scores[HALF:, HALF:]).astype(BF16)
        sum_ref[:HALF] += top_sum
        sum_ref[HALF:, HALF:] += low_sum
    top = mm(top_ref[...], later)
    low = mm(low_ref[...], later[HALF:, HALF:])
    for head in range(GROUP):
        part = slice(head * HALF, (head + 1) * HALF)
        top_row = jnp.sum(jnp.where(top_less, top[part], 0.0), axis=0, keepdims=True)
        low_row = jnp.sum(jnp.where(low_less, low[part], 0.0), axis=0, keepdims=True)
        rows.append(jnp.concatenate([top_row[:, :HALF], top_row[:, HALF:] + low_row], axis=1))
    to_end = jnp.exp2(spread_columns(columns[SPAN - 1 : SPAN] - columns))
    scaled = x_ref[...].astype(F32) * to_end
    ends = dot(one_hot(BF16), (scaled * mm(b, q_ref[0])).astype(BF16), ((1,), (1,)))
    d_ref[...] = jnp.concatenate(rows, axis=0) + sum_over(ends, before())
    grad_b_ref[...] += dot(scaled.astype(BF16), q_ref[0], ((1,), (1,)))

    @pl.when(step == pl.num_programs(1) - 1)
    def _():
        total = sum_ref[...].astype(BF16)
        grad_b_ref[...] += mm(total, c)
        part = dot(total, b, ((0,), (0,)))
        grad_c_ref[...] = part + so_far[1][...] if so_far else part


def state_kernel(
    rt_ref, g_ref, c_ref, s_ref, e_ref, q_ref, a_ref, d_part_ref, c_part_ref, *refs
):
    d_ref, grad_c_ref, held = refs[-3:]
    span, group = pl.program_id(0), pl.program_id(1)

    @pl.when(group == 0)
    def _():
        grad_c_ref[...] = c_part_ref[...]

    @pl.when(span == 0)
    def _():
        held[group] = s_ref[...]

    state = held[group]
    low = state.astype(BF16)
    scaled = g_ref[...].astype(F32) * jnp.exp2(spread_columns(rt_ref[0]))
    ends = dot(one_hot(BF16), (scaled * mm(c_ref[...], low)).astype(BF16), ((1,), (1,)))
    grad_c_ref[...] += dot(scaled.astype(BF16), low, ((1,), (1,)))
    product = jnp.sum(q_ref[0].astype(F32) * state, axis=0, keepdims=True) * a_ref[0, :1]
    high, middle, last = thirds(product)
    row = iota((8, WIDE), 0)
    stacked = jnp.where(row == 0, high, jnp.where(row == 1, middle, jnp.where(row == 2, last, 0.0)))
    kept = dot(one_hot(BF16), stacked.astype(BF16), ((1,), (1,)))
    kept = jnp.sum(kept, axis=1, keepdims=True)
    d_ref[...] = d_part_ref[...] + sum_over(ends, not_before()) + kept
    held[group] = e_ref[0] + a_ref[0, :1] * state


def call(kernel, grid, in_specs, out_specs, out_shape, flops, size, scratch=()):
    return pl.pallas_call(
        kernel,
        grid=grid,
        in_specs=in_specs,
        out_specs=out_specs,
        out_shape=out_shape,
        scratch_shapes=list(scratch),
        cost_estimate=pl.CostEstimate(flops=flops, bytes_accessed=size, transcendentals=0),
        compiler_params=pltpu.CompilerParams(
            dimension_semantics=("arbitrary",) * len(grid), vmem_limit_bytes=GRANT
        ),
    )


def run_spec(at=0):
    return pl.BlockSpec((GROUP, SPAN), lambda k, h: (h + at, k))


def run_t_spec(at=0):
    return pl.BlockSpec((1, SPAN, GROUP), lambda k, h: (h + at, k, 0))


def rows_spec(at=0):
    return pl.BlockSpec((SPAN, WIDE), lambda k, h: (k, h + at))


def state_spec(at=0):
    return pl.BlockSpec((1, 2 * P_SIZE, WIDE), lambda k, h: (k, 0, h + at))


def kept_spec(at=0):
    return pl.BlockSpec((1, 8, WIDE), lambda k, h: (k, 0, h + at))


SHARED = pl.BlockSpec((SPAN, 2 * P_SIZE), lambda k, h: (k, 0))
GAIN = pl.BlockSpec((1, WIDE), lambda k, h: (0, h))
ANYWHERE = pl.BlockSpec(memory_space=pl.ANY)
INNER_SCRATCH = [
    pltpu.VMEM((SPAN, SPAN), F32),
    pltpu.VMEM((GROUP * HALF, SPAN), BF16),
    pltpu.VMEM((GROUP * HALF, HALF), BF16),
]
SCALARS = pl.BlockSpec(memory_space=pltpu.SMEM)


def shape(*dims, dtype=F32):
    return jax.ShapeDtypeStruct(dims, dtype)


def swap(value, axis, bit):
    count = lax.axis_size(axis)
    return lax.ppermute(value, axis, [(i, i ^ bit) for i in range(count)])


def block_products(kept):
    count = lax.axis_size("ctx")
    place = lax.axis_index("ctx")
    steps = []
    before_me = jnp.ones_like(kept)
    after_me = jnp.ones_like(kept)
    bit = 1
    while bit < count:
        other = swap(kept, "ctx", bit)
        upper = (place & bit) != 0
        steps.append((bit, upper, kept, other, before_me, after_me))
        before_me = jnp.where(upper, before_me * other, before_me)
        after_me = jnp.where(upper, after_me, after_me * other)
        kept = kept * other
        bit *= 2
    return steps


def scan_states(total, steps, reverse):
    entering = jnp.zeros_like(total)
    for bit, upper, kept, other, before_me, after_me in steps:
        got = swap(total.astype(BF16), "ctx", bit).astype(F32)
        if reverse:
            entering = entering + jnp.where(upper, 0.0, after_me) * got
            total = jnp.where(upper, got + other * total, total + kept * got)
        else:
            entering = entering + jnp.where(upper, before_me, 0.0) * got
            total = jnp.where(upper, kept * got + total, other * total + got)
    return entering


def head_sum(value):
    bit = 1
    while bit < lax.axis_size("head"):
        value = value.astype(BF16)
        value = value.astype(F32) + swap(value, "head", bit).astype(F32)
        bit *= 2
    return value


PLANE = 4


def after(values, *tokens):
    out = pl.pallas_call(
        after_kernel,
        in_specs=[ANYWHERE] * (len(values) + len(tokens)),
        out_specs=[ANYWHERE] * len(values),
        out_shape=[shape(*value.shape, dtype=value.dtype) for value in values],
        input_output_aliases={index: index for index in range(len(values))},
        cost_estimate=pl.CostEstimate(flops=0, bytes_accessed=0, transcendentals=0),
        compiler_params=pltpu.CompilerParams(vmem_limit_bytes=GRANT),
    )(*values, *tokens)
    return list(out)


def along_z(value, moves):
    pairs = [(a * PLANE + i, b * PLANE + i) for a, b in moves for i in range(PLANE)]
    return lax.ppermute(value, "ctx", pairs)


MIDDLE = ((1, 2), (2, 1))
OUTWARD = ((1, 0), (2, 3))


def swap_x(value):
    return swap(value, "ctx", 1)


def swap_y(value):
    return swap(value, "ctx", 2)


LAYERS = ((0, 1, 2, 3), (1, 0, 3, 2), (2, 2, 1, 1), (3, 3, 0, 0))
EARLY = [(k, flip) for k in (0, 1, 2) for flip in range(3)]
LATE = [(0, 3), (1, 3), (2, 3), (3, 0), (3, 1), (3, 2), (3, 3)]


def block_order():
    place = lax.axis_index("ctx")
    layer, spot = place // PLANE, place % PLANE
    layers = jnp.array(LAYERS, jnp.int32)[:, layer]
    order = [layers[k] * PLANE + (spot ^ flip) for k, flip in EARLY + LATE]
    return jnp.stack(order).astype(jnp.int32)


def gather_weight(w, sizes):
    ends = [sum(sizes[: j + 1]) * P_SIZE for j in range(len(sizes))]
    parts = [w[:, end - size * P_SIZE : end] for end, size in zip(ends, sizes)]
    return [lax.all_gather(part, "ctx", axis=0, tiled=True) for part in parts]


def forward(features, first, weight, running_t, b_rows, here):
    own, other = features
    length = own.shape[0]
    n = b_rows.shape[1]
    width, wide = weight.shape
    deep = width // 4
    spans = length // SPAN

    def depth(k, first_ref):
        return (k // 2 ^ first_ref[0]) * 2 + k % 2

    return pl.pallas_call(
        forward_kernel,
        grid_spec=pltpu.PrefetchScalarGridSpec(
            num_scalar_prefetch=1,
            grid=(wide // WIDE, 4),
            in_specs=[
                pl.BlockSpec((length, deep), lambda h, k, first_ref: (0, jnp.minimum(k, 1))),
                pl.BlockSpec((length, deep), lambda h, k, first_ref: (0, jnp.maximum(k - 2, 0))),
                pl.BlockSpec((deep, WIDE), lambda h, k, first_ref: (depth(k, first_ref), h)),
                pl.BlockSpec((1, length, GROUP), lambda h, k, first_ref: (h + here, 0, 0)),
                pl.BlockSpec((length, n), lambda h, k, first_ref: (0, 0)),
            ],
            out_specs=[
                pl.BlockSpec((length, WIDE), lambda h, k, first_ref: (0, h)),
                pl.BlockSpec((spans, n, WIDE), lambda h, k, first_ref: (0, 0, h)),
            ],
            scratch_shapes=[pltpu.VMEM((length, WIDE), F32)],
        ),
        out_shape=[shape(length, wide, dtype=BF16), shape(spans, n, wide)],
        cost_estimate=pl.CostEstimate(
            flops=2 * length * wide * width, bytes_accessed=2 * wide * width, transcendentals=0
        ),
        compiler_params=pltpu.CompilerParams(
            dimension_semantics=("arbitrary", "arbitrary"), vmem_limit_bytes=GRANT
        ),
    )(first, own, other, weight, running_t, b_rows)


def multiply(grad_x, weight, at, half, halves, before=None, other=None):
    length = grad_x.shape[0]
    width, wide = weight.shape
    tiles = width // halves // WIDE
    tile = pl.BlockSpec((length, WIDE), lambda j, half_ref: (0, half_ref[0] * tiles + j))
    plain = pl.BlockSpec((length, WIDE), lambda j, half_ref: (0, j))
    in_specs = [
        pl.BlockSpec((length, wide), lambda j, half_ref: (0, at)),
        pl.BlockSpec((WIDE, wide), lambda j, half_ref: (half_ref[0] * tiles + j, 0)),
    ]
    operands = [grad_x, weight]
    if before is not None:
        in_specs.append(tile)
        operands.append(before)
    if other is not None:
        in_specs.append(plain)
        operands.append(other)
    return pl.pallas_call(
        functools.partial(product_kernel, before is not None, other is not None),
        grid_spec=pltpu.PrefetchScalarGridSpec(
            num_scalar_prefetch=1,
            grid=(tiles,),
            in_specs=in_specs,
            out_specs=plain,
        ),
        out_shape=shape(length, width // halves, dtype=BF16),
        cost_estimate=pl.CostEstimate(
            flops=2 * length * wide * width // halves,
            bytes_accessed=2 * wide * width // halves,
            transcendentals=0,
        ),
        compiler_params=pltpu.CompilerParams(
            dimension_semantics=("arbitrary",), vmem_limit_bytes=GRANT
        ),
    )(half, *operands)


def early_forward(features, pieces):
    length = features.shape[0]
    rows, columns = pieces[0].shape
    deep = rows * len(pieces)
    return call(
        functools.partial(early_forward_kernel, len(pieces)),
        (columns // WIDE,),
        [pl.BlockSpec((length, deep), lambda h: (0, 0))]
        + [pl.BlockSpec((rows, WIDE), lambda h: (0, h))] * len(pieces),
        pl.BlockSpec((length, WIDE), lambda h: (0, h)),
        shape(length, columns),
        2 * length * columns * deep,
        2 * columns * deep,
        [pltpu.VMEM((deep, WIDE), BF16)],
    )(features, *pieces)


def late_forward(features, part, pieces, running_t, b_rows, kept, here):
    length = features.shape[0]
    rows, columns = pieces[0].shape
    deep = rows * len(pieces)
    n = b_rows.shape[1]
    spans = length // SPAN
    state = pl.BlockSpec((n, WIDE), lambda h: (0, h))
    return call(
        functools.partial(late_forward_kernel, len(pieces)),
        (columns // WIDE,),
        [
            pl.BlockSpec((length, deep), lambda h: (0, 0)),
            pl.BlockSpec((length, WIDE), lambda h: (0, h + here)),
            pl.BlockSpec((1, length, GROUP), lambda h: (h + here, 0, 0)),
            pl.BlockSpec((length, n), lambda h: (0, 0)),
            pl.BlockSpec((spans, 8, WIDE), lambda h: (0, 0, h + here)),
        ]
        + [pl.BlockSpec((rows, WIDE), lambda h: (0, h))] * len(pieces),
        [
            pl.BlockSpec((length, WIDE), lambda h: (0, h)),
            pl.BlockSpec((spans, n, WIDE), lambda h: (0, 0, h)),
            state,
            state,
        ],
        [
            shape(length, columns, dtype=BF16),
            shape(spans, n, columns),
            shape(n, columns),
            shape(n, columns, dtype=BF16),
        ],
        2 * length * columns * deep,
        2 * columns * deep,
        [pltpu.VMEM((deep, WIDE), BF16)],
    )(features, part, running_t, b_rows, kept, *pieces)


def multiply_blocks(order, grad_x, pieces, so_far):
    columns, length = grad_x.shape
    arrays = [array for piece in pieces for array in piece]
    rows = arrays[0].shape[0]
    count = len(pieces)
    half = shape(length, lax.axis_size("ctx") * rows // 2, dtype=BF16)
    first = 2 + len(arrays)
    return pl.pallas_call(
        functools.partial(blocks_kernel, [len(piece) for piece in pieces], bool(so_far)),
        grid=(1,),
        in_specs=[SCALARS, pl.BlockSpec((columns, length), lambda h: (0, 0))]
        + [ANYWHERE] * (len(arrays) + len(so_far)),
        out_specs=[ANYWHERE, ANYWHERE],
        out_shape=[half, half],
        input_output_aliases={first + k: k for k in range(len(so_far))},
        scratch_shapes=[
            pltpu.VMEM((rows * count, columns), BF16),
            pltpu.VMEM((count, length, rows), BF16),
            pltpu.SemaphoreType.DMA((len(arrays),)),
            pltpu.SemaphoreType.DMA((count,)),
        ],
        cost_estimate=pl.CostEstimate(
            flops=2 * length * columns * rows * count,
            bytes_accessed=2 * columns * rows * count,
            transcendentals=0,
        ),
        compiler_params=pltpu.CompilerParams(
            dimension_semantics=("arbitrary",), vmem_limit_bytes=GRANT
        ),
    )(order, grad_x, *arrays, *so_far)


def back_start(own_grads, kept):
    spans, n, columns = own_grads.shape
    return call(
        start_kernel,
        (columns // WIDE,),
        [
            pl.BlockSpec((spans, n, WIDE), lambda h: (0, 0, h)),
            pl.BlockSpec((spans, 8, WIDE), lambda h: (0, 0, h)),
        ],
        [pl.BlockSpec((rows, WIDE), lambda h: (0, h)) for rows in (n, 8, n + TAIL)],
        [shape(n, columns), shape(8, columns), shape(n + TAIL, columns, dtype=BF16)],
        0,
        14 * n * columns,
    )(own_grads, kept)


def back_step(place, log, total, sent, entering, bit):
    got = swap(sent, "ctx", bit)
    n, columns = total.shape
    tall = [pl.BlockSpec((rows, WIDE), lambda h: (0, h)) for rows in (8, n, n + TAIL)]
    return call(
        functools.partial(back_kernel, bit),
        (columns // WIDE,),
        [SCALARS] + tall + [tall[1]] * len(entering),
        [tall[1], tall[1], tall[2], tall[0], tall[0]],
        [
            shape(n, columns),
            shape(n, columns),
            shape(n + TAIL, columns, dtype=BF16),
            shape(8, columns),
            shape(8, columns),
        ],
        0,
        18 * n * columns,
    )(place, log, total, got, *entering)


def scan_step(factors, here, total, sent, entering, bit, last=False):
    got = swap(sent, "ctx", bit)
    n, columns = total.shape
    block = pl.BlockSpec((n, WIDE), lambda h: (0, h))
    outs = [shape(n, columns), shape(n, columns), shape(n, columns, dtype=BF16)]
    outs = outs[:1] if last else outs
    out = call(
        scan_kernel,
        (columns // WIDE,),
        [pl.BlockSpec((8, WIDE), lambda h: (0, h + here)), block, block] + [block] * len(entering),
        [block] * len(outs),
        outs,
        0,
        14 * n * columns,
    )(factors, total, got, *entering)
    return out if last else (out[1], out[0], out[2])


def local(inputs, w_in, b_rows, c_rows, log_decay, skip_gain, grad_out):
    groups = log_decay.shape[0] // GROUP
    layered = lax.axis_size("ctx") == 4 * PLANE and lax.axis_size("head") == 2
    if layered and groups % 2 == 0 and w_in.shape[0] == 256:
        return local_layered(inputs, w_in, b_rows, c_rows, log_decay, skip_gain, grad_out)
    return local_plain(inputs, w_in, b_rows, c_rows, log_decay, skip_gain, grad_out)


def prepare(log_decay, grad_out, c_rows):
    length, columns = grad_out.shape
    heads = log_decay.shape[0]
    spans = length // SPAN
    groups = heads // GROUP
    n = c_rows.shape[1]
    return call(
        decay_kernel,
        (spans, groups),
        [run_spec(), rows_spec(), SHARED],
        [run_spec(), run_t_spec(), kept_spec(), state_spec()],
        [
            shape(heads, length),
            shape(groups, length, GROUP),
            shape(spans, 8, columns),
            shape(spans, n, columns),
        ],
        2 * length * columns * n,
        6 * length * columns,
    )(log_decay, grad_out, c_rows)


def inner(grid, here, wide, operands, so_far):
    length = operands[2].shape[0]
    n = operands[4].shape[1]
    specs = [
        run_spec(here),
        run_t_spec(here),
        rows_spec(here),
        rows_spec(),
        SHARED,
        SHARED,
        state_spec(here),
    ]
    return call(
        inner_kernel,
        grid,
        specs + [SHARED] * len(so_far),
        [run_spec(), SHARED, SHARED],
        [shape(wide // P_SIZE, length), shape(length, n), shape(length, n)],
        12 * length * wide * SPAN,
        6 * length * wide,
        INNER_SCRATCH,
    )(*operands, *so_far)


def state_terms(grid, here, wide, operands, heads=None, so_far=None):
    length = operands[1].shape[0]
    n = operands[2].shape[1]
    heads = heads or wide // P_SIZE
    at = here if heads > wide // P_SIZE else 0
    extra = () if so_far is None else (so_far,)
    return pl.pallas_call(
        state_kernel,
        grid=grid,
        in_specs=[
            run_t_spec(here),
            rows_spec(here),
            SHARED,
            pl.BlockSpec((n, WIDE), lambda k, h: (0, h)),
            state_spec(),
            state_spec(here),
            kept_spec(here),
            run_spec(),
            SHARED,
        ]
        + [ANYWHERE] * len(extra),
        out_specs=[run_spec(at), SHARED],
        out_shape=[shape(heads, length), shape(length, n)],
        scratch_shapes=[pltpu.VMEM((grid[1], n, WIDE), F32)],
        input_output_aliases={len(operands): 0} if extra else {},
        cost_estimate=pl.CostEstimate(
            flops=4 * length * wide * n, bytes_accessed=6 * length * wide, transcendentals=0
        ),
        compiler_params=pltpu.CompilerParams(
            dimension_semantics=("arbitrary", "arbitrary"), vmem_limit_bytes=GRANT
        ),
    )(*operands, *extra)


def local_layered(inputs, w_in, b_rows, c_rows, log_decay, skip_gain, grad_out):
    length, columns = grad_out.shape
    heads = log_decay.shape[0]
    spans = length // SPAN
    groups = heads // GROUP
    place = lax.axis_index("head").astype(jnp.int32)
    half = columns // 2
    order = block_order()
    blocks = order.shape[0]
    width = blocks * w_in.shape[0]

    z1, inner2 = swap(w_in, "ctx", PLANE), along_z(w_in, MIDDLE)
    own_x, own_y = swap_x(w_in), swap_y(w_in)
    other = swap(inputs, "head", 1)
    running, running_t, kept, own_grads = prepare(log_decay, grad_out, c_rows)
    spot = lax.axis_index("ctx").astype(jnp.int32)[None]
    back, log, sent = back_start(own_grads, kept)
    sent = after([sent], other)[0]
    back, leaving, sent, log, factors_1 = back_step(spot, log, back, sent, (), 1)

    z1, inner2, own_y, sent = after([z1, inner2, own_y, sent], own_x)
    x1, y1 = swap_x(z1), swap_y(z1)
    inner3, outer2 = along_z(z1, MIDDLE), along_z(inner2, OUTWARD)
    own_y_a, own_y_b = own_y[:, :half], own_y[:, half:]
    back, leaving, sent, log, factors_2 = back_step(spot, log, back, sent, (leaving,), 2)
    order_own = (order + place * (blocks // 2)) % blocks
    cut = len(EARLY) * w_in.shape[0]
    early_features, late_features = call(
        arrange_kernel,
        (1,),
        [SCALARS] + [pl.BlockSpec((length, width // 2), lambda h: (0, 0))] * 2,
        [pl.BlockSpec((length, wide), lambda h: (0, 0)) for wide in (cut, width - cut)],
        [shape(length, wide, dtype=BF16) for wide in (cut, width - cut)],
        0,
        4 * length * width,
        [pltpu.VMEM((length, width), BF16)],
    )(order_own, inputs, other)

    inner2, inner3, outer2, x1, sent, own_y_a, own_y_b = after(
        [inner2, inner3, outer2, x1, sent, own_y_a, own_y_b], y1, early_features
    )
    z3 = inner2 + outer2
    x3, y3 = swap_x(z3), swap_y(z3)
    outer3 = along_z(inner3, OUTWARD)
    x1_a, x1_b = x1[:, :half], x1[:, half:]
    back, leaving, sent, log, factors_4 = back_step(spot, log, back, sent, (leaving,), 4)

    inner3, outer3, y3, x1_a, x1_b, sent = after([inner3, outer3, y3, x1_a, x1_b, sent], x3)
    z2a = inner3[:, :half] + outer3[:, :half]
    z2b = inner3[:, half:] + outer3[:, half:]
    y3_a, y3_b = y3[:, :half], y3[:, half:]
    x2a, y2a = swap_x(z2a), swap_y(z2a)
    d3a, d1a = swap_x(y3_a), swap_y(x1_a)
    back, leaving, sent, log, factors_8 = back_step(spot, log, back, sent, (leaving,), 8)
    early = [w_in, own_x, own_y, z1, x1, y1, z3, x3, y3]
    part = early_forward(early_features, early)

    own_y_a, x2a, z2b, y3_b, x1_b, leaving = after(
        [own_y_a, x2a, z2b, y3_b, x1_b, leaving], y2a, d3a, d1a, part
    )
    d0a, d2a = swap_x(own_y_a), swap_y(x2a)
    x2b, y2b = swap_x(z2b), swap_y(z2b)
    d3b, d1b = swap_x(y3_b), swap_y(x1_b)
    leaving_all = [leaving]
    for k in range(spans - 1, 0, -1):
        leaving_all.insert(0, own_grads[k] + kept[k, :1] * leaving_all[0])
    leaving_all = jnp.stack([value.astype(BF16) for value in leaving_all])
    skip = jnp.repeat(skip_gain, P_SIZE)[None]
    grad_x = grad_rows(running, running_t, grad_out, b_rows, c_rows, leaving_all, skip, True)
    order_away = (order + (1 - place) * (blocks // 2)) % blocks
    early_order, late_order = order_away[: len(EARLY)], order_away[len(EARLY) :]
    product = multiply_blocks(early_order, grad_x, [[piece] for piece in early], ())
    late_a = [d0a, d1a, d3a, z2a, x2a, y2a, d2a]
    x_a, states_a, total_a, sent_a = late_forward(
        late_features, part, late_a, running_t, b_rows, kept, 0
    )

    own_y_b, x2b, sent_a, x_a = after(
        [own_y_b, x2b, sent_a, x_a], y2b, d3b, d1b, product[0]
    )
    d0b, d2b = swap_x(own_y_b), swap_y(x2b)
    total_a, entering_a, sent_a = scan_step(factors_1, 0, total_a, sent_a, (), 1)
    shared = (running, running_t, grad_out)
    here = groups // 2
    grid = (spans, here)
    inner_a = shared + (x_a, b_rows, c_rows, leaving_all)
    decay_a, grad_b, grad_c = inner(grid, 0, half, inner_a, ())

    d0b, d2b = after([d0b, d2b], sent_a, grad_b)
    late_b = [d0b, d1b, d3b, z2b, x2b, y2b, d2b]
    x_b, states_b, total_b, sent_b = late_forward(
        late_features, part, late_b, running_t, b_rows, kept, here
    )
    pairs = list(zip(late_a, late_b))
    sent_a, sent_b, *product = after([sent_a, sent_b, *product])
    total_b, entering_b, sent_b = scan_step(factors_1, here, total_b, sent_b, (), 1)
    total_a, entering_a, sent_a = scan_step(factors_2, 0, total_a, sent_a, (entering_a,), 2)
    away, own = multiply_blocks(late_order, grad_x, pairs, product)

    sent_a, sent_b, x_b, away = after([sent_a, sent_b, x_b, away])
    total_b, entering_b, sent_b = scan_step(factors_2, here, total_b, sent_b, (entering_b,), 2)
    total_a, entering_a, sent_a = scan_step(factors_4, 0, total_a, sent_a, (entering_a,), 4)
    got = swap(away, "head", 1)
    inner_b = shared + (x_b, b_rows, c_rows, leaving_all)
    decay_b, grad_b, grad_c = inner(grid, here, half, inner_b, (grad_b, grad_c))

    sent_a, sent_b, got, grad_b = after([sent_a, sent_b, got, grad_b])
    total_b, entering_b, sent_b = scan_step(factors_4, here, total_b, sent_b, (entering_b,), 4)
    (entering_a,) = scan_step(factors_8, 0, total_a, sent_a, (entering_a,), 8, True)
    grad_inputs = (own.astype(F32) + got.astype(F32)).astype(BF16)
    grad_b = head_sum(grad_b)

    sent_b, entering_a = after([sent_b, entering_a], grad_inputs, grad_b)
    (entering_b,) = scan_step(factors_8, here, total_b, sent_b, (entering_b,), 8, True)
    common = (running_t, grad_out, c_rows)
    state_a = common + (entering_a, states_a, leaving_all, kept, decay_a, grad_c)
    decays, grad_c = state_terms(grid, 0, half, state_a, heads)
    state_b = common + (entering_b, states_b, leaving_all, kept, decay_b, grad_c)
    decays, grad_c = state_terms(grid, here, half, state_b, heads, decays)
    return (grad_inputs, grad_b, head_sum(grad_c), decays)


def grad_rows(running, running_t, grad_out, b_rows, c_rows, leaving, skip, transposed):
    length, columns = grad_out.shape
    spec, dims = rows_spec(), (length, columns)
    if transposed:
        spec, dims = pl.BlockSpec((WIDE, SPAN), lambda k, h: (h, k)), (columns, length)
    return call(
        functools.partial(grad_x_kernel, transposed),
        (length // SPAN, running_t.shape[0]),
        [run_spec(), run_t_spec(), rows_spec(), SHARED, SHARED, state_spec(), GAIN],
        spec,
        shape(*dims, dtype=BF16),
        8 * length * columns * SPAN,
        6 * length * columns,
    )(running, running_t, grad_out, b_rows, c_rows, leaving, skip)


def local_plain(inputs, w_in, b_rows, c_rows, log_decay, skip_gain, grad_out):
    length, columns = grad_out.shape
    heads = log_decay.shape[0]
    spans = length // SPAN
    groups = heads // GROUP
    n = b_rows.shape[1]
    grid = (spans, groups)

    sizes = (heads // 2, heads // 4, heads // 4) if heads % (4 * GROUP) == 0 else (heads,)
    weights = gather_weight(w_in, sizes)
    two = lax.axis_size("head") == 2
    place = lax.axis_index("head").astype(jnp.int32)[None]
    width = weights[0].shape[0]
    if two:
        features = (inputs, swap(inputs, "head", 1))
        first = place
    else:
        features = lax.all_gather(inputs, "head", axis=1, tiled=True)
        features = (features[:, : width // 2], features[:, width // 2 :])
        first = jnp.zeros((1,), jnp.int32)

    running, running_t, kept, own_grads = call(
        decay_kernel,
        grid,
        [run_spec(), rows_spec(), SHARED],
        [run_spec(), run_t_spec(), kept_spec(), state_spec()],
        [
            shape(heads, length),
            shape(groups, length, GROUP),
            shape(spans, 8, columns),
            shape(spans, n, columns),
        ],
        2 * length * columns * n,
        6 * length * columns,
    )(log_decay, grad_out, c_rows)

    kept_total = kept[0, :1]
    for k in range(1, spans):
        kept_total = kept_total * kept[k, :1]
    steps = block_products(kept_total)

    total = own_grads[spans - 1]
    for k in range(spans - 2, -1, -1):
        total = own_grads[k] + kept[k, :1] * total
    leaving = [scan_states(total, steps, True)]
    for k in range(spans - 1, 0, -1):
        leaving.insert(0, own_grads[k] + kept[k, :1] * leaving[0])
    leaving = jnp.stack([value.astype(BF16) for value in leaving])

    skip = jnp.repeat(skip_gain, P_SIZE)[None]
    grad_x = grad_rows(running, running_t, grad_out, b_rows, c_rows, leaving, skip, False)

    grad_b = grad_c = product = None
    tokens = ()
    decay_parts = []
    at = 0
    for index, size in enumerate(sizes):
        wide = size * P_SIZE
        here = at // GROUP
        count = size // GROUP
        weight = weights[index]
        if tokens:
            weight = after([weight], *tokens)[0]
        x, own_states = forward(features, first, weight, running_t, b_rows, here)

        chunk = slice(at * P_SIZE, at * P_SIZE + wide)
        total = own_states[0]
        for k in range(1, spans):
            total = kept[k, :1, chunk] * total + own_states[k]
        cut = [step[:2] + tuple(value[:, chunk] for value in step[2:]) for step in steps]
        entering = scan_states(total, cut, False)

        so_far = () if grad_b is None else (grad_b, grad_c)
        decay_part, grad_b, grad_c = call(
            inner_kernel,
            (spans, count),
            [
                run_spec(here),
                run_t_spec(here),
                rows_spec(here),
                rows_spec(),
                SHARED,
                SHARED,
                state_spec(here),
            ]
            + [SHARED] * len(so_far),
            [run_spec(), SHARED, SHARED],
            [shape(size, length), shape(length, n), shape(length, n)],
            12 * length * wide * SPAN,
            6 * length * wide,
            INNER_SCRATCH,
        )(running, running_t, grad_out, x, b_rows, c_rows, leaving, *so_far)
        decay_part, grad_c = call(
            state_kernel,
            (spans, count),
            [
                run_t_spec(here),
                rows_spec(here),
                SHARED,
                pl.BlockSpec((n, WIDE), lambda k, h: (0, h)),
                state_spec(),
                state_spec(here),
                kept_spec(here),
                run_spec(),
                SHARED,
            ],
            [run_spec(), SHARED],
            [shape(size, length), shape(length, n)],
            4 * length * wide * n,
            6 * length * wide,
            [pltpu.VMEM((count, n, WIDE), F32)],
        )(running_t, grad_out, c_rows, entering, own_states, leaving, kept, decay_part, grad_c)
        decay_parts.append(decay_part)

        if index < len(sizes) - 1:
            zero = jnp.zeros((1,), jnp.int32)
            product = multiply(grad_x, weight, at // size, zero, 1, product)
            tokens = (product, grad_b, entering)
        elif two:
            sent = multiply(grad_x, weight, at // size, 1 - place, 2, product)
            got = swap(sent, "head", 1)
            grad_inputs = multiply(grad_x, weight, at // size, place, 2, product, got)
        else:
            zero = jnp.zeros((1,), jnp.int32)
            product = multiply(grad_x, weight, at // size, zero, 1, product)
            grad_inputs = lax.psum_scatter(product, "head", scatter_dimension=1, tiled=True)
        at += size

    return (grad_inputs, head_sum(grad_b), head_sum(grad_c), jnp.concatenate(decay_parts, axis=0))


def solution(mesh):
    in_specs = (
        P("ctx", "head"),
        P("ctx", "head"),
        P("ctx", None),
        P("ctx", None),
        P("head", "ctx"),
        P("head"),
        P("ctx", "head"),
    )
    out_specs = (P("ctx", "head"), P("ctx", None), P("ctx", None), P("head", "ctx"))
    return jax.shard_map(local, mesh=mesh, in_specs=in_specs, out_specs=out_specs, check_vma=False)
```

```python
import functools

import jax
import jax.numpy as jnp
from jax import lax
from jax.experimental import pallas as pl
from jax.experimental.pallas import tpu as pltpu
from jax.sharding import PartitionSpec as P

SPAN = 256
HALF = SPAN // 2
P_SIZE = 64
GROUP = 8
WIDE = GROUP * P_SIZE
LOG2E = 1.4426950408889634
NEVER = -1e30
GRANT = 64 * 2**20

F32 = jnp.float32
BF16 = jnp.bfloat16
EXACT = lax.Precision.HIGHEST


def dot(a, b, dims, precision=None):
    return lax.dot_general(a, b, (dims, ((), ())), precision=precision, preferred_element_type=F32)


def mm(a, b, precision=None):
    return dot(a, b, ((1,), (0,)), precision)


def iota(shape, dim):
    return lax.broadcasted_iota(jnp.int32, shape, dim)


def one_hot(dtype):
    return (iota((GROUP, WIDE), 0) == iota((GROUP, WIDE), 1) // P_SIZE).astype(dtype)


def not_before():
    return (iota((SPAN, SPAN), 0) >= iota((SPAN, SPAN), 1)).astype(F32)


def before():
    return (iota((SPAN, SPAN), 0) < iota((SPAN, SPAN), 1)).astype(F32)


def same():
    return (iota((SPAN, SPAN), 0) == iota((SPAN, SPAN), 1)).astype(F32)


def first_head():
    return iota((SPAN, 2 * P_SIZE), 1) < P_SIZE


def pair_columns(columns, pair):
    shape = (columns.shape[0], 2 * P_SIZE)
    left = jnp.broadcast_to(columns[:, 2 * pair : 2 * pair + 1], shape)
    right = jnp.broadcast_to(columns[:, 2 * pair + 1 : 2 * pair + 2], shape)
    return jnp.where(iota(shape, 1) < P_SIZE, left, right)


def spread_columns(columns):
    return jnp.concatenate([pair_columns(columns, pair) for pair in range(GROUP // 2)], axis=1)


def thirds(value):
    high = value.astype(BF16).astype(F32)
    middle = (value - high).astype(BF16).astype(F32)
    return high, middle, value - high - middle


def sum_over(value, mask):
    rows = value.shape[0]
    parts = mm(jnp.concatenate(thirds(value), axis=0).astype(BF16), mask.astype(BF16))
    return parts[:rows] + parts[rows : 2 * rows] + parts[2 * rows :]


def decay_kernel(d_ref, g_ref, c_ref, r_ref, rt_ref, a_ref, gt_ref):
    row_sums = sum_over(d_ref[...] * LOG2E, 1.0 - not_before() + same())
    r_ref[...] = row_sums
    padded = jnp.concatenate([row_sums, jnp.zeros((2 * P_SIZE - GROUP, SPAN), F32)], axis=0)
    running = padded.T[:, :GROUP]
    rt_ref[0] = running
    growth = jnp.exp2(spread_columns(running))
    last = spread_columns(running[SPAN - 1 : SPAN])
    a_ref[0] = jnp.where(iota((8, WIDE), 0) < 4, jnp.exp2(last), last)
    scaled = (g_ref[...].astype(F32) * growth).astype(BF16)
    gt_ref[0] = dot(c_ref[...], scaled, ((0,), (0,)))


def grad_x_kernel(transposed, r_ref, rt_ref, g_ref, b_ref, c_ref, q_ref, skip_ref, out_ref):
    b = b_ref[...]
    scores = dot(b, c_ref[...], ((1,), (1,)))
    running = r_ref[...]
    columns = rt_ref[0]
    top_keep = iota((HALF, SPAN), 1) >= iota((HALF, SPAN), 0)
    low_keep = iota((HALF, HALF), 1) >= iota((HALF, HALF), 0)
    to_end = jnp.exp2(spread_columns(columns[SPAN - 1 : SPAN] - columns))
    from_state = mm(b, q_ref[0]) * to_end
    for pair in range(GROUP // 2):
        lanes = slice(pair * 2 * P_SIZE, (pair + 1) * 2 * P_SIZE)
        g = g_ref[:, lanes]
        parts = []
        for head in (2 * pair, 2 * pair + 1):
            row = running[head : head + 1]
            top = jnp.where(top_keep, row - columns[:HALF, head : head + 1], NEVER)
            low = jnp.where(low_keep, row[:, HALF:] - columns[HALF:, head : head + 1], NEVER)
            parts.append((jnp.exp2(top) * scores[:HALF]).astype(BF16))
            low = (jnp.exp2(low) * scores[HALF:, HALF:]).astype(BF16)
            parts.append(jnp.concatenate([jnp.zeros((HALF, HALF), BF16), low], axis=1))
        product = mm(jnp.concatenate(parts, axis=0), g)
        parts = [product[:SPAN], product[SPAN:]]
        inner = jnp.where(first_head(), parts[0], parts[1])
        total = inner + skip_ref[:, lanes] * g.astype(F32) + from_state[:, lanes]
        if transposed:
            out_ref[lanes, :] = total.T.astype(BF16)
        else:
            out_ref[:, lanes] = total.astype(BF16)


def forward_kernel(half_ref, own_ref, other_ref, w_ref, rt_ref, b_ref, x_ref, e_ref, total_ref):
    step = pl.program_id(1)

    @pl.when(step == 0)
    def _():
        total_ref[...] = jnp.zeros_like(total_ref)

    half = pl.num_programs(1) // 2

    @pl.when(step < half)
    def _():
        total_ref[...] += mm(own_ref[...], w_ref[...])

    @pl.when(step >= half)
    def _():
        total_ref[...] += mm(other_ref[...], w_ref[...])

    @pl.when(step == pl.num_programs(1) - 1)
    def _():
        x = total_ref[...].astype(BF16)
        x_ref[...] = x
        for k in range(e_ref.shape[0]):
            rows = slice(k * SPAN, (k + 1) * SPAN)
            columns = rt_ref[0, rows]
            to_end = jnp.exp2(spread_columns(columns[SPAN - 1 : SPAN] - columns))
            scaled = (x[rows].astype(F32) * to_end).astype(BF16)
            e_ref[k] = dot(b_ref[rows], scaled, ((0,), (0,)))


def product_kernel(has_before, has_other, half_ref, g_ref, w_ref, *refs):
    refs = list(refs)
    total = dot(g_ref[...], w_ref[...], ((1,), (1,)))
    if has_before:
        total = total + refs.pop(0)[...].astype(F32)
    if has_other:
        total = total.astype(BF16).astype(F32) + refs.pop(0)[...].astype(F32)
    refs[0][...] = total.astype(BF16)


def arrange_kernel(order_ref, own_ref, other_ref, early_ref, late_ref, both_ref):
    half = own_ref.shape[1]
    both_ref[:, :half] = own_ref[...]
    both_ref[:, half:] = other_ref[...]
    unit = 2 * half // order_ref.shape[0]
    cut = early_ref.shape[1]
    for index in range(order_ref.shape[0]):
        source = pl.ds(pl.multiple_of(order_ref[index] * unit, 128), unit)
        at = index * unit
        if at < cut:
            early_ref[:, at : at + unit] = both_ref[:, source]
        else:
            late_ref[:, at - cut : at - cut + unit] = both_ref[:, source]


TAIL = 16


def message(total, log):
    high, middle, last = thirds(log)
    line = iota((TAIL, total.shape[1]), 0)
    tail = jnp.where(line == 0, high, jnp.where(line == 1, middle, jnp.where(line == 2, last, 0.0)))
    return total.astype(BF16), tail.astype(BF16)


def start_kernel(own_ref, kept_ref, log_ref, sent_ref):
    spans = own_ref.shape[0]
    total = own_ref[spans - 1]
    log = kept_ref[spans - 1, 4:5]
    for k in range(spans - 2, -1, -1):
        total = own_ref[k] + kept_ref[k, :1] * total
        log = log + kept_ref[k, 4:5]
    line = iota(log_ref.shape, 0)
    log_ref[...] = jnp.where(line == 0, log, 0.0)
    n = total.shape[0]
    sent_ref[:n], sent_ref[n:] = message(total, log)


def back_kernel(bit, place_ref, log_ref, mine_ref, got_ref, *refs):
    entering_ref = refs[0] if len(refs) == 5 else None
    entering_out, sent_out, log_out, factor_out = refs[-4:]
    n = entering_out.shape[0]
    got = got_ref[:n].astype(F32)
    tail = got_ref[n:].astype(F32)
    other_log = tail[0:1] + tail[1:2] + tail[2:3]
    log, before_me, after_me = log_ref[0:1], log_ref[1:2], log_ref[2:3]
    line = iota(log_ref.shape, 0)
    upper = (place_ref[0] // bit % 2 + 0 * line[0:1]) == 1
    kept, other = jnp.exp2(log), jnp.exp2(other_log)
    mine = mine_ref[:n].astype(F32)
    total = jnp.where(upper, other, 1.0) * mine + jnp.where(upper, 1.0, kept) * got
    passed = jnp.where(upper, 0.0, jnp.exp2(after_me)) * got
    entering_out[...] = passed if entering_ref is None else entering_ref[...] + passed
    first = jnp.where(upper, 1.0, other)
    second = jnp.where(upper, kept, 1.0)
    third = jnp.where(upper, jnp.exp2(before_me), 0.0)
    factor_out[...] = jnp.where(line == 0, first, jnp.where(line == 1, second, third))
    log = log + other_log
    before_me = jnp.where(upper, before_me + other_log, before_me)
    after_me = jnp.where(upper, after_me, after_me + other_log)
    log_out[...] = jnp.where(line == 0, log, jnp.where(line == 1, before_me, after_me))
    sent_out[:n], sent_out[n:] = message(total, log)


def scan_kernel(last, factor_ref, mine_ref, got_ref, *refs):
    refs = list(refs)
    entering_ref = refs.pop(0) if len(refs) == 3 - last else None
    factors = factor_ref[...]
    got = got_ref[...].astype(F32)
    if not last:
        total = factors[0:1] * mine_ref[...].astype(F32) + factors[1:2] * got
        refs[1][...] = total.astype(BF16)
    passed = factors[2:3] * got
    refs[0][...] = passed if entering_ref is None else entering_ref[...] + passed


def early_forward_kernel(count, f_ref, *refs):
    pieces, (out_ref, buffer) = refs[:count], refs[count:]
    rows = pieces[0].shape[0]
    for index, piece in enumerate(pieces):
        buffer[index * rows : (index + 1) * rows] = piece[...]
    out_ref[...] = mm(f_ref[...], buffer[...])


def late_forward_kernel(count, f_ref, part_ref, rt_ref, b_ref, kept_ref, *refs):
    pieces, (x_ref, e_ref, sent_ref, buffer) = refs[:count], refs[count:]
    rows = pieces[0].shape[0]
    for index, piece in enumerate(pieces):
        buffer[index * rows : (index + 1) * rows] = piece[...]
    x = (part_ref[...] + mm(f_ref[...], buffer[...])).astype(BF16)
    x_ref[...] = x
    total = None
    for k in range(e_ref.shape[0]):
        part = slice(k * SPAN, (k + 1) * SPAN)
        columns = rt_ref[0, part]
        to_end = jnp.exp2(spread_columns(columns[SPAN - 1 : SPAN] - columns))
        scaled = (x[part].astype(F32) * to_end).astype(BF16)
        state = dot(b_ref[part], scaled, ((0,), (0,)))
        e_ref[k] = state
        total = state if total is None else kept_ref[k, :1] * total + state
    sent_ref[...] = total.astype(BF16)


def blocks_kernel(halves, has_before, order_ref, g_ref, *refs):
    count = len(halves)
    number = sum(halves)
    arrays, refs = refs[:number], refs[number:]
    if has_before:
        refs = refs[2:]
    away_ref, own_ref, buffer, slots, sems, out_sems = refs
    rows = arrays[0].shape[0]
    wide = g_ref.shape[0]
    copies = []
    at = 0
    for index, parts in enumerate(halves):
        mine = []
        for part in range(parts):
            lanes = pl.ds(part * (wide // parts), wide // parts)
            target = buffer.at[pl.ds(index * rows, rows), lanes]
            copy = pltpu.make_async_copy(arrays[at], target, sems.at[at])
            copy.start()
            mine.append(copy)
            at += 1
        copies.append(mine)
    g = g_ref[...]
    half = away_ref.shape[1] // rows
    starts = [0]
    while starts[-1] < count:
        starts.append(starts[-1] + (2 if count - starts[-1] in (2, 4) else 3))
    for index in range(count):
        for copy in copies[index]:
            copy.wait()
        if index + 1 not in starts:
            continue
        start = starts[starts.index(index + 1) - 1]
        product = mm(buffer[start * rows : (index + 1) * rows], g)
        for done in range(start, index + 1):
            part = product[(done - start) * rows : (done - start + 1) * rows]
            slots[done] = part.T.astype(BF16)
            place = order_ref[done]
            lanes = pl.ds(pl.multiple_of(place % half * rows, 128), rows)

            @pl.when(place < half)
            def _():
                target = away_ref.at[:, lanes]
                pltpu.make_async_copy(slots.at[done], target, out_sems.at[done]).start()

            @pl.when(place >= half)
            def _():
                target = own_ref.at[:, lanes]
                pltpu.make_async_copy(slots.at[done], target, out_sems.at[done]).start()

    for index in range(count):
        target = away_ref.at[:, pl.ds(0, rows)]
        pltpu.make_async_copy(slots.at[index], target, out_sems.at[index]).wait()


def after_kernel(*refs):
    pass


def inner_kernel(
    r_ref, rt_ref, g_ref, x_ref, b_ref, c_ref, q_ref, *refs
):
    d_ref, grad_b_ref, grad_c_ref, sum_ref, top_ref, low_ref = refs[-6:]
    so_far = refs[:-6]
    step = pl.program_id(1)
    b = b_ref[...]
    c = c_ref[...]
    scores = dot(b, c, ((1,), (1,)))
    running = r_ref[...]
    columns = rt_ref[0]
    top_keep = iota((HALF, SPAN), 1) >= iota((HALF, SPAN), 0)
    low_keep = iota((HALF, HALF), 1) >= iota((HALF, HALF), 0)

    @pl.when(step == 0)
    def _():
        sum_ref[...] = jnp.zeros_like(sum_ref)
        grad_b_ref[...] = so_far[0][...] if so_far else jnp.zeros_like(grad_b_ref)

    rows = []
    lane = iota((SPAN, 2 * P_SIZE), 1)
    later = not_before().astype(BF16)
    top_less = iota((HALF, SPAN), 1) > iota((HALF, SPAN), 0)
    low_less = iota((HALF, HALF), 1) > iota((HALF, HALF), 0)
    for pair in range(GROUP // 2):
        lanes = slice(pair * 2 * P_SIZE, (pair + 1) * 2 * P_SIZE)
        x = x_ref[:, lanes]
        none = jnp.zeros_like(x)
        x = [jnp.where(lane < P_SIZE, x, none), jnp.where(lane < P_SIZE, none, x)]
        product = mm(jnp.concatenate(x, axis=0), g_ref[:, lanes].T)
        top_sum = low_sum = None
        for number in range(2):
            head = 2 * pair + number
            row = running[head : head + 1]
            at = number * SPAN
            top = jnp.where(top_keep, row - columns[:HALF, head : head + 1], NEVER)
            low = jnp.where(low_keep, row[:, HALF:] - columns[HALF:, head : head + 1], NEVER)
            top = jnp.exp2(top) * product[at : at + HALF]
            low = jnp.exp2(low) * product[at + HALF : at + SPAN, HALF:]
            top_sum = top if number == 0 else top_sum + top
            low_sum = low if number == 0 else low_sum + low
            part = slice(head * HALF, (head + 1) * HALF)
            top_ref[part] = (top * scores[:HALF]).astype(BF16)
            low_ref[part] = (low * scores[HALF:, HALF:]).astype(BF16)
        sum_ref[:HALF] += top_sum
        sum_ref[HALF:, HALF:] += low_sum
    top = mm(top_ref[...], later)
    low = mm(low_ref[...], later[HALF:, HALF:])
    for head in range(GROUP):
        part = slice(head * HALF, (head + 1) * HALF)
        top_row = jnp.sum(jnp.where(top_less, top[part], 0.0), axis=0, keepdims=True)
        low_row = jnp.sum(jnp.where(low_less, low[part], 0.0), axis=0, keepdims=True)
        rows.append(jnp.concatenate([top_row[:, :HALF], top_row[:, HALF:] + low_row], axis=1))
    to_end = jnp.exp2(spread_columns(columns[SPAN - 1 : SPAN] - columns))
    scaled = x_ref[...].astype(F32) * to_end
    ends = dot(one_hot(BF16), (scaled * mm(b, q_ref[0])).astype(BF16), ((1,), (1,)))
    d_ref[...] = jnp.concatenate(rows, axis=0) + sum_over(ends, before())
    grad_b_ref[...] += dot(scaled.astype(BF16), q_ref[0], ((1,), (1,)))

    @pl.when(step == pl.num_programs(1) - 1)
    def _():
        total = sum_ref[...].astype(BF16)
        grad_b_ref[...] += mm(total, c)
        part = dot(total, b, ((0,), (0,)))
        grad_c_ref[...] = part + so_far[1][...] if so_far else part


def state_kernel(
    rt_ref, g_ref, c_ref, s_ref, e_ref, q_ref, a_ref, d_part_ref, c_part_ref, *refs
):
    d_ref, grad_c_ref, held = refs[-3:]
    span, group = pl.program_id(0), pl.program_id(1)

    @pl.when(group == 0)
    def _():
        grad_c_ref[...] = c_part_ref[...]

    @pl.when(span == 0)
    def _():
        held[group] = s_ref[...]

    state = held[group]
    low = state.astype(BF16)
    scaled = g_ref[...].astype(F32) * jnp.exp2(spread_columns(rt_ref[0]))
    ends = dot(one_hot(BF16), (scaled * mm(c_ref[...], low)).astype(BF16), ((1,), (1,)))
    grad_c_ref[...] += dot(scaled.astype(BF16), low, ((1,), (1,)))
    product = jnp.sum(q_ref[0].astype(F32) * state, axis=0, keepdims=True) * a_ref[0, :1]
    high, middle, last = thirds(product)
    row = iota((8, WIDE), 0)
    stacked = jnp.where(row == 0, high, jnp.where(row == 1, middle, jnp.where(row == 2, last, 0.0)))
    kept = dot(one_hot(BF16), stacked.astype(BF16), ((1,), (1,)))
    kept = jnp.sum(kept, axis=1, keepdims=True)
    d_ref[...] = d_part_ref[...] + sum_over(ends, not_before()) + kept
    held[group] = e_ref[0] + a_ref[0, :1] * state


def call(kernel, grid, in_specs, out_specs, out_shape, flops, size, scratch=()):
    return pl.pallas_call(
        kernel,
        grid=grid,
        in_specs=in_specs,
        out_specs=out_specs,
        out_shape=out_shape,
        scratch_shapes=list(scratch),
        cost_estimate=pl.CostEstimate(flops=flops, bytes_accessed=size, transcendentals=0),
        compiler_params=pltpu.CompilerParams(
            dimension_semantics=("arbitrary",) * len(grid), vmem_limit_bytes=GRANT
        ),
    )


def run_spec(at=0):
    return pl.BlockSpec((GROUP, SPAN), lambda k, h: (h + at, k))


def run_t_spec(at=0):
    return pl.BlockSpec((1, SPAN, GROUP), lambda k, h: (h + at, k, 0))


def rows_spec(at=0):
    return pl.BlockSpec((SPAN, WIDE), lambda k, h: (k, h + at))


def state_spec(at=0):
    return pl.BlockSpec((1, 2 * P_SIZE, WIDE), lambda k, h: (k, 0, h + at))


def kept_spec(at=0):
    return pl.BlockSpec((1, 8, WIDE), lambda k, h: (k, 0, h + at))


SHARED = pl.BlockSpec((SPAN, 2 * P_SIZE), lambda k, h: (k, 0))
GAIN = pl.BlockSpec((1, WIDE), lambda k, h: (0, h))
ANYWHERE = pl.BlockSpec(memory_space=pl.ANY)
INNER_SCRATCH = [
    pltpu.VMEM((SPAN, SPAN), F32),
    pltpu.VMEM((GROUP * HALF, SPAN), BF16),
    pltpu.VMEM((GROUP * HALF, HALF), BF16),
]
SCALARS = pl.BlockSpec(memory_space=pltpu.SMEM)


def shape(*dims, dtype=F32):
    return jax.ShapeDtypeStruct(dims, dtype)


def swap(value, axis, bit):
    count = lax.axis_size(axis)
    return lax.ppermute(value, axis, [(i, i ^ bit) for i in range(count)])


def block_products(kept):
    count = lax.axis_size("ctx")
    place = lax.axis_index("ctx")
    steps = []
    before_me = jnp.ones_like(kept)
    after_me = jnp.ones_like(kept)
    bit = 1
    while bit < count:
        other = swap(kept, "ctx", bit)
        upper = (place & bit) != 0
        steps.append((bit, upper, kept, other, before_me, after_me))
        before_me = jnp.where(upper, before_me * other, before_me)
        after_me = jnp.where(upper, after_me, after_me * other)
        kept = kept * other
        bit *= 2
    return steps


def scan_states(total, steps, reverse):
    entering = jnp.zeros_like(total)
    for bit, upper, kept, other, before_me, after_me in steps:
        got = swap(total.astype(BF16), "ctx", bit).astype(F32)
        if reverse:
            entering = entering + jnp.where(upper, 0.0, after_me) * got
            total = jnp.where(upper, got + other * total, total + kept * got)
        else:
            entering = entering + jnp.where(upper, before_me, 0.0) * got
            total = jnp.where(upper, kept * got + total, other * total + got)
    return entering


def head_sum(value):
    bit = 1
    while bit < lax.axis_size("head"):
        value = value.astype(BF16)
        value = value.astype(F32) + swap(value, "head", bit).astype(F32)
        bit *= 2
    return value


PLANE = 4


def after(values, *tokens):
    out = pl.pallas_call(
        after_kernel,
        in_specs=[ANYWHERE] * (len(values) + len(tokens)),
        out_specs=[ANYWHERE] * len(values),
        out_shape=[shape(*value.shape, dtype=value.dtype) for value in values],
        input_output_aliases={index: index for index in range(len(values))},
        cost_estimate=pl.CostEstimate(flops=0, bytes_accessed=0, transcendentals=0),
        compiler_params=pltpu.CompilerParams(vmem_limit_bytes=GRANT),
    )(*values, *tokens)
    return list(out)


def along_z(value, moves):
    pairs = [(a * PLANE + i, b * PLANE + i) for a, b in moves for i in range(PLANE)]
    return lax.ppermute(value, "ctx", pairs)


MIDDLE = ((1, 2), (2, 1))
OUTWARD = ((1, 0), (2, 3))


def swap_x(value):
    return swap(value, "ctx", 1)


def swap_y(value):
    return swap(value, "ctx", 2)


LAYERS = ((0, 1, 2, 3), (1, 0, 3, 2), (2, 2, 1, 1), (3, 3, 0, 0))
EARLY = [(k, flip) for k in (0, 1, 2) for flip in range(3)]
LATE = [(0, 3), (1, 3), (2, 3), (3, 0), (3, 1), (3, 2), (3, 3)]


def block_order():
    place = lax.axis_index("ctx")
    layer, spot = place // PLANE, place % PLANE
    layers = jnp.array(LAYERS, jnp.int32)[:, layer]
    order = [layers[k] * PLANE + (spot ^ flip) for k, flip in EARLY + LATE]
    return jnp.stack(order).astype(jnp.int32)


def gather_weight(w, sizes):
    ends = [sum(sizes[: j + 1]) * P_SIZE for j in range(len(sizes))]
    parts = [w[:, end - size * P_SIZE : end] for end, size in zip(ends, sizes)]
    return [lax.all_gather(part, "ctx", axis=0, tiled=True) for part in parts]


def forward(features, first, weight, running_t, b_rows, here):
    own, other = features
    length = own.shape[0]
    n = b_rows.shape[1]
    width, wide = weight.shape
    deep = width // 4
    spans = length // SPAN

    def depth(k, first_ref):
        return (k // 2 ^ first_ref[0]) * 2 + k % 2

    return pl.pallas_call(
        forward_kernel,
        grid_spec=pltpu.PrefetchScalarGridSpec(
            num_scalar_prefetch=1,
            grid=(wide // WIDE, 4),
            in_specs=[
                pl.BlockSpec((length, deep), lambda h, k, first_ref: (0, jnp.minimum(k, 1))),
                pl.BlockSpec((length, deep), lambda h, k, first_ref: (0, jnp.maximum(k - 2, 0))),
                pl.BlockSpec((deep, WIDE), lambda h, k, first_ref: (depth(k, first_ref), h)),
                pl.BlockSpec((1, length, GROUP), lambda h, k, first_ref: (h + here, 0, 0)),
                pl.BlockSpec((length, n), lambda h, k, first_ref: (0, 0)),
            ],
            out_specs=[
                pl.BlockSpec((length, WIDE), lambda h, k, first_ref: (0, h)),
                pl.BlockSpec((spans, n, WIDE), lambda h, k, first_ref: (0, 0, h)),
            ],
            scratch_shapes=[pltpu.VMEM((length, WIDE), F32)],
        ),
        out_shape=[shape(length, wide, dtype=BF16), shape(spans, n, wide)],
        cost_estimate=pl.CostEstimate(
            flops=2 * length * wide * width, bytes_accessed=2 * wide * width, transcendentals=0
        ),
        compiler_params=pltpu.CompilerParams(
            dimension_semantics=("arbitrary", "arbitrary"), vmem_limit_bytes=GRANT
        ),
    )(first, own, other, weight, running_t, b_rows)


def multiply(grad_x, weight, at, half, halves, before=None, other=None):
    length = grad_x.shape[0]
    width, wide = weight.shape
    tiles = width // halves // WIDE
    tile = pl.BlockSpec((length, WIDE), lambda j, half_ref: (0, half_ref[0] * tiles + j))
    plain = pl.BlockSpec((length, WIDE), lambda j, half_ref: (0, j))
    in_specs = [
        pl.BlockSpec((length, wide), lambda j, half_ref: (0, at)),
        pl.BlockSpec((WIDE, wide), lambda j, half_ref: (half_ref[0] * tiles + j, 0)),
    ]
    operands = [grad_x, weight]
    if before is not None:
        in_specs.append(tile)
        operands.append(before)
    if other is not None:
        in_specs.append(plain)
        operands.append(other)
    return pl.pallas_call(
        functools.partial(product_kernel, before is not None, other is not None),
        grid_spec=pltpu.PrefetchScalarGridSpec(
            num_scalar_prefetch=1,
            grid=(tiles,),
            in_specs=in_specs,
            out_specs=plain,
        ),
        out_shape=shape(length, width // halves, dtype=BF16),
        cost_estimate=pl.CostEstimate(
            flops=2 * length * wide * width // halves,
            bytes_accessed=2 * wide * width // halves,
            transcendentals=0,
        ),
        compiler_params=pltpu.CompilerParams(
            dimension_semantics=("arbitrary",), vmem_limit_bytes=GRANT
        ),
    )(half, *operands)


def early_forward(features, pieces):
    length = features.shape[0]
    rows, columns = pieces[0].shape
    deep = rows * len(pieces)
    return call(
        functools.partial(early_forward_kernel, len(pieces)),
        (columns // WIDE,),
        [pl.BlockSpec((length, deep), lambda h: (0, 0))]
        + [pl.BlockSpec((rows, WIDE), lambda h: (0, h))] * len(pieces),
        pl.BlockSpec((length, WIDE), lambda h: (0, h)),
        shape(length, columns),
        2 * length * columns * deep,
        2 * columns * deep,
        [pltpu.VMEM((deep, WIDE), BF16)],
    )(features, *pieces)


def late_forward(features, part, pieces, running_t, b_rows, kept, here):
    length = features.shape[0]
    rows, columns = pieces[0].shape
    deep = rows * len(pieces)
    n = b_rows.shape[1]
    spans = length // SPAN
    state = pl.BlockSpec((n, WIDE), lambda h: (0, h))
    return call(
        functools.partial(late_forward_kernel, len(pieces)),
        (columns // WIDE,),
        [
            pl.BlockSpec((length, deep), lambda h: (0, 0)),
            pl.BlockSpec((length, WIDE), lambda h: (0, h + here)),
            pl.BlockSpec((1, length, GROUP), lambda h: (h + here, 0, 0)),
            pl.BlockSpec((length, n), lambda h: (0, 0)),
            pl.BlockSpec((spans, 8, WIDE), lambda h: (0, 0, h + here)),
        ]
        + [pl.BlockSpec((rows, WIDE), lambda h: (0, h))] * len(pieces),
        [
            pl.BlockSpec((length, WIDE), lambda h: (0, h)),
            pl.BlockSpec((spans, n, WIDE), lambda h: (0, 0, h)),
            state,
        ],
        [
            shape(length, columns, dtype=BF16),
            shape(spans, n, columns),
            shape(n, columns, dtype=BF16),
        ],
        2 * length * columns * deep,
        2 * columns * deep,
        [pltpu.VMEM((deep, WIDE), BF16)],
    )(features, part, running_t, b_rows, kept, *pieces)


def multiply_blocks(order, grad_x, pieces, so_far):
    columns, length = grad_x.shape
    arrays = [array for piece in pieces for array in piece]
    rows = arrays[0].shape[0]
    count = len(pieces)
    half = shape(length, lax.axis_size("ctx") * rows // 2, dtype=BF16)
    first = 2 + len(arrays)
    return pl.pallas_call(
        functools.partial(blocks_kernel, [len(piece) for piece in pieces], bool(so_far)),
        grid=(1,),
        in_specs=[SCALARS, pl.BlockSpec((columns, length), lambda h: (0, 0))]
        + [ANYWHERE] * (len(arrays) + len(so_far)),
        out_specs=[ANYWHERE, ANYWHERE],
        out_shape=[half, half],
        input_output_aliases={first + k: k for k in range(len(so_far))},
        scratch_shapes=[
            pltpu.VMEM((rows * count, columns), BF16),
            pltpu.VMEM((count, length, rows), BF16),
            pltpu.SemaphoreType.DMA((len(arrays),)),
            pltpu.SemaphoreType.DMA((count,)),
        ],
        cost_estimate=pl.CostEstimate(
            flops=2 * length * columns * rows * count,
            bytes_accessed=2 * columns * rows * count,
            transcendentals=0,
        ),
        compiler_params=pltpu.CompilerParams(
            dimension_semantics=("arbitrary",), vmem_limit_bytes=GRANT
        ),
    )(order, grad_x, *arrays, *so_far)


def back_start(own_grads, kept):
    spans, n, columns = own_grads.shape
    return call(
        start_kernel,
        (columns // WIDE,),
        [
            pl.BlockSpec((spans, n, WIDE), lambda h: (0, 0, h)),
            pl.BlockSpec((spans, 8, WIDE), lambda h: (0, 0, h)),
        ],
        [pl.BlockSpec((rows, WIDE), lambda h: (0, h)) for rows in (8, n + TAIL)],
        [shape(8, columns), shape(n + TAIL, columns, dtype=BF16)],
        0,
        14 * n * columns,
    )(own_grads, kept)


def back_step(place, log, sent, entering, bit):
    got = swap(sent, "ctx", bit)
    columns = sent.shape[1]
    n = sent.shape[0] - TAIL
    short, state, tall = [
        pl.BlockSpec((rows, 2 * WIDE), lambda h: (0, h)) for rows in (8, n, n + TAIL)
    ]
    return call(
        functools.partial(back_kernel, bit),
        (columns // (2 * WIDE),),
        [SCALARS, short, tall, tall] + [state] * len(entering),
        [state, tall, short, short],
        [
            shape(n, columns),
            shape(n + TAIL, columns, dtype=BF16),
            shape(8, columns),
            shape(8, columns),
        ],
        0,
        14 * n * columns,
    )(place, log, sent, got, *entering)


def scan_step(factors, here, sent, entering, bit, last=False):
    got = swap(sent, "ctx", bit)
    n, columns = sent.shape
    block = pl.BlockSpec((n, columns), lambda h: (0, 0))
    at = here * WIDE // columns
    outs = [shape(n, columns), shape(n, columns, dtype=BF16)][: 2 - last]
    return call(
        functools.partial(scan_kernel, last),
        (1,),
        [pl.BlockSpec((8, columns), lambda h: (0, at)), block, block] + [block] * len(entering),
        [block] * len(outs),
        outs,
        0,
        10 * n * columns,
    )(factors, sent, got, *entering)


def local(inputs, w_in, b_rows, c_rows, log_decay, skip_gain, grad_out):
    groups = log_decay.shape[0] // GROUP
    layered = lax.axis_size("ctx") == 4 * PLANE and lax.axis_size("head") == 2
    if layered and groups % 2 == 0 and w_in.shape[0] == 256:
        return local_layered(inputs, w_in, b_rows, c_rows, log_decay, skip_gain, grad_out)
    return local_plain(inputs, w_in, b_rows, c_rows, log_decay, skip_gain, grad_out)


def prepare(log_decay, grad_out, c_rows):
    length, columns = grad_out.shape
    heads = log_decay.shape[0]
    spans = length // SPAN
    groups = heads // GROUP
    n = c_rows.shape[1]
    return call(
        decay_kernel,
        (spans, groups),
        [run_spec(), rows_spec(), SHARED],
        [run_spec(), run_t_spec(), kept_spec(), state_spec()],
        [
            shape(heads, length),
            shape(groups, length, GROUP),
            shape(spans, 8, columns),
            shape(spans, n, columns),
        ],
        2 * length * columns * n,
        6 * length * columns,
    )(log_decay, grad_out, c_rows)


def inner(grid, here, wide, operands, so_far):
    length = operands[2].shape[0]
    n = operands[4].shape[1]
    specs = [
        run_spec(here),
        run_t_spec(here),
        rows_spec(here),
        rows_spec(),
        SHARED,
        SHARED,
        state_spec(here),
    ]
    return call(
        inner_kernel,
        grid,
        specs + [SHARED] * len(so_far),
        [run_spec(), SHARED, SHARED],
        [shape(wide // P_SIZE, length), shape(length, n), shape(length, n)],
        12 * length * wide * SPAN,
        6 * length * wide,
        INNER_SCRATCH,
    )(*operands, *so_far)


def state_terms(grid, here, wide, operands, heads=None, so_far=None):
    length = operands[1].shape[0]
    n = operands[2].shape[1]
    heads = heads or wide // P_SIZE
    at = here if heads > wide // P_SIZE else 0
    extra = () if so_far is None else (so_far,)
    return pl.pallas_call(
        state_kernel,
        grid=grid,
        in_specs=[
            run_t_spec(here),
            rows_spec(here),
            SHARED,
            pl.BlockSpec((n, WIDE), lambda k, h: (0, h)),
            state_spec(),
            state_spec(here),
            kept_spec(here),
            run_spec(),
            SHARED,
        ]
        + [ANYWHERE] * len(extra),
        out_specs=[run_spec(at), SHARED],
        out_shape=[shape(heads, length), shape(length, n)],
        scratch_shapes=[pltpu.VMEM((grid[1], n, WIDE), F32)],
        input_output_aliases={len(operands): 0} if extra else {},
        cost_estimate=pl.CostEstimate(
            flops=4 * length * wide * n, bytes_accessed=6 * length * wide, transcendentals=0
        ),
        compiler_params=pltpu.CompilerParams(
            dimension_semantics=("arbitrary", "arbitrary"), vmem_limit_bytes=GRANT
        ),
    )(*operands, *extra)


def local_layered(inputs, w_in, b_rows, c_rows, log_decay, skip_gain, grad_out):
    length, columns = grad_out.shape
    heads = log_decay.shape[0]
    spans = length // SPAN
    groups = heads // GROUP
    place = lax.axis_index("head").astype(jnp.int32)
    half = columns // 2
    order = block_order()
    blocks = order.shape[0]
    width = blocks * w_in.shape[0]

    z1, inner2 = swap(w_in, "ctx", PLANE), along_z(w_in, MIDDLE)
    own_x, own_y = swap_x(w_in), swap_y(w_in)
    other = swap(inputs, "head", 1)
    running, running_t, kept, own_grads = prepare(log_decay, grad_out, c_rows)
    spot = lax.axis_index("ctx").astype(jnp.int32)[None]
    log, sent = back_start(own_grads, kept)
    sent = after([sent], other)[0]
    leaving, moved, log, factors_1 = back_step(spot, log, sent, (), 1)

    z1, inner2, own_y = after([z1, inner2, own_y], own_x, sent)
    sent = moved
    x1, y1 = swap_x(z1), swap_y(z1)
    inner3, outer2 = along_z(z1, MIDDLE), along_z(inner2, OUTWARD)
    own_y_a, own_y_b = own_y[:, :half], own_y[:, half:]
    leaving, sent, log, factors_2 = back_step(spot, log, sent, (leaving,), 2)
    order_own = (order + place * (blocks // 2)) % blocks
    cut = len(EARLY) * w_in.shape[0]
    early_features, late_features = call(
        arrange_kernel,
        (1,),
        [SCALARS] + [pl.BlockSpec((length, width // 2), lambda h: (0, 0))] * 2,
        [pl.BlockSpec((length, wide), lambda h: (0, 0)) for wide in (cut, width - cut)],
        [shape(length, wide, dtype=BF16) for wide in (cut, width - cut)],
        0,
        4 * length * width,
        [pltpu.VMEM((length, width), BF16)],
    )(order_own, inputs, other)

    inner2, inner3, outer2, x1, sent, own_y_a, own_y_b = after(
        [inner2, inner3, outer2, x1, sent, own_y_a, own_y_b], y1, early_features
    )
    z3 = inner2 + outer2
    x3, y3 = swap_x(z3), swap_y(z3)
    outer3 = along_z(inner3, OUTWARD)
    x1_a, x1_b = x1[:, :half], x1[:, half:]
    leaving, sent, log, factors_4 = back_step(spot, log, sent, (leaving,), 4)

    inner3, outer3, y3, x1_a, x1_b = after([inner3, outer3, y3, x1_a, x1_b], x3)
    z2a = inner3[:, :half] + outer3[:, :half]
    z2b = inner3[:, half:] + outer3[:, half:]
    y3_a, y3_b = y3[:, :half], y3[:, half:]
    x2a, y2a = swap_x(z2a), swap_y(z2a)
    d3a, d1a = swap_x(y3_a), swap_y(x1_a)
    leaving, sent, log, factors_8 = back_step(spot, log, sent, (leaving,), 8)
    early = [w_in, own_x, own_y, z1, x1, y1, z3, x3, y3]
    part = early_forward(early_features, early)

    own_y_a, x2a, z2b, leaving = after([own_y_a, x2a, z2b, leaving], y2a, d3a, d1a, part)
    d0a, d2a = swap_x(own_y_a), swap_y(x2a)
    x2b, y2b = swap_x(z2b), swap_y(z2b)
    leaving_all = [leaving]
    for k in range(spans - 1, 0, -1):
        leaving_all.insert(0, own_grads[k] + kept[k, :1] * leaving_all[0])
    leaving_all = jnp.stack([value.astype(BF16) for value in leaving_all])
    skip = jnp.repeat(skip_gain, P_SIZE)[None]
    grad_x = grad_rows(running, running_t, grad_out, b_rows, c_rows, leaving_all, skip, True)
    order_away = (order + (1 - place) * (blocks // 2)) % blocks
    early_order, late_order = order_away[: len(EARLY)], order_away[len(EARLY) :]
    late_a = [d0a, d1a, d3a, z2a, x2a, y2a, d2a]
    x_a, states_a, sent_a = late_forward(
        late_features, part, late_a, running_t, b_rows, kept, 0
    )

    own_y_b, x2b, y3_b, x1_b, sent_a, x_a, grad_x = after(
        [own_y_b, x2b, y3_b, x1_b, sent_a, x_a, grad_x], y2b
    )
    d0b, d2b = swap_x(own_y_b), swap_y(x2b)
    d3b, d1b = swap_x(y3_b), swap_y(x1_b)
    entering_a, sent_a = scan_step(factors_1, 0, sent_a, (), 1)
    product = multiply_blocks(early_order, grad_x, [[piece] for piece in early], ())
    shared = (running, running_t, grad_out)
    here = groups // 2
    grid = (spans, here)
    inner_a = shared + (x_a, b_rows, c_rows, leaving_all)
    decay_a, grad_b, grad_c = inner(grid, 0, half, inner_a, ())

    d0b, d2b = after([d0b, d2b], d3b, d1b, sent_a, grad_b, product[0])
    late_b = [d0b, d1b, d3b, z2b, x2b, y2b, d2b]
    x_b, states_b, sent_b = late_forward(
        late_features, part, late_b, running_t, b_rows, kept, here
    )
    pairs = list(zip(late_a, late_b))
    sent_a, sent_b, *product = after([sent_a, sent_b, *product])
    entering_b, sent_b = scan_step(factors_1, here, sent_b, (), 1)
    entering_a, sent_a = scan_step(factors_2, 0, sent_a, (entering_a,), 2)
    away, own = multiply_blocks(late_order, grad_x, pairs, product)

    sent_a, sent_b, x_b, away = after([sent_a, sent_b, x_b, away])
    entering_b, sent_b = scan_step(factors_2, here, sent_b, (entering_b,), 2)
    entering_a, sent_a = scan_step(factors_4, 0, sent_a, (entering_a,), 4)
    got = swap(away, "head", 1)
    inner_b = shared + (x_b, b_rows, c_rows, leaving_all)
    decay_b, grad_b, grad_c = inner(grid, here, half, inner_b, (grad_b, grad_c))

    sent_a, sent_b, got, grad_b = after([sent_a, sent_b, got, grad_b])
    entering_b, sent_b = scan_step(factors_4, here, sent_b, (entering_b,), 4)
    (entering_a,) = scan_step(factors_8, 0, sent_a, (entering_a,), 8, True)
    grad_b = head_sum(grad_b)

    sent_b, entering_a, got = after([sent_b, entering_a, got], grad_b)
    grad_inputs = (own.astype(F32) + got.astype(F32)).astype(BF16)
    (entering_b,) = scan_step(factors_8, here, sent_b, (entering_b,), 8, True)
    common = (running_t, grad_out, c_rows)
    state_a = common + (entering_a, states_a, leaving_all, kept, decay_a, grad_c)
    decays, grad_c = state_terms(grid, 0, half, state_a, heads)
    (entering_b,) = after([entering_b], grad_inputs, grad_c)
    state_b = common + (entering_b, states_b, leaving_all, kept, decay_b, grad_c)
    decays, grad_c = state_terms(grid, here, half, state_b, heads, decays)
    return (grad_inputs, grad_b, head_sum(grad_c), decays)


def grad_rows(running, running_t, grad_out, b_rows, c_rows, leaving, skip, transposed):
    length, columns = grad_out.shape
    spec, dims = rows_spec(), (length, columns)
    if transposed:
        spec, dims = pl.BlockSpec((WIDE, SPAN), lambda k, h: (h, k)), (columns, length)
    return call(
        functools.partial(grad_x_kernel, transposed),
        (length // SPAN, running_t.shape[0]),
        [run_spec(), run_t_spec(), rows_spec(), SHARED, SHARED, state_spec(), GAIN],
        spec,
        shape(*dims, dtype=BF16),
        8 * length * columns * SPAN,
        6 * length * columns,
    )(running, running_t, grad_out, b_rows, c_rows, leaving, skip)


def local_plain(inputs, w_in, b_rows, c_rows, log_decay, skip_gain, grad_out):
    length, columns = grad_out.shape
    heads = log_decay.shape[0]
    spans = length // SPAN
    groups = heads // GROUP
    n = b_rows.shape[1]
    grid = (spans, groups)

    sizes = (heads // 2, heads // 4, heads // 4) if heads % (4 * GROUP) == 0 else (heads,)
    weights = gather_weight(w_in, sizes)
    two = lax.axis_size("head") == 2
    place = lax.axis_index("head").astype(jnp.int32)[None]
    width = weights[0].shape[0]
    if two:
        features = (inputs, swap(inputs, "head", 1))
        first = place
    else:
        features = lax.all_gather(inputs, "head", axis=1, tiled=True)
        features = (features[:, : width // 2], features[:, width // 2 :])
        first = jnp.zeros((1,), jnp.int32)

    running, running_t, kept, own_grads = call(
        decay_kernel,
        grid,
        [run_spec(), rows_spec(), SHARED],
        [run_spec(), run_t_spec(), kept_spec(), state_spec()],
        [
            shape(heads, length),
            shape(groups, length, GROUP),
            shape(spans, 8, columns),
            shape(spans, n, columns),
        ],
        2 * length * columns * n,
        6 * length * columns,
    )(log_decay, grad_out, c_rows)

    kept_total = kept[0, :1]
    for k in range(1, spans):
        kept_total = kept_total * kept[k, :1]
    steps = block_products(kept_total)

    total = own_grads[spans - 1]
    for k in range(spans - 2, -1, -1):
        total = own_grads[k] + kept[k, :1] * total
    leaving = [scan_states(total, steps, True)]
    for k in range(spans - 1, 0, -1):
        leaving.insert(0, own_grads[k] + kept[k, :1] * leaving[0])
    leaving = jnp.stack([value.astype(BF16) for value in leaving])

    skip = jnp.repeat(skip_gain, P_SIZE)[None]
    grad_x = grad_rows(running, running_t, grad_out, b_rows, c_rows, leaving, skip, False)

    grad_b = grad_c = product = None
    tokens = ()
    decay_parts = []
    at = 0
    for index, size in enumerate(sizes):
        wide = size * P_SIZE
        here = at // GROUP
        count = size // GROUP
        weight = weights[index]
        if tokens:
            weight = after([weight], *tokens)[0]
        x, own_states = forward(features, first, weight, running_t, b_rows, here)

        chunk = slice(at * P_SIZE, at * P_SIZE + wide)
        total = own_states[0]
        for k in range(1, spans):
            total = kept[k, :1, chunk] * total + own_states[k]
        cut = [step[:2] + tuple(value[:, chunk] for value in step[2:]) for step in steps]
        entering = scan_states(total, cut, False)

        so_far = () if grad_b is None else (grad_b, grad_c)
        decay_part, grad_b, grad_c = call(
            inner_kernel,
            (spans, count),
            [
                run_spec(here),
                run_t_spec(here),
                rows_spec(here),
                rows_spec(),
                SHARED,
                SHARED,
                state_spec(here),
            ]
            + [SHARED] * len(so_far),
            [run_spec(), SHARED, SHARED],
            [shape(size, length), shape(length, n), shape(length, n)],
            12 * length * wide * SPAN,
            6 * length * wide,
            INNER_SCRATCH,
        )(running, running_t, grad_out, x, b_rows, c_rows, leaving, *so_far)
        decay_part, grad_c = call(
            state_kernel,
            (spans, count),
            [
                run_t_spec(here),
                rows_spec(here),
                SHARED,
                pl.BlockSpec((n, WIDE), lambda k, h: (0, h)),
                state_spec(),
                state_spec(here),
                kept_spec(here),
                run_spec(),
                SHARED,
            ],
            [run_spec(), SHARED],
            [shape(size, length), shape(length, n)],
            4 * length * wide * n,
            6 * length * wide,
            [pltpu.VMEM((count, n, WIDE), F32)],
        )(running_t, grad_out, c_rows, entering, own_states, leaving, kept, decay_part, grad_c)
        decay_parts.append(decay_part)

        if index < len(sizes) - 1:
            zero = jnp.zeros((1,), jnp.int32)
            product = multiply(grad_x, weight, at // size, zero, 1, product)
            tokens = (product, grad_b, entering)
        elif two:
            sent = multiply(grad_x, weight, at // size, 1 - place, 2, product)
            got = swap(sent, "head", 1)
            grad_inputs = multiply(grad_x, weight, at // size, place, 2, product, got)
        else:
            zero = jnp.zeros((1,), jnp.int32)
            product = multiply(grad_x, weight, at // size, zero, 1, product)
            grad_inputs = lax.psum_scatter(product, "head", scatter_dimension=1, tiled=True)
        at += size

    return (grad_inputs, head_sum(grad_b), head_sum(grad_c), jnp.concatenate(decay_parts, axis=0))


def solution(mesh):
    in_specs = (
        P("ctx", "head"),
        P("ctx", "head"),
        P("ctx", None),
        P("ctx", None),
        P("head", "ctx"),
        P("head"),
        P("ctx", "head"),
    )
    out_specs = (P("ctx", "head"), P("ctx", None), P("ctx", None), P("head", "ctx"))
    return jax.shard_map(local, mesh=mesh, in_specs=in_specs, out_specs=out_specs, check_vma=False)
```

```python
import functools

import jax
import jax.numpy as jnp
from jax import lax
from jax.experimental import pallas as pl
from jax.experimental.pallas import tpu as pltpu
from jax.sharding import PartitionSpec as P

SPAN = 256
HALF = SPAN // 2
P_SIZE = 64
GROUP = 8
WIDE = GROUP * P_SIZE
LOG2E = 1.4426950408889634
NEVER = -1e30
GRANT = 64 * 2**20

F32 = jnp.float32
BF16 = jnp.bfloat16
EXACT = lax.Precision.HIGHEST


def dot(a, b, dims, precision=None):
    return lax.dot_general(a, b, (dims, ((), ())), precision=precision, preferred_element_type=F32)


def mm(a, b, precision=None):
    return dot(a, b, ((1,), (0,)), precision)


def iota(shape, dim):
    return lax.broadcasted_iota(jnp.int32, shape, dim)


def one_hot(dtype):
    return (iota((GROUP, WIDE), 0) == iota((GROUP, WIDE), 1) // P_SIZE).astype(dtype)


def not_before():
    return (iota((SPAN, SPAN), 0) >= iota((SPAN, SPAN), 1)).astype(F32)


def before():
    return (iota((SPAN, SPAN), 0) < iota((SPAN, SPAN), 1)).astype(F32)


def same():
    return (iota((SPAN, SPAN), 0) == iota((SPAN, SPAN), 1)).astype(F32)


def first_head():
    return iota((SPAN, 2 * P_SIZE), 1) < P_SIZE


def pair_columns(columns, pair):
    shape = (columns.shape[0], 2 * P_SIZE)
    left = jnp.broadcast_to(columns[:, 2 * pair : 2 * pair + 1], shape)
    right = jnp.broadcast_to(columns[:, 2 * pair + 1 : 2 * pair + 2], shape)
    return jnp.where(iota(shape, 1) < P_SIZE, left, right)


def spread_columns(columns):
    return jnp.concatenate([pair_columns(columns, pair) for pair in range(GROUP // 2)], axis=1)


def thirds(value):
    high = value.astype(BF16).astype(F32)
    middle = (value - high).astype(BF16).astype(F32)
    return high, middle, value - high - middle


def sum_over(value, mask):
    rows = value.shape[0]
    parts = mm(jnp.concatenate(thirds(value), axis=0).astype(BF16), mask.astype(BF16))
    return parts[:rows] + parts[rows : 2 * rows] + parts[2 * rows :]


def decay_kernel(d_ref, g_ref, c_ref, r_ref, rt_ref, a_ref, gt_ref):
    row_sums = sum_over(d_ref[...] * LOG2E, 1.0 - not_before() + same())
    r_ref[...] = row_sums
    padded = jnp.concatenate([row_sums, jnp.zeros((2 * P_SIZE - GROUP, SPAN), F32)], axis=0)
    running = padded.T[:, :GROUP]
    rt_ref[0] = running
    growth = jnp.exp2(spread_columns(running))
    last = spread_columns(running[SPAN - 1 : SPAN])
    a_ref[0] = jnp.where(iota((8, WIDE), 0) < 4, jnp.exp2(last), last)
    scaled = (g_ref[...].astype(F32) * growth).astype(BF16)
    gt_ref[0] = dot(c_ref[...], scaled, ((0,), (0,)))


def grad_x_kernel(transposed, r_ref, rt_ref, g_ref, b_ref, c_ref, q_ref, skip_ref, out_ref):
    b = b_ref[...]
    scores = dot(b, c_ref[...], ((1,), (1,)))
    running = r_ref[...]
    columns = rt_ref[0]
    top_keep = iota((HALF, SPAN), 1) >= iota((HALF, SPAN), 0)
    low_keep = iota((HALF, HALF), 1) >= iota((HALF, HALF), 0)
    to_end = jnp.exp2(spread_columns(columns[SPAN - 1 : SPAN] - columns))
    from_state = mm(b, q_ref[0]) * to_end
    for pair in range(GROUP // 2):
        lanes = slice(pair * 2 * P_SIZE, (pair + 1) * 2 * P_SIZE)
        g = g_ref[:, lanes]
        parts = []
        for head in (2 * pair, 2 * pair + 1):
            row = running[head : head + 1]
            top = jnp.where(top_keep, row - columns[:HALF, head : head + 1], NEVER)
            low = jnp.where(low_keep, row[:, HALF:] - columns[HALF:, head : head + 1], NEVER)
            parts.append((jnp.exp2(top) * scores[:HALF]).astype(BF16))
            low = (jnp.exp2(low) * scores[HALF:, HALF:]).astype(BF16)
            parts.append(jnp.concatenate([jnp.zeros((HALF, HALF), BF16), low], axis=1))
        product = mm(jnp.concatenate(parts, axis=0), g)
        parts = [product[:SPAN], product[SPAN:]]
        inner = jnp.where(first_head(), parts[0], parts[1])
        total = inner + skip_ref[:, lanes] * g.astype(F32) + from_state[:, lanes]
        if transposed:
            out_ref[lanes, :] = total.T.astype(BF16)
        else:
            out_ref[:, lanes] = total.astype(BF16)


def forward_kernel(half_ref, own_ref, other_ref, w_ref, rt_ref, b_ref, x_ref, e_ref, total_ref):
    step = pl.program_id(1)

    @pl.when(step == 0)
    def _():
        total_ref[...] = jnp.zeros_like(total_ref)

    half = pl.num_programs(1) // 2

    @pl.when(step < half)
    def _():
        total_ref[...] += mm(own_ref[...], w_ref[...])

    @pl.when(step >= half)
    def _():
        total_ref[...] += mm(other_ref[...], w_ref[...])

    @pl.when(step == pl.num_programs(1) - 1)
    def _():
        x = total_ref[...].astype(BF16)
        x_ref[...] = x
        for k in range(e_ref.shape[0]):
            rows = slice(k * SPAN, (k + 1) * SPAN)
            columns = rt_ref[0, rows]
            to_end = jnp.exp2(spread_columns(columns[SPAN - 1 : SPAN] - columns))
            scaled = (x[rows].astype(F32) * to_end).astype(BF16)
            e_ref[k] = dot(b_ref[rows], scaled, ((0,), (0,)))


def product_kernel(has_before, has_other, half_ref, g_ref, w_ref, *refs):
    refs = list(refs)
    total = dot(g_ref[...], w_ref[...], ((1,), (1,)))
    if has_before:
        total = total + refs.pop(0)[...].astype(F32)
    if has_other:
        total = total.astype(BF16).astype(F32) + refs.pop(0)[...].astype(F32)
    refs[0][...] = total.astype(BF16)


def arrange_kernel(order_ref, own_ref, other_ref, early_ref, late_ref, both_ref):
    half = own_ref.shape[1]
    both_ref[:, :half] = own_ref[...]
    both_ref[:, half:] = other_ref[...]
    unit = 2 * half // order_ref.shape[0]
    cut = early_ref.shape[1]
    for index in range(order_ref.shape[0]):
        source = pl.ds(pl.multiple_of(order_ref[index] * unit, 128), unit)
        at = index * unit
        if at < cut:
            early_ref[:, at : at + unit] = both_ref[:, source]
        else:
            late_ref[:, at - cut : at - cut + unit] = both_ref[:, source]


TAIL = 16


def message(total, log):
    high, middle, last = thirds(log)
    line = iota((TAIL, total.shape[1]), 0)
    tail = jnp.where(line == 0, high, jnp.where(line == 1, middle, jnp.where(line == 2, last, 0.0)))
    return total.astype(BF16), tail.astype(BF16)


def start_kernel(own_ref, kept_ref, log_ref, sent_ref):
    spans = own_ref.shape[0]
    total = own_ref[spans - 1]
    log = kept_ref[spans - 1, 4:5]
    for k in range(spans - 2, -1, -1):
        total = own_ref[k] + kept_ref[k, :1] * total
        log = log + kept_ref[k, 4:5]
    line = iota(log_ref.shape, 0)
    log_ref[...] = jnp.where(line == 0, log, 0.0)
    n = total.shape[0]
    sent_ref[:n], sent_ref[n:] = message(total, log)


def back_kernel(bit, place_ref, log_ref, mine_ref, got_ref, *refs):
    entering_ref = refs[0] if len(refs) == 5 else None
    entering_out, sent_out, log_out, factor_out = refs[-4:]
    n = entering_out.shape[0]
    got = got_ref[:n].astype(F32)
    tail = got_ref[n:].astype(F32)
    other_log = tail[0:1] + tail[1:2] + tail[2:3]
    log, before_me, after_me = log_ref[0:1], log_ref[1:2], log_ref[2:3]
    line = iota(log_ref.shape, 0)
    upper = (place_ref[0] // bit % 2 + 0 * line[0:1]) == 1
    kept, other = jnp.exp2(log), jnp.exp2(other_log)
    mine = mine_ref[:n].astype(F32)
    total = jnp.where(upper, other, 1.0) * mine + jnp.where(upper, 1.0, kept) * got
    passed = jnp.where(upper, 0.0, jnp.exp2(after_me)) * got
    entering_out[...] = passed if entering_ref is None else entering_ref[...] + passed
    first = jnp.where(upper, 1.0, other)
    second = jnp.where(upper, kept, 1.0)
    third = jnp.where(upper, jnp.exp2(before_me), 0.0)
    factor_out[...] = jnp.where(line == 0, first, jnp.where(line == 1, second, third))
    log = log + other_log
    before_me = jnp.where(upper, before_me + other_log, before_me)
    after_me = jnp.where(upper, after_me, after_me + other_log)
    log_out[...] = jnp.where(line == 0, log, jnp.where(line == 1, before_me, after_me))
    sent_out[:n], sent_out[n:] = message(total, log)


def scan_kernel(last, factor_ref, mine_ref, got_ref, *refs):
    refs = list(refs)
    entering_ref = refs.pop(0) if len(refs) == 3 - last else None
    factors = factor_ref[...]
    got = got_ref[...].astype(F32)
    if not last:
        total = factors[0:1] * mine_ref[...].astype(F32) + factors[1:2] * got
        refs[1][...] = total.astype(BF16)
    passed = factors[2:3] * got
    refs[0][...] = passed if entering_ref is None else entering_ref[...] + passed


def scan_pair_kernel(number, last, *refs):
    first, second, outs = refs[:number], refs[number : number + 4], refs[number + 4 :]
    scan_kernel(False, *first, *outs[:2])
    scan_kernel(last, *second, *outs[2:])


def early_forward_kernel(count, f_ref, *refs):
    pieces, (out_ref, buffer) = refs[:count], refs[count:]
    rows = pieces[0].shape[0]
    for index, piece in enumerate(pieces):
        buffer[index * rows : (index + 1) * rows] = piece[...]
    out_ref[...] = mm(f_ref[...], buffer[...])


def late_forward_kernel(count, f_ref, part_ref, rt_ref, b_ref, kept_ref, *refs):
    pieces, (x_ref, e_ref, sent_ref, buffer) = refs[:count], refs[count:]
    rows = pieces[0].shape[0]
    for index, piece in enumerate(pieces):
        buffer[index * rows : (index + 1) * rows] = piece[...]
    x = (part_ref[...] + mm(f_ref[...], buffer[...])).astype(BF16)
    x_ref[...] = x
    total = None
    for k in range(e_ref.shape[0]):
        part = slice(k * SPAN, (k + 1) * SPAN)
        columns = rt_ref[0, part]
        to_end = jnp.exp2(spread_columns(columns[SPAN - 1 : SPAN] - columns))
        scaled = (x[part].astype(F32) * to_end).astype(BF16)
        state = dot(b_ref[part], scaled, ((0,), (0,)))
        e_ref[k] = state
        total = state if total is None else kept_ref[k, :1] * total + state
    sent_ref[...] = total.astype(BF16)


def blocks_kernel(halves, has_before, order_ref, g_ref, *refs):
    count = len(halves)
    number = sum(halves)
    arrays, refs = refs[:number], refs[number:]
    if has_before:
        refs = refs[2:]
    away_ref, own_ref, buffer, slots, sems, out_sems = refs
    rows = arrays[0].shape[0]
    wide = g_ref.shape[0]
    copies = []
    at = 0
    for index, parts in enumerate(halves):
        mine = []
        for part in range(parts):
            lanes = pl.ds(part * (wide // parts), wide // parts)
            target = buffer.at[pl.ds(index * rows, rows), lanes]
            copy = pltpu.make_async_copy(arrays[at], target, sems.at[at])
            copy.start()
            mine.append(copy)
            at += 1
        copies.append(mine)
    g = g_ref[...]
    half = away_ref.shape[1] // rows
    starts = [0]
    while starts[-1] < count:
        starts.append(starts[-1] + (2 if count - starts[-1] in (2, 4) else 3))
    for index in range(count):
        for copy in copies[index]:
            copy.wait()
        if index + 1 not in starts:
            continue
        start = starts[starts.index(index + 1) - 1]
        product = mm(buffer[start * rows : (index + 1) * rows], g)
        for done in range(start, index + 1):
            part = product[(done - start) * rows : (done - start + 1) * rows]
            slots[done] = part.T.astype(BF16)
            place = order_ref[done]
            lanes = pl.ds(pl.multiple_of(place % half * rows, 128), rows)

            @pl.when(place < half)
            def _():
                target = away_ref.at[:, lanes]
                pltpu.make_async_copy(slots.at[done], target, out_sems.at[done]).start()

            @pl.when(place >= half)
            def _():
                target = own_ref.at[:, lanes]
                pltpu.make_async_copy(slots.at[done], target, out_sems.at[done]).start()

    for index in range(count):
        target = away_ref.at[:, pl.ds(0, rows)]
        pltpu.make_async_copy(slots.at[index], target, out_sems.at[index]).wait()


def after_kernel(*refs):
    pass


def inner_kernel(
    r_ref, rt_ref, g_ref, x_ref, b_ref, c_ref, q_ref, *refs
):
    d_ref, grad_b_ref, grad_c_ref, sum_ref, top_ref, low_ref = refs[-6:]
    so_far = refs[:-6]
    step = pl.program_id(1)
    b = b_ref[...]
    c = c_ref[...]
    scores = dot(b, c, ((1,), (1,)))
    running = r_ref[...]
    columns = rt_ref[0]
    top_keep = iota((HALF, SPAN), 1) >= iota((HALF, SPAN), 0)
    low_keep = iota((HALF, HALF), 1) >= iota((HALF, HALF), 0)

    @pl.when(step == 0)
    def _():
        sum_ref[...] = jnp.zeros_like(sum_ref)
        grad_b_ref[...] = so_far[0][...] if so_far else jnp.zeros_like(grad_b_ref)

    rows = []
    lane = iota((SPAN, 2 * P_SIZE), 1)
    later = not_before().astype(BF16)
    top_less = iota((HALF, SPAN), 1) > iota((HALF, SPAN), 0)
    low_less = iota((HALF, HALF), 1) > iota((HALF, HALF), 0)
    for pair in range(GROUP // 2):
        lanes = slice(pair * 2 * P_SIZE, (pair + 1) * 2 * P_SIZE)
        x = x_ref[:, lanes]
        none = jnp.zeros_like(x)
        x = [jnp.where(lane < P_SIZE, x, none), jnp.where(lane < P_SIZE, none, x)]
        product = mm(jnp.concatenate(x, axis=0), g_ref[:, lanes].T)
        top_sum = low_sum = None
        for number in range(2):
            head = 2 * pair + number
            row = running[head : head + 1]
            at = number * SPAN
            top = jnp.where(top_keep, row - columns[:HALF, head : head + 1], NEVER)
            low = jnp.where(low_keep, row[:, HALF:] - columns[HALF:, head : head + 1], NEVER)
            top = jnp.exp2(top) * product[at : at + HALF]
            low = jnp.exp2(low) * product[at + HALF : at + SPAN, HALF:]
            top_sum = top if number == 0 else top_sum + top
            low_sum = low if number == 0 else low_sum + low
            part = slice(head * HALF, (head + 1) * HALF)
            top_ref[part] = (top * scores[:HALF]).astype(BF16)
            low_ref[part] = (low * scores[HALF:, HALF:]).astype(BF16)
        sum_ref[:HALF] += top_sum
        sum_ref[HALF:, HALF:] += low_sum
    top = mm(top_ref[...], later)
    low = mm(low_ref[...], later[HALF:, HALF:])
    for head in range(GROUP):
        part = slice(head * HALF, (head + 1) * HALF)
        top_row = jnp.sum(jnp.where(top_less, top[part], 0.0), axis=0, keepdims=True)
        low_row = jnp.sum(jnp.where(low_less, low[part], 0.0), axis=0, keepdims=True)
        rows.append(jnp.concatenate([top_row[:, :HALF], top_row[:, HALF:] + low_row], axis=1))
    to_end = jnp.exp2(spread_columns(columns[SPAN - 1 : SPAN] - columns))
    scaled = x_ref[...].astype(F32) * to_end
    ends = dot(one_hot(BF16), (scaled * mm(b, q_ref[0])).astype(BF16), ((1,), (1,)))
    d_ref[...] = jnp.concatenate(rows, axis=0) + sum_over(ends, before())
    grad_b_ref[...] += dot(scaled.astype(BF16), q_ref[0], ((1,), (1,)))

    @pl.when(step == pl.num_programs(1) - 1)
    def _():
        total = sum_ref[...].astype(BF16)
        grad_b_ref[...] += mm(total, c)
        part = dot(total, b, ((0,), (0,)))
        grad_c_ref[...] = part + so_far[1][...] if so_far else part


def state_kernel(
    rt_ref, g_ref, c_ref, s_ref, e_ref, q_ref, a_ref, d_part_ref, c_part_ref, *refs
):
    d_ref, grad_c_ref, held = refs[-3:]
    span, group = pl.program_id(0), pl.program_id(1)

    @pl.when(group == 0)
    def _():
        grad_c_ref[...] = c_part_ref[...]

    @pl.when(span == 0)
    def _():
        held[group] = s_ref[...]

    state = held[group]
    low = state.astype(BF16)
    scaled = g_ref[...].astype(F32) * jnp.exp2(spread_columns(rt_ref[0]))
    ends = dot(one_hot(BF16), (scaled * mm(c_ref[...], low)).astype(BF16), ((1,), (1,)))
    grad_c_ref[...] += dot(scaled.astype(BF16), low, ((1,), (1,)))
    product = jnp.sum(q_ref[0].astype(F32) * state, axis=0, keepdims=True) * a_ref[0, :1]
    high, middle, last = thirds(product)
    row = iota((8, WIDE), 0)
    stacked = jnp.where(row == 0, high, jnp.where(row == 1, middle, jnp.where(row == 2, last, 0.0)))
    kept = dot(one_hot(BF16), stacked.astype(BF16), ((1,), (1,)))
    kept = jnp.sum(kept, axis=1, keepdims=True)
    d_ref[...] = d_part_ref[...] + sum_over(ends, not_before()) + kept
    held[group] = e_ref[0] + a_ref[0, :1] * state


def call(kernel, grid, in_specs, out_specs, out_shape, flops, size, scratch=()):
    return pl.pallas_call(
        kernel,
        grid=grid,
        in_specs=in_specs,
        out_specs=out_specs,
        out_shape=out_shape,
        scratch_shapes=list(scratch),
        cost_estimate=pl.CostEstimate(flops=flops, bytes_accessed=size, transcendentals=0),
        compiler_params=pltpu.CompilerParams(
            dimension_semantics=("arbitrary",) * len(grid), vmem_limit_bytes=GRANT
        ),
    )


def run_spec(at=0):
    return pl.BlockSpec((GROUP, SPAN), lambda k, h: (h + at, k))


def run_t_spec(at=0):
    return pl.BlockSpec((1, SPAN, GROUP), lambda k, h: (h + at, k, 0))


def rows_spec(at=0):
    return pl.BlockSpec((SPAN, WIDE), lambda k, h: (k, h + at))


def state_spec(at=0):
    return pl.BlockSpec((1, 2 * P_SIZE, WIDE), lambda k, h: (k, 0, h + at))


def kept_spec(at=0):
    return pl.BlockSpec((1, 8, WIDE), lambda k, h: (k, 0, h + at))


SHARED = pl.BlockSpec((SPAN, 2 * P_SIZE), lambda k, h: (k, 0))
GAIN = pl.BlockSpec((1, WIDE), lambda k, h: (0, h))
ANYWHERE = pl.BlockSpec(memory_space=pl.ANY)
INNER_SCRATCH = [
    pltpu.VMEM((SPAN, SPAN), F32),
    pltpu.VMEM((GROUP * HALF, SPAN), BF16),
    pltpu.VMEM((GROUP * HALF, HALF), BF16),
]
SCALARS = pl.BlockSpec(memory_space=pltpu.SMEM)


def shape(*dims, dtype=F32):
    return jax.ShapeDtypeStruct(dims, dtype)


def swap(value, axis, bit):
    count = lax.axis_size(axis)
    return lax.ppermute(value, axis, [(i, i ^ bit) for i in range(count)])


def block_products(kept):
    count = lax.axis_size("ctx")
    place = lax.axis_index("ctx")
    steps = []
    before_me = jnp.ones_like(kept)
    after_me = jnp.ones_like(kept)
    bit = 1
    while bit < count:
        other = swap(kept, "ctx", bit)
        upper = (place & bit) != 0
        steps.append((bit, upper, kept, other, before_me, after_me))
        before_me = jnp.where(upper, before_me * other, before_me)
        after_me = jnp.where(upper, after_me, after_me * other)
        kept = kept * other
        bit *= 2
    return steps


def scan_states(total, steps, reverse):
    entering = jnp.zeros_like(total)
    for bit, upper, kept, other, before_me, after_me in steps:
        got = swap(total.astype(BF16), "ctx", bit).astype(F32)
        if reverse:
            entering = entering + jnp.where(upper, 0.0, after_me) * got
            total = jnp.where(upper, got + other * total, total + kept * got)
        else:
            entering = entering + jnp.where(upper, before_me, 0.0) * got
            total = jnp.where(upper, kept * got + total, other * total + got)
    return entering


def head_sum(value):
    bit = 1
    while bit < lax.axis_size("head"):
        value = value.astype(BF16)
        value = value.astype(F32) + swap(value, "head", bit).astype(F32)
        bit *= 2
    return value


PLANE = 4


def after(values, *tokens):
    out = pl.pallas_call(
        after_kernel,
        in_specs=[ANYWHERE] * (len(values) + len(tokens)),
        out_specs=[ANYWHERE] * len(values),
        out_shape=[shape(*value.shape, dtype=value.dtype) for value in values],
        input_output_aliases={index: index for index in range(len(values))},
        cost_estimate=pl.CostEstimate(flops=0, bytes_accessed=0, transcendentals=0),
        compiler_params=pltpu.CompilerParams(vmem_limit_bytes=GRANT),
    )(*values, *tokens)
    return list(out)


def along_z(value, moves):
    pairs = [(a * PLANE + i, b * PLANE + i) for a, b in moves for i in range(PLANE)]
    return lax.ppermute(value, "ctx", pairs)


MIDDLE = ((1, 2), (2, 1))
OUTWARD = ((1, 0), (2, 3))


def swap_x(value):
    return swap(value, "ctx", 1)


def swap_y(value):
    return swap(value, "ctx", 2)


LAYERS = ((0, 1, 2, 3), (1, 0, 3, 2), (2, 2, 1, 1), (3, 3, 0, 0))
EARLY = [(k, flip) for k in (0, 1, 2) for flip in range(3)]
LATE = [(0, 3), (1, 3), (2, 3), (3, 0), (3, 1), (3, 2), (3, 3)]


def block_order():
    place = lax.axis_index("ctx")
    layer, spot = place // PLANE, place % PLANE
    layers = jnp.array(LAYERS, jnp.int32)[:, layer]
    order = [layers[k] * PLANE + (spot ^ flip) for k, flip in EARLY + LATE]
    return jnp.stack(order).astype(jnp.int32)


def gather_weight(w, sizes):
    ends = [sum(sizes[: j + 1]) * P_SIZE for j in range(len(sizes))]
    parts = [w[:, end - size * P_SIZE : end] for end, size in zip(ends, sizes)]
    return [lax.all_gather(part, "ctx", axis=0, tiled=True) for part in parts]


def forward(features, first, weight, running_t, b_rows, here):
    own, other = features
    length = own.shape[0]
    n = b_rows.shape[1]
    width, wide = weight.shape
    deep = width // 4
    spans = length // SPAN

    def depth(k, first_ref):
        return (k // 2 ^ first_ref[0]) * 2 + k % 2

    return pl.pallas_call(
        forward_kernel,
        grid_spec=pltpu.PrefetchScalarGridSpec(
            num_scalar_prefetch=1,
            grid=(wide // WIDE, 4),
            in_specs=[
                pl.BlockSpec((length, deep), lambda h, k, first_ref: (0, jnp.minimum(k, 1))),
                pl.BlockSpec((length, deep), lambda h, k, first_ref: (0, jnp.maximum(k - 2, 0))),
                pl.BlockSpec((deep, WIDE), lambda h, k, first_ref: (depth(k, first_ref), h)),
                pl.BlockSpec((1, length, GROUP), lambda h, k, first_ref: (h + here, 0, 0)),
                pl.BlockSpec((length, n), lambda h, k, first_ref: (0, 0)),
            ],
            out_specs=[
                pl.BlockSpec((length, WIDE), lambda h, k, first_ref: (0, h)),
                pl.BlockSpec((spans, n, WIDE), lambda h, k, first_ref: (0, 0, h)),
            ],
            scratch_shapes=[pltpu.VMEM((length, WIDE), F32)],
        ),
        out_shape=[shape(length, wide, dtype=BF16), shape(spans, n, wide)],
        cost_estimate=pl.CostEstimate(
            flops=2 * length * wide * width, bytes_accessed=2 * wide * width, transcendentals=0
        ),
        compiler_params=pltpu.CompilerParams(
            dimension_semantics=("arbitrary", "arbitrary"), vmem_limit_bytes=GRANT
        ),
    )(first, own, other, weight, running_t, b_rows)


def multiply(grad_x, weight, at, half, halves, before=None, other=None):
    length = grad_x.shape[0]
    width, wide = weight.shape
    tiles = width // halves // WIDE
    tile = pl.BlockSpec((length, WIDE), lambda j, half_ref: (0, half_ref[0] * tiles + j))
    plain = pl.BlockSpec((length, WIDE), lambda j, half_ref: (0, j))
    in_specs = [
        pl.BlockSpec((length, wide), lambda j, half_ref: (0, at)),
        pl.BlockSpec((WIDE, wide), lambda j, half_ref: (half_ref[0] * tiles + j, 0)),
    ]
    operands = [grad_x, weight]
    if before is not None:
        in_specs.append(tile)
        operands.append(before)
    if other is not None:
        in_specs.append(plain)
        operands.append(other)
    return pl.pallas_call(
        functools.partial(product_kernel, before is not None, other is not None),
        grid_spec=pltpu.PrefetchScalarGridSpec(
            num_scalar_prefetch=1,
            grid=(tiles,),
            in_specs=in_specs,
            out_specs=plain,
        ),
        out_shape=shape(length, width // halves, dtype=BF16),
        cost_estimate=pl.CostEstimate(
            flops=2 * length * wide * width // halves,
            bytes_accessed=2 * wide * width // halves,
            transcendentals=0,
        ),
        compiler_params=pltpu.CompilerParams(
            dimension_semantics=("arbitrary",), vmem_limit_bytes=GRANT
        ),
    )(half, *operands)


def early_forward(features, pieces):
    length = features.shape[0]
    rows, columns = pieces[0].shape
    deep = rows * len(pieces)
    return call(
        functools.partial(early_forward_kernel, len(pieces)),
        (columns // WIDE,),
        [pl.BlockSpec((length, deep), lambda h: (0, 0))]
        + [pl.BlockSpec((rows, WIDE), lambda h: (0, h))] * len(pieces),
        pl.BlockSpec((length, WIDE), lambda h: (0, h)),
        shape(length, columns),
        2 * length * columns * deep,
        2 * columns * deep,
        [pltpu.VMEM((deep, WIDE), BF16)],
    )(features, *pieces)


def late_forward(features, part, pieces, running_t, b_rows, kept, here):
    length = features.shape[0]
    rows, columns = pieces[0].shape
    deep = rows * len(pieces)
    n = b_rows.shape[1]
    spans = length // SPAN
    state = pl.BlockSpec((n, WIDE), lambda h: (0, h))
    return call(
        functools.partial(late_forward_kernel, len(pieces)),
        (columns // WIDE,),
        [
            pl.BlockSpec((length, deep), lambda h: (0, 0)),
            pl.BlockSpec((length, WIDE), lambda h: (0, h + here)),
            pl.BlockSpec((1, length, GROUP), lambda h: (h + here, 0, 0)),
            pl.BlockSpec((length, n), lambda h: (0, 0)),
            pl.BlockSpec((spans, 8, WIDE), lambda h: (0, 0, h + here)),
        ]
        + [pl.BlockSpec((rows, WIDE), lambda h: (0, h))] * len(pieces),
        [
            pl.BlockSpec((length, WIDE), lambda h: (0, h)),
            pl.BlockSpec((spans, n, WIDE), lambda h: (0, 0, h)),
            state,
        ],
        [
            shape(length, columns, dtype=BF16),
            shape(spans, n, columns),
            shape(n, columns, dtype=BF16),
        ],
        2 * length * columns * deep,
        2 * columns * deep,
        [pltpu.VMEM((deep, WIDE), BF16)],
    )(features, part, running_t, b_rows, kept, *pieces)


def multiply_blocks(order, grad_x, pieces, so_far):
    columns, length = grad_x.shape
    arrays = [array for piece in pieces for array in piece]
    rows = arrays[0].shape[0]
    count = len(pieces)
    half = shape(length, lax.axis_size("ctx") * rows // 2, dtype=BF16)
    first = 2 + len(arrays)
    return pl.pallas_call(
        functools.partial(blocks_kernel, [len(piece) for piece in pieces], bool(so_far)),
        grid=(1,),
        in_specs=[SCALARS, pl.BlockSpec((columns, length), lambda h: (0, 0))]
        + [ANYWHERE] * (len(arrays) + len(so_far)),
        out_specs=[ANYWHERE, ANYWHERE],
        out_shape=[half, half],
        input_output_aliases={first + k: k for k in range(len(so_far))},
        scratch_shapes=[
            pltpu.VMEM((rows * count, columns), BF16),
            pltpu.VMEM((count, length, rows), BF16),
            pltpu.SemaphoreType.DMA((len(arrays),)),
            pltpu.SemaphoreType.DMA((count,)),
        ],
        cost_estimate=pl.CostEstimate(
            flops=2 * length * columns * rows * count,
            bytes_accessed=2 * columns * rows * count,
            transcendentals=0,
        ),
        compiler_params=pltpu.CompilerParams(
            dimension_semantics=("arbitrary",), vmem_limit_bytes=GRANT
        ),
    )(order, grad_x, *arrays, *so_far)


def back_start(own_grads, kept):
    spans, n, columns = own_grads.shape
    return call(
        start_kernel,
        (columns // WIDE,),
        [
            pl.BlockSpec((spans, n, WIDE), lambda h: (0, 0, h)),
            pl.BlockSpec((spans, 8, WIDE), lambda h: (0, 0, h)),
        ],
        [pl.BlockSpec((rows, WIDE), lambda h: (0, h)) for rows in (8, n + TAIL)],
        [shape(8, columns), shape(n + TAIL, columns, dtype=BF16)],
        0,
        14 * n * columns,
    )(own_grads, kept)


def back_step(place, log, sent, entering, bit):
    got = swap(sent, "ctx", bit)
    columns = sent.shape[1]
    n = sent.shape[0] - TAIL
    short, state, tall = [
        pl.BlockSpec((rows, 2 * WIDE), lambda h: (0, h)) for rows in (8, n, n + TAIL)
    ]
    return call(
        functools.partial(back_kernel, bit),
        (columns // (2 * WIDE),),
        [SCALARS, short, tall, tall] + [state] * len(entering),
        [state, tall, short, short],
        [
            shape(n, columns),
            shape(n + TAIL, columns, dtype=BF16),
            shape(8, columns),
            shape(8, columns),
        ],
        0,
        14 * n * columns,
    )(place, log, sent, got, *entering)


def scan_step(factors, here, sent, entering, bit, last=False):
    got = swap(sent, "ctx", bit)
    n, columns = sent.shape
    block = pl.BlockSpec((n, columns), lambda h: (0, 0))
    at = here * WIDE // columns
    outs = [shape(n, columns), shape(n, columns, dtype=BF16)][: 2 - last]
    return call(
        functools.partial(scan_kernel, last),
        (1,),
        [pl.BlockSpec((8, columns), lambda h: (0, at)), block, block] + [block] * len(entering),
        [block] * len(outs),
        outs,
        0,
        10 * n * columns,
    )(factors, sent, got, *entering)


def scan_pair(first, second, last=False):
    operands, specs, outs = [], [], []
    for factors, here, sent, entering, bit in (first, second):
        got = swap(sent, "ctx", bit)
        n, columns = sent.shape
        block = pl.BlockSpec((n, columns), lambda h: (0, 0))
        at = here * WIDE // columns
        operands += [factors, sent, got, *entering]
        specs += [pl.BlockSpec((8, columns), lambda h, at=at: (0, at))]
        specs += [block] * (2 + len(entering))
        outs += [shape(n, columns), shape(n, columns, dtype=BF16)]
    outs = outs[: 4 - last]
    return call(
        functools.partial(scan_pair_kernel, 3 + len(first[3]), last),
        (1,),
        specs,
        [block] * len(outs),
        outs,
        0,
        20 * n * columns,
    )(*operands)


def local(inputs, w_in, b_rows, c_rows, log_decay, skip_gain, grad_out):
    groups = log_decay.shape[0] // GROUP
    layered = lax.axis_size("ctx") == 4 * PLANE and lax.axis_size("head") == 2
    if layered and groups % 2 == 0 and w_in.shape[0] == 256:
        return local_layered(inputs, w_in, b_rows, c_rows, log_decay, skip_gain, grad_out)
    return local_plain(inputs, w_in, b_rows, c_rows, log_decay, skip_gain, grad_out)


def prepare(log_decay, grad_out, c_rows):
    length, columns = grad_out.shape
    heads = log_decay.shape[0]
    spans = length // SPAN
    groups = heads // GROUP
    n = c_rows.shape[1]
    return call(
        decay_kernel,
        (spans, groups),
        [run_spec(), rows_spec(), SHARED],
        [run_spec(), run_t_spec(), kept_spec(), state_spec()],
        [
            shape(heads, length),
            shape(groups, length, GROUP),
            shape(spans, 8, columns),
            shape(spans, n, columns),
        ],
        2 * length * columns * n,
        6 * length * columns,
    )(log_decay, grad_out, c_rows)


def inner(grid, here, wide, operands, so_far):
    length = operands[2].shape[0]
    n = operands[4].shape[1]
    specs = [
        run_spec(here),
        run_t_spec(here),
        rows_spec(here),
        rows_spec(),
        SHARED,
        SHARED,
        state_spec(here),
    ]
    return call(
        inner_kernel,
        grid,
        specs + [SHARED] * len(so_far),
        [run_spec(), SHARED, SHARED],
        [shape(wide // P_SIZE, length), shape(length, n), shape(length, n)],
        12 * length * wide * SPAN,
        6 * length * wide,
        INNER_SCRATCH,
    )(*operands, *so_far)


def state_terms(grid, here, wide, operands, heads=None, so_far=None):
    length = operands[1].shape[0]
    n = operands[2].shape[1]
    heads = heads or wide // P_SIZE
    at = here if heads > wide // P_SIZE else 0
    extra = () if so_far is None else (so_far,)
    return pl.pallas_call(
        state_kernel,
        grid=grid,
        in_specs=[
            run_t_spec(here),
            rows_spec(here),
            SHARED,
            pl.BlockSpec((n, WIDE), lambda k, h: (0, h)),
            state_spec(),
            state_spec(here),
            kept_spec(here),
            run_spec(),
            SHARED,
        ]
        + [ANYWHERE] * len(extra),
        out_specs=[run_spec(at), SHARED],
        out_shape=[shape(heads, length), shape(length, n)],
        scratch_shapes=[pltpu.VMEM((grid[1], n, WIDE), F32)],
        input_output_aliases={len(operands): 0} if extra else {},
        cost_estimate=pl.CostEstimate(
            flops=4 * length * wide * n, bytes_accessed=6 * length * wide, transcendentals=0
        ),
        compiler_params=pltpu.CompilerParams(
            dimension_semantics=("arbitrary", "arbitrary"), vmem_limit_bytes=GRANT
        ),
    )(*operands, *extra)


def local_layered(inputs, w_in, b_rows, c_rows, log_decay, skip_gain, grad_out):
    length, columns = grad_out.shape
    heads = log_decay.shape[0]
    spans = length // SPAN
    groups = heads // GROUP
    place = lax.axis_index("head").astype(jnp.int32)
    half = columns // 2
    order = block_order()
    blocks = order.shape[0]
    width = blocks * w_in.shape[0]

    z1, inner2 = swap(w_in, "ctx", PLANE), along_z(w_in, MIDDLE)
    own_x, own_y = swap_x(w_in), swap_y(w_in)
    other = swap(inputs, "head", 1)
    running, running_t, kept, own_grads = prepare(log_decay, grad_out, c_rows)
    spot = lax.axis_index("ctx").astype(jnp.int32)[None]
    log, sent = back_start(own_grads, kept)
    sent = after([sent], other)[0]
    leaving, moved, log, factors_1 = back_step(spot, log, sent, (), 1)

    z1, inner2, own_y = after([z1, inner2, own_y], own_x, sent)
    sent = moved
    x1, y1 = swap_x(z1), swap_y(z1)
    inner3, outer2 = along_z(z1, MIDDLE), along_z(inner2, OUTWARD)
    own_y_a, own_y_b = own_y[:, :half], own_y[:, half:]
    leaving, sent, log, factors_2 = back_step(spot, log, sent, (leaving,), 2)
    order_own = (order + place * (blocks // 2)) % blocks
    cut = len(EARLY) * w_in.shape[0]
    early_features, late_features = call(
        arrange_kernel,
        (1,),
        [SCALARS] + [pl.BlockSpec((length, width // 2), lambda h: (0, 0))] * 2,
        [pl.BlockSpec((length, wide), lambda h: (0, 0)) for wide in (cut, width - cut)],
        [shape(length, wide, dtype=BF16) for wide in (cut, width - cut)],
        0,
        4 * length * width,
        [pltpu.VMEM((length, width), BF16)],
    )(order_own, inputs, other)

    inner2, inner3, outer2, x1, own_y_a, own_y_b = after(
        [inner2, inner3, outer2, x1, own_y_a, own_y_b], y1, early_features, moved
    )
    z3 = inner2 + outer2
    x3, y3 = swap_x(z3), swap_y(z3)
    outer3 = along_z(inner3, OUTWARD)
    x1_a, x1_b = x1[:, :half], x1[:, half:]
    leaving, sent, log, factors_4 = back_step(spot, log, sent, (leaving,), 4)

    inner3, outer3, y3, x1_a, x1_b = after([inner3, outer3, y3, x1_a, x1_b], x3)
    z2a = inner3[:, :half] + outer3[:, :half]
    z2b = inner3[:, half:] + outer3[:, half:]
    y3_a, y3_b = y3[:, :half], y3[:, half:]
    x2a, y2a = swap_x(z2a), swap_y(z2a)
    d3a, d1a = swap_x(y3_a), swap_y(x1_a)
    leaving, sent, log, factors_8 = back_step(spot, log, sent, (leaving,), 8)
    early = [w_in, own_x, own_y, z1, x1, y1, z3, x3, y3]
    part = early_forward(early_features, early)

    own_y_a, x2a, z2b, leaving = after([own_y_a, x2a, z2b, leaving], y2a, d3a, d1a, part)
    d0a, d2a = swap_x(own_y_a), swap_y(x2a)
    leaving_all = [leaving]
    for k in range(spans - 1, 0, -1):
        leaving_all.insert(0, own_grads[k] + kept[k, :1] * leaving_all[0])
    leaving_all = jnp.stack([value.astype(BF16) for value in leaving_all])
    (z2b,) = after([z2b], leaving_all)
    x2b, y2b = swap_x(z2b), swap_y(z2b)
    skip = jnp.repeat(skip_gain, P_SIZE)[None]
    grad_x = grad_rows(running, running_t, grad_out, b_rows, c_rows, leaving_all, skip, True)
    order_away = (order + (1 - place) * (blocks // 2)) % blocks
    early_order, late_order = order_away[: len(EARLY)], order_away[len(EARLY) :]
    late_a = [d0a, d1a, d3a, z2a, x2a, y2a, d2a]
    x_a, states_a, sent_a = late_forward(
        late_features, part, late_a, running_t, b_rows, kept, 0
    )

    own_y_b, x2b, y3_b, x1_b, sent_a, x_a, grad_x = after(
        [own_y_b, x2b, y3_b, x1_b, sent_a, x_a, grad_x], y2b
    )
    d0b, d2b = swap_x(own_y_b), swap_y(x2b)
    d3b, d1b = swap_x(y3_b), swap_y(x1_b)
    entering_a, sent_a = scan_step(factors_1, 0, sent_a, (), 1)
    product = multiply_blocks(early_order, grad_x, [[piece] for piece in early], ())
    shared = (running, running_t, grad_out)
    here = groups // 2
    grid = (spans, here)
    inner_a = shared + (x_a, b_rows, c_rows, leaving_all)
    decay_a, grad_b, grad_c = inner(grid, 0, half, inner_a, ())

    d0b, d2b = after([d0b, d2b], d3b, d1b, sent_a, grad_b, product[0])
    late_b = [d0b, d1b, d3b, z2b, x2b, y2b, d2b]
    x_b, states_b, sent_b = late_forward(
        late_features, part, late_b, running_t, b_rows, kept, here
    )
    pairs = list(zip(late_a, late_b))
    sent_a, sent_b, *product = after([sent_a, sent_b, *product])
    entering_b, sent_b, entering_a, sent_a = scan_pair(
        (factors_1, here, sent_b, (), 1), (factors_2, 0, sent_a, (entering_a,), 2)
    )
    away, own = multiply_blocks(late_order, grad_x, pairs, product)

    sent_a, sent_b, x_b, away = after([sent_a, sent_b, x_b, away])
    entering_b, sent_b, entering_a, sent_a = scan_pair(
        (factors_2, here, sent_b, (entering_b,), 2), (factors_4, 0, sent_a, (entering_a,), 4)
    )
    got = swap(away, "head", 1)

    sent_a, sent_b, x_b = after([sent_a, sent_b, x_b])
    entering_b, sent_b, entering_a = scan_pair(
        (factors_4, here, sent_b, (entering_b,), 4),
        (factors_8, 0, sent_a, (entering_a,), 8),
        True,
    )
    inner_b = shared + (x_b, b_rows, c_rows, leaving_all)
    decay_b, grad_b, grad_c = inner(grid, here, half, inner_b, (grad_b, grad_c))

    sent_b, entering_a, got, grad_b = after([sent_b, entering_a, got, grad_b])
    grad_b = head_sum(grad_b)
    grad_inputs = (own.astype(F32) + got.astype(F32)).astype(BF16)
    (entering_b,) = scan_step(factors_8, here, sent_b, (entering_b,), 8, True)
    common = (running_t, grad_out, c_rows)
    state_a = common + (entering_a, states_a, leaving_all, kept, decay_a, grad_c)
    decays, grad_c = state_terms(grid, 0, half, state_a, heads)
    (entering_b,) = after([entering_b], grad_inputs, grad_c)
    state_b = common + (entering_b, states_b, leaving_all, kept, decay_b, grad_c)
    decays, grad_c = state_terms(grid, here, half, state_b, heads, decays)
    return (grad_inputs, grad_b, head_sum(grad_c), decays)


def grad_rows(running, running_t, grad_out, b_rows, c_rows, leaving, skip, transposed):
    length, columns = grad_out.shape
    spec, dims = rows_spec(), (length, columns)
    if transposed:
        spec, dims = pl.BlockSpec((WIDE, SPAN), lambda k, h: (h, k)), (columns, length)
    return call(
        functools.partial(grad_x_kernel, transposed),
        (length // SPAN, running_t.shape[0]),
        [run_spec(), run_t_spec(), rows_spec(), SHARED, SHARED, state_spec(), GAIN],
        spec,
        shape(*dims, dtype=BF16),
        8 * length * columns * SPAN,
        6 * length * columns,
    )(running, running_t, grad_out, b_rows, c_rows, leaving, skip)


def local_plain(inputs, w_in, b_rows, c_rows, log_decay, skip_gain, grad_out):
    length, columns = grad_out.shape
    heads = log_decay.shape[0]
    spans = length // SPAN
    groups = heads // GROUP
    n = b_rows.shape[1]
    grid = (spans, groups)

    sizes = (heads // 2, heads // 4, heads // 4) if heads % (4 * GROUP) == 0 else (heads,)
    weights = gather_weight(w_in, sizes)
    two = lax.axis_size("head") == 2
    place = lax.axis_index("head").astype(jnp.int32)[None]
    width = weights[0].shape[0]
    if two:
        features = (inputs, swap(inputs, "head", 1))
        first = place
    else:
        features = lax.all_gather(inputs, "head", axis=1, tiled=True)
        features = (features[:, : width // 2], features[:, width // 2 :])
        first = jnp.zeros((1,), jnp.int32)

    running, running_t, kept, own_grads = call(
        decay_kernel,
        grid,
        [run_spec(), rows_spec(), SHARED],
        [run_spec(), run_t_spec(), kept_spec(), state_spec()],
        [
            shape(heads, length),
            shape(groups, length, GROUP),
            shape(spans, 8, columns),
            shape(spans, n, columns),
        ],
        2 * length * columns * n,
        6 * length * columns,
    )(log_decay, grad_out, c_rows)

    kept_total = kept[0, :1]
    for k in range(1, spans):
        kept_total = kept_total * kept[k, :1]
    steps = block_products(kept_total)

    total = own_grads[spans - 1]
    for k in range(spans - 2, -1, -1):
        total = own_grads[k] + kept[k, :1] * total
    leaving = [scan_states(total, steps, True)]
    for k in range(spans - 1, 0, -1):
        leaving.insert(0, own_grads[k] + kept[k, :1] * leaving[0])
    leaving = jnp.stack([value.astype(BF16) for value in leaving])

    skip = jnp.repeat(skip_gain, P_SIZE)[None]
    grad_x = grad_rows(running, running_t, grad_out, b_rows, c_rows, leaving, skip, False)

    grad_b = grad_c = product = None
    tokens = ()
    decay_parts = []
    at = 0
    for index, size in enumerate(sizes):
        wide = size * P_SIZE
        here = at // GROUP
        count = size // GROUP
        weight = weights[index]
        if tokens:
            weight = after([weight], *tokens)[0]
        x, own_states = forward(features, first, weight, running_t, b_rows, here)

        chunk = slice(at * P_SIZE, at * P_SIZE + wide)
        total = own_states[0]
        for k in range(1, spans):
            total = kept[k, :1, chunk] * total + own_states[k]
        cut = [step[:2] + tuple(value[:, chunk] for value in step[2:]) for step in steps]
        entering = scan_states(total, cut, False)

        so_far = () if grad_b is None else (grad_b, grad_c)
        decay_part, grad_b, grad_c = call(
            inner_kernel,
            (spans, count),
            [
                run_spec(here),
                run_t_spec(here),
                rows_spec(here),
                rows_spec(),
                SHARED,
                SHARED,
                state_spec(here),
            ]
            + [SHARED] * len(so_far),
            [run_spec(), SHARED, SHARED],
            [shape(size, length), shape(length, n), shape(length, n)],
            12 * length * wide * SPAN,
            6 * length * wide,
            INNER_SCRATCH,
        )(running, running_t, grad_out, x, b_rows, c_rows, leaving, *so_far)
        decay_part, grad_c = call(
            state_kernel,
            (spans, count),
            [
                run_t_spec(here),
                rows_spec(here),
                SHARED,
                pl.BlockSpec((n, WIDE), lambda k, h: (0, h)),
                state_spec(),
                state_spec(here),
                kept_spec(here),
                run_spec(),
                SHARED,
            ],
            [run_spec(), SHARED],
            [shape(size, length), shape(length, n)],
            4 * length * wide * n,
            6 * length * wide,
            [pltpu.VMEM((count, n, WIDE), F32)],
        )(running_t, grad_out, c_rows, entering, own_states, leaving, kept, decay_part, grad_c)
        decay_parts.append(decay_part)

        if index < len(sizes) - 1:
            zero = jnp.zeros((1,), jnp.int32)
            product = multiply(grad_x, weight, at // size, zero, 1, product)
            tokens = (product, grad_b, entering)
        elif two:
            sent = multiply(grad_x, weight, at // size, 1 - place, 2, product)
            got = swap(sent, "head", 1)
            grad_inputs = multiply(grad_x, weight, at // size, place, 2, product, got)
        else:
            zero = jnp.zeros((1,), jnp.int32)
            product = multiply(grad_x, weight, at // size, zero, 1, product)
            grad_inputs = lax.psum_scatter(product, "head", scatter_dimension=1, tiled=True)
        at += size

    return (grad_inputs, head_sum(grad_b), head_sum(grad_c), jnp.concatenate(decay_parts, axis=0))


def solution(mesh):
    in_specs = (
        P("ctx", "head"),
        P("ctx", "head"),
        P("ctx", None),
        P("ctx", None),
        P("head", "ctx"),
        P("head"),
        P("ctx", "head"),
    )
    out_specs = (P("ctx", "head"), P("ctx", None), P("ctx", None), P("head", "ctx"))
    return jax.shard_map(local, mesh=mesh, in_specs=in_specs, out_specs=out_specs, check_vma=False)
```

```python
import functools

import jax
import jax.numpy as jnp
from jax import lax
from jax.experimental import pallas as pl
from jax.experimental.pallas import tpu as pltpu
from jax.sharding import PartitionSpec as P

SPAN = 256
HALF = SPAN // 2
P_SIZE = 64
GROUP = 8
WIDE = GROUP * P_SIZE
LOG2E = 1.4426950408889634
NEVER = -1e30
GRANT = 64 * 2**20

F32 = jnp.float32
BF16 = jnp.bfloat16
EXACT = lax.Precision.HIGHEST


def dot(a, b, dims, precision=None):
    return lax.dot_general(a, b, (dims, ((), ())), precision=precision, preferred_element_type=F32)


def mm(a, b, precision=None):
    return dot(a, b, ((1,), (0,)), precision)


def iota(shape, dim):
    return lax.broadcasted_iota(jnp.int32, shape, dim)


def one_hot(dtype):
    return (iota((GROUP, WIDE), 0) == iota((GROUP, WIDE), 1) // P_SIZE).astype(dtype)


def not_before():
    return (iota((SPAN, SPAN), 0) >= iota((SPAN, SPAN), 1)).astype(F32)


def before():
    return (iota((SPAN, SPAN), 0) < iota((SPAN, SPAN), 1)).astype(F32)


def same():
    return (iota((SPAN, SPAN), 0) == iota((SPAN, SPAN), 1)).astype(F32)


def first_head():
    return iota((SPAN, 2 * P_SIZE), 1) < P_SIZE


def pair_columns(columns, pair):
    shape = (columns.shape[0], 2 * P_SIZE)
    left = jnp.broadcast_to(columns[:, 2 * pair : 2 * pair + 1], shape)
    right = jnp.broadcast_to(columns[:, 2 * pair + 1 : 2 * pair + 2], shape)
    return jnp.where(iota(shape, 1) < P_SIZE, left, right)


def spread_columns(columns):
    return jnp.concatenate([pair_columns(columns, pair) for pair in range(GROUP // 2)], axis=1)


def thirds(value):
    high = value.astype(BF16).astype(F32)
    middle = (value - high).astype(BF16).astype(F32)
    return high, middle, value - high - middle


def sum_over(value, mask):
    rows = value.shape[0]
    parts = mm(jnp.concatenate(thirds(value), axis=0).astype(BF16), mask.astype(BF16))
    return parts[:rows] + parts[rows : 2 * rows] + parts[2 * rows :]


def decay_kernel(d_ref, g_ref, c_ref, r_ref, rt_ref, a_ref, gt_ref):
    row_sums = sum_over(d_ref[...] * LOG2E, 1.0 - not_before() + same())
    r_ref[...] = row_sums
    padded = jnp.concatenate([row_sums, jnp.zeros((2 * P_SIZE - GROUP, SPAN), F32)], axis=0)
    running = padded.T[:, :GROUP]
    rt_ref[0] = running
    growth = jnp.exp2(spread_columns(running))
    last = spread_columns(running[SPAN - 1 : SPAN])
    a_ref[0] = jnp.where(iota((8, WIDE), 0) < 4, jnp.exp2(last), last)
    scaled = (g_ref[...].astype(F32) * growth).astype(BF16)
    gt_ref[0] = dot(c_ref[...], scaled, ((0,), (0,)))


def grad_x_kernel(transposed, r_ref, rt_ref, g_ref, b_ref, c_ref, q_ref, skip_ref, out_ref):
    b = b_ref[...]
    scores = dot(b, c_ref[...], ((1,), (1,)))
    running = r_ref[...]
    columns = rt_ref[0]
    top_keep = iota((HALF, SPAN), 1) >= iota((HALF, SPAN), 0)
    low_keep = iota((HALF, HALF), 1) >= iota((HALF, HALF), 0)
    to_end = jnp.exp2(spread_columns(columns[SPAN - 1 : SPAN] - columns))
    from_state = mm(b, q_ref[0]) * to_end
    for pair in range(GROUP // 2):
        lanes = slice(pair * 2 * P_SIZE, (pair + 1) * 2 * P_SIZE)
        g = g_ref[:, lanes]
        parts = []
        for head in (2 * pair, 2 * pair + 1):
            row = running[head : head + 1]
            top = jnp.where(top_keep, row - columns[:HALF, head : head + 1], NEVER)
            low = jnp.where(low_keep, row[:, HALF:] - columns[HALF:, head : head + 1], NEVER)
            parts.append((jnp.exp2(top) * scores[:HALF]).astype(BF16))
            low = (jnp.exp2(low) * scores[HALF:, HALF:]).astype(BF16)
            parts.append(jnp.concatenate([jnp.zeros((HALF, HALF), BF16), low], axis=1))
        product = mm(jnp.concatenate(parts, axis=0), g)
        parts = [product[:SPAN], product[SPAN:]]
        inner = jnp.where(first_head(), parts[0], parts[1])
        total = inner + skip_ref[:, lanes] * g.astype(F32) + from_state[:, lanes]
        if transposed:
            out_ref[lanes, :] = total.T.astype(BF16)
        else:
            out_ref[:, lanes] = total.astype(BF16)


def forward_kernel(half_ref, own_ref, other_ref, w_ref, rt_ref, b_ref, x_ref, e_ref, total_ref):
    step = pl.program_id(1)

    @pl.when(step == 0)
    def _():
        total_ref[...] = jnp.zeros_like(total_ref)

    half = pl.num_programs(1) // 2

    @pl.when(step < half)
    def _():
        total_ref[...] += mm(own_ref[...], w_ref[...])

    @pl.when(step >= half)
    def _():
        total_ref[...] += mm(other_ref[...], w_ref[...])

    @pl.when(step == pl.num_programs(1) - 1)
    def _():
        x = total_ref[...].astype(BF16)
        x_ref[...] = x
        for k in range(e_ref.shape[0]):
            rows = slice(k * SPAN, (k + 1) * SPAN)
            columns = rt_ref[0, rows]
            to_end = jnp.exp2(spread_columns(columns[SPAN - 1 : SPAN] - columns))
            scaled = (x[rows].astype(F32) * to_end).astype(BF16)
            e_ref[k] = dot(b_ref[rows], scaled, ((0,), (0,)))


def product_kernel(has_before, has_other, half_ref, g_ref, w_ref, *refs):
    refs = list(refs)
    total = dot(g_ref[...], w_ref[...], ((1,), (1,)))
    if has_before:
        total = total + refs.pop(0)[...].astype(F32)
    if has_other:
        total = total.astype(BF16).astype(F32) + refs.pop(0)[...].astype(F32)
    refs[0][...] = total.astype(BF16)


def arrange_kernel(order_ref, own_ref, other_ref, early_ref, late_ref, both_ref):
    half = own_ref.shape[1]
    both_ref[:, :half] = own_ref[...]
    both_ref[:, half:] = other_ref[...]
    unit = 2 * half // order_ref.shape[0]
    cut = early_ref.shape[1]
    for index in range(order_ref.shape[0]):
        source = pl.ds(pl.multiple_of(order_ref[index] * unit, 128), unit)
        at = index * unit
        if at < cut:
            early_ref[:, at : at + unit] = both_ref[:, source]
        else:
            late_ref[:, at - cut : at - cut + unit] = both_ref[:, source]


TAIL = 16


def message(total, log):
    high, middle, last = thirds(log)
    line = iota((TAIL, total.shape[1]), 0)
    tail = jnp.where(line == 0, high, jnp.where(line == 1, middle, jnp.where(line == 2, last, 0.0)))
    return total.astype(BF16), tail.astype(BF16)


def start_kernel(own_ref, kept_ref, log_ref, sent_ref):
    spans = own_ref.shape[0]
    total = own_ref[spans - 1]
    log = kept_ref[spans - 1, 4:5]
    for k in range(spans - 2, -1, -1):
        total = own_ref[k] + kept_ref[k, :1] * total
        log = log + kept_ref[k, 4:5]
    line = iota(log_ref.shape, 0)
    log_ref[...] = jnp.where(line == 0, log, 0.0)
    n = total.shape[0]
    sent_ref[:n], sent_ref[n:] = message(total, log)


def back_kernel(bit, place_ref, log_ref, mine_ref, got_ref, *refs):
    entering_ref = refs[0] if len(refs) == 5 else None
    entering_out, sent_out, log_out, factor_out = refs[-4:]
    n = entering_out.shape[0]
    got = got_ref[:n].astype(F32)
    tail = got_ref[n:].astype(F32)
    other_log = tail[0:1] + tail[1:2] + tail[2:3]
    log, before_me, after_me = log_ref[0:1], log_ref[1:2], log_ref[2:3]
    line = iota(log_ref.shape, 0)
    upper = (place_ref[0] // bit % 2 + 0 * line[0:1]) == 1
    kept, other = jnp.exp2(log), jnp.exp2(other_log)
    mine = mine_ref[:n].astype(F32)
    total = jnp.where(upper, other, 1.0) * mine + jnp.where(upper, 1.0, kept) * got
    passed = jnp.where(upper, 0.0, jnp.exp2(after_me)) * got
    entering_out[...] = passed if entering_ref is None else entering_ref[...] + passed
    first = jnp.where(upper, 1.0, other)
    second = jnp.where(upper, kept, 1.0)
    third = jnp.where(upper, jnp.exp2(before_me), 0.0)
    factor_out[...] = jnp.where(line == 0, first, jnp.where(line == 1, second, third))
    log = log + other_log
    before_me = jnp.where(upper, before_me + other_log, before_me)
    after_me = jnp.where(upper, after_me, after_me + other_log)
    log_out[...] = jnp.where(line == 0, log, jnp.where(line == 1, before_me, after_me))
    sent_out[:n], sent_out[n:] = message(total, log)


def scan_kernel(last, factor_ref, mine_ref, got_ref, *refs):
    refs = list(refs)
    entering_ref = refs.pop(0) if len(refs) == 3 - last else None
    factors = factor_ref[...]
    got = got_ref[...].astype(F32)
    if not last:
        total = factors[0:1] * mine_ref[...].astype(F32) + factors[1:2] * got
        refs[1][...] = total.astype(BF16)
    passed = factors[2:3] * got
    refs[0][...] = passed if entering_ref is None else entering_ref[...] + passed


def scan_pair_kernel(number, last, *refs):
    first, second, outs = refs[:number], refs[number : number + 4], refs[number + 4 :]
    scan_kernel(False, *first, *outs[:2])
    scan_kernel(last, *second, *outs[2:])


def early_forward_kernel(count, f_ref, *refs):
    pieces, (out_ref, buffer) = refs[:count], refs[count:]
    rows = pieces[0].shape[0]
    for index, piece in enumerate(pieces):
        buffer[index * rows : (index + 1) * rows] = piece[...]
    out_ref[...] = mm(f_ref[...], buffer[...])


def late_forward_kernel(count, f_ref, part_ref, rt_ref, b_ref, kept_ref, *refs):
    pieces, (x_ref, e_ref, sent_ref, buffer) = refs[:count], refs[count:]
    rows = pieces[0].shape[0]
    for index, piece in enumerate(pieces):
        buffer[index * rows : (index + 1) * rows] = piece[...]
    x = (part_ref[...] + mm(f_ref[...], buffer[...])).astype(BF16)
    x_ref[...] = x
    total = None
    for k in range(e_ref.shape[0]):
        part = slice(k * SPAN, (k + 1) * SPAN)
        columns = rt_ref[0, part]
        to_end = jnp.exp2(spread_columns(columns[SPAN - 1 : SPAN] - columns))
        scaled = (x[part].astype(F32) * to_end).astype(BF16)
        state = dot(b_ref[part], scaled, ((0,), (0,)))
        e_ref[k] = state
        total = state if total is None else kept_ref[k, :1] * total + state
    sent_ref[...] = total.astype(BF16)


def blocks_kernel(halves, has_before, order_ref, g_ref, *refs):
    count = len(halves)
    number = sum(halves)
    arrays, refs = refs[:number], refs[number:]
    if has_before:
        refs = refs[2:]
    away_ref, own_ref, buffer, slots, sems, out_sems = refs
    rows = arrays[0].shape[0]
    wide = g_ref.shape[0]
    copies = []
    at = 0
    for index, parts in enumerate(halves):
        mine = []
        for part in range(parts):
            lanes = pl.ds(part * (wide // parts), wide // parts)
            target = buffer.at[pl.ds(index * rows, rows), lanes]
            copy = pltpu.make_async_copy(arrays[at], target, sems.at[at])
            copy.start()
            mine.append(copy)
            at += 1
        copies.append(mine)
    g = g_ref[...]
    half = away_ref.shape[1] // rows
    starts = [0]
    while starts[-1] < count:
        starts.append(starts[-1] + (2 if count - starts[-1] in (2, 4) else 3))
    for index in range(count):
        for copy in copies[index]:
            copy.wait()
        if index + 1 not in starts:
            continue
        start = starts[starts.index(index + 1) - 1]
        product = mm(buffer[start * rows : (index + 1) * rows], g)
        for done in range(start, index + 1):
            part = product[(done - start) * rows : (done - start + 1) * rows]
            slots[done] = part.T.astype(BF16)
            place = order_ref[done]
            lanes = pl.ds(pl.multiple_of(place % half * rows, 128), rows)

            @pl.when(place < half)
            def _():
                target = away_ref.at[:, lanes]
                pltpu.make_async_copy(slots.at[done], target, out_sems.at[done]).start()

            @pl.when(place >= half)
            def _():
                target = own_ref.at[:, lanes]
                pltpu.make_async_copy(slots.at[done], target, out_sems.at[done]).start()

    for index in range(count):
        target = away_ref.at[:, pl.ds(0, rows)]
        pltpu.make_async_copy(slots.at[index], target, out_sems.at[index]).wait()


def after_kernel(*refs):
    pass


def inner_kernel(
    r_ref, rt_ref, g_ref, x_ref, b_ref, c_ref, q_ref, *refs
):
    d_ref, grad_b_ref, grad_c_ref, sum_ref, top_ref, low_ref = refs[-6:]
    so_far = refs[:-6]
    step = pl.program_id(1)
    b = b_ref[...]
    c = c_ref[...]
    scores = dot(b, c, ((1,), (1,)))
    running = r_ref[...]
    columns = rt_ref[0]
    top_keep = iota((HALF, SPAN), 1) >= iota((HALF, SPAN), 0)
    low_keep = iota((HALF, HALF), 1) >= iota((HALF, HALF), 0)

    @pl.when(step == 0)
    def _():
        sum_ref[...] = jnp.zeros_like(sum_ref)
        grad_b_ref[...] = so_far[0][...] if so_far else jnp.zeros_like(grad_b_ref)

    rows = []
    lane = iota((SPAN, 2 * P_SIZE), 1)
    later = not_before().astype(BF16)
    top_less = iota((HALF, SPAN), 1) > iota((HALF, SPAN), 0)
    low_less = iota((HALF, HALF), 1) > iota((HALF, HALF), 0)
    for pair in range(GROUP // 2):
        lanes = slice(pair * 2 * P_SIZE, (pair + 1) * 2 * P_SIZE)
        x = x_ref[:, lanes]
        none = jnp.zeros_like(x)
        x = [jnp.where(lane < P_SIZE, x, none), jnp.where(lane < P_SIZE, none, x)]
        product = mm(jnp.concatenate(x, axis=0), g_ref[:, lanes].T)
        top_sum = low_sum = None
        for number in range(2):
            head = 2 * pair + number
            row = running[head : head + 1]
            at = number * SPAN
            top = jnp.where(top_keep, row - columns[:HALF, head : head + 1], NEVER)
            low = jnp.where(low_keep, row[:, HALF:] - columns[HALF:, head : head + 1], NEVER)
            top = jnp.exp2(top) * product[at : at + HALF]
            low = jnp.exp2(low) * product[at + HALF : at + SPAN, HALF:]
            top_sum = top if number == 0 else top_sum + top
            low_sum = low if number == 0 else low_sum + low
            part = slice(head * HALF, (head + 1) * HALF)
            top_ref[part] = (top * scores[:HALF]).astype(BF16)
            low_ref[part] = (low * scores[HALF:, HALF:]).astype(BF16)
        sum_ref[:HALF] += top_sum
        sum_ref[HALF:, HALF:] += low_sum
    top = mm(top_ref[...], later)
    low = mm(low_ref[...], later[HALF:, HALF:])
    for head in range(GROUP):
        part = slice(head * HALF, (head + 1) * HALF)
        top_row = jnp.sum(jnp.where(top_less, top[part], 0.0), axis=0, keepdims=True)
        low_row = jnp.sum(jnp.where(low_less, low[part], 0.0), axis=0, keepdims=True)
        rows.append(jnp.concatenate([top_row[:, :HALF], top_row[:, HALF:] + low_row], axis=1))
    to_end = jnp.exp2(spread_columns(columns[SPAN - 1 : SPAN] - columns))
    scaled = x_ref[...].astype(F32) * to_end
    ends = dot(one_hot(BF16), (scaled * mm(b, q_ref[0])).astype(BF16), ((1,), (1,)))
    d_ref[...] = jnp.concatenate(rows, axis=0) + sum_over(ends, before())
    grad_b_ref[...] += dot(scaled.astype(BF16), q_ref[0], ((1,), (1,)))

    @pl.when(step == pl.num_programs(1) - 1)
    def _():
        total = sum_ref[...].astype(BF16)
        grad_b_ref[...] += mm(total, c)
        part = dot(total, b, ((0,), (0,)))
        grad_c_ref[...] = part + so_far[1][...] if so_far else part


def state_kernel(
    rt_ref, g_ref, c_ref, s_ref, e_ref, q_ref, a_ref, d_part_ref, c_part_ref, *refs
):
    d_ref, grad_c_ref, held = refs[-3:]
    span, group = pl.program_id(0), pl.program_id(1)

    @pl.when(group == 0)
    def _():
        grad_c_ref[...] = c_part_ref[...]

    @pl.when(span == 0)
    def _():
        held[group] = s_ref[...]

    state = held[group]
    low = state.astype(BF16)
    scaled = g_ref[...].astype(F32) * jnp.exp2(spread_columns(rt_ref[0]))
    ends = dot(one_hot(BF16), (scaled * mm(c_ref[...], low)).astype(BF16), ((1,), (1,)))
    grad_c_ref[...] += dot(scaled.astype(BF16), low, ((1,), (1,)))
    product = jnp.sum(q_ref[0].astype(F32) * state, axis=0, keepdims=True) * a_ref[0, :1]
    high, middle, last = thirds(product)
    row = iota((8, WIDE), 0)
    stacked = jnp.where(row == 0, high, jnp.where(row == 1, middle, jnp.where(row == 2, last, 0.0)))
    kept = dot(one_hot(BF16), stacked.astype(BF16), ((1,), (1,)))
    kept = jnp.sum(kept, axis=1, keepdims=True)
    d_ref[...] = d_part_ref[...] + sum_over(ends, not_before()) + kept
    held[group] = e_ref[0] + a_ref[0, :1] * state


def call(kernel, grid, in_specs, out_specs, out_shape, flops, size, scratch=()):
    return pl.pallas_call(
        kernel,
        grid=grid,
        in_specs=in_specs,
        out_specs=out_specs,
        out_shape=out_shape,
        scratch_shapes=list(scratch),
        cost_estimate=pl.CostEstimate(flops=flops, bytes_accessed=size, transcendentals=0),
        compiler_params=pltpu.CompilerParams(
            dimension_semantics=("arbitrary",) * len(grid), vmem_limit_bytes=GRANT
        ),
    )


def run_spec(at=0):
    return pl.BlockSpec((GROUP, SPAN), lambda k, h: (h + at, k))


def run_t_spec(at=0):
    return pl.BlockSpec((1, SPAN, GROUP), lambda k, h: (h + at, k, 0))


def rows_spec(at=0):
    return pl.BlockSpec((SPAN, WIDE), lambda k, h: (k, h + at))


def state_spec(at=0):
    return pl.BlockSpec((1, 2 * P_SIZE, WIDE), lambda k, h: (k, 0, h + at))


def kept_spec(at=0):
    return pl.BlockSpec((1, 8, WIDE), lambda k, h: (k, 0, h + at))


SHARED = pl.BlockSpec((SPAN, 2 * P_SIZE), lambda k, h: (k, 0))
GAIN = pl.BlockSpec((1, WIDE), lambda k, h: (0, h))
ANYWHERE = pl.BlockSpec(memory_space=pl.ANY)
INNER_SCRATCH = [
    pltpu.VMEM((SPAN, SPAN), F32),
    pltpu.VMEM((GROUP * HALF, SPAN), BF16),
    pltpu.VMEM((GROUP * HALF, HALF), BF16),
]
SCALARS = pl.BlockSpec(memory_space=pltpu.SMEM)


def shape(*dims, dtype=F32):
    return jax.ShapeDtypeStruct(dims, dtype)


def swap(value, axis, bit):
    count = lax.axis_size(axis)
    return lax.ppermute(value, axis, [(i, i ^ bit) for i in range(count)])


def block_products(kept):
    count = lax.axis_size("ctx")
    place = lax.axis_index("ctx")
    steps = []
    before_me = jnp.ones_like(kept)
    after_me = jnp.ones_like(kept)
    bit = 1
    while bit < count:
        other = swap(kept, "ctx", bit)
        upper = (place & bit) != 0
        steps.append((bit, upper, kept, other, before_me, after_me))
        before_me = jnp.where(upper, before_me * other, before_me)
        after_me = jnp.where(upper, after_me, after_me * other)
        kept = kept * other
        bit *= 2
    return steps


def scan_states(total, steps, reverse):
    entering = jnp.zeros_like(total)
    for bit, upper, kept, other, before_me, after_me in steps:
        got = swap(total.astype(BF16), "ctx", bit).astype(F32)
        if reverse:
            entering = entering + jnp.where(upper, 0.0, after_me) * got
            total = jnp.where(upper, got + other * total, total + kept * got)
        else:
            entering = entering + jnp.where(upper, before_me, 0.0) * got
            total = jnp.where(upper, kept * got + total, other * total + got)
    return entering


def head_sum(value):
    bit = 1
    while bit < lax.axis_size("head"):
        value = value.astype(BF16)
        value = value.astype(F32) + swap(value, "head", bit).astype(F32)
        bit *= 2
    return value


PLANE = 4


def after(values, *tokens):
    out = pl.pallas_call(
        after_kernel,
        in_specs=[ANYWHERE] * (len(values) + len(tokens)),
        out_specs=[ANYWHERE] * len(values),
        out_shape=[shape(*value.shape, dtype=value.dtype) for value in values],
        input_output_aliases={index: index for index in range(len(values))},
        cost_estimate=pl.CostEstimate(flops=0, bytes_accessed=0, transcendentals=0),
        compiler_params=pltpu.CompilerParams(vmem_limit_bytes=GRANT),
    )(*values, *tokens)
    return list(out)


def along_z(value, moves):
    pairs = [(a * PLANE + i, b * PLANE + i) for a, b in moves for i in range(PLANE)]
    return lax.ppermute(value, "ctx", pairs)


MIDDLE = ((1, 2), (2, 1))
OUTWARD = ((1, 0), (2, 3))


def swap_x(value):
    return swap(value, "ctx", 1)


def swap_y(value):
    return swap(value, "ctx", 2)


LAYERS = ((0, 1, 2, 3), (1, 0, 3, 2), (2, 2, 1, 1), (3, 3, 0, 0))
EARLY = [(k, flip) for k in (0, 1, 2) for flip in range(3)]
LATE = [(0, 3), (1, 3), (2, 3), (3, 0), (3, 1), (3, 2), (3, 3)]


def block_order():
    place = lax.axis_index("ctx")
    layer, spot = place // PLANE, place % PLANE
    layers = jnp.array(LAYERS, jnp.int32)[:, layer]
    order = [layers[k] * PLANE + (spot ^ flip) for k, flip in EARLY + LATE]
    return jnp.stack(order).astype(jnp.int32)


def gather_weight(w, sizes):
    ends = [sum(sizes[: j + 1]) * P_SIZE for j in range(len(sizes))]
    parts = [w[:, end - size * P_SIZE : end] for end, size in zip(ends, sizes)]
    return [lax.all_gather(part, "ctx", axis=0, tiled=True) for part in parts]


def forward(features, first, weight, running_t, b_rows, here):
    own, other = features
    length = own.shape[0]
    n = b_rows.shape[1]
    width, wide = weight.shape
    deep = width // 4
    spans = length // SPAN

    def depth(k, first_ref):
        return (k // 2 ^ first_ref[0]) * 2 + k % 2

    return pl.pallas_call(
        forward_kernel,
        grid_spec=pltpu.PrefetchScalarGridSpec(
            num_scalar_prefetch=1,
            grid=(wide // WIDE, 4),
            in_specs=[
                pl.BlockSpec((length, deep), lambda h, k, first_ref: (0, jnp.minimum(k, 1))),
                pl.BlockSpec((length, deep), lambda h, k, first_ref: (0, jnp.maximum(k - 2, 0))),
                pl.BlockSpec((deep, WIDE), lambda h, k, first_ref: (depth(k, first_ref), h)),
                pl.BlockSpec((1, length, GROUP), lambda h, k, first_ref: (h + here, 0, 0)),
                pl.BlockSpec((length, n), lambda h, k, first_ref: (0, 0)),
            ],
            out_specs=[
                pl.BlockSpec((length, WIDE), lambda h, k, first_ref: (0, h)),
                pl.BlockSpec((spans, n, WIDE), lambda h, k, first_ref: (0, 0, h)),
            ],
            scratch_shapes=[pltpu.VMEM((length, WIDE), F32)],
        ),
        out_shape=[shape(length, wide, dtype=BF16), shape(spans, n, wide)],
        cost_estimate=pl.CostEstimate(
            flops=2 * length * wide * width, bytes_accessed=2 * wide * width, transcendentals=0
        ),
        compiler_params=pltpu.CompilerParams(
            dimension_semantics=("arbitrary", "arbitrary"), vmem_limit_bytes=GRANT
        ),
    )(first, own, other, weight, running_t, b_rows)


def multiply(grad_x, weight, at, half, halves, before=None, other=None):
    length = grad_x.shape[0]
    width, wide = weight.shape
    tiles = width // halves // WIDE
    tile = pl.BlockSpec((length, WIDE), lambda j, half_ref: (0, half_ref[0] * tiles + j))
    plain = pl.BlockSpec((length, WIDE), lambda j, half_ref: (0, j))
    in_specs = [
        pl.BlockSpec((length, wide), lambda j, half_ref: (0, at)),
        pl.BlockSpec((WIDE, wide), lambda j, half_ref: (half_ref[0] * tiles + j, 0)),
    ]
    operands = [grad_x, weight]
    if before is not None:
        in_specs.append(tile)
        operands.append(before)
    if other is not None:
        in_specs.append(plain)
        operands.append(other)
    return pl.pallas_call(
        functools.partial(product_kernel, before is not None, other is not None),
        grid_spec=pltpu.PrefetchScalarGridSpec(
            num_scalar_prefetch=1,
            grid=(tiles,),
            in_specs=in_specs,
            out_specs=plain,
        ),
        out_shape=shape(length, width // halves, dtype=BF16),
        cost_estimate=pl.CostEstimate(
            flops=2 * length * wide * width // halves,
            bytes_accessed=2 * wide * width // halves,
            transcendentals=0,
        ),
        compiler_params=pltpu.CompilerParams(
            dimension_semantics=("arbitrary",), vmem_limit_bytes=GRANT
        ),
    )(half, *operands)


def early_forward(features, pieces):
    length = features.shape[0]
    rows, columns = pieces[0].shape
    deep = rows * len(pieces)
    return call(
        functools.partial(early_forward_kernel, len(pieces)),
        (columns // WIDE,),
        [pl.BlockSpec((length, deep), lambda h: (0, 0))]
        + [pl.BlockSpec((rows, WIDE), lambda h: (0, h))] * len(pieces),
        pl.BlockSpec((length, WIDE), lambda h: (0, h)),
        shape(length, columns),
        2 * length * columns * deep,
        2 * columns * deep,
        [pltpu.VMEM((deep, WIDE), BF16)],
    )(features, *pieces)


def late_forward(features, part, pieces, running_t, b_rows, kept, here):
    length = features.shape[0]
    rows, columns = pieces[0].shape
    deep = rows * len(pieces)
    n = b_rows.shape[1]
    spans = length // SPAN
    state = pl.BlockSpec((n, WIDE), lambda h: (0, h))
    return call(
        functools.partial(late_forward_kernel, len(pieces)),
        (columns // WIDE,),
        [
            pl.BlockSpec((length, deep), lambda h: (0, 0)),
            pl.BlockSpec((length, WIDE), lambda h: (0, h + here)),
            pl.BlockSpec((1, length, GROUP), lambda h: (h + here, 0, 0)),
            pl.BlockSpec((length, n), lambda h: (0, 0)),
            pl.BlockSpec((spans, 8, WIDE), lambda h: (0, 0, h + here)),
        ]
        + [pl.BlockSpec((rows, WIDE), lambda h: (0, h))] * len(pieces),
        [
            pl.BlockSpec((length, WIDE), lambda h: (0, h)),
            pl.BlockSpec((spans, n, WIDE), lambda h: (0, 0, h)),
            state,
        ],
        [
            shape(length, columns, dtype=BF16),
            shape(spans, n, columns),
            shape(n, columns, dtype=BF16),
        ],
        2 * length * columns * deep,
        2 * columns * deep,
        [pltpu.VMEM((deep, WIDE), BF16)],
    )(features, part, running_t, b_rows, kept, *pieces)


def multiply_blocks(order, grad_x, pieces, so_far):
    columns, length = grad_x.shape
    arrays = [array for piece in pieces for array in piece]
    rows = arrays[0].shape[0]
    count = len(pieces)
    half = shape(length, lax.axis_size("ctx") * rows // 2, dtype=BF16)
    first = 2 + len(arrays)
    return pl.pallas_call(
        functools.partial(blocks_kernel, [len(piece) for piece in pieces], bool(so_far)),
        grid=(1,),
        in_specs=[SCALARS, pl.BlockSpec((columns, length), lambda h: (0, 0))]
        + [ANYWHERE] * (len(arrays) + len(so_far)),
        out_specs=[ANYWHERE, ANYWHERE],
        out_shape=[half, half],
        input_output_aliases={first + k: k for k in range(len(so_far))},
        scratch_shapes=[
            pltpu.VMEM((rows * count, columns), BF16),
            pltpu.VMEM((count, length, rows), BF16),
            pltpu.SemaphoreType.DMA((len(arrays),)),
            pltpu.SemaphoreType.DMA((count,)),
        ],
        cost_estimate=pl.CostEstimate(
            flops=2 * length * columns * rows * count,
            bytes_accessed=2 * columns * rows * count,
            transcendentals=0,
        ),
        compiler_params=pltpu.CompilerParams(
            dimension_semantics=("arbitrary",), vmem_limit_bytes=GRANT
        ),
    )(order, grad_x, *arrays, *so_far)


def back_start(own_grads, kept):
    spans, n, columns = own_grads.shape
    return call(
        start_kernel,
        (columns // WIDE,),
        [
            pl.BlockSpec((spans, n, WIDE), lambda h: (0, 0, h)),
            pl.BlockSpec((spans, 8, WIDE), lambda h: (0, 0, h)),
        ],
        [pl.BlockSpec((rows, WIDE), lambda h: (0, h)) for rows in (8, n + TAIL)],
        [shape(8, columns), shape(n + TAIL, columns, dtype=BF16)],
        0,
        14 * n * columns,
    )(own_grads, kept)


def back_step(place, log, sent, entering, bit):
    got = swap(sent, "ctx", bit)
    columns = sent.shape[1]
    n = sent.shape[0] - TAIL
    short, state, tall = [
        pl.BlockSpec((rows, 2 * WIDE), lambda h: (0, h)) for rows in (8, n, n + TAIL)
    ]
    return call(
        functools.partial(back_kernel, bit),
        (columns // (2 * WIDE),),
        [SCALARS, short, tall, tall] + [state] * len(entering),
        [state, tall, short, short],
        [
            shape(n, columns),
            shape(n + TAIL, columns, dtype=BF16),
            shape(8, columns),
            shape(8, columns),
        ],
        0,
        14 * n * columns,
    )(place, log, sent, got, *entering)


def scan_step(factors, here, sent, entering, bit, last=False):
    got = swap(sent, "ctx", bit)
    n, columns = sent.shape
    block = pl.BlockSpec((n, columns), lambda h: (0, 0))
    at = here * WIDE // columns
    outs = [shape(n, columns), shape(n, columns, dtype=BF16)][: 2 - last]
    return call(
        functools.partial(scan_kernel, last),
        (1,),
        [pl.BlockSpec((8, columns), lambda h: (0, at)), block, block] + [block] * len(entering),
        [block] * len(outs),
        outs,
        0,
        10 * n * columns,
    )(factors, sent, got, *entering)


def scan_pair(first, second, last=False):
    operands, specs, outs = [], [], []
    for factors, here, sent, entering, bit in (first, second):
        got = swap(sent, "ctx", bit)
        n, columns = sent.shape
        block = pl.BlockSpec((n, columns), lambda h: (0, 0))
        at = here * WIDE // columns
        operands += [factors, sent, got, *entering]
        specs += [pl.BlockSpec((8, columns), lambda h, at=at: (0, at))]
        specs += [block] * (2 + len(entering))
        outs += [shape(n, columns), shape(n, columns, dtype=BF16)]
    outs = outs[: 4 - last]
    return call(
        functools.partial(scan_pair_kernel, 3 + len(first[3]), last),
        (1,),
        specs,
        [block] * len(outs),
        outs,
        0,
        20 * n * columns,
    )(*operands)


def local(inputs, w_in, b_rows, c_rows, log_decay, skip_gain, grad_out):
    groups = log_decay.shape[0] // GROUP
    layered = lax.axis_size("ctx") == 4 * PLANE and lax.axis_size("head") == 2
    if layered and groups % 2 == 0 and w_in.shape[0] == 256:
        return local_layered(inputs, w_in, b_rows, c_rows, log_decay, skip_gain, grad_out)
    return local_plain(inputs, w_in, b_rows, c_rows, log_decay, skip_gain, grad_out)


def prepare(log_decay, grad_out, c_rows):
    length, columns = grad_out.shape
    heads = log_decay.shape[0]
    spans = length // SPAN
    groups = heads // GROUP
    n = c_rows.shape[1]
    return call(
        decay_kernel,
        (spans, groups),
        [run_spec(), rows_spec(), SHARED],
        [run_spec(), run_t_spec(), kept_spec(), state_spec()],
        [
            shape(heads, length),
            shape(groups, length, GROUP),
            shape(spans, 8, columns),
            shape(spans, n, columns),
        ],
        2 * length * columns * n,
        6 * length * columns,
    )(log_decay, grad_out, c_rows)


def inner(grid, here, wide, operands, so_far):
    length = operands[2].shape[0]
    n = operands[4].shape[1]
    specs = [
        run_spec(here),
        run_t_spec(here),
        rows_spec(here),
        rows_spec(),
        SHARED,
        SHARED,
        state_spec(here),
    ]
    return call(
        inner_kernel,
        grid,
        specs + [SHARED] * len(so_far),
        [run_spec(), SHARED, SHARED],
        [shape(wide // P_SIZE, length), shape(length, n), shape(length, n)],
        12 * length * wide * SPAN,
        6 * length * wide,
        INNER_SCRATCH,
    )(*operands, *so_far)


def state_terms(grid, here, wide, operands, heads=None, so_far=None):
    length = operands[1].shape[0]
    n = operands[2].shape[1]
    heads = heads or wide // P_SIZE
    at = here if heads > wide // P_SIZE else 0
    extra = () if so_far is None else (so_far,)
    return pl.pallas_call(
        state_kernel,
        grid=grid,
        in_specs=[
            run_t_spec(here),
            rows_spec(here),
            SHARED,
            pl.BlockSpec((n, WIDE), lambda k, h: (0, h)),
            state_spec(),
            state_spec(here),
            kept_spec(here),
            run_spec(),
            SHARED,
        ]
        + [ANYWHERE] * len(extra),
        out_specs=[run_spec(at), SHARED],
        out_shape=[shape(heads, length), shape(length, n)],
        scratch_shapes=[pltpu.VMEM((grid[1], n, WIDE), F32)],
        input_output_aliases={len(operands): 0} if extra else {},
        cost_estimate=pl.CostEstimate(
            flops=4 * length * wide * n, bytes_accessed=6 * length * wide, transcendentals=0
        ),
        compiler_params=pltpu.CompilerParams(
            dimension_semantics=("arbitrary", "arbitrary"), vmem_limit_bytes=GRANT
        ),
    )(*operands, *extra)


def local_layered(inputs, w_in, b_rows, c_rows, log_decay, skip_gain, grad_out):
    length, columns = grad_out.shape
    heads = log_decay.shape[0]
    spans = length // SPAN
    groups = heads // GROUP
    place = lax.axis_index("head").astype(jnp.int32)
    half = columns // 2
    order = block_order()
    blocks = order.shape[0]
    width = blocks * w_in.shape[0]

    z1, inner2 = swap(w_in, "ctx", PLANE), along_z(w_in, MIDDLE)
    own_x, own_y = swap_x(w_in), swap_y(w_in)
    other = swap(inputs, "head", 1)
    running, running_t, kept, own_grads = prepare(log_decay, grad_out, c_rows)
    spot = lax.axis_index("ctx").astype(jnp.int32)[None]
    log, sent = back_start(own_grads, kept)
    sent = after([sent], other)[0]
    leaving, moved, log, factors_1 = back_step(spot, log, sent, (), 1)

    z1, inner2, own_y = after([z1, inner2, own_y], own_x, sent)
    sent = moved
    x1, y1 = swap_x(z1), swap_y(z1)
    inner3, outer2 = along_z(z1, MIDDLE), along_z(inner2, OUTWARD)
    own_y_a, own_y_b = own_y[:, :half], own_y[:, half:]
    leaving, sent, log, factors_2 = back_step(spot, log, sent, (leaving,), 2)
    order_own = (order + place * (blocks // 2)) % blocks
    cut = len(EARLY) * w_in.shape[0]
    early_features, late_features = call(
        arrange_kernel,
        (1,),
        [SCALARS] + [pl.BlockSpec((length, width // 2), lambda h: (0, 0))] * 2,
        [pl.BlockSpec((length, wide), lambda h: (0, 0)) for wide in (cut, width - cut)],
        [shape(length, wide, dtype=BF16) for wide in (cut, width - cut)],
        0,
        4 * length * width,
        [pltpu.VMEM((length, width), BF16)],
    )(order_own, inputs, other)

    inner2, inner3, outer2, x1, sent, own_y_a, own_y_b = after(
        [inner2, inner3, outer2, x1, sent, own_y_a, own_y_b], y1, early_features
    )
    z3 = inner2 + outer2
    x3, y3 = swap_x(z3), swap_y(z3)
    outer3 = along_z(inner3, OUTWARD)
    x1_a, x1_b = x1[:, :half], x1[:, half:]
    leaving, sent, log, factors_4 = back_step(spot, log, sent, (leaving,), 4)

    inner3, outer3, y3, x1_a, x1_b = after([inner3, outer3, y3, x1_a, x1_b], x3)
    z2a = inner3[:, :half] + outer3[:, :half]
    z2b = inner3[:, half:] + outer3[:, half:]
    y3_a, y3_b = y3[:, :half], y3[:, half:]
    x2a, y2a = swap_x(z2a), swap_y(z2a)
    d3a, d1a = swap_x(y3_a), swap_y(x1_a)
    leaving, sent, log, factors_8 = back_step(spot, log, sent, (leaving,), 8)
    early = [w_in, own_x, own_y, z1, x1, y1, z3, x3, y3]
    part = early_forward(early_features, early)

    own_y_a, x2a, z2b, leaving = after([own_y_a, x2a, z2b, leaving], y2a, d3a, d1a, part)
    d0a, d2a = swap_x(own_y_a), swap_y(x2a)
    leaving_all = [leaving]
    for k in range(spans - 1, 0, -1):
        leaving_all.insert(0, own_grads[k] + kept[k, :1] * leaving_all[0])
    leaving_all = jnp.stack([value.astype(BF16) for value in leaving_all])
    (z2b,) = after([z2b], leaving_all)
    x2b, y2b = swap_x(z2b), swap_y(z2b)
    skip = jnp.repeat(skip_gain, P_SIZE)[None]
    grad_x = grad_rows(running, running_t, grad_out, b_rows, c_rows, leaving_all, skip, True)
    order_away = (order + (1 - place) * (blocks // 2)) % blocks
    early_order, late_order = order_away[: len(EARLY)], order_away[len(EARLY) :]
    late_a = [d0a, d1a, d3a, z2a, x2a, y2a, d2a]
    x_a, states_a, sent_a = late_forward(
        late_features, part, late_a, running_t, b_rows, kept, 0
    )

    own_y_b, x2b, y3_b, x1_b, grad_x = after([own_y_b, x2b, y3_b, x1_b, grad_x], y2b, sent_a)
    d0b, d2b = swap_x(own_y_b), swap_y(x2b)
    d3b, d1b = swap_x(y3_b), swap_y(x1_b)
    product = multiply_blocks(early_order, grad_x, [[piece] for piece in early], ())
    shared = (running, running_t, grad_out)
    here = groups // 2
    grid = (spans, here)

    d0b, d2b, sent_a = after([d0b, d2b, sent_a], d3b, d1b, product[0])
    entering_a, sent_a = scan_step(factors_1, 0, sent_a, (), 1)
    late_b = [d0b, d1b, d3b, z2b, x2b, y2b, d2b]
    x_b, states_b, sent_b = late_forward(
        late_features, part, late_b, running_t, b_rows, kept, here
    )
    pairs = list(zip(late_a, late_b))
    sent_a, sent_b, *product = after([sent_a, sent_b, *product])
    entering_b, sent_b, entering_a, sent_a = scan_pair(
        (factors_1, here, sent_b, (), 1), (factors_2, 0, sent_a, (entering_a,), 2)
    )
    away, own = multiply_blocks(late_order, grad_x, pairs, product)

    sent_a, sent_b, x_a, away = after([sent_a, sent_b, x_a, away])
    entering_b, sent_b, entering_a, sent_a = scan_pair(
        (factors_2, here, sent_b, (entering_b,), 2), (factors_4, 0, sent_a, (entering_a,), 4)
    )
    got = swap(away, "head", 1)
    inner_a = shared + (x_a, b_rows, c_rows, leaving_all)
    decay_a, grad_b, grad_c = inner(grid, 0, half, inner_a, ())

    sent_a, sent_b, x_b, grad_b = after([sent_a, sent_b, x_b, grad_b])
    entering_b, sent_b, entering_a = scan_pair(
        (factors_4, here, sent_b, (entering_b,), 4),
        (factors_8, 0, sent_a, (entering_a,), 8),
        True,
    )
    inner_b = shared + (x_b, b_rows, c_rows, leaving_all)
    decay_b, grad_b, grad_c = inner(grid, here, half, inner_b, (grad_b, grad_c))

    sent_b, entering_a, got, grad_b = after([sent_b, entering_a, got, grad_b])
    grad_b = head_sum(grad_b)
    grad_inputs = (own.astype(F32) + got.astype(F32)).astype(BF16)
    (entering_b,) = scan_step(factors_8, here, sent_b, (entering_b,), 8, True)
    common = (running_t, grad_out, c_rows)
    state_a = common + (entering_a, states_a, leaving_all, kept, decay_a, grad_c)
    decays, grad_c = state_terms(grid, 0, half, state_a, heads)
    (entering_b,) = after([entering_b], grad_inputs, grad_c)
    state_b = common + (entering_b, states_b, leaving_all, kept, decay_b, grad_c)
    decays, grad_c = state_terms(grid, here, half, state_b, heads, decays)
    return (grad_inputs, grad_b, head_sum(grad_c), decays)


def grad_rows(running, running_t, grad_out, b_rows, c_rows, leaving, skip, transposed):
    length, columns = grad_out.shape
    spec, dims = rows_spec(), (length, columns)
    if transposed:
        spec, dims = pl.BlockSpec((WIDE, SPAN), lambda k, h: (h, k)), (columns, length)
    return call(
        functools.partial(grad_x_kernel, transposed),
        (length // SPAN, running_t.shape[0]),
        [run_spec(), run_t_spec(), rows_spec(), SHARED, SHARED, state_spec(), GAIN],
        spec,
        shape(*dims, dtype=BF16),
        8 * length * columns * SPAN,
        6 * length * columns,
    )(running, running_t, grad_out, b_rows, c_rows, leaving, skip)


def local_plain(inputs, w_in, b_rows, c_rows, log_decay, skip_gain, grad_out):
    length, columns = grad_out.shape
    heads = log_decay.shape[0]
    spans = length // SPAN
    groups = heads // GROUP
    n = b_rows.shape[1]
    grid = (spans, groups)

    sizes = (heads // 2, heads // 4, heads // 4) if heads % (4 * GROUP) == 0 else (heads,)
    weights = gather_weight(w_in, sizes)
    two = lax.axis_size("head") == 2
    place = lax.axis_index("head").astype(jnp.int32)[None]
    width = weights[0].shape[0]
    if two:
        features = (inputs, swap(inputs, "head", 1))
        first = place
    else:
        features = lax.all_gather(inputs, "head", axis=1, tiled=True)
        features = (features[:, : width // 2], features[:, width // 2 :])
        first = jnp.zeros((1,), jnp.int32)

    running, running_t, kept, own_grads = call(
        decay_kernel,
        grid,
        [run_spec(), rows_spec(), SHARED],
        [run_spec(), run_t_spec(), kept_spec(), state_spec()],
        [
            shape(heads, length),
            shape(groups, length, GROUP),
            shape(spans, 8, columns),
            shape(spans, n, columns),
        ],
        2 * length * columns * n,
        6 * length * columns,
    )(log_decay, grad_out, c_rows)

    kept_total = kept[0, :1]
    for k in range(1, spans):
        kept_total = kept_total * kept[k, :1]
    steps = block_products(kept_total)

    total = own_grads[spans - 1]
    for k in range(spans - 2, -1, -1):
        total = own_grads[k] + kept[k, :1] * total
    leaving = [scan_states(total, steps, True)]
    for k in range(spans - 1, 0, -1):
        leaving.insert(0, own_grads[k] + kept[k, :1] * leaving[0])
    leaving = jnp.stack([value.astype(BF16) for value in leaving])

    skip = jnp.repeat(skip_gain, P_SIZE)[None]
    grad_x = grad_rows(running, running_t, grad_out, b_rows, c_rows, leaving, skip, False)

    grad_b = grad_c = product = None
    tokens = ()
    decay_parts = []
    at = 0
    for index, size in enumerate(sizes):
        wide = size * P_SIZE
        here = at // GROUP
        count = size // GROUP
        weight = weights[index]
        if tokens:
            weight = after([weight], *tokens)[0]
        x, own_states = forward(features, first, weight, running_t, b_rows, here)

        chunk = slice(at * P_SIZE, at * P_SIZE + wide)
        total = own_states[0]
        for k in range(1, spans):
            total = kept[k, :1, chunk] * total + own_states[k]
        cut = [step[:2] + tuple(value[:, chunk] for value in step[2:]) for step in steps]
        entering = scan_states(total, cut, False)

        so_far = () if grad_b is None else (grad_b, grad_c)
        decay_part, grad_b, grad_c = call(
            inner_kernel,
            (spans, count),
            [
                run_spec(here),
                run_t_spec(here),
                rows_spec(here),
                rows_spec(),
                SHARED,
                SHARED,
                state_spec(here),
            ]
            + [SHARED] * len(so_far),
            [run_spec(), SHARED, SHARED],
            [shape(size, length), shape(length, n), shape(length, n)],
            12 * length * wide * SPAN,
            6 * length * wide,
            INNER_SCRATCH,
        )(running, running_t, grad_out, x, b_rows, c_rows, leaving, *so_far)
        decay_part, grad_c = call(
            state_kernel,
            (spans, count),
            [
                run_t_spec(here),
                rows_spec(here),
                SHARED,
                pl.BlockSpec((n, WIDE), lambda k, h: (0, h)),
                state_spec(),
                state_spec(here),
                kept_spec(here),
                run_spec(),
                SHARED,
            ],
            [run_spec(), SHARED],
            [shape(size, length), shape(length, n)],
            4 * length * wide * n,
            6 * length * wide,
            [pltpu.VMEM((count, n, WIDE), F32)],
        )(running_t, grad_out, c_rows, entering, own_states, leaving, kept, decay_part, grad_c)
        decay_parts.append(decay_part)

        if index < len(sizes) - 1:
            zero = jnp.zeros((1,), jnp.int32)
            product = multiply(grad_x, weight, at // size, zero, 1, product)
            tokens = (product, grad_b, entering)
        elif two:
            sent = multiply(grad_x, weight, at // size, 1 - place, 2, product)
            got = swap(sent, "head", 1)
            grad_inputs = multiply(grad_x, weight, at // size, place, 2, product, got)
        else:
            zero = jnp.zeros((1,), jnp.int32)
            product = multiply(grad_x, weight, at // size, zero, 1, product)
            grad_inputs = lax.psum_scatter(product, "head", scatter_dimension=1, tiled=True)
        at += size

    return (grad_inputs, head_sum(grad_b), head_sum(grad_c), jnp.concatenate(decay_parts, axis=0))


def solution(mesh):
    in_specs = (
        P("ctx", "head"),
        P("ctx", "head"),
        P("ctx", None),
        P("ctx", None),
        P("head", "ctx"),
        P("head"),
        P("ctx", "head"),
    )
    out_specs = (P("ctx", "head"), P("ctx", None), P("ctx", None), P("head", "ctx"))
    return jax.shard_map(local, mesh=mesh, in_specs=in_specs, out_specs=out_specs, check_vma=False)
```

```python
import functools

import jax
import jax.numpy as jnp
from jax import lax
from jax.experimental import pallas as pl
from jax.experimental.pallas import tpu as pltpu
from jax.sharding import PartitionSpec as P

SPAN = 256
HALF = SPAN // 2
P_SIZE = 64
GROUP = 8
WIDE = GROUP * P_SIZE
LOG2E = 1.4426950408889634
NEVER = -1e30
GRANT = 64 * 2**20

F32 = jnp.float32
BF16 = jnp.bfloat16
EXACT = lax.Precision.HIGHEST


def dot(a, b, dims, precision=None):
    return lax.dot_general(a, b, (dims, ((), ())), precision=precision, preferred_element_type=F32)


def mm(a, b, precision=None):
    return dot(a, b, ((1,), (0,)), precision)


def iota(shape, dim):
    return lax.broadcasted_iota(jnp.int32, shape, dim)


def one_hot(dtype):
    return (iota((GROUP, WIDE), 0) == iota((GROUP, WIDE), 1) // P_SIZE).astype(dtype)


def not_before():
    return (iota((SPAN, SPAN), 0) >= iota((SPAN, SPAN), 1)).astype(F32)


def before():
    return (iota((SPAN, SPAN), 0) < iota((SPAN, SPAN), 1)).astype(F32)


def same():
    return (iota((SPAN, SPAN), 0) == iota((SPAN, SPAN), 1)).astype(F32)


def first_head():
    return iota((SPAN, 2 * P_SIZE), 1) < P_SIZE


def pair_columns(columns, pair):
    shape = (columns.shape[0], 2 * P_SIZE)
    left = jnp.broadcast_to(columns[:, 2 * pair : 2 * pair + 1], shape)
    right = jnp.broadcast_to(columns[:, 2 * pair + 1 : 2 * pair + 2], shape)
    return jnp.where(iota(shape, 1) < P_SIZE, left, right)


def spread_columns(columns):
    return jnp.concatenate([pair_columns(columns, pair) for pair in range(GROUP // 2)], axis=1)


def thirds(value):
    high = value.astype(BF16).astype(F32)
    middle = (value - high).astype(BF16).astype(F32)
    return high, middle, value - high - middle


def sum_over(value, mask):
    rows = value.shape[0]
    parts = mm(jnp.concatenate(thirds(value), axis=0).astype(BF16), mask.astype(BF16))
    return parts[:rows] + parts[rows : 2 * rows] + parts[2 * rows :]


def decay_kernel(d_ref, g_ref, c_ref, r_ref, rt_ref, a_ref, gt_ref):
    row_sums = sum_over(d_ref[...] * LOG2E, 1.0 - not_before() + same())
    r_ref[...] = row_sums
    padded = jnp.concatenate([row_sums, jnp.zeros((2 * P_SIZE - GROUP, SPAN), F32)], axis=0)
    running = padded.T[:, :GROUP]
    rt_ref[0] = running
    growth = jnp.exp2(spread_columns(running))
    last = spread_columns(running[SPAN - 1 : SPAN])
    a_ref[0] = jnp.where(iota((8, WIDE), 0) < 4, jnp.exp2(last), last)
    scaled = (g_ref[...].astype(F32) * growth).astype(BF16)
    gt_ref[0] = dot(c_ref[...], scaled, ((0,), (0,)))


def grad_x_kernel(transposed, r_ref, rt_ref, g_ref, b_ref, c_ref, q_ref, skip_ref, out_ref):
    b = b_ref[...]
    scores = dot(b, c_ref[...], ((1,), (1,)))
    running = r_ref[...]
    columns = rt_ref[0]
    top_keep = iota((HALF, SPAN), 1) >= iota((HALF, SPAN), 0)
    low_keep = iota((HALF, HALF), 1) >= iota((HALF, HALF), 0)
    to_end = jnp.exp2(spread_columns(columns[SPAN - 1 : SPAN] - columns))
    from_state = mm(b, q_ref[0]) * to_end
    for pair in range(GROUP // 2):
        lanes = slice(pair * 2 * P_SIZE, (pair + 1) * 2 * P_SIZE)
        g = g_ref[:, lanes]
        parts = []
        for head in (2 * pair, 2 * pair + 1):
            row = running[head : head + 1]
            top = jnp.where(top_keep, row - columns[:HALF, head : head + 1], NEVER)
            low = jnp.where(low_keep, row[:, HALF:] - columns[HALF:, head : head + 1], NEVER)
            parts.append((jnp.exp2(top) * scores[:HALF]).astype(BF16))
            low = (jnp.exp2(low) * scores[HALF:, HALF:]).astype(BF16)
            parts.append(jnp.concatenate([jnp.zeros((HALF, HALF), BF16), low], axis=1))
        product = mm(jnp.concatenate(parts, axis=0), g)
        parts = [product[:SPAN], product[SPAN:]]
        inner = jnp.where(first_head(), parts[0], parts[1])
        total = inner + skip_ref[:, lanes] * g.astype(F32) + from_state[:, lanes]
        if transposed:
            out_ref[lanes, :] = total.T.astype(BF16)
        else:
            out_ref[:, lanes] = total.astype(BF16)


def forward_kernel(half_ref, own_ref, other_ref, w_ref, rt_ref, b_ref, x_ref, e_ref, total_ref):
    step = pl.program_id(1)

    @pl.when(step == 0)
    def _():
        total_ref[...] = jnp.zeros_like(total_ref)

    half = pl.num_programs(1) // 2

    @pl.when(step < half)
    def _():
        total_ref[...] += mm(own_ref[...], w_ref[...])

    @pl.when(step >= half)
    def _():
        total_ref[...] += mm(other_ref[...], w_ref[...])

    @pl.when(step == pl.num_programs(1) - 1)
    def _():
        x = total_ref[...].astype(BF16)
        x_ref[...] = x
        for k in range(e_ref.shape[0]):
            rows = slice(k * SPAN, (k + 1) * SPAN)
            columns = rt_ref[0, rows]
            to_end = jnp.exp2(spread_columns(columns[SPAN - 1 : SPAN] - columns))
            scaled = (x[rows].astype(F32) * to_end).astype(BF16)
            e_ref[k] = dot(b_ref[rows], scaled, ((0,), (0,)))


def product_kernel(has_before, has_other, half_ref, g_ref, w_ref, *refs):
    refs = list(refs)
    total = dot(g_ref[...], w_ref[...], ((1,), (1,)))
    if has_before:
        total = total + refs.pop(0)[...].astype(F32)
    if has_other:
        total = total.astype(BF16).astype(F32) + refs.pop(0)[...].astype(F32)
    refs[0][...] = total.astype(BF16)


def arrange_kernel(order_ref, own_ref, other_ref, early_ref, late_ref, both_ref):
    half = own_ref.shape[1]
    both_ref[:, :half] = own_ref[...]
    both_ref[:, half:] = other_ref[...]
    unit = 2 * half // order_ref.shape[0]
    cut = early_ref.shape[1]
    for index in range(order_ref.shape[0]):
        source = pl.ds(pl.multiple_of(order_ref[index] * unit, 128), unit)
        at = index * unit
        if at < cut:
            early_ref[:, at : at + unit] = both_ref[:, source]
        else:
            late_ref[:, at - cut : at - cut + unit] = both_ref[:, source]


TAIL = 16


def message(total, log):
    high, middle, last = thirds(log)
    line = iota((TAIL, total.shape[1]), 0)
    tail = jnp.where(line == 0, high, jnp.where(line == 1, middle, jnp.where(line == 2, last, 0.0)))
    return total.astype(BF16), tail.astype(BF16)


def start_kernel(own_ref, kept_ref, log_ref, sent_ref):
    spans = own_ref.shape[0]
    total = own_ref[spans - 1]
    log = kept_ref[spans - 1, 4:5]
    for k in range(spans - 2, -1, -1):
        total = own_ref[k] + kept_ref[k, :1] * total
        log = log + kept_ref[k, 4:5]
    line = iota(log_ref.shape, 0)
    log_ref[...] = jnp.where(line == 0, log, 0.0)
    n = total.shape[0]
    sent_ref[:n], sent_ref[n:] = message(total, log)


def back_kernel(bit, place_ref, log_ref, mine_ref, got_ref, *refs):
    entering_ref = refs[0] if len(refs) == 5 else None
    entering_out, sent_out, log_out, factor_out = refs[-4:]
    n = entering_out.shape[0]
    got = got_ref[:n].astype(F32)
    tail = got_ref[n:].astype(F32)
    other_log = tail[0:1] + tail[1:2] + tail[2:3]
    log, before_me, after_me = log_ref[0:1], log_ref[1:2], log_ref[2:3]
    line = iota(log_ref.shape, 0)
    upper = (place_ref[0] // bit % 2 + 0 * line[0:1]) == 1
    kept, other = jnp.exp2(log), jnp.exp2(other_log)
    mine = mine_ref[:n].astype(F32)
    total = jnp.where(upper, other, 1.0) * mine + jnp.where(upper, 1.0, kept) * got
    passed = jnp.where(upper, 0.0, jnp.exp2(after_me)) * got
    entering_out[...] = passed if entering_ref is None else entering_ref[...] + passed
    first = jnp.where(upper, 1.0, other)
    second = jnp.where(upper, kept, 1.0)
    third = jnp.where(upper, jnp.exp2(before_me), 0.0)
    factor_out[...] = jnp.where(line == 0, first, jnp.where(line == 1, second, third))
    log = log + other_log
    before_me = jnp.where(upper, before_me + other_log, before_me)
    after_me = jnp.where(upper, after_me, after_me + other_log)
    log_out[...] = jnp.where(line == 0, log, jnp.where(line == 1, before_me, after_me))
    sent_out[:n], sent_out[n:] = message(total, log)


def scan_kernel(last, factor_ref, mine_ref, got_ref, *refs):
    refs = list(refs)
    entering_ref = refs.pop(0) if len(refs) == 3 - last else None
    factors = factor_ref[...]
    got = got_ref[...].astype(F32)
    if not last:
        total = factors[0:1] * mine_ref[...].astype(F32) + factors[1:2] * got
        refs[1][...] = total.astype(BF16)
    passed = factors[2:3] * got
    refs[0][...] = passed if entering_ref is None else entering_ref[...] + passed


def scan_pair_kernel(number, last, *refs):
    first, second, outs = refs[:number], refs[number : number + 4], refs[number + 4 :]
    scan_kernel(False, *first, *outs[:2])
    scan_kernel(last, *second, *outs[2:])


def early_forward_kernel(count, f_ref, *refs):
    pieces, (out_ref, buffer) = refs[:count], refs[count:]
    rows = pieces[0].shape[0]
    for index, piece in enumerate(pieces):
        buffer[index * rows : (index + 1) * rows] = piece[...]
    out_ref[...] = mm(f_ref[...], buffer[...])


def late_forward_kernel(count, f_ref, part_ref, rt_ref, b_ref, kept_ref, *refs):
    pieces, (x_ref, e_ref, sent_ref, buffer) = refs[:count], refs[count:]
    rows = pieces[0].shape[0]
    for index, piece in enumerate(pieces):
        buffer[index * rows : (index + 1) * rows] = piece[...]
    x = (part_ref[...] + mm(f_ref[...], buffer[...])).astype(BF16)
    x_ref[...] = x
    total = None
    for k in range(e_ref.shape[0]):
        part = slice(k * SPAN, (k + 1) * SPAN)
        columns = rt_ref[0, part]
        to_end = jnp.exp2(spread_columns(columns[SPAN - 1 : SPAN] - columns))
        scaled = (x[part].astype(F32) * to_end).astype(BF16)
        state = dot(b_ref[part], scaled, ((0,), (0,)))
        e_ref[k] = state
        total = state if total is None else kept_ref[k, :1] * total + state
    sent_ref[...] = total.astype(BF16)


def blocks_kernel(halves, has_before, order_ref, g_ref, *refs):
    count = len(halves)
    number = sum(halves)
    arrays, refs = refs[:number], refs[number:]
    if has_before:
        refs = refs[2:]
    away_ref, own_ref, buffer, slots, sems, out_sems = refs
    rows = arrays[0].shape[0]
    wide = g_ref.shape[0]
    copies = []
    at = 0
    for index, parts in enumerate(halves):
        mine = []
        for part in range(parts):
            lanes = pl.ds(part * (wide // parts), wide // parts)
            target = buffer.at[pl.ds(index * rows, rows), lanes]
            copy = pltpu.make_async_copy(arrays[at], target, sems.at[at])
            copy.start()
            mine.append(copy)
            at += 1
        copies.append(mine)
    g = g_ref[...]
    half = away_ref.shape[1] // rows
    starts = [0]
    while starts[-1] < count:
        starts.append(starts[-1] + (2 if count - starts[-1] in (2, 4) else 3))
    for index in range(count):
        for copy in copies[index]:
            copy.wait()
        if index + 1 not in starts:
            continue
        start = starts[starts.index(index + 1) - 1]
        product = mm(buffer[start * rows : (index + 1) * rows], g)
        for done in range(start, index + 1):
            part = product[(done - start) * rows : (done - start + 1) * rows]
            slots[done] = part.T.astype(BF16)
            place = order_ref[done]
            lanes = pl.ds(pl.multiple_of(place % half * rows, 128), rows)

            @pl.when(place < half)
            def _():
                target = away_ref.at[:, lanes]
                pltpu.make_async_copy(slots.at[done], target, out_sems.at[done]).start()

            @pl.when(place >= half)
            def _():
                target = own_ref.at[:, lanes]
                pltpu.make_async_copy(slots.at[done], target, out_sems.at[done]).start()

    for index in range(count):
        target = away_ref.at[:, pl.ds(0, rows)]
        pltpu.make_async_copy(slots.at[index], target, out_sems.at[index]).wait()


def after_kernel(*refs):
    pass


def inner_kernel(
    r_ref, rt_ref, g_ref, x_ref, b_ref, c_ref, q_ref, *refs
):
    d_ref, grad_b_ref, grad_c_ref, sum_ref, top_ref, low_ref = refs[-6:]
    so_far = refs[:-6]
    step = pl.program_id(1)
    b = b_ref[...]
    c = c_ref[...]
    scores = dot(b, c, ((1,), (1,)))
    running = r_ref[...]
    columns = rt_ref[0]
    top_keep = iota((HALF, SPAN), 1) >= iota((HALF, SPAN), 0)
    low_keep = iota((HALF, HALF), 1) >= iota((HALF, HALF), 0)

    @pl.when(step == 0)
    def _():
        sum_ref[...] = jnp.zeros_like(sum_ref)
        grad_b_ref[...] = so_far[0][...] if so_far else jnp.zeros_like(grad_b_ref)

    rows = []
    lane = iota((SPAN, 2 * P_SIZE), 1)
    later = not_before().astype(BF16)
    top_less = iota((HALF, SPAN), 1) > iota((HALF, SPAN), 0)
    low_less = iota((HALF, HALF), 1) > iota((HALF, HALF), 0)
    for pair in range(GROUP // 2):
        lanes = slice(pair * 2 * P_SIZE, (pair + 1) * 2 * P_SIZE)
        x = x_ref[:, lanes]
        none = jnp.zeros_like(x)
        x = [jnp.where(lane < P_SIZE, x, none), jnp.where(lane < P_SIZE, none, x)]
        product = mm(jnp.concatenate(x, axis=0), g_ref[:, lanes].T)
        top_sum = low_sum = None
        for number in range(2):
            head = 2 * pair + number
            row = running[head : head + 1]
            at = number * SPAN
            top = jnp.where(top_keep, row - columns[:HALF, head : head + 1], NEVER)
            low = jnp.where(low_keep, row[:, HALF:] - columns[HALF:, head : head + 1], NEVER)
            top = jnp.exp2(top) * product[at : at + HALF]
            low = jnp.exp2(low) * product[at + HALF : at + SPAN, HALF:]
            top_sum = top if number == 0 else top_sum + top
            low_sum = low if number == 0 else low_sum + low
            part = slice(head * HALF, (head + 1) * HALF)
            top_ref[part] = (top * scores[:HALF]).astype(BF16)
            low_ref[part] = (low * scores[HALF:, HALF:]).astype(BF16)
        sum_ref[:HALF] += top_sum
        sum_ref[HALF:, HALF:] += low_sum
    top = mm(top_ref[...], later)
    low = mm(low_ref[...], later[HALF:, HALF:])
    for head in range(GROUP):
        part = slice(head * HALF, (head + 1) * HALF)
        top_row = jnp.sum(jnp.where(top_less, top[part], 0.0), axis=0, keepdims=True)
        low_row = jnp.sum(jnp.where(low_less, low[part], 0.0), axis=0, keepdims=True)
        rows.append(jnp.concatenate([top_row[:, :HALF], top_row[:, HALF:] + low_row], axis=1))
    to_end = jnp.exp2(spread_columns(columns[SPAN - 1 : SPAN] - columns))
    scaled = x_ref[...].astype(F32) * to_end
    ends = dot(one_hot(BF16), (scaled * mm(b, q_ref[0])).astype(BF16), ((1,), (1,)))
    d_ref[...] = jnp.concatenate(rows, axis=0) + sum_over(ends, before())
    grad_b_ref[...] += dot(scaled.astype(BF16), q_ref[0], ((1,), (1,)))

    @pl.when(step == pl.num_programs(1) - 1)
    def _():
        total = sum_ref[...].astype(BF16)
        grad_b_ref[...] += mm(total, c)
        part = dot(total, b, ((0,), (0,)))
        grad_c_ref[...] = part + so_far[1][...] if so_far else part


def state_kernel(
    rt_ref, g_ref, c_ref, s_ref, e_ref, q_ref, a_ref, d_part_ref, c_part_ref, *refs
):
    d_ref, grad_c_ref, held = refs[-3:]
    span, group = pl.program_id(0), pl.program_id(1)

    @pl.when(group == 0)
    def _():
        grad_c_ref[...] = c_part_ref[...]

    @pl.when(span == 0)
    def _():
        held[group] = s_ref[...]

    state = held[group]
    low = state.astype(BF16)
    scaled = g_ref[...].astype(F32) * jnp.exp2(spread_columns(rt_ref[0]))
    ends = dot(one_hot(BF16), (scaled * mm(c_ref[...], low)).astype(BF16), ((1,), (1,)))
    grad_c_ref[...] += dot(scaled.astype(BF16), low, ((1,), (1,)))
    product = jnp.sum(q_ref[0].astype(F32) * state, axis=0, keepdims=True) * a_ref[0, :1]
    high, middle, last = thirds(product)
    row = iota((8, WIDE), 0)
    stacked = jnp.where(row == 0, high, jnp.where(row == 1, middle, jnp.where(row == 2, last, 0.0)))
    kept = dot(one_hot(BF16), stacked.astype(BF16), ((1,), (1,)))
    kept = jnp.sum(kept, axis=1, keepdims=True)
    d_ref[...] = d_part_ref[...] + sum_over(ends, not_before()) + kept
    held[group] = e_ref[0] + a_ref[0, :1] * state


def call(kernel, grid, in_specs, out_specs, out_shape, flops, size, scratch=()):
    return pl.pallas_call(
        kernel,
        grid=grid,
        in_specs=in_specs,
        out_specs=out_specs,
        out_shape=out_shape,
        scratch_shapes=list(scratch),
        cost_estimate=pl.CostEstimate(flops=flops, bytes_accessed=size, transcendentals=0),
        compiler_params=pltpu.CompilerParams(
            dimension_semantics=("arbitrary",) * len(grid), vmem_limit_bytes=GRANT
        ),
    )


def run_spec(at=0):
    return pl.BlockSpec((GROUP, SPAN), lambda k, h: (h + at, k))


def run_t_spec(at=0):
    return pl.BlockSpec((1, SPAN, GROUP), lambda k, h: (h + at, k, 0))


def rows_spec(at=0):
    return pl.BlockSpec((SPAN, WIDE), lambda k, h: (k, h + at))


def state_spec(at=0):
    return pl.BlockSpec((1, 2 * P_SIZE, WIDE), lambda k, h: (k, 0, h + at))


def kept_spec(at=0):
    return pl.BlockSpec((1, 8, WIDE), lambda k, h: (k, 0, h + at))


SHARED = pl.BlockSpec((SPAN, 2 * P_SIZE), lambda k, h: (k, 0))
GAIN = pl.BlockSpec((1, WIDE), lambda k, h: (0, h))
ANYWHERE = pl.BlockSpec(memory_space=pl.ANY)
INNER_SCRATCH = [
    pltpu.VMEM((SPAN, SPAN), F32),
    pltpu.VMEM((GROUP * HALF, SPAN), BF16),
    pltpu.VMEM((GROUP * HALF, HALF), BF16),
]
SCALARS = pl.BlockSpec(memory_space=pltpu.SMEM)


def shape(*dims, dtype=F32):
    return jax.ShapeDtypeStruct(dims, dtype)


def swap(value, axis, bit):
    count = lax.axis_size(axis)
    return lax.ppermute(value, axis, [(i, i ^ bit) for i in range(count)])


def block_products(kept):
    count = lax.axis_size("ctx")
    place = lax.axis_index("ctx")
    steps = []
    before_me = jnp.ones_like(kept)
    after_me = jnp.ones_like(kept)
    bit = 1
    while bit < count:
        other = swap(kept, "ctx", bit)
        upper = (place & bit) != 0
        steps.append((bit, upper, kept, other, before_me, after_me))
        before_me = jnp.where(upper, before_me * other, before_me)
        after_me = jnp.where(upper, after_me, after_me * other)
        kept = kept * other
        bit *= 2
    return steps


def scan_states(total, steps, reverse):
    entering = jnp.zeros_like(total)
    for bit, upper, kept, other, before_me, after_me in steps:
        got = swap(total.astype(BF16), "ctx", bit).astype(F32)
        if reverse:
            entering = entering + jnp.where(upper, 0.0, after_me) * got
            total = jnp.where(upper, got + other * total, total + kept * got)
        else:
            entering = entering + jnp.where(upper, before_me, 0.0) * got
            total = jnp.where(upper, kept * got + total, other * total + got)
    return entering


def head_sum(value):
    bit = 1
    while bit < lax.axis_size("head"):
        value = value.astype(BF16)
        value = value.astype(F32) + swap(value, "head", bit).astype(F32)
        bit *= 2
    return value


PLANE = 4


def after(values, *tokens):
    out = pl.pallas_call(
        after_kernel,
        in_specs=[ANYWHERE] * (len(values) + len(tokens)),
        out_specs=[ANYWHERE] * len(values),
        out_shape=[shape(*value.shape, dtype=value.dtype) for value in values],
        input_output_aliases={index: index for index in range(len(values))},
        cost_estimate=pl.CostEstimate(flops=0, bytes_accessed=0, transcendentals=0),
        compiler_params=pltpu.CompilerParams(vmem_limit_bytes=GRANT),
    )(*values, *tokens)
    return list(out)


def along_z(value, moves):
    pairs = [(a * PLANE + i, b * PLANE + i) for a, b in moves for i in range(PLANE)]
    return lax.ppermute(value, "ctx", pairs)


MIDDLE = ((1, 2), (2, 1))
OUTWARD = ((1, 0), (2, 3))


def swap_x(value):
    return swap(value, "ctx", 1)


def swap_y(value):
    return swap(value, "ctx", 2)


LAYERS = ((0, 1, 2, 3), (1, 0, 3, 2), (2, 2, 1, 1), (3, 3, 0, 0))
EARLY = [(k, flip) for k in (0, 1, 2) for flip in range(3)]
LATE = [(0, 3), (1, 3), (2, 3), (3, 0), (3, 1), (3, 2), (3, 3)]


def block_order():
    place = lax.axis_index("ctx")
    layer, spot = place // PLANE, place % PLANE
    layers = jnp.array(LAYERS, jnp.int32)[:, layer]
    order = [layers[k] * PLANE + (spot ^ flip) for k, flip in EARLY + LATE]
    return jnp.stack(order).astype(jnp.int32)


def gather_weight(w, sizes):
    ends = [sum(sizes[: j + 1]) * P_SIZE for j in range(len(sizes))]
    parts = [w[:, end - size * P_SIZE : end] for end, size in zip(ends, sizes)]
    return [lax.all_gather(part, "ctx", axis=0, tiled=True) for part in parts]


def forward(features, first, weight, running_t, b_rows, here):
    own, other = features
    length = own.shape[0]
    n = b_rows.shape[1]
    width, wide = weight.shape
    deep = width // 4
    spans = length // SPAN

    def depth(k, first_ref):
        return (k // 2 ^ first_ref[0]) * 2 + k % 2

    return pl.pallas_call(
        forward_kernel,
        grid_spec=pltpu.PrefetchScalarGridSpec(
            num_scalar_prefetch=1,
            grid=(wide // WIDE, 4),
            in_specs=[
                pl.BlockSpec((length, deep), lambda h, k, first_ref: (0, jnp.minimum(k, 1))),
                pl.BlockSpec((length, deep), lambda h, k, first_ref: (0, jnp.maximum(k - 2, 0))),
                pl.BlockSpec((deep, WIDE), lambda h, k, first_ref: (depth(k, first_ref), h)),
                pl.BlockSpec((1, length, GROUP), lambda h, k, first_ref: (h + here, 0, 0)),
                pl.BlockSpec((length, n), lambda h, k, first_ref: (0, 0)),
            ],
            out_specs=[
                pl.BlockSpec((length, WIDE), lambda h, k, first_ref: (0, h)),
                pl.BlockSpec((spans, n, WIDE), lambda h, k, first_ref: (0, 0, h)),
            ],
            scratch_shapes=[pltpu.VMEM((length, WIDE), F32)],
        ),
        out_shape=[shape(length, wide, dtype=BF16), shape(spans, n, wide)],
        cost_estimate=pl.CostEstimate(
            flops=2 * length * wide * width, bytes_accessed=2 * wide * width, transcendentals=0
        ),
        compiler_params=pltpu.CompilerParams(
            dimension_semantics=("arbitrary", "arbitrary"), vmem_limit_bytes=GRANT
        ),
    )(first, own, other, weight, running_t, b_rows)


def multiply(grad_x, weight, at, half, halves, before=None, other=None):
    length = grad_x.shape[0]
    width, wide = weight.shape
    tiles = width // halves // WIDE
    tile = pl.BlockSpec((length, WIDE), lambda j, half_ref: (0, half_ref[0] * tiles + j))
    plain = pl.BlockSpec((length, WIDE), lambda j, half_ref: (0, j))
    in_specs = [
        pl.BlockSpec((length, wide), lambda j, half_ref: (0, at)),
        pl.BlockSpec((WIDE, wide), lambda j, half_ref: (half_ref[0] * tiles + j, 0)),
    ]
    operands = [grad_x, weight]
    if before is not None:
        in_specs.append(tile)
        operands.append(before)
    if other is not None:
        in_specs.append(plain)
        operands.append(other)
    return pl.pallas_call(
        functools.partial(product_kernel, before is not None, other is not None),
        grid_spec=pltpu.PrefetchScalarGridSpec(
            num_scalar_prefetch=1,
            grid=(tiles,),
            in_specs=in_specs,
            out_specs=plain,
        ),
        out_shape=shape(length, width // halves, dtype=BF16),
        cost_estimate=pl.CostEstimate(
            flops=2 * length * wide * width // halves,
            bytes_accessed=2 * wide * width // halves,
            transcendentals=0,
        ),
        compiler_params=pltpu.CompilerParams(
            dimension_semantics=("arbitrary",), vmem_limit_bytes=GRANT
        ),
    )(half, *operands)


def early_forward(features, pieces):
    length = features.shape[0]
    rows, columns = pieces[0].shape
    deep = rows * len(pieces)
    return call(
        functools.partial(early_forward_kernel, len(pieces)),
        (columns // WIDE,),
        [pl.BlockSpec((length, deep), lambda h: (0, 0))]
        + [pl.BlockSpec((rows, WIDE), lambda h: (0, h))] * len(pieces),
        pl.BlockSpec((length, WIDE), lambda h: (0, h)),
        shape(length, columns),
        2 * length * columns * deep,
        2 * columns * deep,
        [pltpu.VMEM((deep, WIDE), BF16)],
    )(features, *pieces)


def late_forward(features, part, pieces, running_t, b_rows, kept, here):
    length = features.shape[0]
    rows, columns = pieces[0].shape
    deep = rows * len(pieces)
    n = b_rows.shape[1]
    spans = length // SPAN
    state = pl.BlockSpec((n, WIDE), lambda h: (0, h))
    return call(
        functools.partial(late_forward_kernel, len(pieces)),
        (columns // WIDE,),
        [
            pl.BlockSpec((length, deep), lambda h: (0, 0)),
            pl.BlockSpec((length, WIDE), lambda h: (0, h + here)),
            pl.BlockSpec((1, length, GROUP), lambda h: (h + here, 0, 0)),
            pl.BlockSpec((length, n), lambda h: (0, 0)),
            pl.BlockSpec((spans, 8, WIDE), lambda h: (0, 0, h + here)),
        ]
        + [pl.BlockSpec((rows, WIDE), lambda h: (0, h))] * len(pieces),
        [
            pl.BlockSpec((length, WIDE), lambda h: (0, h)),
            pl.BlockSpec((spans, n, WIDE), lambda h: (0, 0, h)),
            state,
        ],
        [
            shape(length, columns, dtype=BF16),
            shape(spans, n, columns),
            shape(n, columns, dtype=BF16),
        ],
        2 * length * columns * deep,
        2 * columns * deep,
        [pltpu.VMEM((deep, WIDE), BF16)],
    )(features, part, running_t, b_rows, kept, *pieces)


def multiply_blocks(order, grad_x, pieces, so_far):
    columns, length = grad_x.shape
    arrays = [array for piece in pieces for array in piece]
    rows = arrays[0].shape[0]
    count = len(pieces)
    half = shape(length, lax.axis_size("ctx") * rows // 2, dtype=BF16)
    first = 2 + len(arrays)
    return pl.pallas_call(
        functools.partial(blocks_kernel, [len(piece) for piece in pieces], bool(so_far)),
        grid=(1,),
        in_specs=[SCALARS, pl.BlockSpec((columns, length), lambda h: (0, 0))]
        + [ANYWHERE] * (len(arrays) + len(so_far)),
        out_specs=[ANYWHERE, ANYWHERE],
        out_shape=[half, half],
        input_output_aliases={first + k: k for k in range(len(so_far))},
        scratch_shapes=[
            pltpu.VMEM((rows * count, columns), BF16),
            pltpu.VMEM((count, length, rows), BF16),
            pltpu.SemaphoreType.DMA((len(arrays),)),
            pltpu.SemaphoreType.DMA((count,)),
        ],
        cost_estimate=pl.CostEstimate(
            flops=2 * length * columns * rows * count,
            bytes_accessed=2 * columns * rows * count,
            transcendentals=0,
        ),
        compiler_params=pltpu.CompilerParams(
            dimension_semantics=("arbitrary",), vmem_limit_bytes=GRANT
        ),
    )(order, grad_x, *arrays, *so_far)


def back_start(own_grads, kept):
    spans, n, columns = own_grads.shape
    return call(
        start_kernel,
        (columns // WIDE,),
        [
            pl.BlockSpec((spans, n, WIDE), lambda h: (0, 0, h)),
            pl.BlockSpec((spans, 8, WIDE), lambda h: (0, 0, h)),
        ],
        [pl.BlockSpec((rows, WIDE), lambda h: (0, h)) for rows in (8, n + TAIL)],
        [shape(8, columns), shape(n + TAIL, columns, dtype=BF16)],
        0,
        14 * n * columns,
    )(own_grads, kept)


def back_step(place, log, sent, entering, bit):
    got = swap(sent, "ctx", bit)
    columns = sent.shape[1]
    n = sent.shape[0] - TAIL
    short, state, tall = [
        pl.BlockSpec((rows, 2 * WIDE), lambda h: (0, h)) for rows in (8, n, n + TAIL)
    ]
    return call(
        functools.partial(back_kernel, bit),
        (columns // (2 * WIDE),),
        [SCALARS, short, tall, tall] + [state] * len(entering),
        [state, tall, short, short],
        [
            shape(n, columns),
            shape(n + TAIL, columns, dtype=BF16),
            shape(8, columns),
            shape(8, columns),
        ],
        0,
        14 * n * columns,
    )(place, log, sent, got, *entering)


def scan_step(factors, here, sent, entering, bit, last=False):
    got = swap(sent, "ctx", bit)
    n, columns = sent.shape
    block = pl.BlockSpec((n, columns), lambda h: (0, 0))
    at = here * WIDE // columns
    outs = [shape(n, columns), shape(n, columns, dtype=BF16)][: 2 - last]
    return call(
        functools.partial(scan_kernel, last),
        (1,),
        [pl.BlockSpec((8, columns), lambda h: (0, at)), block, block] + [block] * len(entering),
        [block] * len(outs),
        outs,
        0,
        10 * n * columns,
    )(factors, sent, got, *entering)


def scan_pair(first, second, last=False):
    operands, specs, outs = [], [], []
    for factors, here, sent, entering, bit in (first, second):
        got = swap(sent, "ctx", bit)
        n, columns = sent.shape
        block = pl.BlockSpec((n, columns), lambda h: (0, 0))
        at = here * WIDE // columns
        operands += [factors, sent, got, *entering]
        specs += [pl.BlockSpec((8, columns), lambda h, at=at: (0, at))]
        specs += [block] * (2 + len(entering))
        outs += [shape(n, columns), shape(n, columns, dtype=BF16)]
    outs = outs[: 4 - last]
    return call(
        functools.partial(scan_pair_kernel, 3 + len(first[3]), last),
        (1,),
        specs,
        [block] * len(outs),
        outs,
        0,
        20 * n * columns,
    )(*operands)


def local(inputs, w_in, b_rows, c_rows, log_decay, skip_gain, grad_out):
    groups = log_decay.shape[0] // GROUP
    layered = lax.axis_size("ctx") == 4 * PLANE and lax.axis_size("head") == 2
    if layered and groups % 2 == 0 and w_in.shape[0] == 256:
        return local_layered(inputs, w_in, b_rows, c_rows, log_decay, skip_gain, grad_out)
    return local_plain(inputs, w_in, b_rows, c_rows, log_decay, skip_gain, grad_out)


def prepare(log_decay, grad_out, c_rows):
    length, columns = grad_out.shape
    heads = log_decay.shape[0]
    spans = length // SPAN
    groups = heads // GROUP
    n = c_rows.shape[1]
    return call(
        decay_kernel,
        (spans, groups),
        [run_spec(), rows_spec(), SHARED],
        [run_spec(), run_t_spec(), kept_spec(), state_spec()],
        [
            shape(heads, length),
            shape(groups, length, GROUP),
            shape(spans, 8, columns),
            shape(spans, n, columns),
        ],
        2 * length * columns * n,
        6 * length * columns,
    )(log_decay, grad_out, c_rows)


def inner(grid, here, wide, operands, so_far):
    length = operands[2].shape[0]
    n = operands[4].shape[1]
    specs = [
        run_spec(here),
        run_t_spec(here),
        rows_spec(here),
        rows_spec(),
        SHARED,
        SHARED,
        state_spec(here),
    ]
    return call(
        inner_kernel,
        grid,
        specs + [SHARED] * len(so_far),
        [run_spec(), SHARED, SHARED],
        [shape(wide // P_SIZE, length), shape(length, n), shape(length, n)],
        12 * length * wide * SPAN,
        6 * length * wide,
        INNER_SCRATCH,
    )(*operands, *so_far)


def state_terms(grid, here, wide, operands, heads=None, so_far=None):
    length = operands[1].shape[0]
    n = operands[2].shape[1]
    heads = heads or wide // P_SIZE
    at = here if heads > wide // P_SIZE else 0
    extra = () if so_far is None else (so_far,)
    return pl.pallas_call(
        state_kernel,
        grid=grid,
        in_specs=[
            run_t_spec(here),
            rows_spec(here),
            SHARED,
            pl.BlockSpec((n, WIDE), lambda k, h: (0, h)),
            state_spec(),
            state_spec(here),
            kept_spec(here),
            run_spec(),
            SHARED,
        ]
        + [ANYWHERE] * len(extra),
        out_specs=[run_spec(at), SHARED],
        out_shape=[shape(heads, length), shape(length, n)],
        scratch_shapes=[pltpu.VMEM((grid[1], n, WIDE), F32)],
        input_output_aliases={len(operands): 0} if extra else {},
        cost_estimate=pl.CostEstimate(
            flops=4 * length * wide * n, bytes_accessed=6 * length * wide, transcendentals=0
        ),
        compiler_params=pltpu.CompilerParams(
            dimension_semantics=("arbitrary", "arbitrary"), vmem_limit_bytes=GRANT
        ),
    )(*operands, *extra)


def local_layered(inputs, w_in, b_rows, c_rows, log_decay, skip_gain, grad_out):
    length, columns = grad_out.shape
    heads = log_decay.shape[0]
    spans = length // SPAN
    groups = heads // GROUP
    place = lax.axis_index("head").astype(jnp.int32)
    half = columns // 2
    order = block_order()
    blocks = order.shape[0]
    width = blocks * w_in.shape[0]

    z1, inner2 = swap(w_in, "ctx", PLANE), along_z(w_in, MIDDLE)
    own_x, own_y = swap_x(w_in), swap_y(w_in)
    other = swap(inputs, "head", 1)
    running, running_t, kept, own_grads = prepare(log_decay, grad_out, c_rows)
    spot = lax.axis_index("ctx").astype(jnp.int32)[None]
    log, sent = back_start(own_grads, kept)
    sent = after([sent], other)[0]
    leaving, moved, log, factors_1 = back_step(spot, log, sent, (), 1)

    z1, inner2, own_y = after([z1, inner2, own_y], own_x, sent)
    sent = moved
    x1, y1 = swap_x(z1), swap_y(z1)
    inner3, outer2 = along_z(z1, MIDDLE), along_z(inner2, OUTWARD)
    own_y_a, own_y_b = own_y[:, :half], own_y[:, half:]
    inner3_a, inner3_b = inner3[:, :half], inner3[:, half:]
    leaving, sent, log, factors_2 = back_step(spot, log, sent, (leaving,), 2)
    order_own = (order + place * (blocks // 2)) % blocks
    cut = len(EARLY) * w_in.shape[0]
    early_features, late_features = call(
        arrange_kernel,
        (1,),
        [SCALARS] + [pl.BlockSpec((length, width // 2), lambda h: (0, 0))] * 2,
        [pl.BlockSpec((length, wide), lambda h: (0, 0)) for wide in (cut, width - cut)],
        [shape(length, wide, dtype=BF16) for wide in (cut, width - cut)],
        0,
        4 * length * width,
        [pltpu.VMEM((length, width), BF16)],
    )(order_own, inputs, other)

    inner2, inner3_a, inner3_b, outer2, x1, sent, own_y_a, own_y_b = after(
        [inner2, inner3_a, inner3_b, outer2, x1, sent, own_y_a, own_y_b], y1, early_features
    )
    z3 = inner2 + outer2
    x3, y3 = swap_x(z3), swap_y(z3)
    outer3_a = along_z(inner3_a, OUTWARD)
    x1_a, x1_b = x1[:, :half], x1[:, half:]
    leaving, sent, log, factors_4 = back_step(spot, log, sent, (leaving,), 4)

    inner3_a, inner3_b, outer3_a, y3, x1_a, x1_b = after(
        [inner3_a, inner3_b, outer3_a, y3, x1_a, x1_b], x3
    )
    z2a = inner3_a + outer3_a
    outer3_b = along_z(inner3_b, OUTWARD)
    y3_a, y3_b = y3[:, :half], y3[:, half:]
    x2a, y2a = swap_x(z2a), swap_y(z2a)
    d3a, d1a = swap_x(y3_a), swap_y(x1_a)
    leaving, sent, log, factors_8 = back_step(spot, log, sent, (leaving,), 8)
    early = [w_in, own_x, own_y, z1, x1, y1, z3, x3, y3]
    part = early_forward(early_features, early)

    own_y_a, x2a, leaving = after([own_y_a, x2a, leaving], y2a, d3a, d1a, part)
    d0a, d2a = swap_x(own_y_a), swap_y(x2a)
    leaving_all = [leaving]
    for k in range(spans - 1, 0, -1):
        leaving_all.insert(0, own_grads[k] + kept[k, :1] * leaving_all[0])
    leaving_all = jnp.stack([value.astype(BF16) for value in leaving_all])
    (z2b,) = after([inner3_b + outer3_b], leaving_all)
    x2b, y2b = swap_x(z2b), swap_y(z2b)
    skip = jnp.repeat(skip_gain, P_SIZE)[None]
    grad_x = grad_rows(running, running_t, grad_out, b_rows, c_rows, leaving_all, skip, True)
    order_away = (order + (1 - place) * (blocks // 2)) % blocks
    early_order, late_order = order_away[: len(EARLY)], order_away[len(EARLY) :]
    late_a = [d0a, d1a, d3a, z2a, x2a, y2a, d2a]
    x_a, states_a, sent_a = late_forward(
        late_features, part, late_a, running_t, b_rows, kept, 0
    )

    own_y_b, x2b, y3_b, x1_b, grad_x = after([own_y_b, x2b, y3_b, x1_b, grad_x], y2b, sent_a)
    d0b, d2b = swap_x(own_y_b), swap_y(x2b)
    d3b, d1b = swap_x(y3_b), swap_y(x1_b)
    product = multiply_blocks(early_order, grad_x, [[piece] for piece in early], ())
    shared = (running, running_t, grad_out)
    here = groups // 2
    grid = (spans, here)

    d0b, d2b, sent_a = after([d0b, d2b, sent_a], d3b, d1b, product[0])
    entering_a, sent_a = scan_step(factors_1, 0, sent_a, (), 1)
    late_b = [d0b, d1b, d3b, z2b, x2b, y2b, d2b]
    x_b, states_b, sent_b = late_forward(
        late_features, part, late_b, running_t, b_rows, kept, here
    )
    pairs = list(zip(late_a, late_b))
    sent_a, sent_b, *product = after([sent_a, sent_b, *product])
    entering_b, sent_b, entering_a, sent_a = scan_pair(
        (factors_1, here, sent_b, (), 1), (factors_2, 0, sent_a, (entering_a,), 2)
    )
    away, own = multiply_blocks(late_order, grad_x, pairs, product)

    sent_a, sent_b, x_a, away = after([sent_a, sent_b, x_a, away])
    entering_b, sent_b, entering_a, sent_a = scan_pair(
        (factors_2, here, sent_b, (entering_b,), 2), (factors_4, 0, sent_a, (entering_a,), 4)
    )
    got = swap(away, "head", 1)
    inner_a = shared + (x_a, b_rows, c_rows, leaving_all)
    decay_a, grad_b, grad_c = inner(grid, 0, half, inner_a, ())

    sent_a, sent_b, x_b, grad_b = after([sent_a, sent_b, x_b, grad_b])
    entering_b, sent_b, entering_a = scan_pair(
        (factors_4, here, sent_b, (entering_b,), 4),
        (factors_8, 0, sent_a, (entering_a,), 8),
        True,
    )
    inner_b = shared + (x_b, b_rows, c_rows, leaving_all)
    decay_b, grad_b, grad_c = inner(grid, here, half, inner_b, (grad_b, grad_c))

    sent_b, entering_a, got, grad_b = after([sent_b, entering_a, got, grad_b])
    grad_b = head_sum(grad_b)
    grad_inputs = (own.astype(F32) + got.astype(F32)).astype(BF16)
    (entering_b,) = scan_step(factors_8, here, sent_b, (entering_b,), 8, True)
    common = (running_t, grad_out, c_rows)
    state_a = common + (entering_a, states_a, leaving_all, kept, decay_a, grad_c)
    decays, grad_c = state_terms(grid, 0, half, state_a, heads)
    (entering_b,) = after([entering_b], grad_inputs, grad_c)
    state_b = common + (entering_b, states_b, leaving_all, kept, decay_b, grad_c)
    decays, grad_c = state_terms(grid, here, half, state_b, heads, decays)
    return (grad_inputs, grad_b, head_sum(grad_c), decays)


def grad_rows(running, running_t, grad_out, b_rows, c_rows, leaving, skip, transposed):
    length, columns = grad_out.shape
    spec, dims = rows_spec(), (length, columns)
    if transposed:
        spec, dims = pl.BlockSpec((WIDE, SPAN), lambda k, h: (h, k)), (columns, length)
    return call(
        functools.partial(grad_x_kernel, transposed),
        (length // SPAN, running_t.shape[0]),
        [run_spec(), run_t_spec(), rows_spec(), SHARED, SHARED, state_spec(), GAIN],
        spec,
        shape(*dims, dtype=BF16),
        8 * length * columns * SPAN,
        6 * length * columns,
    )(running, running_t, grad_out, b_rows, c_rows, leaving, skip)


def local_plain(inputs, w_in, b_rows, c_rows, log_decay, skip_gain, grad_out):
    length, columns = grad_out.shape
    heads = log_decay.shape[0]
    spans = length // SPAN
    groups = heads // GROUP
    n = b_rows.shape[1]
    grid = (spans, groups)

    sizes = (heads // 2, heads // 4, heads // 4) if heads % (4 * GROUP) == 0 else (heads,)
    weights = gather_weight(w_in, sizes)
    two = lax.axis_size("head") == 2
    place = lax.axis_index("head").astype(jnp.int32)[None]
    width = weights[0].shape[0]
    if two:
        features = (inputs, swap(inputs, "head", 1))
        first = place
    else:
        features = lax.all_gather(inputs, "head", axis=1, tiled=True)
        features = (features[:, : width // 2], features[:, width // 2 :])
        first = jnp.zeros((1,), jnp.int32)

    running, running_t, kept, own_grads = call(
        decay_kernel,
        grid,
        [run_spec(), rows_spec(), SHARED],
        [run_spec(), run_t_spec(), kept_spec(), state_spec()],
        [
            shape(heads, length),
            shape(groups, length, GROUP),
            shape(spans, 8, columns),
            shape(spans, n, columns),
        ],
        2 * length * columns * n,
        6 * length * columns,
    )(log_decay, grad_out, c_rows)

    kept_total = kept[0, :1]
    for k in range(1, spans):
        kept_total = kept_total * kept[k, :1]
    steps = block_products(kept_total)

    total = own_grads[spans - 1]
    for k in range(spans - 2, -1, -1):
        total = own_grads[k] + kept[k, :1] * total
    leaving = [scan_states(total, steps, True)]
    for k in range(spans - 1, 0, -1):
        leaving.insert(0, own_grads[k] + kept[k, :1] * leaving[0])
    leaving = jnp.stack([value.astype(BF16) for value in leaving])

    skip = jnp.repeat(skip_gain, P_SIZE)[None]
    grad_x = grad_rows(running, running_t, grad_out, b_rows, c_rows, leaving, skip, False)

    grad_b = grad_c = product = None
    tokens = ()
    decay_parts = []
    at = 0
    for index, size in enumerate(sizes):
        wide = size * P_SIZE
        here = at // GROUP
        count = size // GROUP
        weight = weights[index]
        if tokens:
            weight = after([weight], *tokens)[0]
        x, own_states = forward(features, first, weight, running_t, b_rows, here)

        chunk = slice(at * P_SIZE, at * P_SIZE + wide)
        total = own_states[0]
        for k in range(1, spans):
            total = kept[k, :1, chunk] * total + own_states[k]
        cut = [step[:2] + tuple(value[:, chunk] for value in step[2:]) for step in steps]
        entering = scan_states(total, cut, False)

        so_far = () if grad_b is None else (grad_b, grad_c)
        decay_part, grad_b, grad_c = call(
            inner_kernel,
            (spans, count),
            [
                run_spec(here),
                run_t_spec(here),
                rows_spec(here),
                rows_spec(),
                SHARED,
                SHARED,
                state_spec(here),
            ]
            + [SHARED] * len(so_far),
            [run_spec(), SHARED, SHARED],
            [shape(size, length), shape(length, n), shape(length, n)],
            12 * length * wide * SPAN,
            6 * length * wide,
            INNER_SCRATCH,
        )(running, running_t, grad_out, x, b_rows, c_rows, leaving, *so_far)
        decay_part, grad_c = call(
            state_kernel,
            (spans, count),
            [
                run_t_spec(here),
                rows_spec(here),
                SHARED,
                pl.BlockSpec((n, WIDE), lambda k, h: (0, h)),
                state_spec(),
                state_spec(here),
                kept_spec(here),
                run_spec(),
                SHARED,
            ],
            [run_spec(), SHARED],
            [shape(size, length), shape(length, n)],
            4 * length * wide * n,
            6 * length * wide,
            [pltpu.VMEM((count, n, WIDE), F32)],
        )(running_t, grad_out, c_rows, entering, own_states, leaving, kept, decay_part, grad_c)
        decay_parts.append(decay_part)

        if index < len(sizes) - 1:
            zero = jnp.zeros((1,), jnp.int32)
            product = multiply(grad_x, weight, at // size, zero, 1, product)
            tokens = (product, grad_b, entering)
        elif two:
            sent = multiply(grad_x, weight, at // size, 1 - place, 2, product)
            got = swap(sent, "head", 1)
            grad_inputs = multiply(grad_x, weight, at // size, place, 2, product, got)
        else:
            zero = jnp.zeros((1,), jnp.int32)
            product = multiply(grad_x, weight, at // size, zero, 1, product)
            grad_inputs = lax.psum_scatter(product, "head", scatter_dimension=1, tiled=True)
        at += size

    return (grad_inputs, head_sum(grad_b), head_sum(grad_c), jnp.concatenate(decay_parts, axis=0))


def solution(mesh):
    in_specs = (
        P("ctx", "head"),
        P("ctx", "head"),
        P("ctx", None),
        P("ctx", None),
        P("head", "ctx"),
        P("head"),
        P("ctx", "head"),
    )
    out_specs = (P("ctx", "head"), P("ctx", None), P("ctx", None), P("head", "ctx"))
    return jax.shard_map(local, mesh=mesh, in_specs=in_specs, out_specs=out_specs, check_vma=False)
```

```python
import functools

import jax
import jax.numpy as jnp
from jax import lax
from jax.experimental import pallas as pl
from jax.experimental.pallas import tpu as pltpu
from jax.sharding import PartitionSpec as P

SPAN = 256
HALF = SPAN // 2
P_SIZE = 64
GROUP = 8
WIDE = GROUP * P_SIZE
LOG2E = 1.4426950408889634
NEVER = -1e30
GRANT = 64 * 2**20

F32 = jnp.float32
BF16 = jnp.bfloat16
EXACT = lax.Precision.HIGHEST


def dot(a, b, dims, precision=None):
    return lax.dot_general(a, b, (dims, ((), ())), precision=precision, preferred_element_type=F32)


def mm(a, b, precision=None):
    return dot(a, b, ((1,), (0,)), precision)


def iota(shape, dim):
    return lax.broadcasted_iota(jnp.int32, shape, dim)


def one_hot(dtype):
    return (iota((GROUP, WIDE), 0) == iota((GROUP, WIDE), 1) // P_SIZE).astype(dtype)


def not_before():
    return (iota((SPAN, SPAN), 0) >= iota((SPAN, SPAN), 1)).astype(F32)


def before():
    return (iota((SPAN, SPAN), 0) < iota((SPAN, SPAN), 1)).astype(F32)


def same():
    return (iota((SPAN, SPAN), 0) == iota((SPAN, SPAN), 1)).astype(F32)


def first_head():
    return iota((SPAN, 2 * P_SIZE), 1) < P_SIZE


def pair_columns(columns, pair):
    shape = (columns.shape[0], 2 * P_SIZE)
    left = jnp.broadcast_to(columns[:, 2 * pair : 2 * pair + 1], shape)
    right = jnp.broadcast_to(columns[:, 2 * pair + 1 : 2 * pair + 2], shape)
    return jnp.where(iota(shape, 1) < P_SIZE, left, right)


def spread_columns(columns):
    return jnp.concatenate([pair_columns(columns, pair) for pair in range(GROUP // 2)], axis=1)


def thirds(value):
    high = value.astype(BF16).astype(F32)
    middle = (value - high).astype(BF16).astype(F32)
    return high, middle, value - high - middle


def sum_over(value, mask):
    rows = value.shape[0]
    parts = mm(jnp.concatenate(thirds(value), axis=0).astype(BF16), mask.astype(BF16))
    return parts[:rows] + parts[rows : 2 * rows] + parts[2 * rows :]


def decay_kernel(d_ref, g_ref, c_ref, r_ref, rt_ref, a_ref, gt_ref):
    row_sums = sum_over(d_ref[...] * LOG2E, 1.0 - not_before() + same())
    r_ref[...] = row_sums
    padded = jnp.concatenate([row_sums, jnp.zeros((2 * P_SIZE - GROUP, SPAN), F32)], axis=0)
    running = padded.T[:, :GROUP]
    rt_ref[0] = running
    growth = jnp.exp2(spread_columns(running))
    last = spread_columns(running[SPAN - 1 : SPAN])
    a_ref[0] = jnp.where(iota((8, WIDE), 0) < 4, jnp.exp2(last), last)
    scaled = (g_ref[...].astype(F32) * growth).astype(BF16)
    gt_ref[0] = dot(c_ref[...], scaled, ((0,), (0,)))


def grad_x_kernel(transposed, r_ref, rt_ref, g_ref, b_ref, c_ref, q_ref, skip_ref, out_ref):
    b = b_ref[...]
    scores = dot(b, c_ref[...], ((1,), (1,)))
    running = r_ref[...]
    columns = rt_ref[0]
    top_keep = iota((HALF, SPAN), 1) >= iota((HALF, SPAN), 0)
    low_keep = iota((HALF, HALF), 1) >= iota((HALF, HALF), 0)
    from_state = None
    if q_ref is not None:
        to_end = jnp.exp2(spread_columns(columns[SPAN - 1 : SPAN] - columns))
        from_state = mm(b, q_ref[0]) * to_end
    for pair in range(GROUP // 2):
        lanes = slice(pair * 2 * P_SIZE, (pair + 1) * 2 * P_SIZE)
        g = g_ref[:, lanes]
        parts = []
        for head in (2 * pair, 2 * pair + 1):
            row = running[head : head + 1]
            top = jnp.where(top_keep, row - columns[:HALF, head : head + 1], NEVER)
            low = jnp.where(low_keep, row[:, HALF:] - columns[HALF:, head : head + 1], NEVER)
            parts.append((jnp.exp2(top) * scores[:HALF]).astype(BF16))
            low = (jnp.exp2(low) * scores[HALF:, HALF:]).astype(BF16)
            parts.append(jnp.concatenate([jnp.zeros((HALF, HALF), BF16), low], axis=1))
        product = mm(jnp.concatenate(parts, axis=0), g)
        parts = [product[:SPAN], product[SPAN:]]
        inner = jnp.where(first_head(), parts[0], parts[1])
        total = inner + skip_ref[:, lanes] * g.astype(F32)
        if from_state is not None:
            total = total + from_state[:, lanes]
        if transposed:
            out_ref[lanes, :] = total.T.astype(out_ref.dtype)
        else:
            out_ref[:, lanes] = total.astype(BF16)


def forward_kernel(half_ref, own_ref, other_ref, w_ref, rt_ref, b_ref, x_ref, e_ref, total_ref):
    step = pl.program_id(1)

    @pl.when(step == 0)
    def _():
        total_ref[...] = jnp.zeros_like(total_ref)

    half = pl.num_programs(1) // 2

    @pl.when(step < half)
    def _():
        total_ref[...] += mm(own_ref[...], w_ref[...])

    @pl.when(step >= half)
    def _():
        total_ref[...] += mm(other_ref[...], w_ref[...])

    @pl.when(step == pl.num_programs(1) - 1)
    def _():
        x = total_ref[...].astype(BF16)
        x_ref[...] = x
        for k in range(e_ref.shape[0]):
            rows = slice(k * SPAN, (k + 1) * SPAN)
            columns = rt_ref[0, rows]
            to_end = jnp.exp2(spread_columns(columns[SPAN - 1 : SPAN] - columns))
            scaled = (x[rows].astype(F32) * to_end).astype(BF16)
            e_ref[k] = dot(b_ref[rows], scaled, ((0,), (0,)))


def product_kernel(has_before, has_other, half_ref, g_ref, w_ref, *refs):
    refs = list(refs)
    total = dot(g_ref[...], w_ref[...], ((1,), (1,)))
    if has_before:
        total = total + refs.pop(0)[...].astype(F32)
    if has_other:
        total = total.astype(BF16).astype(F32) + refs.pop(0)[...].astype(F32)
    refs[0][...] = total.astype(BF16)


def arrange_kernel(order_ref, own_ref, other_ref, early_ref, late_ref, both_ref):
    half = own_ref.shape[1]
    both_ref[:, :half] = own_ref[...]
    both_ref[:, half:] = other_ref[...]
    unit = 2 * half // order_ref.shape[0]
    cut = early_ref.shape[1]
    for index in range(order_ref.shape[0]):
        source = pl.ds(pl.multiple_of(order_ref[index] * unit, 128), unit)
        at = index * unit
        if at < cut:
            early_ref[:, at : at + unit] = both_ref[:, source]
        else:
            late_ref[:, at - cut : at - cut + unit] = both_ref[:, source]


TAIL = 16


def message(total, log):
    high, middle, last = thirds(log)
    line = iota((TAIL, total.shape[1]), 0)
    tail = jnp.where(line == 0, high, jnp.where(line == 1, middle, jnp.where(line == 2, last, 0.0)))
    return total.astype(BF16), tail.astype(BF16)


def start_kernel(own_ref, kept_ref, log_ref, sent_ref):
    spans = own_ref.shape[0]
    total = own_ref[spans - 1]
    log = kept_ref[spans - 1, 4:5]
    for k in range(spans - 2, -1, -1):
        total = own_ref[k] + kept_ref[k, :1] * total
        log = log + kept_ref[k, 4:5]
    line = iota(log_ref.shape, 0)
    log_ref[...] = jnp.where(line == 0, log, 0.0)
    n = total.shape[0]
    sent_ref[:n], sent_ref[n:] = message(total, log)


def back_kernel(bit, place_ref, log_ref, mine_ref, got_ref, *refs):
    entering_ref = refs[0] if len(refs) == 5 else None
    entering_out, sent_out, log_out, factor_out = refs[-4:]
    n = entering_out.shape[0]
    got = got_ref[:n].astype(F32)
    tail = got_ref[n:].astype(F32)
    other_log = tail[0:1] + tail[1:2] + tail[2:3]
    log, before_me, after_me = log_ref[0:1], log_ref[1:2], log_ref[2:3]
    line = iota(log_ref.shape, 0)
    upper = (place_ref[0] // bit % 2 + 0 * line[0:1]) == 1
    kept, other = jnp.exp2(log), jnp.exp2(other_log)
    mine = mine_ref[:n].astype(F32)
    total = jnp.where(upper, other, 1.0) * mine + jnp.where(upper, 1.0, kept) * got
    passed = jnp.where(upper, 0.0, jnp.exp2(after_me)) * got
    entering_out[...] = passed if entering_ref is None else entering_ref[...] + passed
    first = jnp.where(upper, 1.0, other)
    second = jnp.where(upper, kept, 1.0)
    third = jnp.where(upper, jnp.exp2(before_me), 0.0)
    factor_out[...] = jnp.where(line == 0, first, jnp.where(line == 1, second, third))
    log = log + other_log
    before_me = jnp.where(upper, before_me + other_log, before_me)
    after_me = jnp.where(upper, after_me, after_me + other_log)
    log_out[...] = jnp.where(line == 0, log, jnp.where(line == 1, before_me, after_me))
    sent_out[:n], sent_out[n:] = message(total, log)


def scan_kernel(last, factor_ref, mine_ref, got_ref, *refs):
    refs = list(refs)
    entering_ref = refs.pop(0) if len(refs) == 3 - last else None
    factors = factor_ref[...]
    got = got_ref[...].astype(F32)
    if not last:
        total = factors[0:1] * mine_ref[...].astype(F32) + factors[1:2] * got
        refs[1][...] = total.astype(BF16)
    passed = factors[2:3] * got
    refs[0][...] = passed if entering_ref is None else entering_ref[...] + passed


def inner_rows_kernel(r_ref, rt_ref, g_ref, b_ref, c_ref, skip_ref, out_ref):
    grad_x_kernel(True, r_ref, rt_ref, g_ref, b_ref, c_ref, None, skip_ref, out_ref)


def state_rows_kernel(rt_ref, b_ref, q_ref, part_ref, out_ref):
    columns = rt_ref[0]
    to_end = jnp.exp2(spread_columns(columns[SPAN - 1 : SPAN] - columns))
    from_state = mm(b_ref[...], q_ref[0]) * to_end
    out_ref[...] = (part_ref[...] + from_state.T).astype(BF16)


def scan_pair_kernel(number, last, *refs):
    first, second, outs = refs[:number], refs[number : number + 4], refs[number + 4 :]
    scan_kernel(False, *first, *outs[:2])
    scan_kernel(last, *second, *outs[2:])


def early_forward_kernel(count, f_ref, *refs):
    pieces, (out_ref, buffer) = refs[:count], refs[count:]
    rows = pieces[0].shape[0]
    for index, piece in enumerate(pieces):
        buffer[index * rows : (index + 1) * rows] = piece[...]
    out_ref[...] = mm(f_ref[...], buffer[...])


def late_forward_kernel(count, f_ref, part_ref, rt_ref, b_ref, kept_ref, *refs):
    pieces, (x_ref, e_ref, sent_ref, buffer) = refs[:count], refs[count:]
    rows = pieces[0].shape[0]
    for index, piece in enumerate(pieces):
        buffer[index * rows : (index + 1) * rows] = piece[...]
    x = (part_ref[...] + mm(f_ref[...], buffer[...])).astype(BF16)
    x_ref[...] = x
    total = None
    for k in range(e_ref.shape[0]):
        part = slice(k * SPAN, (k + 1) * SPAN)
        columns = rt_ref[0, part]
        to_end = jnp.exp2(spread_columns(columns[SPAN - 1 : SPAN] - columns))
        scaled = (x[part].astype(F32) * to_end).astype(BF16)
        state = dot(b_ref[part], scaled, ((0,), (0,)))
        e_ref[k] = state
        total = state if total is None else kept_ref[k, :1] * total + state
    sent_ref[...] = total.astype(BF16)


def blocks_kernel(halves, has_before, order_ref, g_ref, *refs):
    count = len(halves)
    number = sum(halves)
    arrays, refs = refs[:number], refs[number:]
    if has_before:
        refs = refs[2:]
    away_ref, own_ref, buffer, slots, sems, out_sems = refs
    rows = arrays[0].shape[0]
    wide = g_ref.shape[0]
    copies = []
    at = 0
    for index, parts in enumerate(halves):
        mine = []
        for part in range(parts):
            lanes = pl.ds(part * (wide // parts), wide // parts)
            target = buffer.at[pl.ds(index * rows, rows), lanes]
            copy = pltpu.make_async_copy(arrays[at], target, sems.at[at])
            copy.start()
            mine.append(copy)
            at += 1
        copies.append(mine)
    g = g_ref[...]
    half = away_ref.shape[1] // rows
    starts = [0]
    while starts[-1] < count:
        starts.append(starts[-1] + (2 if count - starts[-1] in (2, 4) else 3))
    for index in range(count):
        for copy in copies[index]:
            copy.wait()
        if index + 1 not in starts:
            continue
        start = starts[starts.index(index + 1) - 1]
        product = mm(buffer[start * rows : (index + 1) * rows], g)
        for done in range(start, index + 1):
            part = product[(done - start) * rows : (done - start + 1) * rows]
            slots[done] = part.T.astype(BF16)
            place = order_ref[done]
            lanes = pl.ds(pl.multiple_of(place % half * rows, 128), rows)

            @pl.when(place < half)
            def _():
                target = away_ref.at[:, lanes]
                pltpu.make_async_copy(slots.at[done], target, out_sems.at[done]).start()

            @pl.when(place >= half)
            def _():
                target = own_ref.at[:, lanes]
                pltpu.make_async_copy(slots.at[done], target, out_sems.at[done]).start()

    for index in range(count):
        target = away_ref.at[:, pl.ds(0, rows)]
        pltpu.make_async_copy(slots.at[index], target, out_sems.at[index]).wait()


def after_kernel(*refs):
    pass


def inner_kernel(
    r_ref, rt_ref, g_ref, x_ref, b_ref, c_ref, q_ref, *refs
):
    d_ref, grad_b_ref, grad_c_ref, sum_ref, top_ref, low_ref = refs[-6:]
    so_far = refs[:-6]
    step = pl.program_id(1)
    b = b_ref[...]
    c = c_ref[...]
    scores = dot(b, c, ((1,), (1,)))
    running = r_ref[...]
    columns = rt_ref[0]
    top_keep = iota((HALF, SPAN), 1) >= iota((HALF, SPAN), 0)
    low_keep = iota((HALF, HALF), 1) >= iota((HALF, HALF), 0)

    @pl.when(step == 0)
    def _():
        sum_ref[...] = jnp.zeros_like(sum_ref)
        grad_b_ref[...] = so_far[0][...] if so_far else jnp.zeros_like(grad_b_ref)

    rows = []
    lane = iota((SPAN, 2 * P_SIZE), 1)
    later = not_before().astype(BF16)
    top_less = iota((HALF, SPAN), 1) > iota((HALF, SPAN), 0)
    low_less = iota((HALF, HALF), 1) > iota((HALF, HALF), 0)
    for pair in range(GROUP // 2):
        lanes = slice(pair * 2 * P_SIZE, (pair + 1) * 2 * P_SIZE)
        x = x_ref[:, lanes]
        none = jnp.zeros_like(x)
        x = [jnp.where(lane < P_SIZE, x, none), jnp.where(lane < P_SIZE, none, x)]
        product = mm(jnp.concatenate(x, axis=0), g_ref[:, lanes].T)
        top_sum = low_sum = None
        for number in range(2):
            head = 2 * pair + number
            row = running[head : head + 1]
            at = number * SPAN
            top = jnp.where(top_keep, row - columns[:HALF, head : head + 1], NEVER)
            low = jnp.where(low_keep, row[:, HALF:] - columns[HALF:, head : head + 1], NEVER)
            top = jnp.exp2(top) * product[at : at + HALF]
            low = jnp.exp2(low) * product[at + HALF : at + SPAN, HALF:]
            top_sum = top if number == 0 else top_sum + top
            low_sum = low if number == 0 else low_sum + low
            part = slice(head * HALF, (head + 1) * HALF)
            top_ref[part] = (top * scores[:HALF]).astype(BF16)
            low_ref[part] = (low * scores[HALF:, HALF:]).astype(BF16)
        sum_ref[:HALF] += top_sum
        sum_ref[HALF:, HALF:] += low_sum
    top = mm(top_ref[...], later)
    low = mm(low_ref[...], later[HALF:, HALF:])
    for head in range(GROUP):
        part = slice(head * HALF, (head + 1) * HALF)
        top_row = jnp.sum(jnp.where(top_less, top[part], 0.0), axis=0, keepdims=True)
        low_row = jnp.sum(jnp.where(low_less, low[part], 0.0), axis=0, keepdims=True)
        rows.append(jnp.concatenate([top_row[:, :HALF], top_row[:, HALF:] + low_row], axis=1))
    to_end = jnp.exp2(spread_columns(columns[SPAN - 1 : SPAN] - columns))
    scaled = x_ref[...].astype(F32) * to_end
    ends = dot(one_hot(BF16), (scaled * mm(b, q_ref[0])).astype(BF16), ((1,), (1,)))
    d_ref[...] = jnp.concatenate(rows, axis=0) + sum_over(ends, before())
    grad_b_ref[...] += dot(scaled.astype(BF16), q_ref[0], ((1,), (1,)))

    @pl.when(step == pl.num_programs(1) - 1)
    def _():
        total = sum_ref[...].astype(BF16)
        grad_b_ref[...] += mm(total, c)
        part = dot(total, b, ((0,), (0,)))
        grad_c_ref[...] = part + so_far[1][...] if so_far else part


def state_kernel(
    rt_ref, g_ref, c_ref, s_ref, e_ref, q_ref, a_ref, d_part_ref, c_part_ref, *refs
):
    d_ref, grad_c_ref, held = refs[-3:]
    span, group = pl.program_id(0), pl.program_id(1)

    @pl.when(group == 0)
    def _():
        grad_c_ref[...] = c_part_ref[...]

    @pl.when(span == 0)
    def _():
        held[group] = s_ref[...]

    state = held[group]
    low = state.astype(BF16)
    scaled = g_ref[...].astype(F32) * jnp.exp2(spread_columns(rt_ref[0]))
    ends = dot(one_hot(BF16), (scaled * mm(c_ref[...], low)).astype(BF16), ((1,), (1,)))
    grad_c_ref[...] += dot(scaled.astype(BF16), low, ((1,), (1,)))
    product = jnp.sum(q_ref[0].astype(F32) * state, axis=0, keepdims=True) * a_ref[0, :1]
    high, middle, last = thirds(product)
    row = iota((8, WIDE), 0)
    stacked = jnp.where(row == 0, high, jnp.where(row == 1, middle, jnp.where(row == 2, last, 0.0)))
    kept = dot(one_hot(BF16), stacked.astype(BF16), ((1,), (1,)))
    kept = jnp.sum(kept, axis=1, keepdims=True)
    d_ref[...] = d_part_ref[...] + sum_over(ends, not_before()) + kept
    held[group] = e_ref[0] + a_ref[0, :1] * state


def call(kernel, grid, in_specs, out_specs, out_shape, flops, size, scratch=()):
    return pl.pallas_call(
        kernel,
        grid=grid,
        in_specs=in_specs,
        out_specs=out_specs,
        out_shape=out_shape,
        scratch_shapes=list(scratch),
        cost_estimate=pl.CostEstimate(flops=flops, bytes_accessed=size, transcendentals=0),
        compiler_params=pltpu.CompilerParams(
            dimension_semantics=("arbitrary",) * len(grid), vmem_limit_bytes=GRANT
        ),
    )


def run_spec(at=0):
    return pl.BlockSpec((GROUP, SPAN), lambda k, h: (h + at, k))


def run_t_spec(at=0):
    return pl.BlockSpec((1, SPAN, GROUP), lambda k, h: (h + at, k, 0))


def rows_spec(at=0):
    return pl.BlockSpec((SPAN, WIDE), lambda k, h: (k, h + at))


def state_spec(at=0):
    return pl.BlockSpec((1, 2 * P_SIZE, WIDE), lambda k, h: (k, 0, h + at))


def kept_spec(at=0):
    return pl.BlockSpec((1, 8, WIDE), lambda k, h: (k, 0, h + at))


SHARED = pl.BlockSpec((SPAN, 2 * P_SIZE), lambda k, h: (k, 0))
GAIN = pl.BlockSpec((1, WIDE), lambda k, h: (0, h))
ANYWHERE = pl.BlockSpec(memory_space=pl.ANY)
INNER_SCRATCH = [
    pltpu.VMEM((SPAN, SPAN), F32),
    pltpu.VMEM((GROUP * HALF, SPAN), BF16),
    pltpu.VMEM((GROUP * HALF, HALF), BF16),
]
SCALARS = pl.BlockSpec(memory_space=pltpu.SMEM)


def shape(*dims, dtype=F32):
    return jax.ShapeDtypeStruct(dims, dtype)


def swap(value, axis, bit):
    count = lax.axis_size(axis)
    return lax.ppermute(value, axis, [(i, i ^ bit) for i in range(count)])


def block_products(kept):
    count = lax.axis_size("ctx")
    place = lax.axis_index("ctx")
    steps = []
    before_me = jnp.ones_like(kept)
    after_me = jnp.ones_like(kept)
    bit = 1
    while bit < count:
        other = swap(kept, "ctx", bit)
        upper = (place & bit) != 0
        steps.append((bit, upper, kept, other, before_me, after_me))
        before_me = jnp.where(upper, before_me * other, before_me)
        after_me = jnp.where(upper, after_me, after_me * other)
        kept = kept * other
        bit *= 2
    return steps


def scan_states(total, steps, reverse):
    entering = jnp.zeros_like(total)
    for bit, upper, kept, other, before_me, after_me in steps:
        got = swap(total.astype(BF16), "ctx", bit).astype(F32)
        if reverse:
            entering = entering + jnp.where(upper, 0.0, after_me) * got
            total = jnp.where(upper, got + other * total, total + kept * got)
        else:
            entering = entering + jnp.where(upper, before_me, 0.0) * got
            total = jnp.where(upper, kept * got + total, other * total + got)
    return entering


def head_sum(value):
    bit = 1
    while bit < lax.axis_size("head"):
        value = value.astype(BF16)
        value = value.astype(F32) + swap(value, "head", bit).astype(F32)
        bit *= 2
    return value


PLANE = 4


def after(values, *tokens):
    out = pl.pallas_call(
        after_kernel,
        in_specs=[ANYWHERE] * (len(values) + len(tokens)),
        out_specs=[ANYWHERE] * len(values),
        out_shape=[shape(*value.shape, dtype=value.dtype) for value in values],
        input_output_aliases={index: index for index in range(len(values))},
        cost_estimate=pl.CostEstimate(flops=0, bytes_accessed=0, transcendentals=0),
        compiler_params=pltpu.CompilerParams(vmem_limit_bytes=GRANT),
    )(*values, *tokens)
    return list(out)


def along_z(value, moves):
    pairs = [(a * PLANE + i, b * PLANE + i) for a, b in moves for i in range(PLANE)]
    return lax.ppermute(value, "ctx", pairs)


MIDDLE = ((1, 2), (2, 1))
OUTWARD = ((1, 0), (2, 3))


def swap_x(value):
    return swap(value, "ctx", 1)


def swap_y(value):
    return swap(value, "ctx", 2)


LAYERS = ((0, 1, 2, 3), (1, 0, 3, 2), (2, 2, 1, 1), (3, 3, 0, 0))
EARLY = [(k, flip) for k in (0, 1, 2) for flip in range(3)]
LATE = [(0, 3), (1, 3), (2, 3), (3, 0), (3, 1), (3, 2), (3, 3)]


def block_order():
    place = lax.axis_index("ctx")
    layer, spot = place // PLANE, place % PLANE
    layers = jnp.array(LAYERS, jnp.int32)[:, layer]
    order = [layers[k] * PLANE + (spot ^ flip) for k, flip in EARLY + LATE]
    return jnp.stack(order).astype(jnp.int32)


def gather_weight(w, sizes):
    ends = [sum(sizes[: j + 1]) * P_SIZE for j in range(len(sizes))]
    parts = [w[:, end - size * P_SIZE : end] for end, size in zip(ends, sizes)]
    return [lax.all_gather(part, "ctx", axis=0, tiled=True) for part in parts]


def forward(features, first, weight, running_t, b_rows, here):
    own, other = features
    length = own.shape[0]
    n = b_rows.shape[1]
    width, wide = weight.shape
    deep = width // 4
    spans = length // SPAN

    def depth(k, first_ref):
        return (k // 2 ^ first_ref[0]) * 2 + k % 2

    return pl.pallas_call(
        forward_kernel,
        grid_spec=pltpu.PrefetchScalarGridSpec(
            num_scalar_prefetch=1,
            grid=(wide // WIDE, 4),
            in_specs=[
                pl.BlockSpec((length, deep), lambda h, k, first_ref: (0, jnp.minimum(k, 1))),
                pl.BlockSpec((length, deep), lambda h, k, first_ref: (0, jnp.maximum(k - 2, 0))),
                pl.BlockSpec((deep, WIDE), lambda h, k, first_ref: (depth(k, first_ref), h)),
                pl.BlockSpec((1, length, GROUP), lambda h, k, first_ref: (h + here, 0, 0)),
                pl.BlockSpec((length, n), lambda h, k, first_ref: (0, 0)),
            ],
            out_specs=[
                pl.BlockSpec((length, WIDE), lambda h, k, first_ref: (0, h)),
                pl.BlockSpec((spans, n, WIDE), lambda h, k, first_ref: (0, 0, h)),
            ],
            scratch_shapes=[pltpu.VMEM((length, WIDE), F32)],
        ),
        out_shape=[shape(length, wide, dtype=BF16), shape(spans, n, wide)],
        cost_estimate=pl.CostEstimate(
            flops=2 * length * wide * width, bytes_accessed=2 * wide * width, transcendentals=0
        ),
        compiler_params=pltpu.CompilerParams(
            dimension_semantics=("arbitrary", "arbitrary"), vmem_limit_bytes=GRANT
        ),
    )(first, own, other, weight, running_t, b_rows)


def multiply(grad_x, weight, at, half, halves, before=None, other=None):
    length = grad_x.shape[0]
    width, wide = weight.shape
    tiles = width // halves // WIDE
    tile = pl.BlockSpec((length, WIDE), lambda j, half_ref: (0, half_ref[0] * tiles + j))
    plain = pl.BlockSpec((length, WIDE), lambda j, half_ref: (0, j))
    in_specs = [
        pl.BlockSpec((length, wide), lambda j, half_ref: (0, at)),
        pl.BlockSpec((WIDE, wide), lambda j, half_ref: (half_ref[0] * tiles + j, 0)),
    ]
    operands = [grad_x, weight]
    if before is not None:
        in_specs.append(tile)
        operands.append(before)
    if other is not None:
        in_specs.append(plain)
        operands.append(other)
    return pl.pallas_call(
        functools.partial(product_kernel, before is not None, other is not None),
        grid_spec=pltpu.PrefetchScalarGridSpec(
            num_scalar_prefetch=1,
            grid=(tiles,),
            in_specs=in_specs,
            out_specs=plain,
        ),
        out_shape=shape(length, width // halves, dtype=BF16),
        cost_estimate=pl.CostEstimate(
            flops=2 * length * wide * width // halves,
            bytes_accessed=2 * wide * width // halves,
            transcendentals=0,
        ),
        compiler_params=pltpu.CompilerParams(
            dimension_semantics=("arbitrary",), vmem_limit_bytes=GRANT
        ),
    )(half, *operands)


def early_forward(features, pieces):
    length = features.shape[0]
    rows, columns = pieces[0].shape
    deep = rows * len(pieces)
    return call(
        functools.partial(early_forward_kernel, len(pieces)),
        (columns // WIDE,),
        [pl.BlockSpec((length, deep), lambda h: (0, 0))]
        + [pl.BlockSpec((rows, WIDE), lambda h: (0, h))] * len(pieces),
        pl.BlockSpec((length, WIDE), lambda h: (0, h)),
        shape(length, columns),
        2 * length * columns * deep,
        2 * columns * deep,
        [pltpu.VMEM((deep, WIDE), BF16)],
    )(features, *pieces)


def late_forward(features, part, pieces, running_t, b_rows, kept, here):
    length = features.shape[0]
    rows, columns = pieces[0].shape
    deep = rows * len(pieces)
    n = b_rows.shape[1]
    spans = length // SPAN
    state = pl.BlockSpec((n, WIDE), lambda h: (0, h))
    return call(
        functools.partial(late_forward_kernel, len(pieces)),
        (columns // WIDE,),
        [
            pl.BlockSpec((length, deep), lambda h: (0, 0)),
            pl.BlockSpec((length, WIDE), lambda h: (0, h + here)),
            pl.BlockSpec((1, length, GROUP), lambda h: (h + here, 0, 0)),
            pl.BlockSpec((length, n), lambda h: (0, 0)),
            pl.BlockSpec((spans, 8, WIDE), lambda h: (0, 0, h + here)),
        ]
        + [pl.BlockSpec((rows, WIDE), lambda h: (0, h))] * len(pieces),
        [
            pl.BlockSpec((length, WIDE), lambda h: (0, h)),
            pl.BlockSpec((spans, n, WIDE), lambda h: (0, 0, h)),
            state,
        ],
        [
            shape(length, columns, dtype=BF16),
            shape(spans, n, columns),
            shape(n, columns, dtype=BF16),
        ],
        2 * length * columns * deep,
        2 * columns * deep,
        [pltpu.VMEM((deep, WIDE), BF16)],
    )(features, part, running_t, b_rows, kept, *pieces)


def multiply_blocks(order, grad_x, pieces, so_far):
    columns, length = grad_x.shape
    arrays = [array for piece in pieces for array in piece]
    rows = arrays[0].shape[0]
    count = len(pieces)
    half = shape(length, lax.axis_size("ctx") * rows // 2, dtype=BF16)
    first = 2 + len(arrays)
    return pl.pallas_call(
        functools.partial(blocks_kernel, [len(piece) for piece in pieces], bool(so_far)),
        grid=(1,),
        in_specs=[SCALARS, pl.BlockSpec((columns, length), lambda h: (0, 0))]
        + [ANYWHERE] * (len(arrays) + len(so_far)),
        out_specs=[ANYWHERE, ANYWHERE],
        out_shape=[half, half],
        input_output_aliases={first + k: k for k in range(len(so_far))},
        scratch_shapes=[
            pltpu.VMEM((rows * count, columns), BF16),
            pltpu.VMEM((count, length, rows), BF16),
            pltpu.SemaphoreType.DMA((len(arrays),)),
            pltpu.SemaphoreType.DMA((count,)),
        ],
        cost_estimate=pl.CostEstimate(
            flops=2 * length * columns * rows * count,
            bytes_accessed=2 * columns * rows * count,
            transcendentals=0,
        ),
        compiler_params=pltpu.CompilerParams(
            dimension_semantics=("arbitrary",), vmem_limit_bytes=GRANT
        ),
    )(order, grad_x, *arrays, *so_far)


def back_start(own_grads, kept):
    spans, n, columns = own_grads.shape
    return call(
        start_kernel,
        (columns // WIDE,),
        [
            pl.BlockSpec((spans, n, WIDE), lambda h: (0, 0, h)),
            pl.BlockSpec((spans, 8, WIDE), lambda h: (0, 0, h)),
        ],
        [pl.BlockSpec((rows, WIDE), lambda h: (0, h)) for rows in (8, n + TAIL)],
        [shape(8, columns), shape(n + TAIL, columns, dtype=BF16)],
        0,
        14 * n * columns,
    )(own_grads, kept)


def back_step(place, log, sent, entering, bit):
    got = swap(sent, "ctx", bit)
    columns = sent.shape[1]
    n = sent.shape[0] - TAIL
    short, state, tall = [
        pl.BlockSpec((rows, 2 * WIDE), lambda h: (0, h)) for rows in (8, n, n + TAIL)
    ]
    return call(
        functools.partial(back_kernel, bit),
        (columns // (2 * WIDE),),
        [SCALARS, short, tall, tall] + [state] * len(entering),
        [state, tall, short, short],
        [
            shape(n, columns),
            shape(n + TAIL, columns, dtype=BF16),
            shape(8, columns),
            shape(8, columns),
        ],
        0,
        14 * n * columns,
    )(place, log, sent, got, *entering)


def scan_step(factors, here, sent, entering, bit, last=False):
    got = swap(sent, "ctx", bit)
    n, columns = sent.shape
    block = pl.BlockSpec((n, columns), lambda h: (0, 0))
    at = here * WIDE // columns
    outs = [shape(n, columns), shape(n, columns, dtype=BF16)][: 2 - last]
    return call(
        functools.partial(scan_kernel, last),
        (1,),
        [pl.BlockSpec((8, columns), lambda h: (0, at)), block, block] + [block] * len(entering),
        [block] * len(outs),
        outs,
        0,
        10 * n * columns,
    )(factors, sent, got, *entering)


def scan_pair(first, second, last=False):
    operands, specs, outs = [], [], []
    for factors, here, sent, entering, bit in (first, second):
        got = swap(sent, "ctx", bit)
        n, columns = sent.shape
        block = pl.BlockSpec((n, columns), lambda h: (0, 0))
        at = here * WIDE // columns
        operands += [factors, sent, got, *entering]
        specs += [pl.BlockSpec((8, columns), lambda h, at=at: (0, at))]
        specs += [block] * (2 + len(entering))
        outs += [shape(n, columns), shape(n, columns, dtype=BF16)]
    outs = outs[: 4 - last]
    return call(
        functools.partial(scan_pair_kernel, 3 + len(first[3]), last),
        (1,),
        specs,
        [block] * len(outs),
        outs,
        0,
        20 * n * columns,
    )(*operands)


def local(inputs, w_in, b_rows, c_rows, log_decay, skip_gain, grad_out):
    groups = log_decay.shape[0] // GROUP
    layered = lax.axis_size("ctx") == 4 * PLANE and lax.axis_size("head") == 2
    if layered and groups % 2 == 0 and w_in.shape[0] == 256:
        return local_layered(inputs, w_in, b_rows, c_rows, log_decay, skip_gain, grad_out)
    return local_plain(inputs, w_in, b_rows, c_rows, log_decay, skip_gain, grad_out)


def prepare(log_decay, grad_out, c_rows):
    length, columns = grad_out.shape
    heads = log_decay.shape[0]
    spans = length // SPAN
    groups = heads // GROUP
    n = c_rows.shape[1]
    return call(
        decay_kernel,
        (spans, groups),
        [run_spec(), rows_spec(), SHARED],
        [run_spec(), run_t_spec(), kept_spec(), state_spec()],
        [
            shape(heads, length),
            shape(groups, length, GROUP),
            shape(spans, 8, columns),
            shape(spans, n, columns),
        ],
        2 * length * columns * n,
        6 * length * columns,
    )(log_decay, grad_out, c_rows)


def inner(grid, here, wide, operands, so_far):
    length = operands[2].shape[0]
    n = operands[4].shape[1]
    specs = [
        run_spec(here),
        run_t_spec(here),
        rows_spec(here),
        rows_spec(),
        SHARED,
        SHARED,
        state_spec(here),
    ]
    return call(
        inner_kernel,
        grid,
        specs + [SHARED] * len(so_far),
        [run_spec(), SHARED, SHARED],
        [shape(wide // P_SIZE, length), shape(length, n), shape(length, n)],
        12 * length * wide * SPAN,
        6 * length * wide,
        INNER_SCRATCH,
    )(*operands, *so_far)


def state_terms(grid, here, wide, operands, heads=None, so_far=None):
    length = operands[1].shape[0]
    n = operands[2].shape[1]
    heads = heads or wide // P_SIZE
    at = here if heads > wide // P_SIZE else 0
    extra = () if so_far is None else (so_far,)
    return pl.pallas_call(
        state_kernel,
        grid=grid,
        in_specs=[
            run_t_spec(here),
            rows_spec(here),
            SHARED,
            pl.BlockSpec((n, WIDE), lambda k, h: (0, h)),
            state_spec(),
            state_spec(here),
            kept_spec(here),
            run_spec(),
            SHARED,
        ]
        + [ANYWHERE] * len(extra),
        out_specs=[run_spec(at), SHARED],
        out_shape=[shape(heads, length), shape(length, n)],
        scratch_shapes=[pltpu.VMEM((grid[1], n, WIDE), F32)],
        input_output_aliases={len(operands): 0} if extra else {},
        cost_estimate=pl.CostEstimate(
            flops=4 * length * wide * n, bytes_accessed=6 * length * wide, transcendentals=0
        ),
        compiler_params=pltpu.CompilerParams(
            dimension_semantics=("arbitrary", "arbitrary"), vmem_limit_bytes=GRANT
        ),
    )(*operands, *extra)


def local_layered(inputs, w_in, b_rows, c_rows, log_decay, skip_gain, grad_out):
    length, columns = grad_out.shape
    heads = log_decay.shape[0]
    spans = length // SPAN
    groups = heads // GROUP
    place = lax.axis_index("head").astype(jnp.int32)
    half = columns // 2
    order = block_order()
    blocks = order.shape[0]
    width = blocks * w_in.shape[0]

    z1, inner2 = swap(w_in, "ctx", PLANE), along_z(w_in, MIDDLE)
    own_x, own_y = swap_x(w_in), swap_y(w_in)
    other = swap(inputs, "head", 1)
    running, running_t, kept, own_grads = prepare(log_decay, grad_out, c_rows)
    spot = lax.axis_index("ctx").astype(jnp.int32)[None]
    log, sent = back_start(own_grads, kept)
    sent = after([sent], other)[0]
    leaving, moved, log, factors_1 = back_step(spot, log, sent, (), 1)

    z1, inner2, own_y = after([z1, inner2, own_y], own_x, sent)
    sent = moved
    x1, y1 = swap_x(z1), swap_y(z1)
    inner3, outer2 = along_z(z1, MIDDLE), along_z(inner2, OUTWARD)
    own_y_a, own_y_b = own_y[:, :half], own_y[:, half:]
    inner3_a, inner3_b = inner3[:, :half], inner3[:, half:]
    leaving, sent, log, factors_2 = back_step(spot, log, sent, (leaving,), 2)
    order_own = (order + place * (blocks // 2)) % blocks
    cut = len(EARLY) * w_in.shape[0]
    early_features, late_features = call(
        arrange_kernel,
        (1,),
        [SCALARS] + [pl.BlockSpec((length, width // 2), lambda h: (0, 0))] * 2,
        [pl.BlockSpec((length, wide), lambda h: (0, 0)) for wide in (cut, width - cut)],
        [shape(length, wide, dtype=BF16) for wide in (cut, width - cut)],
        0,
        4 * length * width,
        [pltpu.VMEM((length, width), BF16)],
    )(order_own, inputs, other)

    inner2, inner3_a, inner3_b, outer2, x1, sent, own_y_a, own_y_b = after(
        [inner2, inner3_a, inner3_b, outer2, x1, sent, own_y_a, own_y_b], y1, early_features
    )
    z3 = inner2 + outer2
    x3, y3 = swap_x(z3), swap_y(z3)
    outer3_a = along_z(inner3_a, OUTWARD)
    skip = jnp.repeat(skip_gain, P_SIZE)[None]
    (running,) = after([running], z3)
    rows_part = inner_rows(running, running_t, grad_out, b_rows, c_rows, skip)
    x1_a, x1_b = x1[:, :half], x1[:, half:]
    leaving, sent, log, factors_4 = back_step(spot, log, sent, (leaving,), 4)

    inner3_a, inner3_b, outer3_a, y3, x1_a, x1_b = after(
        [inner3_a, inner3_b, outer3_a, y3, x1_a, x1_b], x3, rows_part
    )
    z2a = inner3_a + outer3_a
    outer3_b = along_z(inner3_b, OUTWARD)
    y3_a, y3_b = y3[:, :half], y3[:, half:]
    x2a, y2a = swap_x(z2a), swap_y(z2a)
    d3a, d1a = swap_x(y3_a), swap_y(x1_a)
    leaving, sent, log, factors_8 = back_step(spot, log, sent, (leaving,), 8)
    early = [w_in, own_x, own_y, z1, x1, y1, z3, x3, y3]
    part = early_forward(early_features, early)

    own_y_a, x2a, leaving = after([own_y_a, x2a, leaving], y2a, d3a, d1a, part)
    d0a, d2a = swap_x(own_y_a), swap_y(x2a)
    leaving_all = [leaving]
    for k in range(spans - 1, 0, -1):
        leaving_all.insert(0, own_grads[k] + kept[k, :1] * leaving_all[0])
    leaving_all = jnp.stack([value.astype(BF16) for value in leaving_all])
    (z2b,) = after([inner3_b + outer3_b], leaving_all)
    x2b, y2b = swap_x(z2b), swap_y(z2b)
    grad_x = state_rows(running_t, b_rows, leaving_all, rows_part)
    order_away = (order + (1 - place) * (blocks // 2)) % blocks
    early_order, late_order = order_away[: len(EARLY)], order_away[len(EARLY) :]
    late_a = [d0a, d1a, d3a, z2a, x2a, y2a, d2a]
    x_a, states_a, sent_a = late_forward(
        late_features, part, late_a, running_t, b_rows, kept, 0
    )

    own_y_b, x2b, y3_b, x1_b, grad_x = after([own_y_b, x2b, y3_b, x1_b, grad_x], y2b, sent_a)
    d0b, d2b = swap_x(own_y_b), swap_y(x2b)
    d3b, d1b = swap_x(y3_b), swap_y(x1_b)
    product = multiply_blocks(early_order, grad_x, [[piece] for piece in early], ())
    shared = (running, running_t, grad_out)
    here = groups // 2
    grid = (spans, here)

    d0b, d2b, sent_a = after([d0b, d2b, sent_a], d3b, d1b, product[0])
    entering_a, sent_a = scan_step(factors_1, 0, sent_a, (), 1)
    late_b = [d0b, d1b, d3b, z2b, x2b, y2b, d2b]
    x_b, states_b, sent_b = late_forward(
        late_features, part, late_b, running_t, b_rows, kept, here
    )
    pairs = list(zip(late_a, late_b))
    sent_a, sent_b, *product = after([sent_a, sent_b, *product])
    entering_b, sent_b, entering_a, sent_a = scan_pair(
        (factors_1, here, sent_b, (), 1), (factors_2, 0, sent_a, (entering_a,), 2)
    )
    away, own = multiply_blocks(late_order, grad_x, pairs, product)

    sent_a, sent_b, x_a, away = after([sent_a, sent_b, x_a, away])
    entering_b, sent_b, entering_a, sent_a = scan_pair(
        (factors_2, here, sent_b, (entering_b,), 2), (factors_4, 0, sent_a, (entering_a,), 4)
    )
    got = swap(away, "head", 1)
    inner_a = shared + (x_a, b_rows, c_rows, leaving_all)
    decay_a, grad_b, grad_c = inner(grid, 0, half, inner_a, ())

    sent_a, sent_b, x_b, grad_b = after([sent_a, sent_b, x_b, grad_b])
    entering_b, sent_b, entering_a = scan_pair(
        (factors_4, here, sent_b, (entering_b,), 4),
        (factors_8, 0, sent_a, (entering_a,), 8),
        True,
    )
    inner_b = shared + (x_b, b_rows, c_rows, leaving_all)
    decay_b, grad_b, grad_c = inner(grid, here, half, inner_b, (grad_b, grad_c))

    sent_b, entering_a, got, grad_b = after([sent_b, entering_a, got, grad_b])
    grad_b = head_sum(grad_b)
    grad_inputs = (own.astype(F32) + got.astype(F32)).astype(BF16)
    (entering_b,) = scan_step(factors_8, here, sent_b, (entering_b,), 8, True)
    common = (running_t, grad_out, c_rows)
    state_a = common + (entering_a, states_a, leaving_all, kept, decay_a, grad_c)
    decays, grad_c = state_terms(grid, 0, half, state_a, heads)
    (entering_b,) = after([entering_b], grad_inputs, grad_c)
    state_b = common + (entering_b, states_b, leaving_all, kept, decay_b, grad_c)
    decays, grad_c = state_terms(grid, here, half, state_b, heads, decays)
    return (grad_inputs, grad_b, head_sum(grad_c), decays)


TURNED = pl.BlockSpec((WIDE, SPAN), lambda k, h: (h, k))


def inner_rows(running, running_t, grad_out, b_rows, c_rows, skip):
    length, columns = grad_out.shape
    return call(
        inner_rows_kernel,
        (length // SPAN, running_t.shape[0]),
        [run_spec(), run_t_spec(), rows_spec(), SHARED, SHARED, GAIN],
        TURNED,
        shape(columns, length),
        8 * length * columns * SPAN,
        6 * length * columns,
    )(running, running_t, grad_out, b_rows, c_rows, skip)


def state_rows(running_t, b_rows, leaving, part):
    columns, length = part.shape
    return call(
        state_rows_kernel,
        (length // SPAN, running_t.shape[0]),
        [run_t_spec(), SHARED, state_spec(), TURNED],
        TURNED,
        shape(columns, length, dtype=BF16),
        2 * length * columns * SPAN,
        8 * length * columns,
    )(running_t, b_rows, leaving, part)


def grad_rows(running, running_t, grad_out, b_rows, c_rows, leaving, skip, transposed):
    length, columns = grad_out.shape
    spec, dims = rows_spec(), (length, columns)
    if transposed:
        spec, dims = pl.BlockSpec((WIDE, SPAN), lambda k, h: (h, k)), (columns, length)
    return call(
        functools.partial(grad_x_kernel, transposed),
        (length // SPAN, running_t.shape[0]),
        [run_spec(), run_t_spec(), rows_spec(), SHARED, SHARED, state_spec(), GAIN],
        spec,
        shape(*dims, dtype=BF16),
        8 * length * columns * SPAN,
        6 * length * columns,
    )(running, running_t, grad_out, b_rows, c_rows, leaving, skip)


def local_plain(inputs, w_in, b_rows, c_rows, log_decay, skip_gain, grad_out):
    length, columns = grad_out.shape
    heads = log_decay.shape[0]
    spans = length // SPAN
    groups = heads // GROUP
    n = b_rows.shape[1]
    grid = (spans, groups)

    sizes = (heads // 2, heads // 4, heads // 4) if heads % (4 * GROUP) == 0 else (heads,)
    weights = gather_weight(w_in, sizes)
    two = lax.axis_size("head") == 2
    place = lax.axis_index("head").astype(jnp.int32)[None]
    width = weights[0].shape[0]
    if two:
        features = (inputs, swap(inputs, "head", 1))
        first = place
    else:
        features = lax.all_gather(inputs, "head", axis=1, tiled=True)
        features = (features[:, : width // 2], features[:, width // 2 :])
        first = jnp.zeros((1,), jnp.int32)

    running, running_t, kept, own_grads = call(
        decay_kernel,
        grid,
        [run_spec(), rows_spec(), SHARED],
        [run_spec(), run_t_spec(), kept_spec(), state_spec()],
        [
            shape(heads, length),
            shape(groups, length, GROUP),
            shape(spans, 8, columns),
            shape(spans, n, columns),
        ],
        2 * length * columns * n,
        6 * length * columns,
    )(log_decay, grad_out, c_rows)

    kept_total = kept[0, :1]
    for k in range(1, spans):
        kept_total = kept_total * kept[k, :1]
    steps = block_products(kept_total)

    total = own_grads[spans - 1]
    for k in range(spans - 2, -1, -1):
        total = own_grads[k] + kept[k, :1] * total
    leaving = [scan_states(total, steps, True)]
    for k in range(spans - 1, 0, -1):
        leaving.insert(0, own_grads[k] + kept[k, :1] * leaving[0])
    leaving = jnp.stack([value.astype(BF16) for value in leaving])

    skip = jnp.repeat(skip_gain, P_SIZE)[None]
    grad_x = grad_rows(running, running_t, grad_out, b_rows, c_rows, leaving, skip, False)

    grad_b = grad_c = product = None
    tokens = ()
    decay_parts = []
    at = 0
    for index, size in enumerate(sizes):
        wide = size * P_SIZE
        here = at // GROUP
        count = size // GROUP
        weight = weights[index]
        if tokens:
            weight = after([weight], *tokens)[0]
        x, own_states = forward(features, first, weight, running_t, b_rows, here)

        chunk = slice(at * P_SIZE, at * P_SIZE + wide)
        total = own_states[0]
        for k in range(1, spans):
            total = kept[k, :1, chunk] * total + own_states[k]
        cut = [step[:2] + tuple(value[:, chunk] for value in step[2:]) for step in steps]
        entering = scan_states(total, cut, False)

        so_far = () if grad_b is None else (grad_b, grad_c)
        decay_part, grad_b, grad_c = call(
            inner_kernel,
            (spans, count),
            [
                run_spec(here),
                run_t_spec(here),
                rows_spec(here),
                rows_spec(),
                SHARED,
                SHARED,
                state_spec(here),
            ]
            + [SHARED] * len(so_far),
            [run_spec(), SHARED, SHARED],
            [shape(size, length), shape(length, n), shape(length, n)],
            12 * length * wide * SPAN,
            6 * length * wide,
            INNER_SCRATCH,
        )(running, running_t, grad_out, x, b_rows, c_rows, leaving, *so_far)
        decay_part, grad_c = call(
            state_kernel,
            (spans, count),
            [
                run_t_spec(here),
                rows_spec(here),
                SHARED,
                pl.BlockSpec((n, WIDE), lambda k, h: (0, h)),
                state_spec(),
                state_spec(here),
                kept_spec(here),
                run_spec(),
                SHARED,
            ],
            [run_spec(), SHARED],
            [shape(size, length), shape(length, n)],
            4 * length * wide * n,
            6 * length * wide,
            [pltpu.VMEM((count, n, WIDE), F32)],
        )(running_t, grad_out, c_rows, entering, own_states, leaving, kept, decay_part, grad_c)
        decay_parts.append(decay_part)

        if index < len(sizes) - 1:
            zero = jnp.zeros((1,), jnp.int32)
            product = multiply(grad_x, weight, at // size, zero, 1, product)
            tokens = (product, grad_b, entering)
        elif two:
            sent = multiply(grad_x, weight, at // size, 1 - place, 2, product)
            got = swap(sent, "head", 1)
            grad_inputs = multiply(grad_x, weight, at // size, place, 2, product, got)
        else:
            zero = jnp.zeros((1,), jnp.int32)
            product = multiply(grad_x, weight, at // size, zero, 1, product)
            grad_inputs = lax.psum_scatter(product, "head", scatter_dimension=1, tiled=True)
        at += size

    return (grad_inputs, head_sum(grad_b), head_sum(grad_c), jnp.concatenate(decay_parts, axis=0))


def solution(mesh):
    in_specs = (
        P("ctx", "head"),
        P("ctx", "head"),
        P("ctx", None),
        P("ctx", None),
        P("head", "ctx"),
        P("head"),
        P("ctx", "head"),
    )
    out_specs = (P("ctx", "head"), P("ctx", None), P("ctx", None), P("head", "ctx"))
    return jax.shard_map(local, mesh=mesh, in_specs=in_specs, out_specs=out_specs, check_vma=False)
```

```python
import functools

import jax
import jax.numpy as jnp
from jax import lax
from jax.experimental import pallas as pl
from jax.experimental.pallas import tpu as pltpu
from jax.sharding import PartitionSpec as P

SPAN = 256
HALF = SPAN // 2
P_SIZE = 64
GROUP = 8
WIDE = GROUP * P_SIZE
LOG2E = 1.4426950408889634
NEVER = -1e30
GRANT = 64 * 2**20

F32 = jnp.float32
BF16 = jnp.bfloat16
EXACT = lax.Precision.HIGHEST


def dot(a, b, dims, precision=None):
    return lax.dot_general(a, b, (dims, ((), ())), precision=precision, preferred_element_type=F32)


def mm(a, b, precision=None):
    return dot(a, b, ((1,), (0,)), precision)


def iota(shape, dim):
    return lax.broadcasted_iota(jnp.int32, shape, dim)


def one_hot(dtype):
    return (iota((GROUP, WIDE), 0) == iota((GROUP, WIDE), 1) // P_SIZE).astype(dtype)


def not_before():
    return (iota((SPAN, SPAN), 0) >= iota((SPAN, SPAN), 1)).astype(F32)


def before():
    return (iota((SPAN, SPAN), 0) < iota((SPAN, SPAN), 1)).astype(F32)


def same():
    return (iota((SPAN, SPAN), 0) == iota((SPAN, SPAN), 1)).astype(F32)


def first_head():
    return iota((SPAN, 2 * P_SIZE), 1) < P_SIZE


def pair_columns(columns, pair):
    shape = (columns.shape[0], 2 * P_SIZE)
    left = jnp.broadcast_to(columns[:, 2 * pair : 2 * pair + 1], shape)
    right = jnp.broadcast_to(columns[:, 2 * pair + 1 : 2 * pair + 2], shape)
    return jnp.where(iota(shape, 1) < P_SIZE, left, right)


def spread_columns(columns):
    return jnp.concatenate([pair_columns(columns, pair) for pair in range(GROUP // 2)], axis=1)


def thirds(value):
    high = value.astype(BF16).astype(F32)
    middle = (value - high).astype(BF16).astype(F32)
    return high, middle, value - high - middle


def sum_over(value, mask):
    rows = value.shape[0]
    parts = mm(jnp.concatenate(thirds(value), axis=0).astype(BF16), mask.astype(BF16))
    return parts[:rows] + parts[rows : 2 * rows] + parts[2 * rows :]


def decay_kernel(d_ref, g_ref, c_ref, r_ref, rt_ref, a_ref, gt_ref):
    row_sums = sum_over(d_ref[...] * LOG2E, 1.0 - not_before() + same())
    r_ref[...] = row_sums
    padded = jnp.concatenate([row_sums, jnp.zeros((2 * P_SIZE - GROUP, SPAN), F32)], axis=0)
    running = padded.T[:, :GROUP]
    rt_ref[0] = running
    growth = jnp.exp2(spread_columns(running))
    last = spread_columns(running[SPAN - 1 : SPAN])
    a_ref[0] = jnp.where(iota((8, WIDE), 0) < 4, jnp.exp2(last), last)
    scaled = (g_ref[...].astype(F32) * growth).astype(BF16)
    gt_ref[0] = dot(c_ref[...], scaled, ((0,), (0,)))


def grad_x_kernel(transposed, r_ref, rt_ref, g_ref, b_ref, c_ref, q_ref, skip_ref, out_ref):
    b = b_ref[...]
    scores = dot(b, c_ref[...], ((1,), (1,)))
    running = r_ref[...]
    columns = rt_ref[0]
    top_keep = iota((HALF, SPAN), 1) >= iota((HALF, SPAN), 0)
    low_keep = iota((HALF, HALF), 1) >= iota((HALF, HALF), 0)
    to_end = jnp.exp2(spread_columns(columns[SPAN - 1 : SPAN] - columns))
    from_state = mm(b, q_ref[0]) * to_end
    for pair in range(GROUP // 2):
        lanes = slice(pair * 2 * P_SIZE, (pair + 1) * 2 * P_SIZE)
        g = g_ref[:, lanes]
        parts = []
        for head in (2 * pair, 2 * pair + 1):
            row = running[head : head + 1]
            top = jnp.where(top_keep, row - columns[:HALF, head : head + 1], NEVER)
            low = jnp.where(low_keep, row[:, HALF:] - columns[HALF:, head : head + 1], NEVER)
            parts.append((jnp.exp2(top) * scores[:HALF]).astype(BF16))
            low = (jnp.exp2(low) * scores[HALF:, HALF:]).astype(BF16)
            parts.append(jnp.concatenate([jnp.zeros((HALF, HALF), BF16), low], axis=1))
        product = mm(jnp.concatenate(parts, axis=0), g)
        parts = [product[:SPAN], product[SPAN:]]
        inner = jnp.where(first_head(), parts[0], parts[1])
        total = inner + skip_ref[:, lanes] * g.astype(F32) + from_state[:, lanes]
        if transposed:
            out_ref[lanes, :] = total.T.astype(BF16)
        else:
            out_ref[:, lanes] = total.astype(BF16)


def forward_kernel(half_ref, own_ref, other_ref, w_ref, rt_ref, b_ref, x_ref, e_ref, total_ref):
    step = pl.program_id(1)

    @pl.when(step == 0)
    def _():
        total_ref[...] = jnp.zeros_like(total_ref)

    half = pl.num_programs(1) // 2

    @pl.when(step < half)
    def _():
        total_ref[...] += mm(own_ref[...], w_ref[...])

    @pl.when(step >= half)
    def _():
        total_ref[...] += mm(other_ref[...], w_ref[...])

    @pl.when(step == pl.num_programs(1) - 1)
    def _():
        x = total_ref[...].astype(BF16)
        x_ref[...] = x
        for k in range(e_ref.shape[0]):
            rows = slice(k * SPAN, (k + 1) * SPAN)
            columns = rt_ref[0, rows]
            to_end = jnp.exp2(spread_columns(columns[SPAN - 1 : SPAN] - columns))
            scaled = (x[rows].astype(F32) * to_end).astype(BF16)
            e_ref[k] = dot(b_ref[rows], scaled, ((0,), (0,)))


def product_kernel(has_before, has_other, half_ref, g_ref, w_ref, *refs):
    refs = list(refs)
    total = dot(g_ref[...], w_ref[...], ((1,), (1,)))
    if has_before:
        total = total + refs.pop(0)[...].astype(F32)
    if has_other:
        total = total.astype(BF16).astype(F32) + refs.pop(0)[...].astype(F32)
    refs[0][...] = total.astype(BF16)


def arrange_kernel(order_ref, own_ref, other_ref, early_ref, late_ref, both_ref):
    half = own_ref.shape[1]
    both_ref[:, :half] = own_ref[...]
    both_ref[:, half:] = other_ref[...]
    unit = 2 * half // order_ref.shape[0]
    cut = early_ref.shape[1]
    for index in range(order_ref.shape[0]):
        source = pl.ds(pl.multiple_of(order_ref[index] * unit, 128), unit)
        at = index * unit
        if at < cut:
            early_ref[:, at : at + unit] = both_ref[:, source]
        else:
            late_ref[:, at - cut : at - cut + unit] = both_ref[:, source]


TAIL = 16


def message(total, log):
    high, middle, last = thirds(log)
    line = iota((TAIL, total.shape[1]), 0)
    tail = jnp.where(line == 0, high, jnp.where(line == 1, middle, jnp.where(line == 2, last, 0.0)))
    return total.astype(BF16), tail.astype(BF16)


def start_kernel(own_ref, kept_ref, log_ref, sent_ref):
    spans = own_ref.shape[0]
    total = own_ref[spans - 1]
    log = kept_ref[spans - 1, 4:5]
    for k in range(spans - 2, -1, -1):
        total = own_ref[k] + kept_ref[k, :1] * total
        log = log + kept_ref[k, 4:5]
    line = iota(log_ref.shape, 0)
    log_ref[...] = jnp.where(line == 0, log, 0.0)
    n = total.shape[0]
    sent_ref[:n], sent_ref[n:] = message(total, log)


def back_kernel(bit, place_ref, log_ref, mine_ref, got_ref, *refs):
    entering_ref = refs[0] if len(refs) == 5 else None
    entering_out, sent_out, log_out, factor_out = refs[-4:]
    n = entering_out.shape[0]
    got = got_ref[:n].astype(F32)
    tail = got_ref[n:].astype(F32)
    other_log = tail[0:1] + tail[1:2] + tail[2:3]
    log, before_me, after_me = log_ref[0:1], log_ref[1:2], log_ref[2:3]
    line = iota(log_ref.shape, 0)
    upper = (place_ref[0] // bit % 2 + 0 * line[0:1]) == 1
    kept, other = jnp.exp2(log), jnp.exp2(other_log)
    mine = mine_ref[:n].astype(F32)
    total = jnp.where(upper, other, 1.0) * mine + jnp.where(upper, 1.0, kept) * got
    passed = jnp.where(upper, 0.0, jnp.exp2(after_me)) * got
    entering_out[...] = passed if entering_ref is None else entering_ref[...] + passed
    first = jnp.where(upper, 1.0, other)
    second = jnp.where(upper, kept, 1.0)
    third = jnp.where(upper, jnp.exp2(before_me), 0.0)
    factor_out[...] = jnp.where(line == 0, first, jnp.where(line == 1, second, third))
    log = log + other_log
    before_me = jnp.where(upper, before_me + other_log, before_me)
    after_me = jnp.where(upper, after_me, after_me + other_log)
    log_out[...] = jnp.where(line == 0, log, jnp.where(line == 1, before_me, after_me))
    sent_out[:n], sent_out[n:] = message(total, log)


def scan_kernel(last, factor_ref, mine_ref, got_ref, *refs):
    refs = list(refs)
    entering_ref = refs.pop(0) if len(refs) == 3 - last else None
    factors = factor_ref[...]
    got = got_ref[...].astype(F32)
    if not last:
        total = factors[0:1] * mine_ref[...].astype(F32) + factors[1:2] * got
        refs[1][...] = total.astype(BF16)
    passed = factors[2:3] * got
    refs[0][...] = passed if entering_ref is None else entering_ref[...] + passed


def scan_pair_kernel(number, last, *refs):
    first, second, outs = refs[:number], refs[number : number + 4], refs[number + 4 :]
    scan_kernel(False, *first, *outs[:2])
    scan_kernel(last, *second, *outs[2:])


def early_forward_kernel(count, f_ref, *refs):
    pieces, (out_ref, buffer) = refs[:count], refs[count:]
    rows = pieces[0].shape[0]
    for index, piece in enumerate(pieces):
        buffer[index * rows : (index + 1) * rows] = piece[...]
    out_ref[...] = mm(f_ref[...], buffer[...])


def late_forward_kernel(count, f_ref, part_ref, rt_ref, b_ref, kept_ref, *refs):
    pieces, (x_ref, e_ref, sent_ref, buffer) = refs[:count], refs[count:]
    rows = pieces[0].shape[0]
    for index, piece in enumerate(pieces):
        buffer[index * rows : (index + 1) * rows] = piece[...]
    x = (part_ref[...] + mm(f_ref[...], buffer[...])).astype(BF16)
    x_ref[...] = x
    total = None
    for k in range(e_ref.shape[0]):
        part = slice(k * SPAN, (k + 1) * SPAN)
        columns = rt_ref[0, part]
        to_end = jnp.exp2(spread_columns(columns[SPAN - 1 : SPAN] - columns))
        scaled = (x[part].astype(F32) * to_end).astype(BF16)
        state = dot(b_ref[part], scaled, ((0,), (0,)))
        e_ref[k] = state
        total = state if total is None else kept_ref[k, :1] * total + state
    sent_ref[...] = total.astype(BF16)


def blocks_kernel(halves, has_before, order_ref, g_ref, *refs):
    count = len(halves)
    number = sum(halves)
    arrays, refs = refs[:number], refs[number:]
    if has_before:
        refs = refs[2:]
    away_ref, own_ref, buffer, slots, sems, out_sems = refs
    rows = arrays[0].shape[0]
    wide = g_ref.shape[0]
    copies = []
    at = 0
    for index, parts in enumerate(halves):
        mine = []
        for part in range(parts):
            lanes = pl.ds(part * (wide // parts), wide // parts)
            target = buffer.at[pl.ds(index * rows, rows), lanes]
            copy = pltpu.make_async_copy(arrays[at], target, sems.at[at])
            copy.start()
            mine.append(copy)
            at += 1
        copies.append(mine)
    g = g_ref[...]
    half = away_ref.shape[1] // rows
    starts = [0]
    while starts[-1] < count:
        starts.append(starts[-1] + (2 if count - starts[-1] in (2, 4) else 3))
    for index in range(count):
        for copy in copies[index]:
            copy.wait()
        if index + 1 not in starts:
            continue
        start = starts[starts.index(index + 1) - 1]
        product = mm(buffer[start * rows : (index + 1) * rows], g)
        for done in range(start, index + 1):
            part = product[(done - start) * rows : (done - start + 1) * rows]
            slots[done] = part.T.astype(BF16)
            place = order_ref[done]
            lanes = pl.ds(pl.multiple_of(place % half * rows, 128), rows)

            @pl.when(place < half)
            def _():
                target = away_ref.at[:, lanes]
                pltpu.make_async_copy(slots.at[done], target, out_sems.at[done]).start()

            @pl.when(place >= half)
            def _():
                target = own_ref.at[:, lanes]
                pltpu.make_async_copy(slots.at[done], target, out_sems.at[done]).start()

    for index in range(count):
        target = away_ref.at[:, pl.ds(0, rows)]
        pltpu.make_async_copy(slots.at[index], target, out_sems.at[index]).wait()


def after_kernel(*refs):
    pass


def inner_kernel(
    r_ref, rt_ref, g_ref, x_ref, b_ref, c_ref, q_ref, *refs
):
    d_ref, grad_b_ref, grad_c_ref, sum_ref, top_ref, low_ref = refs[-6:]
    so_far = refs[:-6]
    step = pl.program_id(1)
    b = b_ref[...]
    c = c_ref[...]
    scores = dot(b, c, ((1,), (1,)))
    running = r_ref[...]
    columns = rt_ref[0]
    top_keep = iota((HALF, SPAN), 1) >= iota((HALF, SPAN), 0)
    low_keep = iota((HALF, HALF), 1) >= iota((HALF, HALF), 0)

    @pl.when(step == 0)
    def _():
        sum_ref[...] = jnp.zeros_like(sum_ref)
        grad_b_ref[...] = so_far[0][...] if so_far else jnp.zeros_like(grad_b_ref)

    rows = []
    lane = iota((SPAN, 2 * P_SIZE), 1)
    later = not_before().astype(BF16)
    top_less = iota((HALF, SPAN), 1) > iota((HALF, SPAN), 0)
    low_less = iota((HALF, HALF), 1) > iota((HALF, HALF), 0)
    for pair in range(GROUP // 2):
        lanes = slice(pair * 2 * P_SIZE, (pair + 1) * 2 * P_SIZE)
        x = x_ref[:, lanes]
        none = jnp.zeros_like(x)
        x = [jnp.where(lane < P_SIZE, x, none), jnp.where(lane < P_SIZE, none, x)]
        product = mm(jnp.concatenate(x, axis=0), g_ref[:, lanes].T)
        top_sum = low_sum = None
        for number in range(2):
            head = 2 * pair + number
            row = running[head : head + 1]
            at = number * SPAN
            top = jnp.where(top_keep, row - columns[:HALF, head : head + 1], NEVER)
            low = jnp.where(low_keep, row[:, HALF:] - columns[HALF:, head : head + 1], NEVER)
            top = jnp.exp2(top) * product[at : at + HALF]
            low = jnp.exp2(low) * product[at + HALF : at + SPAN, HALF:]
            top_sum = top if number == 0 else top_sum + top
            low_sum = low if number == 0 else low_sum + low
            part = slice(head * HALF, (head + 1) * HALF)
            top_ref[part] = (top * scores[:HALF]).astype(BF16)
            low_ref[part] = (low * scores[HALF:, HALF:]).astype(BF16)
        sum_ref[:HALF] += top_sum
        sum_ref[HALF:, HALF:] += low_sum
    top = mm(top_ref[...], later)
    low = mm(low_ref[...], later[HALF:, HALF:])
    for head in range(GROUP):
        part = slice(head * HALF, (head + 1) * HALF)
        top_row = jnp.sum(jnp.where(top_less, top[part], 0.0), axis=0, keepdims=True)
        low_row = jnp.sum(jnp.where(low_less, low[part], 0.0), axis=0, keepdims=True)
        rows.append(jnp.concatenate([top_row[:, :HALF], top_row[:, HALF:] + low_row], axis=1))
    to_end = jnp.exp2(spread_columns(columns[SPAN - 1 : SPAN] - columns))
    scaled = x_ref[...].astype(F32) * to_end
    ends = dot(one_hot(BF16), (scaled * mm(b, q_ref[0])).astype(BF16), ((1,), (1,)))
    d_ref[...] = jnp.concatenate(rows, axis=0) + sum_over(ends, before())
    grad_b_ref[...] += dot(scaled.astype(BF16), q_ref[0], ((1,), (1,)))

    @pl.when(step == pl.num_programs(1) - 1)
    def _():
        total = sum_ref[...].astype(BF16)
        grad_b_ref[...] += mm(total, c)
        part = dot(total, b, ((0,), (0,)))
        grad_c_ref[...] = part + so_far[1][...] if so_far else part


def state_kernel(
    rt_ref, g_ref, c_ref, s_ref, e_ref, q_ref, a_ref, d_part_ref, c_part_ref, *refs
):
    d_ref, grad_c_ref, held = refs[-3:]
    span, group = pl.program_id(0), pl.program_id(1)

    @pl.when(group == 0)
    def _():
        grad_c_ref[...] = c_part_ref[...]

    @pl.when(span == 0)
    def _():
        held[group] = s_ref[...]

    state = held[group]
    low = state.astype(BF16)
    scaled = g_ref[...].astype(F32) * jnp.exp2(spread_columns(rt_ref[0]))
    ends = dot(one_hot(BF16), (scaled * mm(c_ref[...], low)).astype(BF16), ((1,), (1,)))
    grad_c_ref[...] += dot(scaled.astype(BF16), low, ((1,), (1,)))
    product = jnp.sum(q_ref[0].astype(F32) * state, axis=0, keepdims=True) * a_ref[0, :1]
    high, middle, last = thirds(product)
    row = iota((8, WIDE), 0)
    stacked = jnp.where(row == 0, high, jnp.where(row == 1, middle, jnp.where(row == 2, last, 0.0)))
    kept = dot(one_hot(BF16), stacked.astype(BF16), ((1,), (1,)))
    kept = jnp.sum(kept, axis=1, keepdims=True)
    d_ref[...] = d_part_ref[...] + sum_over(ends, not_before()) + kept
    held[group] = e_ref[0] + a_ref[0, :1] * state


def call(kernel, grid, in_specs, out_specs, out_shape, flops, size, scratch=()):
    return pl.pallas_call(
        kernel,
        grid=grid,
        in_specs=in_specs,
        out_specs=out_specs,
        out_shape=out_shape,
        scratch_shapes=list(scratch),
        cost_estimate=pl.CostEstimate(flops=flops, bytes_accessed=size, transcendentals=0),
        compiler_params=pltpu.CompilerParams(
            dimension_semantics=("arbitrary",) * len(grid), vmem_limit_bytes=GRANT
        ),
    )


def run_spec(at=0):
    return pl.BlockSpec((GROUP, SPAN), lambda k, h: (h + at, k))


def run_t_spec(at=0):
    return pl.BlockSpec((1, SPAN, GROUP), lambda k, h: (h + at, k, 0))


def rows_spec(at=0):
    return pl.BlockSpec((SPAN, WIDE), lambda k, h: (k, h + at))


def state_spec(at=0):
    return pl.BlockSpec((1, 2 * P_SIZE, WIDE), lambda k, h: (k, 0, h + at))


def kept_spec(at=0):
    return pl.BlockSpec((1, 8, WIDE), lambda k, h: (k, 0, h + at))


SHARED = pl.BlockSpec((SPAN, 2 * P_SIZE), lambda k, h: (k, 0))
GAIN = pl.BlockSpec((1, WIDE), lambda k, h: (0, h))
ANYWHERE = pl.BlockSpec(memory_space=pl.ANY)
INNER_SCRATCH = [
    pltpu.VMEM((SPAN, SPAN), F32),
    pltpu.VMEM((GROUP * HALF, SPAN), BF16),
    pltpu.VMEM((GROUP * HALF, HALF), BF16),
]
SCALARS = pl.BlockSpec(memory_space=pltpu.SMEM)


def shape(*dims, dtype=F32):
    return jax.ShapeDtypeStruct(dims, dtype)


def swap(value, axis, bit):
    count = lax.axis_size(axis)
    return lax.ppermute(value, axis, [(i, i ^ bit) for i in range(count)])


def block_products(kept):
    count = lax.axis_size("ctx")
    place = lax.axis_index("ctx")
    steps = []
    before_me = jnp.ones_like(kept)
    after_me = jnp.ones_like(kept)
    bit = 1
    while bit < count:
        other = swap(kept, "ctx", bit)
        upper = (place & bit) != 0
        steps.append((bit, upper, kept, other, before_me, after_me))
        before_me = jnp.where(upper, before_me * other, before_me)
        after_me = jnp.where(upper, after_me, after_me * other)
        kept = kept * other
        bit *= 2
    return steps


def scan_states(total, steps, reverse):
    entering = jnp.zeros_like(total)
    for bit, upper, kept, other, before_me, after_me in steps:
        got = swap(total.astype(BF16), "ctx", bit).astype(F32)
        if reverse:
            entering = entering + jnp.where(upper, 0.0, after_me) * got
            total = jnp.where(upper, got + other * total, total + kept * got)
        else:
            entering = entering + jnp.where(upper, before_me, 0.0) * got
            total = jnp.where(upper, kept * got + total, other * total + got)
    return entering


def head_sum(value):
    bit = 1
    while bit < lax.axis_size("head"):
        value = value.astype(BF16)
        value = value.astype(F32) + swap(value, "head", bit).astype(F32)
        bit *= 2
    return value


PLANE = 4


def after(values, *tokens):
    out = pl.pallas_call(
        after_kernel,
        in_specs=[ANYWHERE] * (len(values) + len(tokens)),
        out_specs=[ANYWHERE] * len(values),
        out_shape=[shape(*value.shape, dtype=value.dtype) for value in values],
        input_output_aliases={index: index for index in range(len(values))},
        cost_estimate=pl.CostEstimate(flops=0, bytes_accessed=0, transcendentals=0),
        compiler_params=pltpu.CompilerParams(vmem_limit_bytes=GRANT),
    )(*values, *tokens)
    return list(out)


def along_z(value, moves):
    pairs = [(a * PLANE + i, b * PLANE + i) for a, b in moves for i in range(PLANE)]
    return lax.ppermute(value, "ctx", pairs)


MIDDLE = ((1, 2), (2, 1))
OUTWARD = ((1, 0), (2, 3))


def swap_x(value):
    return swap(value, "ctx", 1)


def swap_y(value):
    return swap(value, "ctx", 2)


LAYERS = ((0, 1, 2, 3), (1, 0, 3, 2), (2, 2, 1, 1), (3, 3, 0, 0))
EARLY = [(k, flip) for k in (0, 1, 2) for flip in range(3)]
LATE = [(0, 3), (1, 3), (2, 3), (3, 0), (3, 1), (3, 2), (3, 3)]


def block_order():
    place = lax.axis_index("ctx")
    layer, spot = place // PLANE, place % PLANE
    layers = jnp.array(LAYERS, jnp.int32)[:, layer]
    order = [layers[k] * PLANE + (spot ^ flip) for k, flip in EARLY + LATE]
    return jnp.stack(order).astype(jnp.int32)


def gather_weight(w, sizes):
    ends = [sum(sizes[: j + 1]) * P_SIZE for j in range(len(sizes))]
    parts = [w[:, end - size * P_SIZE : end] for end, size in zip(ends, sizes)]
    return [lax.all_gather(part, "ctx", axis=0, tiled=True) for part in parts]


def forward(features, first, weight, running_t, b_rows, here):
    own, other = features
    length = own.shape[0]
    n = b_rows.shape[1]
    width, wide = weight.shape
    deep = width // 4
    spans = length // SPAN

    def depth(k, first_ref):
        return (k // 2 ^ first_ref[0]) * 2 + k % 2

    return pl.pallas_call(
        forward_kernel,
        grid_spec=pltpu.PrefetchScalarGridSpec(
            num_scalar_prefetch=1,
            grid=(wide // WIDE, 4),
            in_specs=[
                pl.BlockSpec((length, deep), lambda h, k, first_ref: (0, jnp.minimum(k, 1))),
                pl.BlockSpec((length, deep), lambda h, k, first_ref: (0, jnp.maximum(k - 2, 0))),
                pl.BlockSpec((deep, WIDE), lambda h, k, first_ref: (depth(k, first_ref), h)),
                pl.BlockSpec((1, length, GROUP), lambda h, k, first_ref: (h + here, 0, 0)),
                pl.BlockSpec((length, n), lambda h, k, first_ref: (0, 0)),
            ],
            out_specs=[
                pl.BlockSpec((length, WIDE), lambda h, k, first_ref: (0, h)),
                pl.BlockSpec((spans, n, WIDE), lambda h, k, first_ref: (0, 0, h)),
            ],
            scratch_shapes=[pltpu.VMEM((length, WIDE), F32)],
        ),
        out_shape=[shape(length, wide, dtype=BF16), shape(spans, n, wide)],
        cost_estimate=pl.CostEstimate(
            flops=2 * length * wide * width, bytes_accessed=2 * wide * width, transcendentals=0
        ),
        compiler_params=pltpu.CompilerParams(
            dimension_semantics=("arbitrary", "arbitrary"), vmem_limit_bytes=GRANT
        ),
    )(first, own, other, weight, running_t, b_rows)


def multiply(grad_x, weight, at, half, halves, before=None, other=None):
    length = grad_x.shape[0]
    width, wide = weight.shape
    tiles = width // halves // WIDE
    tile = pl.BlockSpec((length, WIDE), lambda j, half_ref: (0, half_ref[0] * tiles + j))
    plain = pl.BlockSpec((length, WIDE), lambda j, half_ref: (0, j))
    in_specs = [
        pl.BlockSpec((length, wide), lambda j, half_ref: (0, at)),
        pl.BlockSpec((WIDE, wide), lambda j, half_ref: (half_ref[0] * tiles + j, 0)),
    ]
    operands = [grad_x, weight]
    if before is not None:
        in_specs.append(tile)
        operands.append(before)
    if other is not None:
        in_specs.append(plain)
        operands.append(other)
    return pl.pallas_call(
        functools.partial(product_kernel, before is not None, other is not None),
        grid_spec=pltpu.PrefetchScalarGridSpec(
            num_scalar_prefetch=1,
            grid=(tiles,),
            in_specs=in_specs,
            out_specs=plain,
        ),
        out_shape=shape(length, width // halves, dtype=BF16),
        cost_estimate=pl.CostEstimate(
            flops=2 * length * wide * width // halves,
            bytes_accessed=2 * wide * width // halves,
            transcendentals=0,
        ),
        compiler_params=pltpu.CompilerParams(
            dimension_semantics=("arbitrary",), vmem_limit_bytes=GRANT
        ),
    )(half, *operands)


def early_forward(features, pieces):
    length = features.shape[0]
    rows, columns = pieces[0].shape
    deep = rows * len(pieces)
    return call(
        functools.partial(early_forward_kernel, len(pieces)),
        (columns // WIDE,),
        [pl.BlockSpec((length, deep), lambda h: (0, 0))]
        + [pl.BlockSpec((rows, WIDE), lambda h: (0, h))] * len(pieces),
        pl.BlockSpec((length, WIDE), lambda h: (0, h)),
        shape(length, columns),
        2 * length * columns * deep,
        2 * columns * deep,
        [pltpu.VMEM((deep, WIDE), BF16)],
    )(features, *pieces)


def late_forward(features, part, pieces, running_t, b_rows, kept, here):
    length = features.shape[0]
    rows, columns = pieces[0].shape
    deep = rows * len(pieces)
    n = b_rows.shape[1]
    spans = length // SPAN
    state = pl.BlockSpec((n, WIDE), lambda h: (0, h))
    return call(
        functools.partial(late_forward_kernel, len(pieces)),
        (columns // WIDE,),
        [
            pl.BlockSpec((length, deep), lambda h: (0, 0)),
            pl.BlockSpec((length, WIDE), lambda h: (0, h + here)),
            pl.BlockSpec((1, length, GROUP), lambda h: (h + here, 0, 0)),
            pl.BlockSpec((length, n), lambda h: (0, 0)),
            pl.BlockSpec((spans, 8, WIDE), lambda h: (0, 0, h + here)),
        ]
        + [pl.BlockSpec((rows, WIDE), lambda h: (0, h))] * len(pieces),
        [
            pl.BlockSpec((length, WIDE), lambda h: (0, h)),
            pl.BlockSpec((spans, n, WIDE), lambda h: (0, 0, h)),
            state,
        ],
        [
            shape(length, columns, dtype=BF16),
            shape(spans, n, columns),
            shape(n, columns, dtype=BF16),
        ],
        2 * length * columns * deep,
        2 * columns * deep,
        [pltpu.VMEM((deep, WIDE), BF16)],
    )(features, part, running_t, b_rows, kept, *pieces)


def multiply_blocks(order, grad_x, pieces, so_far):
    columns, length = grad_x.shape
    arrays = [array for piece in pieces for array in piece]
    rows = arrays[0].shape[0]
    count = len(pieces)
    half = shape(length, lax.axis_size("ctx") * rows // 2, dtype=BF16)
    first = 2 + len(arrays)
    return pl.pallas_call(
        functools.partial(blocks_kernel, [len(piece) for piece in pieces], bool(so_far)),
        grid=(1,),
        in_specs=[SCALARS, pl.BlockSpec((columns, length), lambda h: (0, 0))]
        + [ANYWHERE] * (len(arrays) + len(so_far)),
        out_specs=[ANYWHERE, ANYWHERE],
        out_shape=[half, half],
        input_output_aliases={first + k: k for k in range(len(so_far))},
        scratch_shapes=[
            pltpu.VMEM((rows * count, columns), BF16),
            pltpu.VMEM((count, length, rows), BF16),
            pltpu.SemaphoreType.DMA((len(arrays),)),
            pltpu.SemaphoreType.DMA((count,)),
        ],
        cost_estimate=pl.CostEstimate(
            flops=2 * length * columns * rows * count,
            bytes_accessed=2 * columns * rows * count,
            transcendentals=0,
        ),
        compiler_params=pltpu.CompilerParams(
            dimension_semantics=("arbitrary",), vmem_limit_bytes=GRANT
        ),
    )(order, grad_x, *arrays, *so_far)


def back_start(own_grads, kept):
    spans, n, columns = own_grads.shape
    return call(
        start_kernel,
        (columns // WIDE,),
        [
            pl.BlockSpec((spans, n, WIDE), lambda h: (0, 0, h)),
            pl.BlockSpec((spans, 8, WIDE), lambda h: (0, 0, h)),
        ],
        [pl.BlockSpec((rows, WIDE), lambda h: (0, h)) for rows in (8, n + TAIL)],
        [shape(8, columns), shape(n + TAIL, columns, dtype=BF16)],
        0,
        14 * n * columns,
    )(own_grads, kept)


def back_step(place, log, sent, entering, bit):
    got = swap(sent, "ctx", bit)
    columns = sent.shape[1]
    n = sent.shape[0] - TAIL
    short, state, tall = [
        pl.BlockSpec((rows, 2 * WIDE), lambda h: (0, h)) for rows in (8, n, n + TAIL)
    ]
    return call(
        functools.partial(back_kernel, bit),
        (columns // (2 * WIDE),),
        [SCALARS, short, tall, tall] + [state] * len(entering),
        [state, tall, short, short],
        [
            shape(n, columns),
            shape(n + TAIL, columns, dtype=BF16),
            shape(8, columns),
            shape(8, columns),
        ],
        0,
        14 * n * columns,
    )(place, log, sent, got, *entering)


def scan_step(factors, here, sent, entering, bit, last=False):
    got = swap(sent, "ctx", bit)
    n, columns = sent.shape
    block = pl.BlockSpec((n, columns), lambda h: (0, 0))
    at = here * WIDE // columns
    outs = [shape(n, columns), shape(n, columns, dtype=BF16)][: 2 - last]
    return call(
        functools.partial(scan_kernel, last),
        (1,),
        [pl.BlockSpec((8, columns), lambda h: (0, at)), block, block] + [block] * len(entering),
        [block] * len(outs),
        outs,
        0,
        10 * n * columns,
    )(factors, sent, got, *entering)


def scan_pair(first, second, last=False):
    operands, specs, outs = [], [], []
    for factors, here, sent, entering, bit in (first, second):
        got = swap(sent, "ctx", bit)
        n, columns = sent.shape
        block = pl.BlockSpec((n, columns), lambda h: (0, 0))
        at = here * WIDE // columns
        operands += [factors, sent, got, *entering]
        specs += [pl.BlockSpec((8, columns), lambda h, at=at: (0, at))]
        specs += [block] * (2 + len(entering))
        outs += [shape(n, columns), shape(n, columns, dtype=BF16)]
    outs = outs[: 4 - last]
    return call(
        functools.partial(scan_pair_kernel, 3 + len(first[3]), last),
        (1,),
        specs,
        [block] * len(outs),
        outs,
        0,
        20 * n * columns,
    )(*operands)


def local(inputs, w_in, b_rows, c_rows, log_decay, skip_gain, grad_out):
    groups = log_decay.shape[0] // GROUP
    layered = lax.axis_size("ctx") == 4 * PLANE and lax.axis_size("head") == 2
    if layered and groups % 2 == 0 and w_in.shape[0] == 256:
        return local_layered(inputs, w_in, b_rows, c_rows, log_decay, skip_gain, grad_out)
    return local_plain(inputs, w_in, b_rows, c_rows, log_decay, skip_gain, grad_out)


def prepare(log_decay, grad_out, c_rows):
    length, columns = grad_out.shape
    heads = log_decay.shape[0]
    spans = length // SPAN
    groups = heads // GROUP
    n = c_rows.shape[1]
    return call(
        decay_kernel,
        (spans, groups),
        [run_spec(), rows_spec(), SHARED],
        [run_spec(), run_t_spec(), kept_spec(), state_spec()],
        [
            shape(heads, length),
            shape(groups, length, GROUP),
            shape(spans, 8, columns),
            shape(spans, n, columns),
        ],
        2 * length * columns * n,
        6 * length * columns,
    )(log_decay, grad_out, c_rows)


def inner(grid, here, wide, operands, so_far):
    length = operands[2].shape[0]
    n = operands[4].shape[1]
    specs = [
        run_spec(here),
        run_t_spec(here),
        rows_spec(here),
        rows_spec(),
        SHARED,
        SHARED,
        state_spec(here),
    ]
    return call(
        inner_kernel,
        grid,
        specs + [SHARED] * len(so_far),
        [run_spec(), SHARED, SHARED],
        [shape(wide // P_SIZE, length), shape(length, n), shape(length, n)],
        12 * length * wide * SPAN,
        6 * length * wide,
        INNER_SCRATCH,
    )(*operands, *so_far)


def state_terms(grid, here, wide, operands, heads=None, so_far=None):
    length = operands[1].shape[0]
    n = operands[2].shape[1]
    heads = heads or wide // P_SIZE
    at = here if heads > wide // P_SIZE else 0
    extra = () if so_far is None else (so_far,)
    return pl.pallas_call(
        state_kernel,
        grid=grid,
        in_specs=[
            run_t_spec(here),
            rows_spec(here),
            SHARED,
            pl.BlockSpec((n, WIDE), lambda k, h: (0, h)),
            state_spec(),
            state_spec(here),
            kept_spec(here),
            run_spec(),
            SHARED,
        ]
        + [ANYWHERE] * len(extra),
        out_specs=[run_spec(at), SHARED],
        out_shape=[shape(heads, length), shape(length, n)],
        scratch_shapes=[pltpu.VMEM((grid[1], n, WIDE), F32)],
        input_output_aliases={len(operands): 0} if extra else {},
        cost_estimate=pl.CostEstimate(
            flops=4 * length * wide * n, bytes_accessed=6 * length * wide, transcendentals=0
        ),
        compiler_params=pltpu.CompilerParams(
            dimension_semantics=("arbitrary", "arbitrary"), vmem_limit_bytes=GRANT
        ),
    )(*operands, *extra)


def local_layered(inputs, w_in, b_rows, c_rows, log_decay, skip_gain, grad_out):
    length, columns = grad_out.shape
    heads = log_decay.shape[0]
    spans = length // SPAN
    groups = heads // GROUP
    place = lax.axis_index("head").astype(jnp.int32)
    half = columns // 2
    order = block_order()
    blocks = order.shape[0]
    width = blocks * w_in.shape[0]

    z1, inner2 = swap(w_in, "ctx", PLANE), along_z(w_in, MIDDLE)
    own_x, own_y = swap_x(w_in), swap_y(w_in)
    other = swap(inputs, "head", 1)
    running, running_t, kept, own_grads = prepare(log_decay, grad_out, c_rows)
    spot = lax.axis_index("ctx").astype(jnp.int32)[None]
    log, sent = back_start(own_grads, kept)
    sent = after([sent], other)[0]
    leaving, moved, log, factors_1 = back_step(spot, log, sent, (), 1)

    z1, inner2, own_y = after([z1, inner2, own_y], own_x, sent)
    sent = moved
    x1, y1 = swap_x(z1), swap_y(z1)
    inner3, outer2 = along_z(z1, MIDDLE), along_z(inner2, OUTWARD)
    own_y_a, own_y_b = own_y[:, :half], own_y[:, half:]
    inner3_a, inner3_b = inner3[:, :half], inner3[:, half:]
    leaving, sent, log, factors_2 = back_step(spot, log, sent, (leaving,), 2)
    order_own = (order + place * (blocks // 2)) % blocks
    cut = len(EARLY) * w_in.shape[0]
    early_features, late_features = call(
        arrange_kernel,
        (1,),
        [SCALARS] + [pl.BlockSpec((length, width // 2), lambda h: (0, 0))] * 2,
        [pl.BlockSpec((length, wide), lambda h: (0, 0)) for wide in (cut, width - cut)],
        [shape(length, wide, dtype=BF16) for wide in (cut, width - cut)],
        0,
        4 * length * width,
        [pltpu.VMEM((length, width), BF16)],
    )(order_own, inputs, other)

    inner2, inner3_a, inner3_b, outer2, x1, sent, own_y_a, own_y_b = after(
        [inner2, inner3_a, inner3_b, outer2, x1, sent, own_y_a, own_y_b], y1, early_features
    )
    z3 = inner2 + outer2
    x3, y3 = swap_x(z3), swap_y(z3)
    outer3_a = along_z(inner3_a, OUTWARD)
    x1_a, x1_b = x1[:, :half], x1[:, half:]
    leaving, sent, log, factors_4 = back_step(spot, log, sent, (leaving,), 4)

    inner3_a, inner3_b, outer3_a, y3, x1_a, x1_b = after(
        [inner3_a, inner3_b, outer3_a, y3, x1_a, x1_b], x3
    )
    z2a = inner3_a + outer3_a
    outer3_b = along_z(inner3_b, OUTWARD)
    y3_a, y3_b = y3[:, :half], y3[:, half:]
    x2a, y2a = swap_x(z2a), swap_y(z2a)
    d3a, d1a = swap_x(y3_a), swap_y(x1_a)
    leaving, sent, log, factors_8 = back_step(spot, log, sent, (leaving,), 8)
    early = [w_in, own_x, own_y, z1, x1, y1, z3, x3, y3]
    part = early_forward(early_features, early)

    own_y_a, x2a, leaving = after([own_y_a, x2a, leaving], y2a, d3a, d1a, part)
    d0a, d2a = swap_x(own_y_a), swap_y(x2a)
    leaving_all = [leaving]
    for k in range(spans - 1, 0, -1):
        leaving_all.insert(0, own_grads[k] + kept[k, :1] * leaving_all[0])
    leaving_all = jnp.stack([value.astype(BF16) for value in leaving_all])
    (z2b,) = after([inner3_b + outer3_b], leaving_all)
    x2b, y2b = swap_x(z2b), swap_y(z2b)
    skip = jnp.repeat(skip_gain, P_SIZE)[None]
    grad_x = grad_rows(running, running_t, grad_out, b_rows, c_rows, leaving_all, skip, True)
    order_away = (order + (1 - place) * (blocks // 2)) % blocks
    early_order, late_order = order_away[: len(EARLY)], order_away[len(EARLY) :]
    late_a = [d0a, d1a, d3a, z2a, x2a, y2a, d2a]
    x_a, states_a, sent_a = late_forward(
        late_features, part, late_a, running_t, b_rows, kept, 0
    )

    own_y_b, x2b, y3_b, x1_b, grad_x, x_a = after(
        [own_y_b, x2b, y3_b, x1_b, grad_x, x_a], y2b, sent_a
    )
    d0b, d2b = swap_x(own_y_b), swap_y(x2b)
    d3b, d1b = swap_x(y3_b), swap_y(x1_b)
    product = multiply_blocks(early_order, grad_x, [[piece] for piece in early], ())
    shared = (running, running_t, grad_out)
    here = groups // 2
    grid = (spans, here)

    inner_a = shared + (x_a, b_rows, c_rows, leaving_all)
    decay_a, grad_b, grad_c = inner(grid, 0, half, inner_a, ())
    d0b, d2b, sent_a = after([d0b, d2b, sent_a], d3b, d1b, product[0], grad_b)
    entering_a, sent_a = scan_step(factors_1, 0, sent_a, (), 1)
    late_b = [d0b, d1b, d3b, z2b, x2b, y2b, d2b]
    x_b, states_b, sent_b = late_forward(
        late_features, part, late_b, running_t, b_rows, kept, here
    )
    pairs = list(zip(late_a, late_b))
    sent_a, sent_b, *product = after([sent_a, sent_b, *product])
    entering_b, sent_b, entering_a, sent_a = scan_pair(
        (factors_1, here, sent_b, (), 1), (factors_2, 0, sent_a, (entering_a,), 2)
    )
    away, own = multiply_blocks(late_order, grad_x, pairs, product)

    sent_a, sent_b, away = after([sent_a, sent_b, away])
    entering_b, sent_b, entering_a, sent_a = scan_pair(
        (factors_2, here, sent_b, (entering_b,), 2), (factors_4, 0, sent_a, (entering_a,), 4)
    )
    got = swap(away, "head", 1)

    sent_a, sent_b, x_b = after([sent_a, sent_b, x_b])
    entering_b, sent_b, entering_a = scan_pair(
        (factors_4, here, sent_b, (entering_b,), 4),
        (factors_8, 0, sent_a, (entering_a,), 8),
        True,
    )
    inner_b = shared + (x_b, b_rows, c_rows, leaving_all)
    decay_b, grad_b, grad_c = inner(grid, here, half, inner_b, (grad_b, grad_c))

    sent_b, entering_a, got, grad_b = after([sent_b, entering_a, got, grad_b])
    grad_b = head_sum(grad_b)
    grad_inputs = (own.astype(F32) + got.astype(F32)).astype(BF16)
    (entering_b,) = scan_step(factors_8, here, sent_b, (entering_b,), 8, True)
    common = (running_t, grad_out, c_rows)
    state_a = common + (entering_a, states_a, leaving_all, kept, decay_a, grad_c)
    decays, grad_c = state_terms(grid, 0, half, state_a, heads)
    (entering_b,) = after([entering_b], grad_inputs, grad_c)
    state_b = common + (entering_b, states_b, leaving_all, kept, decay_b, grad_c)
    decays, grad_c = state_terms(grid, here, half, state_b, heads, decays)
    return (grad_inputs, grad_b, head_sum(grad_c), decays)


def grad_rows(running, running_t, grad_out, b_rows, c_rows, leaving, skip, transposed):
    length, columns = grad_out.shape
    spec, dims = rows_spec(), (length, columns)
    if transposed:
        spec, dims = pl.BlockSpec((WIDE, SPAN), lambda k, h: (h, k)), (columns, length)
    return call(
        functools.partial(grad_x_kernel, transposed),
        (length // SPAN, running_t.shape[0]),
        [run_spec(), run_t_spec(), rows_spec(), SHARED, SHARED, state_spec(), GAIN],
        spec,
        shape(*dims, dtype=BF16),
        8 * length * columns * SPAN,
        6 * length * columns,
    )(running, running_t, grad_out, b_rows, c_rows, leaving, skip)


def local_plain(inputs, w_in, b_rows, c_rows, log_decay, skip_gain, grad_out):
    length, columns = grad_out.shape
    heads = log_decay.shape[0]
    spans = length // SPAN
    groups = heads // GROUP
    n = b_rows.shape[1]
    grid = (spans, groups)

    sizes = (heads // 2, heads // 4, heads // 4) if heads % (4 * GROUP) == 0 else (heads,)
    weights = gather_weight(w_in, sizes)
    two = lax.axis_size("head") == 2
    place = lax.axis_index("head").astype(jnp.int32)[None]
    width = weights[0].shape[0]
    if two:
        features = (inputs, swap(inputs, "head", 1))
        first = place
    else:
        features = lax.all_gather(inputs, "head", axis=1, tiled=True)
        features = (features[:, : width // 2], features[:, width // 2 :])
        first = jnp.zeros((1,), jnp.int32)

    running, running_t, kept, own_grads = call(
        decay_kernel,
        grid,
        [run_spec(), rows_spec(), SHARED],
        [run_spec(), run_t_spec(), kept_spec(), state_spec()],
        [
            shape(heads, length),
            shape(groups, length, GROUP),
            shape(spans, 8, columns),
            shape(spans, n, columns),
        ],
        2 * length * columns * n,
        6 * length * columns,
    )(log_decay, grad_out, c_rows)

    kept_total = kept[0, :1]
    for k in range(1, spans):
        kept_total = kept_total * kept[k, :1]
    steps = block_products(kept_total)

    total = own_grads[spans - 1]
    for k in range(spans - 2, -1, -1):
        total = own_grads[k] + kept[k, :1] * total
    leaving = [scan_states(total, steps, True)]
    for k in range(spans - 1, 0, -1):
        leaving.insert(0, own_grads[k] + kept[k, :1] * leaving[0])
    leaving = jnp.stack([value.astype(BF16) for value in leaving])

    skip = jnp.repeat(skip_gain, P_SIZE)[None]
    grad_x = grad_rows(running, running_t, grad_out, b_rows, c_rows, leaving, skip, False)

    grad_b = grad_c = product = None
    tokens = ()
    decay_parts = []
    at = 0
    for index, size in enumerate(sizes):
        wide = size * P_SIZE
        here = at // GROUP
        count = size // GROUP
        weight = weights[index]
        if tokens:
            weight = after([weight], *tokens)[0]
        x, own_states = forward(features, first, weight, running_t, b_rows, here)

        chunk = slice(at * P_SIZE, at * P_SIZE + wide)
        total = own_states[0]
        for k in range(1, spans):
            total = kept[k, :1, chunk] * total + own_states[k]
        cut = [step[:2] + tuple(value[:, chunk] for value in step[2:]) for step in steps]
        entering = scan_states(total, cut, False)

        so_far = () if grad_b is None else (grad_b, grad_c)
        decay_part, grad_b, grad_c = call(
            inner_kernel,
            (spans, count),
            [
                run_spec(here),
                run_t_spec(here),
                rows_spec(here),
                rows_spec(),
                SHARED,
                SHARED,
                state_spec(here),
            ]
            + [SHARED] * len(so_far),
            [run_spec(), SHARED, SHARED],
            [shape(size, length), shape(length, n), shape(length, n)],
            12 * length * wide * SPAN,
            6 * length * wide,
            INNER_SCRATCH,
        )(running, running_t, grad_out, x, b_rows, c_rows, leaving, *so_far)
        decay_part, grad_c = call(
            state_kernel,
            (spans, count),
            [
                run_t_spec(here),
                rows_spec(here),
                SHARED,
                pl.BlockSpec((n, WIDE), lambda k, h: (0, h)),
                state_spec(),
                state_spec(here),
                kept_spec(here),
                run_spec(),
                SHARED,
            ],
            [run_spec(), SHARED],
            [shape(size, length), shape(length, n)],
            4 * length * wide * n,
            6 * length * wide,
            [pltpu.VMEM((count, n, WIDE), F32)],
        )(running_t, grad_out, c_rows, entering, own_states, leaving, kept, decay_part, grad_c)
        decay_parts.append(decay_part)

        if index < len(sizes) - 1:
            zero = jnp.zeros((1,), jnp.int32)
            product = multiply(grad_x, weight, at // size, zero, 1, product)
            tokens = (product, grad_b, entering)
        elif two:
            sent = multiply(grad_x, weight, at // size, 1 - place, 2, product)
            got = swap(sent, "head", 1)
            grad_inputs = multiply(grad_x, weight, at // size, place, 2, product, got)
        else:
            zero = jnp.zeros((1,), jnp.int32)
            product = multiply(grad_x, weight, at // size, zero, 1, product)
            grad_inputs = lax.psum_scatter(product, "head", scatter_dimension=1, tiled=True)
        at += size

    return (grad_inputs, head_sum(grad_b), head_sum(grad_c), jnp.concatenate(decay_parts, axis=0))


def solution(mesh):
    in_specs = (
        P("ctx", "head"),
        P("ctx", "head"),
        P("ctx", None),
        P("ctx", None),
        P("head", "ctx"),
        P("head"),
        P("ctx", "head"),
    )
    out_specs = (P("ctx", "head"), P("ctx", None), P("ctx", None), P("head", "ctx"))
    return jax.shard_map(local, mesh=mesh, in_specs=in_specs, out_specs=out_specs, check_vma=False)
```
